32 devices in a mesh: grp: 4 (over y, x), tok: 8 (over z, core).
Axes of the slice: x: 2, y: 2, z: 4, core: 2. Of those that a mesh axis runs over, the one named last changes fastest.
Arguments:
- tokens: float32 [32768, 768], P(('grp', 'tok')), may hold values from -6 to 6
- cotangent: float32 [32768, 768], P(('grp', 'tok')), may hold values from -6 to 6
- crop_lengths: int32 [32, 10], P(('grp', 'tok')), may hold values from 54 to 261, as said below
- master: float32 [7088640], P('tok')
- first_moment: float32 [4, 7088640], P('grp', 'tok')
- second_moment: float32 [4, 7088640], P('grp', 'tok')
- outer_momentum: float32 [7088640], P('tok'), may hold values from -0.4375 to 0.4375
Outputs:
- block_output: float32 [32768, 768], P(('grp', 'tok'))
- input_grad: float32 [32768, 768], P(('grp', 'tok'))
- clip_norm: float32 [4], P('grp')
- vector_grads: float32 [4, 10752], P('grp', 'tok')
- first_moment_new: float32 [4, 7088640], P('grp', 'tok')
- second_moment_new: float32 [4, 7088640], P('grp', 'tok')
- mean_difference: float32 [7088640], P('tok')
- outer_momentum_new: float32 [7088640], P('tok')
- new_weights: float32 [7088640], P('tok')
The draws below stay inside these ranges and needn't reach their ends.
Inputs may be any that keep to these rules, and one draw needn't show every extreme that they name: `crop_lengths`: each row holds, for each of its 1 images, 261 * 2 times and 54 * 8 times, in a drawn order.
All inputs are finite; a program needn't handle non-finite values.
Results may differ from the reference program's by a relative error of at most 0.012.
The reference program's roundings to bfloat16 on the way count: a program that leaves them out, or rounds other values in their place, can miss the bound.
Values may be sent and summed in bfloat16 or wider, within the bound.
A program may use at most 256 MiB of HBM per device.

```python
import jax
import jax.numpy as jnp
from jax import lax

D = 768
HEADS = 12
HEAD_DIM = 64
MLP = 3072
GLOBAL_LEN = 261
LOCAL_LEN = 54
GLOBAL_CROPS = 2
LOCAL_CROPS = 8
IMAGES_DEV = 1
TOK_DEV = 1024
CROPS_DEV = 10
PACKS = 32
GROUPS = 4
TOKENS = 32768
MATRIX_PARAMS = 7077888
PARAMS = 7088640
N_GRP = 4
N_TOK = 8


def draw_crop_lengths(key, part):
    base_row = jnp.array([GLOBAL_LEN] * GLOBAL_CROPS + [LOCAL_LEN] * LOCAL_CROPS, dtype=jnp.int32)
    base_row = jnp.tile(base_row, IMAGES_DEV)
    row_keys = jax.random.split(key, PACKS)
    return jax.vmap(lambda row_key: jax.random.permutation(row_key, base_row))(row_keys).astype(jnp.int32)


def draw_master(key, part):
    owners = PACKS // GROUPS
    key_list = jax.random.split(jax.random.fold_in(key, 11), 15)

    def normal_piece(which_key, length, spread):
        return spread * jax.random.truncated_normal(key_list[which_key], -3.0, 3.0, (length,), jnp.float32)

    def uniform_piece(which_key, length, low_end, high_end):
        return jax.random.uniform(key_list[which_key], (length,), jnp.float32, low_end, high_end)
    members = [normal_piece(0, 3 * D * D, D ** (-0.5)), normal_piece(1, D * D, 6.0 * D ** (-0.5)), normal_piece(2, D * MLP, D ** (-0.5)), normal_piece(3, MLP * D, 1.6 * MLP ** (-0.5)), uniform_piece(4, D, 0.6, 1.4), normal_piece(5, D, 0.1), normal_piece(6, D, 0.1), normal_piece(7, D, 0.1), normal_piece(8, D, 0.1), uniform_piece(9, D, 0.5, 1.5), uniform_piece(10, D, 0.6, 1.4), normal_piece(11, D, 0.1), normal_piece(12, MLP, 0.1), normal_piece(13, D, 0.1), uniform_piece(14, D, 0.5, 1.5)]
    return jnp.concatenate([member.reshape(owners, -1) for member in members], axis=1).reshape(-1)


def gradient_scale():
    owners = PACKS // GROUPS
    per_entry = 3.0 / PARAMS ** 0.5
    column = jnp.arange(PARAMS, dtype=jnp.int32) % (PARAMS // owners)
    return jnp.where(column < (4 * D * D + 2 * D * MLP) // owners, per_entry, 3.0 * per_entry).astype(jnp.float32)


def draw_first_moment(key, part):
    noise = jax.random.normal(jax.random.fold_in(key, 21), (GROUPS, PARAMS), jnp.float32)
    return 0.1 / 0.9 * gradient_scale()[None, :] * noise


def draw_second_moment(key, part):
    factor = jnp.exp(jax.random.uniform(jax.random.fold_in(key, 31), (GROUPS, PARAMS), jnp.float32, jnp.log(0.5), jnp.log(8.0)))
    entry_scale = gradient_scale()
    return 0.001 / 0.999 * factor * (entry_scale * entry_scale)[None, :]


def block_scale(rng, dims, shards, least, high):
    level = 1.0
    for axis_at, parts in shards:
        draws = jax.random.uniform(jax.random.fold_in(jax.random.fold_in(rng, 6), axis_at), (parts,), jnp.float32, least / len(shards), high / len(shards))
        level = level * jnp.repeat(jnp.exp(draws), dims[axis_at] // parts).reshape((-1,) + (1,) * (len(dims) - 1 - axis_at))
    return level


def normal_values(key, shape, scale, reach, pieces=(), kind=jnp.bfloat16):
    factor_of = block_scale(key, shape, pieces, -0.22, 0.18) if pieces else 1.0
    drawn = jax.random.normal(key, shape, jnp.float32) * scale * factor_of
    return jnp.minimum(jnp.maximum(drawn, -reach), reach).astype(kind)


def setup_inputs(seed: int = 0) -> dict:
    seeds = jax.random.split(jax.random.key(seed), 8)
    tokens = normal_values(seeds[0], (TOKENS, D), 1.0, 6.0, ((0, 32),), jnp.float32)
    cotangent = normal_values(seeds[1], (TOKENS, D), 1.0, 6.0, ((0, 32),), jnp.float32)
    crop_lengths = draw_crop_lengths(jax.random.fold_in(seeds[7], 71), 0)
    master = draw_master(jax.random.fold_in(seeds[7], 71), 0)
    first_moment = draw_first_moment(jax.random.fold_in(seeds[7], 71), 0)
    second_moment = draw_second_moment(jax.random.fold_in(seeds[7], 71), 0)
    outer_momentum = normal_values(seeds[6], (PARAMS,), 0.03, 0.4375, ((0, 8),), jnp.float32)
    return dict(tokens=tokens, cotangent=cotangent, crop_lengths=crop_lengths, master=master, first_moment=first_moment, second_moment=second_moment, outer_momentum=outer_momentum)


@jax.custom_vjp
def low(v):
    return lax.optimization_barrier(v.astype(jnp.bfloat16)).astype(jnp.float32)

@jax.custom_vjp
def low_back(v):
    return v

def low_keep(v):
    return (low(v), None)

def low_pass(kept, grad):
    return (grad,)

def back_keep(v):
    return (v, None)

def back_low(kept, grad):
    return (low(grad),)
low.defvjp(low_keep, low_pass)
low_back.defvjp(back_keep, back_low)
clip_limit = 3.0
beta_first = 0.9
beta_second = 0.999
adam_epsilon = 1e-08
weight_decay = 0.04
adam_count = 10.0
base_rate = 0.075
rate_scale = 0.9 ** 6
outer_rate = 0.7
outer_beta = 0.9
norm_epsilon = 1e-06

def matmul(left_side, right_side):
    return jnp.dot(left_side, right_side, precision=lax.Precision.HIGHEST, preferred_element_type=jnp.float32)

def member_extents():
    return [(D, 3 * D), (D, D), (D, MLP), (MLP, D)] + [(D,)] * 8 + [(MLP,), (D,), (D,)]

def split_params(flat_params, owners):
    table = flat_params.reshape(owners, -1)
    members = []
    offset = 0
    for extent in member_extents():
        length = 1
        for member in extent:
            length = length * member
        width = length // owners
        members.append(table[:, offset:offset + width].reshape(extent))
        offset = offset + width
    return members

def join_params(members, owners):
    return jnp.concatenate([member.reshape(owners, -1) for member in members], axis=1).reshape(-1)

def layer_norm(values, norm_gain, norm_shift):
    center = values - lax.optimization_barrier(jnp.mean(values, axis=-1, keepdims=True))
    spread = lax.optimization_barrier(jnp.mean(center * center, axis=-1, keepdims=True))
    return center * lax.rsqrt(spread + norm_epsilon) * norm_gain + norm_shift

def pack_layout(lengths_row, row_count):
    ends_at = jnp.cumsum(lengths_row).astype(jnp.int32)
    position = jnp.arange(row_count, dtype=jnp.int32)
    segment = lax.optimization_barrier(jnp.sum((position[:, None] >= ends_at[None, :]).astype(jnp.int32), axis=1)).astype(jnp.int32)
    validity = (position < ends_at[-1]).astype(jnp.float32)
    return (segment, validity)

def block_forward(inputs, params, segment):
    w_qkv, w_proj, w_fc1, w_fc2, gain_one, shift_one, query_bias, value_bias, proj_bias, scale_one, gain_two, shift_two, fc1_bias, fc2_bias, scale_two = [low(member) for member in params]
    row_count = inputs.shape[0]
    normed = low(layer_norm(inputs, gain_one, shift_one))
    qkv_bias = jnp.concatenate([query_bias, jnp.zeros_like(query_bias), value_bias])
    projected = low(low_back(matmul(normed, w_qkv) + qkv_bias))
    queries = projected[:, :D].reshape(row_count, HEADS, HEAD_DIM)
    keys_all = projected[:, D:2 * D].reshape(row_count, HEADS, HEAD_DIM)
    values_all = projected[:, 2 * D:].reshape(row_count, HEADS, HEAD_DIM)
    raw_scores = jnp.einsum('qhd,khd->hqk', queries, keys_all, precision=lax.Precision.HIGHEST, preferred_element_type=jnp.float32)
    scores = low_back(raw_scores * HEAD_DIM ** (-0.5))
    allowed = segment[:, None] == segment[None, :]
    scores = jnp.where(allowed[None], scores, -1e+30)
    largest = lax.optimization_barrier(jnp.max(scores, axis=-1, keepdims=True))
    weights_exp = jnp.exp(scores - largest)
    weights_soft = weights_exp / lax.optimization_barrier(jnp.sum(weights_exp, axis=-1, keepdims=True))
    attended = jnp.einsum('hqk,khd->qhd', low(weights_soft), values_all, precision=lax.Precision.HIGHEST, preferred_element_type=jnp.float32)
    attended = low(low_back(attended.reshape(row_count, D)))
    branch_one = low_back(matmul(attended, w_proj) + proj_bias)
    middle = inputs + scale_one * branch_one
    normed_two = low(layer_norm(middle, gain_two, shift_two))
    hidden_pre = low_back(matmul(normed_two, w_fc1) + fc1_bias)
    hidden = low(jax.nn.gelu(hidden_pre, approximate=False))
    branch_two = low_back(matmul(hidden, w_fc2) + fc2_bias)
    return middle + scale_two * branch_two

def reference(tokens, cotangent, crop_lengths, master, first_moment, second_moment, outer_momentum):
    params = split_params(master, N_TOK)
    inputs_all = tokens.reshape(N_GRP, N_TOK, TOK_DEV, D)
    backs_all = cotangent.reshape(N_GRP, N_TOK, TOK_DEV, D)
    lengths_all = crop_lengths.reshape(N_GRP, N_TOK, CROPS_DEV)
    decay_mask = (jnp.arange(PARAMS, dtype=jnp.int32) % (PARAMS // N_TOK) < MATRIX_PARAMS // N_TOK).astype(jnp.float32)
    step_rate = base_rate * rate_scale
    vector_root = (N_TOK * TOK_DEV) ** 0.5
    output_list, input_list, norm_list, vector_list, first_list, second_list, differences = ([], [], [], [], [], [], [])
    for group_index in range(N_GRP):

        def one_pack(totals, pack_item):
            inputs, cotangent_pack, lengths_row = pack_item
            segment, validity = pack_layout(lengths_row, TOK_DEV)
            result, pullback = jax.vjp(lambda values, weights: block_forward(values, weights, segment), inputs, params)
            input_grad, param_grads = pullback(cotangent_pack * validity[:, None])
            totals = [summed + addend for summed, addend in zip(totals, param_grads)]
            return (totals, (result, input_grad))
        zero_grads = [jnp.zeros_like(member) for member in params]
        totals, (result, input_grad) = lax.scan(one_pack, zero_grads, (inputs_all[group_index], backs_all[group_index], lengths_all[group_index]))
        output_list.append(result)
        input_list.append(input_grad)
        grad_flat = join_params(totals, N_TOK)
        vector_list.append(grad_flat.reshape(N_TOK, -1)[:, MATRIX_PARAMS // N_TOK:].reshape(-1) / vector_root)
        norm_value = jnp.sqrt(jnp.sum(grad_flat * grad_flat))
        clipped = grad_flat * (clip_limit / (norm_value + 1e-06))
        moment_one = beta_first * first_moment[group_index] + (1.0 - beta_first) * clipped
        moment_two = beta_second * second_moment[group_index] + (1.0 - beta_second) * clipped * clipped
        corrected_one = moment_one / (1.0 - beta_first ** adam_count)
        corrected_two = moment_two / (1.0 - beta_second ** adam_count)
        updated = master - step_rate * (corrected_one / (jnp.sqrt(corrected_two) + adam_epsilon) + weight_decay * decay_mask * master)
        norm_list.append(norm_value)
        first_list.append(moment_one)
        second_list.append(moment_two)
        differences.append(master - updated)
    total_difference = differences[0]
    for member in differences[1:]:
        total_difference = total_difference + member
    mean_difference = total_difference / N_GRP
    outer_new = outer_beta * outer_momentum + mean_difference
    new_weights = master - outer_rate * (mean_difference + outer_beta * outer_new)
    block_output = jnp.stack(output_list).reshape(TOKENS, D)
    input_grad = jnp.stack(input_list).reshape(TOKENS, D)
    return (block_output, input_grad, jnp.stack(norm_list), jnp.stack(vector_list), jnp.stack(first_list), jnp.stack(second_list), mean_difference, outer_new, new_weights)
```

```python
import functools

import jax
import jax.numpy as jnp
from jax import lax
from jax.experimental import pallas as pl
from jax.experimental.pallas import tpu as pltpu

from jax.sharding import PartitionSpec as P

D = 768
MLP = 3072
HEADS = 12
HEAD_DIM = 64


clip_limit = 3.0
beta_first = 0.9
beta_second = 0.999
adam_epsilon = 1e-08
weight_decay = 0.04
adam_count = 10.0
base_rate = 0.075
rate_scale = 0.9**6
outer_rate = 0.7
outer_beta = 0.9
norm_epsilon = 1e-06


def member_extents():
    return [(D, 3 * D), (D, D), (D, MLP), (MLP, D)] + [(D,)] * 8 + [(MLP,), (D,), (D,)]


def member_sizes():
    sizes_list = []
    for extent in member_extents():
        length = 1
        for member in extent:
            length = length * member
        sizes_list.append(length)
    return sizes_list


def split_params(flat_params, owners):
    table = flat_params.reshape(owners, -1)
    members = []
    offset = 0
    for extent, length in zip(member_extents(), member_sizes()):
        width = length // owners
        members.append(table[:, offset : offset + width].reshape(extent))
        offset = offset + width
    return members


def join_table(members, owners):
    return jnp.concatenate([member.reshape(owners, -1) for member in members], axis=1)


def layer_norm(values, norm_gain, norm_shift):
    center = values - jnp.mean(values, axis=-1, keepdims=True)
    spread = jnp.mean(center * center, axis=-1, keepdims=True)
    return center * lax.rsqrt(spread + norm_epsilon) * norm_gain + norm_shift


def pack_layout(lengths_row, row_count):
    ends_at = jnp.cumsum(lengths_row)
    position = jnp.arange(row_count, dtype=jnp.int32)
    segment = jnp.sum((position[:, None] >= ends_at[None, :]).astype(jnp.int32), axis=1)
    validity = (position < ends_at[-1]).astype(jnp.float32)
    return (segment, validity)


def cross_rows(left_side, right_side):
    return lax.dot_general(
        left_side, right_side, (((0,), (0,)), ((), ())), preferred_element_type=jnp.float32
    )


def times_transposed(left_side, right_side):
    return lax.dot_general(
        left_side, right_side, (((1,), (1,)), ((), ())), preferred_element_type=jnp.float32
    )


def on_device(tokens, cotangent, crop_lengths, master, first_moment, second_moment, outer_momentum):
    row_count = tokens.shape[0]
    pair_count = HEADS // 2
    score_scale = HEAD_DIM ** (-0.5)
    owners = lax.axis_size("tok")
    segment, validity = pack_layout(crop_lengths[0], row_count)
    allowed = segment[:, None] == segment[None, :]
    master_low = master.astype(jnp.bfloat16)
    gathered = split_params(lax.all_gather(master_low, "tok", axis=0, tiled=True), owners)
    w_qkv, w_proj, w_fc1, w_fc2 = gathered[:4]
    (
        gain_one,
        shift_one,
        query_bias,
        value_bias,
        proj_bias,
        scale_one,
        gain_two,
        shift_two,
        fc1_bias,
        fc2_bias,
        scale_two,
    ) = [member.astype(jnp.float32) for member in gathered[4:]]

    def to_pairs(block_cols):
        return jnp.moveaxis(block_cols.reshape(row_count, pair_count, 2 * HEAD_DIM), 1, 0)

    def from_pairs(paired):
        return jnp.moveaxis(paired, 0, 1).reshape(row_count, D)

    normed = layer_norm(tokens, gain_one, shift_one).astype(jnp.bfloat16)
    qkv_bias = jnp.concatenate([query_bias, jnp.zeros_like(query_bias), value_bias])
    projected = (jnp.dot(normed, w_qkv, preferred_element_type=jnp.float32) + qkv_bias).astype(
        jnp.bfloat16
    )
    query_pairs = to_pairs(projected[:, :D])
    key_pairs = to_pairs(projected[:, D : 2 * D])
    value_pairs = to_pairs(projected[:, 2 * D :])

    def forward_pair(pair_item):
        queries, keys_pair, values_pair = [
            member.reshape(row_count, 2, HEAD_DIM) for member in pair_item
        ]
        raw_scores = jnp.einsum(
            "qhd,khd->hqk", queries, keys_pair, preferred_element_type=jnp.float32
        )
        scores = jnp.where(allowed[None], raw_scores * score_scale, -1e30)
        largest = jnp.max(scores, axis=-1, keepdims=True)
        weights_exp = jnp.exp(scores - largest)
        totals = jnp.sum(weights_exp, axis=-1, keepdims=True)
        weights_low = (weights_exp / totals).astype(jnp.bfloat16)
        attended_pair = jnp.einsum(
            "hqk,khd->qhd", weights_low, values_pair, preferred_element_type=jnp.float32
        )
        return (attended_pair.reshape(row_count, 2 * HEAD_DIM), (largest + jnp.log(totals))[..., 0])

    attended_pairs, log_totals = lax.map(forward_pair, (query_pairs, key_pairs, value_pairs))
    attended = from_pairs(attended_pairs).astype(jnp.bfloat16)
    branch_one = jnp.dot(attended, w_proj, preferred_element_type=jnp.float32) + proj_bias
    middle = tokens + scale_one * branch_one
    normed_two = layer_norm(middle, gain_two, shift_two).astype(jnp.bfloat16)
    hidden_pre = jnp.dot(normed_two, w_fc1, preferred_element_type=jnp.float32) + fc1_bias
    hidden = jax.nn.gelu(hidden_pre, approximate=False).astype(jnp.bfloat16)
    branch_two = jnp.dot(hidden, w_fc2, preferred_element_type=jnp.float32) + fc2_bias
    block_output = middle + scale_two * branch_two
    back_out = cotangent * validity[:, None]
    grad_branch_two = (scale_two * back_out).astype(jnp.bfloat16)
    grad_scale_two = jnp.sum(back_out * branch_two, axis=0)
    grad_fc2_bias = jnp.sum(grad_branch_two.astype(jnp.float32), axis=0)
    grad_w_fc2 = cross_rows(hidden, grad_branch_two)
    grad_hidden = times_transposed(grad_branch_two, w_fc2)
    gelu_pull = jax.vjp(lambda values: jax.nn.gelu(values, approximate=False), hidden_pre)[1]
    grad_pre = gelu_pull(grad_hidden)[0].astype(jnp.bfloat16)
    grad_fc1_bias = jnp.sum(grad_pre.astype(jnp.float32), axis=0)
    grad_w_fc1 = cross_rows(normed_two, grad_pre)
    grad_normed_two = times_transposed(grad_pre, w_fc1)
    norm_pull = jax.vjp(layer_norm, middle, gain_two, shift_two)[1]
    grad_middle_part, grad_gain_two, grad_shift_two = norm_pull(grad_normed_two)
    grad_middle = back_out + grad_middle_part
    grad_scale_one = jnp.sum(grad_middle * branch_one, axis=0)
    grad_branch_one = (scale_one * grad_middle).astype(jnp.bfloat16)
    grad_proj_bias = jnp.sum(grad_branch_one.astype(jnp.float32), axis=0)
    grad_w_proj = cross_rows(attended, grad_branch_one)
    grad_attended = times_transposed(grad_branch_one, w_proj).astype(jnp.bfloat16)

    def backward_pair(pair_item):
        queries, keys_pair, values_pair, grad_pair = [
            member.reshape(row_count, 2, HEAD_DIM) for member in pair_item[:4]
        ]
        log_total = pair_item[4]
        raw_scores = jnp.einsum(
            "qhd,khd->hqk", queries, keys_pair, preferred_element_type=jnp.float32
        )
        scores = jnp.where(allowed[None], raw_scores * score_scale, -1e30)
        weights_soft = jnp.exp(scores - log_total[..., None])
        grad_values = jnp.einsum(
            "hqk,qhd->khd",
            weights_soft.astype(jnp.bfloat16),
            grad_pair,
            preferred_element_type=jnp.float32,
        )
        grad_weights = jnp.einsum(
            "qhd,khd->hqk", grad_pair, values_pair, preferred_element_type=jnp.float32
        )
        row_dot = jnp.sum(weights_soft * grad_weights, axis=-1, keepdims=True)
        grad_scores = (weights_soft * (grad_weights - row_dot)).astype(jnp.bfloat16)
        grad_queries = (
            jnp.einsum("hqk,khd->qhd", grad_scores, keys_pair, preferred_element_type=jnp.float32)
            * score_scale
        )
        grad_keys = (
            jnp.einsum("hqk,qhd->khd", grad_scores, queries, preferred_element_type=jnp.float32)
            * score_scale
        )
        return (
            grad_queries.reshape(row_count, 2 * HEAD_DIM),
            grad_keys.reshape(row_count, 2 * HEAD_DIM),
            grad_values.reshape(row_count, 2 * HEAD_DIM),
        )

    grad_q_pairs, grad_k_pairs, grad_v_pairs = lax.map(
        backward_pair, (query_pairs, key_pairs, value_pairs, to_pairs(grad_attended), log_totals)
    )
    grad_projected = jnp.concatenate(
        [from_pairs(grad_q_pairs), from_pairs(grad_k_pairs), from_pairs(grad_v_pairs)], axis=1
    ).astype(jnp.bfloat16)
    grad_query_bias = jnp.sum(grad_projected[:, :D].astype(jnp.float32), axis=0)
    grad_value_bias = jnp.sum(grad_projected[:, 2 * D :].astype(jnp.float32), axis=0)
    grad_w_qkv = cross_rows(normed, grad_projected)
    grad_normed = times_transposed(grad_projected, w_qkv)
    first_pull = jax.vjp(layer_norm, tokens, gain_one, shift_one)[1]
    grad_tokens_part, grad_gain_one, grad_shift_one = first_pull(grad_normed)
    input_grad = grad_middle + grad_tokens_part
    all_members = [
        grad_w_qkv,
        grad_w_proj,
        grad_w_fc1,
        grad_w_fc2,
        grad_gain_one,
        grad_shift_one,
        grad_query_bias,
        grad_value_bias,
        grad_proj_bias,
        grad_scale_one,
        grad_gain_two,
        grad_shift_two,
        grad_fc1_bias,
        grad_fc2_bias,
        grad_scale_two,
    ]
    received = lax.all_to_all(
        join_table(all_members, owners).astype(jnp.bfloat16),
        "tok",
        split_axis=0,
        concat_axis=0,
        tiled=True,
    ).astype(jnp.float32)
    summed = jnp.sum(received, axis=0)
    matrix_width = (4 * D * D + 2 * D * MLP) // owners
    vector_part = summed[matrix_width:] / (owners * row_count) ** 0.5
    square_total = lax.psum(jnp.sum(summed * summed), "tok")
    norm_value = jnp.sqrt(square_total)
    clipped = summed * (clip_limit / (norm_value + 1e-06))
    moment_one = beta_first * first_moment[0] + (1.0 - beta_first) * clipped
    moment_two = beta_second * second_moment[0] + (1.0 - beta_second) * clipped * clipped
    corrected_one = moment_one / (1.0 - beta_first**adam_count)
    corrected_two = moment_two / (1.0 - beta_second**adam_count)
    shard_size = master.shape[0]
    local_index = jnp.arange(shard_size, dtype=jnp.int32)
    decay_mask = (local_index < matrix_width).astype(jnp.float32)
    step_rate = base_rate * rate_scale
    updated = master - step_rate * (
        corrected_one / (jnp.sqrt(corrected_two) + adam_epsilon)
        + weight_decay * decay_mask * master
    )
    mean_difference = lax.psum((master - updated).astype(jnp.bfloat16), "grp").astype(
        jnp.float32
    ) / lax.axis_size("grp")
    outer_new = outer_beta * outer_momentum + mean_difference
    new_weights = master - outer_rate * (mean_difference + outer_beta * outer_new)
    return (
        block_output,
        input_grad,
        norm_value.reshape(1),
        vector_part[None],
        moment_one[None],
        moment_two[None],
        mean_difference,
        outer_new,
        new_weights,
    )


ROWS = D // 8
ANY = pl.BlockSpec(memory_space=pl.ANY)
DMA = pltpu.SemaphoreType.DMA
MESH_ID = pl.DeviceIdType.MESH
NZ = 4


def place():
    g = lax.axis_index("grp")
    t = lax.axis_index("tok")
    z, c = lax.div(t, 2), lax.rem(t, 2)
    gx = g + 1 - 2 * lax.rem(g, 2)
    gy = g + 2 - 4 * lax.div(g, 2)
    return g, t, z, c, gx, gy


def greet(targets, count):
    barrier = pltpu.get_barrier_semaphore()
    for target in targets:
        pl.semaphore_signal(barrier, inc=1, device_id=target, device_id_type=MESH_ID)
    pl.semaphore_wait(barrier, count)


def remote(src, dst, send, recv, target):
    return pltpu.make_async_remote_copy(
        src_ref=src, dst_ref=dst, send_sem=send, recv_sem=recv,
        device_id=target, device_id_type=MESH_ID,
    )


def rows_at(ref, start, count):
    return ref.at[pl.ds(pl.multiple_of(start, 16), count), :]


def weight_strip(w, ref, t):
    return rows_at(ref, t * (384 if w == 2 else 96), 384 if w == 2 else 96)


def weight_block(w, ref, t, q, half=None):
    lead, count = (0, 96) if half is None else (48 * half, 48)
    if w == 2:
        return rows_at(ref, t * 384 + q * 96 + lead, count)
    return ref.at[
        pl.ds(pl.multiple_of(t * 96 + lead, 16), count),
        pl.ds(pl.multiple_of(q * 768, 768), 768),
    ]


def piece_block(w, ref, q):
    return weight_block(w, ref, 0, q)


def gather_kernel(pa, pb, pc, pv, wa, wb, wc, wv, ls, zs, zr, xs, xr, ys, yr, ds, dr, cs, cr, vs, vr):
    g, t, z, c, gx, gy = place()
    pieces, fulls = (pa, pb, pc), (wa, wb, wc)
    peers = [lax.rem(t + k, 8) for k in range(1, 8)]
    greet([(g, p) for p in peers] + [(gx, t), (gy, t)], 9)
    other = t + 1 - 2 * c

    def z_copy(w, d, s):
        step = 1 if d == 0 else -1
        src_t = t - 2 * step * s
        src = piece_block(w, pieces[w], g) if s == 0 else weight_block(w, fulls[w], src_t, g)
        ok = (z - s >= 0) & (z + 1 < NZ) if d == 0 else (z + s < NZ) & (z - 1 >= 0)
        return ok, remote(src, weight_block(w, fulls[w], src_t, g), zs.at[w, d, s], zr.at[w, d, s], (g, t + 2 * step))

    def from_t(d, s):
        return t - 2 * (s + 1) if d == 0 else t + 2 * (s + 1)

    def here(d, s):
        return z - s - 1 >= 0 if d == 0 else z + s + 1 < NZ

    def z_wait(w, d, s):
        blk = weight_block(w, fulls[w], from_t(d, s), g)
        remote(blk, blk, zs.at[w, d, s], zr.at[w, d, s], (g, other)).wait_recv()

    def side_copy(w, d, s, axis):
        blk = weight_block(w, fulls[w], from_t(d, s), g)
        sems = (xs, xr) if axis == 0 else (ys, yr)
        return remote(blk, blk, sems[0].at[w, d, s], sems[1].at[w, d, s], (gx if axis == 0 else gy, t))

    def side_wait(w, d, s, axis):
        blk = weight_block(w, fulls[w], from_t(d, s), gx if axis == 0 else gy)
        sems = (xs, xr) if axis == 0 else (ys, yr)
        remote(blk, blk, sems[0].at[w, d, s], sems[1].at[w, d, s], (gx, t)).wait_recv()

    def diag_copy(w, d, s, axis):
        blk = weight_block(w, fulls[w], from_t(d, s), gx if axis == 0 else gy, axis)
        return remote(blk, blk, ds.at[w, d, s, axis], dr.at[w, d, s, axis], (gy if axis == 0 else gx, t))

    def diag_wait(w, d, s, axis):
        blk = weight_block(w, fulls[w], from_t(d, s), 3 - g, axis)
        remote(blk, blk, ds.at[w, d, s, axis], dr.at[w, d, s, axis], (gx, t)).wait_recv()

    def core_copy(w, d, s):
        blk = weight_strip(w, fulls[w], from_t(d, s))
        return remote(blk, blk, cs.at[w, d, s], cr.at[w, d, s], (g, other))

    def core_wait(w, d, s):
        blk = weight_strip(w, fulls[w], from_t(d, s) + 1 - 2 * c)
        remote(blk, blk, cs.at[w, d, s], cr.at[w, d, s], (g, other)).wait_recv()

    def own_copy(w):
        return remote(pieces[w], weight_strip(w, fulls[w], t), cs.at[w, 2, 0], cr.at[w, 2, 0], (g, other))

    def both(s, fn):
        for d in (0, 1):
            @pl.when(here(d, s))
            def _():
                fn(d)

    def start_z(w, s):
        for d in (0, 1):
            ok, copy = z_copy(w, d, s)

            @pl.when(ok)
            def _():
                copy.start()

    local_v = pltpu.make_async_copy(pv, wv.at[t], ls.at[3])
    local_v.start()
    v_copies = [remote(pv, wv.at[t], vs.at[k], vr.at[k], (g, peers[k])) for k in range(7)]
    for copy in v_copies:
        copy.start()
    start_z(0, 0)
    locals_ = [pltpu.make_async_copy(pieces[w], weight_strip(w, fulls[w], t), ls.at[w]) for w in range(3)]
    for copy in locals_:
        copy.start()
    own_copy(0).start()

    def arrive(w, s):
        def fn(d):
            z_wait(w, d, s)
        both(s, fn)
        if s < 2:
            start_z(w, s + 1)

        def sides(d):
            side_copy(w, d, s, 0).start()
            side_copy(w, d, s, 1).start()
        both(s, sides)

    def cross(w, s):
        def fn(d):
            for axis in (0, 1):
                side_wait(w, d, s, axis)
                diag_copy(w, d, s, axis).start()
        both(s, fn)

    def finish(w, s):
        def fn(d):
            diag_wait(w, d, s, 0)
            diag_wait(w, d, s, 1)
            core_copy(w, d, s).start()
        both(s, fn)

    for n in range(9):
        w, s = divmod(n, 3)
        arrive(w, s)
        if s == 0 and w < 2:
            start_z(w + 1, 0)
            own_copy(w + 1).start()
        if n >= 2:
            cross((n - 2) // 3, (n - 2) % 3)
        if n >= 3:
            finish((n - 3) // 3, (n - 3) % 3)
    cross(2, 1)
    finish(2, 0)
    cross(2, 2)
    finish(2, 1)
    finish(2, 2)
    for k in range(7):
        remote(pv, wv.at[lax.rem(t + 7 - k, 8)], vs.at[k], vr.at[k], (g, peers[k])).wait_recv()
        v_copies[k].wait_send()
    local_v.wait()
    for w in range(3):
        locals_[w].wait()
        blk = weight_strip(w, fulls[w], other)
        remote(pieces[w], blk, cs.at[w, 2, 0], cr.at[w, 2, 0], (g, other)).wait_recv()
        own_copy(w).wait_send()
        for s in range(3):
            for d in (0, 1):
                ok, copy = z_copy(w, d, s)

                @pl.when(ok)
                def _():
                    copy.wait_send()

            def fn(d):
                core_wait(w, d, s)
                side_copy(w, d, s, 0).wait_send()
                side_copy(w, d, s, 1).wait_send()
                diag_copy(w, d, s, 0).wait_send()
                diag_copy(w, d, s, 1).wait_send()
                core_copy(w, d, s).wait_send()
            both(s, fn)


def gather_weights(pa, pb, pc, pv):
    return pl.pallas_call(
        gather_kernel,
        name="gather_weights",
        out_shape=[
            jax.ShapeDtypeStruct((D, 4 * D), jnp.bfloat16),
            jax.ShapeDtypeStruct((D, MLP), jnp.bfloat16),
            jax.ShapeDtypeStruct((MLP, D), jnp.bfloat16),
            jax.ShapeDtypeStruct((8, 16, 128), jnp.float32),
        ],
        in_specs=[ANY] * 4,
        out_specs=[ANY] * 4,
        scratch_shapes=[
            DMA((4,)),
            DMA((3, 2, 3)), DMA((3, 2, 3)),
            DMA((3, 2, 3)), DMA((3, 2, 3)),
            DMA((3, 2, 3)), DMA((3, 2, 3)),
            DMA((3, 2, 3, 2)), DMA((3, 2, 3, 2)),
            DMA((3, 3, 3)), DMA((3, 3, 3)),
            DMA((7,)), DMA((7,)),
        ],
        compiler_params=pltpu.CompilerParams(collective_id=0, has_side_effects=True),
    )(pa, pb, pc, pv)


def scatter_kernel(ga, gb, gc, gv, sa, sb, sc, sv, sq, own_ab, own_c, core_ab, core_c, z_ab, z_c, vbuf, qbuf, ls, cs, cr, zs, zr, vs, vr, qs, qr):
    g, t, z, c, gx, gy = place()
    peers = [lax.rem(t + k, 8) for k in range(1, 8)]
    greet([(g, p) for p in peers], 7)
    other = t + 1 - 2 * c
    grads = (ga, gb, gc)
    order = (2, 1, 0)
    own = (own_ab.at[0], own_ab.at[1], own_c)
    core = (core_ab.at[0], core_ab.at[1], core_c)
    zbuf = (z_ab.at[0], z_ab.at[1], z_c)

    def core_copy(w, k):
        return remote(weight_strip(w, grads[w], 2 * k + 1 - c), core[w].at[k], cs.at[w, k], cr.at[w, k], (g, other))

    def load(w, k):
        return pltpu.make_async_copy(weight_strip(w, grads[w], 2 * k + c), own[w].at[k], ls.at[w, k])

    v_copies = [remote(gv.at[peers[k]], vbuf.at[k], vs.at[k], vr.at[k], (g, peers[k])) for k in range(7)]
    by_need = (3, 0, 2, 1)
    for w in order:
        for k in by_need:
            core_copy(w, k).start()
            load(w, k).start()
        if w == 2:
            for copy in v_copies:
                copy.start()

    def half_at(w, h):
        n = 192 if w == 2 else 48
        return pl.ds(h * n, n)

    def add_rows(w, k, h, extra, out=None):
        rows = 192 if w == 2 else 48
        chunk = 64 if w == 2 else 16

        def body(i, _):
            at = pl.ds(pl.multiple_of(h * rows + i * chunk, chunk), chunk)
            total = own[w][k, at, :].astype(jnp.float32) + core[w][k, at, :].astype(jnp.float32)
            for d in extra:
                total = total + zbuf[w][d, k, at, :].astype(jnp.float32)
            if out is None:
                own[w][k, at, :] = total.astype(jnp.bfloat16)
            else:
                out[at, :] = total
            return 0
        lax.fori_loop(0, rows // chunk, body, 0)

    def z_copy(w, d, k, h):
        step = 2 if d == 0 else -2
        at = half_at(w, h)
        return remote(
            own[w].at[k, at, :], zbuf[w].at[d, k, at, :], zs.at[w, d, k, h], zr.at[w, d, k, h], (g, t + step)
        )

    def z_wait(w, d, k, h):
        z_copy(w, d, k, h).wait_recv()

    def ready(w, k):
        load(w, k).wait()
        core_copy(w, k).wait_recv()

    def pass_on(i, d, j, h):
        w = order[i]
        reach = NZ - 1 - z if d == 0 else z
        k = z + j if d == 0 else z - j
        first = z == 0 if d == 0 else z == NZ - 1

        @pl.when(j <= reach)
        def _():
            if h == 0:
                ready(w, k)

            @pl.when(first)
            def _():
                add_rows(w, k, h, ())

            @pl.when(jnp.logical_not(first))
            def _():
                z_wait(w, d, k, h)
                add_rows(w, k, h, (d,))

            if i > 0:
                @pl.when(j == reach)
                def _():
                    z_copy(order[i - 1], d, z + 1 if d == 0 else z - 1, h).wait_send()
            if j < NZ - 1:
                @pl.when(j < reach)
                def _():
                    z_copy(w, d, k + 1 if d == 0 else k - 1, h).wait_send()
            z_copy(w, d, k, h).start()

    outs = (sa, sb, sc)

    def settle(w):
        for k in range(NZ):
            @pl.when(z == k)
            def _():
                ready(w, k)
                dirs = [d for d in (0, 1) if not (d == 0 and k == 0) and not (d == 1 and k == NZ - 1)]
                for h in (0, 1):
                    for d in dirs:
                        z_wait(w, d, k, h)
                    add_rows(w, k, h, dirs, outs[w])

    for i, w in enumerate(order):
        for j in (3, 2, 1):
            for h in (0, 1):
                pass_on(i, 0, j, h)
                pass_on(i, 1, j, h)
        if i:
            settle(order[i - 1])
    settle(order[-1])
    sv[...] = gv[t]
    for k in range(7):
        remote(gv.at[t], vbuf.at[k], vs.at[k], vr.at[k], (g, peers[k])).wait_recv()
    for k in range(7):
        sv[...] += vbuf[k]

    def square(ref, rows):
        def body(i, acc):
            v = ref[pl.ds(pl.multiple_of(i * 8, 8), 8), :]
            return acc + v * v
        acc = lax.fori_loop(0, rows // 8, body, jnp.zeros((8, ref.shape[1]), jnp.float32))
        return jnp.sum(acc)
    total = square(sa, 96) + square(sb, 96) + square(sc, 384) + jnp.sum(sv[...] * sv[...])
    qbuf[7] = jnp.full((8, 128), total, jnp.float32)
    q_copies = [remote(qbuf.at[7], qbuf.at[k], qs.at[k], qr.at[k], (g, peers[k])) for k in range(7)]
    for copy in q_copies:
        copy.start()
    for k in range(7):
        q_copies[k].wait_recv()
    acc = qbuf[7]
    for k in range(7):
        acc = acc + qbuf[k]
    sq[...] = acc
    for k in range(7):
        q_copies[k].wait_send()
        v_copies[k].wait_send()
    for w in order:
        for k in range(NZ):
            core_copy(w, k).wait_send()
    for h in (0, 1):
        @pl.when(z < NZ - 1)
        def _():
            z_copy(order[-1], 0, z + 1, h).wait_send()

        @pl.when(z > 0)
        def _():
            z_copy(order[-1], 1, z - 1, h).wait_send()


def scatter_grads(ga, gb, gc, gv):
    vm = pl.BlockSpec(memory_space=pltpu.VMEM)
    return pl.pallas_call(
        scatter_kernel,
        name="scatter_grads",
        out_shape=[
            jax.ShapeDtypeStruct((ROWS, 4 * D), jnp.float32),
            jax.ShapeDtypeStruct((ROWS, MLP), jnp.float32),
            jax.ShapeDtypeStruct((4 * ROWS, D), jnp.float32),
            jax.ShapeDtypeStruct((16, 128), jnp.float32),
            jax.ShapeDtypeStruct((8, 128), jnp.float32),
        ],
        in_specs=[ANY] * 3 + [vm],
        out_specs=[vm] * 5,
        scratch_shapes=[
            pltpu.VMEM((2, NZ, ROWS, MLP), jnp.bfloat16),
            pltpu.VMEM((NZ, 4 * ROWS, D), jnp.bfloat16),
            pltpu.VMEM((2, NZ, ROWS, MLP), jnp.bfloat16),
            pltpu.VMEM((NZ, 4 * ROWS, D), jnp.bfloat16),
            pltpu.VMEM((2, 2, NZ, ROWS, MLP), jnp.bfloat16),
            pltpu.VMEM((2, NZ, 4 * ROWS, D), jnp.bfloat16),
            pltpu.VMEM((7, 16, 128), jnp.float32),
            pltpu.VMEM((8, 8, 128), jnp.float32),
            DMA((3, NZ)), DMA((3, NZ)), DMA((3, NZ)),
            DMA((3, 2, NZ, 2)), DMA((3, 2, NZ, 2)),
            DMA((7,)), DMA((7,)), DMA((7,)), DMA((7,)),
        ],
        compiler_params=pltpu.CompilerParams(
            collective_id=1, has_side_effects=True, vmem_limit_bytes=60 * 2**20
        ),
    )(ga, gb, gc, gv)


SUM_ROWS = 7040
SUM_H, SUM_Q, SUM_E = SUM_ROWS // 2, SUM_ROWS // 4, SUM_ROWS // 8


def mean_kernel(diff, out, part, mid, buf, ss, rs):
    g, t, z, c, gx, gy = place()
    greet([(gx, t), (gy, t)], 2)
    xi, yi = lax.rem(g, 2), lax.div(g, 2)
    hop = [((gx, t), (gy, t)), ((gy, t), (gx, t))]
    mine = [(xi, yi), (yi, xi)]

    def copies(h):
        a, b = mine[h]
        base = h * SUM_H
        sent = rows_at(diff, base + (1 - a) * SUM_Q, SUM_Q)
        one = remote(sent, part.at[h], ss.at[h, 0], rs.at[h, 0], hop[h][0])
        two = remote(rows_at(mid.at[h], (1 - b) * SUM_E, SUM_E), buf.at[h], ss.at[h, 1], rs.at[h, 1], hop[h][1])
        done = rows_at(out, base + a * SUM_Q + b * SUM_E, SUM_E)
        three = remote(done, done, ss.at[h, 2], rs.at[h, 2], hop[h][1])
        whole = rows_at(out, base + a * SUM_Q, SUM_Q)
        four = remote(whole, whole, ss.at[h, 3], rs.at[h, 3], hop[h][0])
        return one, two, three, four

    steps = [copies(0), copies(1)]
    chunk = 80

    def at(lo, i):
        return pl.ds(pl.multiple_of(lo + i * chunk, 16), chunk)

    for h in (0, 1):
        steps[h][0].start()
    for h in (0, 1):
        a, b = mine[h]
        steps[h][0].wait_recv()
        lo, src = (1 - b) * SUM_E, h * SUM_H + a * SUM_Q + (1 - b) * SUM_E

        def first(i, _):
            total = diff[at(src, i), :].astype(jnp.float32) + part[h, at(lo, i), :].astype(jnp.float32)
            mid[h, at(lo, i), :] = total.astype(jnp.bfloat16)
            return 0
        lax.fori_loop(0, SUM_E // chunk, first, 0)
        steps[h][1].start()
    for h in (0, 1):
        a, b = mine[h]
        steps[h][1].wait_recv()
        lo, src = b * SUM_E, h * SUM_H + a * SUM_Q + b * SUM_E

        def second(i, _):
            total = diff[at(src, i), :].astype(jnp.float32) + part[h, at(lo, i), :].astype(jnp.float32)
            total = total + buf[h, at(0, i), :].astype(jnp.float32)
            out[at(src, i), :] = (total * 0.25).astype(jnp.bfloat16)
            return 0
        lax.fori_loop(0, SUM_E // chunk, second, 0)
        steps[h][2].start()
    for h in (0, 1):
        a, b = mine[h]
        other = rows_at(out, h * SUM_H + a * SUM_Q + (1 - b) * SUM_E, SUM_E)
        remote(other, other, ss.at[h, 2], rs.at[h, 2], hop[h][1]).wait_recv()
        steps[h][2].wait_send()
        steps[h][3].start()
    for h in (0, 1):
        a, b = mine[h]
        other = rows_at(out, h * SUM_H + (1 - a) * SUM_Q, SUM_Q)
        remote(other, other, ss.at[h, 3], rs.at[h, 3], hop[h][0]).wait_recv()
        steps[h][0].wait_send()
        steps[h][1].wait_send()
        steps[h][3].wait_send()


def mean_groups(diff):
    vm = pl.BlockSpec(memory_space=pltpu.VMEM)
    return pl.pallas_call(
        mean_kernel,
        name="mean_groups",
        out_shape=jax.ShapeDtypeStruct((SUM_ROWS, 128), jnp.bfloat16),
        in_specs=[vm],
        out_specs=vm,
        scratch_shapes=[
            pltpu.VMEM((2, SUM_Q, 128), jnp.bfloat16),
            pltpu.VMEM((2, SUM_Q, 128), jnp.bfloat16),
            pltpu.VMEM((2, SUM_E, 128), jnp.bfloat16),
            DMA((2, 4)), DMA((2, 4)),
        ],
        compiler_params=pltpu.CompilerParams(collective_id=2, has_side_effects=True),
    )(diff)


MATRIX_WIDTH = (4 * D * D + 2 * D * MLP) // 8


def vector_piece(flat):
    return jnp.pad(flat.reshape(14, ROWS), ((0, 2), (0, 128 - ROWS)))


def split_vectors(wv):
    parts = wv[:, :14, :ROWS]
    singles = [parts[:, j].reshape(-1) for j in (0, 1, 2, 3, 4, 5, 6, 7, 12, 13)]
    return singles[:8] + [parts[:, 8:12].reshape(-1)] + singles[8:]


def join_vectors(vectors):
    rows = [v.reshape(8, -1, ROWS) for v in vectors]
    return jnp.pad(jnp.concatenate(rows, axis=1), ((0, 0), (0, 2), (0, 128 - ROWS)))


def own_pieces(master):
    def piece(offset, rows, cols):
        return master[offset : offset + rows * cols].reshape(rows, cols).astype(jnp.bfloat16)

    size = ROWS * D
    pa = jnp.concatenate([piece(0, ROWS, 3 * D), piece(3 * size, ROWS, D)], axis=1)
    pb = piece(4 * size, ROWS, MLP)
    pc = piece(8 * size, 4 * ROWS, D)
    pv = vector_piece(master[MATRIX_WIDTH:].astype(jnp.bfloat16).astype(jnp.float32))
    return pa, pb, pc, pv


def flat_grads(sa, sb, sc, sv):
    return jnp.concatenate(
        [
            sa[:, : 3 * D].reshape(-1),
            sa[:, 3 * D :].reshape(-1),
            sb.reshape(-1),
            sc.reshape(-1),
            sv[:14, :ROWS].reshape(-1),
        ]
    )


def optimizer(summed, norm_value, master, first_moment, second_moment, outer_momentum):
    clipped = summed * (clip_limit / (norm_value + 1e-06))
    moment_one = beta_first * first_moment[0] + (1.0 - beta_first) * clipped
    moment_two = beta_second * second_moment[0] + (1.0 - beta_second) * clipped * clipped
    corrected_one = moment_one / (1.0 - beta_first**adam_count)
    corrected_two = moment_two / (1.0 - beta_second**adam_count)
    decay_mask = (jnp.arange(master.shape[0], dtype=jnp.int32) < MATRIX_WIDTH).astype(jnp.float32)
    step_rate = base_rate * rate_scale
    difference = step_rate * (
        corrected_one / (jnp.sqrt(corrected_two) + adam_epsilon)
        + weight_decay * decay_mask * master
    )
    low = jnp.pad(difference.astype(jnp.bfloat16), (0, SUM_ROWS * 128 - master.shape[0]))
    mean_difference = mean_groups(low.reshape(SUM_ROWS, 128)).reshape(-1)[: master.shape[0]]
    mean_difference = mean_difference.astype(jnp.float32)
    outer_new = outer_beta * outer_momentum + mean_difference
    new_weights = master - outer_rate * (mean_difference + outer_beta * outer_new)
    return moment_one, moment_two, mean_difference, outer_new, new_weights


def on_small_slice(tokens, cotangent, crop_lengths, master, first_moment, second_moment, outer_momentum):
    row_count = tokens.shape[0]
    pair_count = HEADS // 2
    score_scale = HEAD_DIM ** (-0.5)
    segment, validity = pack_layout(crop_lengths[0], row_count)
    allowed = segment[:, None] == segment[None, :]
    wa, w_fc1, w_fc2, wv = gather_weights(*own_pieces(master))
    w_qkv, w_proj = wa[:, : 3 * D], wa[:, 3 * D :]
    (
        gain_one,
        shift_one,
        query_bias,
        value_bias,
        proj_bias,
        scale_one,
        gain_two,
        shift_two,
        fc1_bias,
        fc2_bias,
        scale_two,
    ) = split_vectors(wv)
    def to_pairs(block_cols):
        return jnp.moveaxis(block_cols.reshape(row_count, pair_count, 2 * HEAD_DIM), 1, 0)

    def from_pairs(paired):
        return jnp.moveaxis(paired, 0, 1).reshape(row_count, D)

    normed = layer_norm(tokens, gain_one, shift_one).astype(jnp.bfloat16)
    qkv_bias = jnp.concatenate([query_bias, jnp.zeros_like(query_bias), value_bias])
    projected = (jnp.dot(normed, w_qkv, preferred_element_type=jnp.float32) + qkv_bias).astype(
        jnp.bfloat16
    )
    query_pairs = to_pairs(projected[:, :D])
    key_pairs = to_pairs(projected[:, D : 2 * D])
    value_pairs = to_pairs(projected[:, 2 * D :])

    def forward_pair(pair_item):
        queries, keys_pair, values_pair = [
            member.reshape(row_count, 2, HEAD_DIM) for member in pair_item
        ]
        raw_scores = jnp.einsum(
            "qhd,khd->hqk", queries, keys_pair, preferred_element_type=jnp.float32
        )
        scores = jnp.where(allowed[None], raw_scores * score_scale, -1e30)
        largest = jnp.max(scores, axis=-1, keepdims=True)
        weights_exp = jnp.exp(scores - largest)
        totals = jnp.sum(weights_exp, axis=-1, keepdims=True)
        weights_low = (weights_exp / totals).astype(jnp.bfloat16)
        attended_pair = jnp.einsum(
            "hqk,khd->qhd", weights_low, values_pair, preferred_element_type=jnp.float32
        )
        return (attended_pair.reshape(row_count, 2 * HEAD_DIM), (largest + jnp.log(totals))[..., 0])

    attended_pairs, log_totals = lax.map(forward_pair, (query_pairs, key_pairs, value_pairs))
    attended = from_pairs(attended_pairs).astype(jnp.bfloat16)
    branch_one = jnp.dot(attended, w_proj, preferred_element_type=jnp.float32) + proj_bias
    middle = tokens + scale_one * branch_one
    normed_two = layer_norm(middle, gain_two, shift_two).astype(jnp.bfloat16)
    hidden_pre = jnp.dot(normed_two, w_fc1, preferred_element_type=jnp.float32) + fc1_bias
    hidden = jax.nn.gelu(hidden_pre, approximate=False).astype(jnp.bfloat16)
    branch_two = jnp.dot(hidden, w_fc2, preferred_element_type=jnp.float32) + fc2_bias
    block_output = middle + scale_two * branch_two
    back_out = cotangent * validity[:, None]
    grad_branch_two = (scale_two * back_out).astype(jnp.bfloat16)
    grad_scale_two = jnp.sum(back_out * branch_two, axis=0)
    grad_fc2_bias = jnp.sum(grad_branch_two.astype(jnp.float32), axis=0)
    grad_w_fc2 = cross_rows(hidden, grad_branch_two)
    grad_hidden = times_transposed(grad_branch_two, w_fc2)
    gelu_pull = jax.vjp(lambda values: jax.nn.gelu(values, approximate=False), hidden_pre)[1]
    grad_pre = gelu_pull(grad_hidden)[0].astype(jnp.bfloat16)
    grad_fc1_bias = jnp.sum(grad_pre.astype(jnp.float32), axis=0)
    grad_w_fc1 = cross_rows(normed_two, grad_pre)
    grad_normed_two = times_transposed(grad_pre, w_fc1)
    norm_pull = jax.vjp(layer_norm, middle, gain_two, shift_two)[1]
    grad_middle_part, grad_gain_two, grad_shift_two = norm_pull(grad_normed_two)
    grad_middle = back_out + grad_middle_part
    grad_scale_one = jnp.sum(grad_middle * branch_one, axis=0)
    grad_branch_one = (scale_one * grad_middle).astype(jnp.bfloat16)
    grad_proj_bias = jnp.sum(grad_branch_one.astype(jnp.float32), axis=0)
    grad_w_proj = cross_rows(attended, grad_branch_one)
    grad_attended = times_transposed(grad_branch_one, w_proj).astype(jnp.bfloat16)

    def backward_pair(pair_item):
        queries, keys_pair, values_pair, grad_pair = [
            member.reshape(row_count, 2, HEAD_DIM) for member in pair_item[:4]
        ]
        log_total = pair_item[4]
        raw_scores = jnp.einsum(
            "qhd,khd->hqk", queries, keys_pair, preferred_element_type=jnp.float32
        )
        scores = jnp.where(allowed[None], raw_scores * score_scale, -1e30)
        weights_soft = jnp.exp(scores - log_total[..., None])
        grad_values = jnp.einsum(
            "hqk,qhd->khd",
            weights_soft.astype(jnp.bfloat16),
            grad_pair,
            preferred_element_type=jnp.float32,
        )
        grad_weights = jnp.einsum(
            "qhd,khd->hqk", grad_pair, values_pair, preferred_element_type=jnp.float32
        )
        row_dot = jnp.sum(weights_soft * grad_weights, axis=-1, keepdims=True)
        grad_scores = (weights_soft * (grad_weights - row_dot)).astype(jnp.bfloat16)
        grad_queries = (
            jnp.einsum("hqk,khd->qhd", grad_scores, keys_pair, preferred_element_type=jnp.float32)
            * score_scale
        )
        grad_keys = (
            jnp.einsum("hqk,qhd->khd", grad_scores, queries, preferred_element_type=jnp.float32)
            * score_scale
        )
        return (
            grad_queries.reshape(row_count, 2 * HEAD_DIM),
            grad_keys.reshape(row_count, 2 * HEAD_DIM),
            grad_values.reshape(row_count, 2 * HEAD_DIM),
        )

    grad_q_pairs, grad_k_pairs, grad_v_pairs = lax.map(
        backward_pair, (query_pairs, key_pairs, value_pairs, to_pairs(grad_attended), log_totals)
    )
    grad_projected = jnp.concatenate(
        [from_pairs(grad_q_pairs), from_pairs(grad_k_pairs), from_pairs(grad_v_pairs)], axis=1
    ).astype(jnp.bfloat16)
    grad_query_bias = jnp.sum(grad_projected[:, :D].astype(jnp.float32), axis=0)
    grad_value_bias = jnp.sum(grad_projected[:, 2 * D :].astype(jnp.float32), axis=0)
    grad_w_qkv = cross_rows(normed, grad_projected)
    grad_normed = times_transposed(grad_projected, w_qkv)
    first_pull = jax.vjp(layer_norm, tokens, gain_one, shift_one)[1]
    grad_tokens_part, grad_gain_one, grad_shift_one = first_pull(grad_normed)
    input_grad = grad_middle + grad_tokens_part
    ga = jnp.concatenate([grad_w_qkv, grad_w_proj], axis=1).astype(jnp.bfloat16)
    sa, sb, sc, sv, sq = scatter_grads(
        ga, grad_w_fc1.astype(jnp.bfloat16), grad_w_fc2.astype(jnp.bfloat16), join_vectors(
            [
                grad_gain_one,
                grad_shift_one,
                grad_query_bias,
                grad_value_bias,
                grad_proj_bias,
                grad_scale_one,
                grad_gain_two,
                grad_shift_two,
                grad_fc1_bias,
                grad_fc2_bias,
                grad_scale_two,
            ]
        )
    )
    summed = flat_grads(sa, sb, sc, sv)
    norm_value = jnp.sqrt(sq[0, 0])
    vector_part = summed[MATRIX_WIDTH:] / (8 * row_count) ** 0.5
    moment_one, moment_two, mean_difference, outer_new, new_weights = optimizer(
        summed, norm_value, master, first_moment, second_moment, outer_momentum
    )
    return (
        block_output,
        input_grad,
        norm_value.reshape(1),
        vector_part[None],
        moment_one[None],
        moment_two[None],
        mean_difference,
        outer_new,
        new_weights,
    )


def solution(mesh):
    small = mesh.shape["grp"] == 4 and mesh.shape["tok"] == 8
    return jax.shard_map(
        on_small_slice if small else on_device,
        mesh=mesh,
        in_specs=(
            P(("grp", "tok"), None),
            P(("grp", "tok"), None),
            P(("grp", "tok"), None),
            P("tok"),
            P("grp", "tok"),
            P("grp", "tok"),
            P("tok"),
        ),
        out_specs=(
            P(("grp", "tok"), None),
            P(("grp", "tok"), None),
            P("grp"),
            P("grp", "tok"),
            P("grp", "tok"),
            P("grp", "tok"),
            P("tok"),
            P("tok"),
            P("tok"),
        ),
        check_vma=False,
    )
```

```python
import jax
import jax.numpy as jnp
from jax import lax
from jax.experimental import pallas as pl
from jax.experimental.pallas import tpu as pltpu
from jax.sharding import PartitionSpec as P

D = 768
MLP = 3072
HEADS = 12
HEAD_DIM = 64
ROWS = D // 8
ANY = pl.BlockSpec(memory_space=pl.ANY)
DMA = pltpu.SemaphoreType.DMA
MESH_ID = pl.DeviceIdType.MESH
NZ = 4
F32, BF16 = jnp.float32, jnp.bfloat16


def place():
    g = lax.axis_index("grp")
    t = lax.axis_index("tok")
    z, c = lax.div(t, 2), lax.rem(t, 2)
    gx = g + 1 - 2 * lax.rem(g, 2)
    gy = g + 2 - 4 * lax.div(g, 2)
    return g, t, z, c, gx, gy


def greet(targets, count):
    barrier = pltpu.get_barrier_semaphore()
    for target in targets:
        pl.semaphore_signal(barrier, inc=1, device_id=target, device_id_type=MESH_ID)
    pl.semaphore_wait(barrier, count)


def remote(src, dst, send, recv, target):
    return pltpu.make_async_remote_copy(
        src_ref=src, dst_ref=dst, send_sem=send, recv_sem=recv,
        device_id=target, device_id_type=MESH_ID,
    )


clip_limit = 3.0
beta_first = 0.9
beta_second = 0.999
adam_epsilon = 1e-08
weight_decay = 0.04
adam_count = 10.0
base_rate = 0.075
rate_scale = 0.9**6
outer_rate = 0.7
outer_beta = 0.9
norm_epsilon = 1e-06


def member_extents():
    return [(D, 3 * D), (D, D), (D, MLP), (MLP, D)] + [(D,)] * 8 + [(MLP,), (D,), (D,)]


def member_sizes():
    sizes_list = []
    for extent in member_extents():
        length = 1
        for member in extent:
            length = length * member
        sizes_list.append(length)
    return sizes_list


def split_params(flat_params, owners):
    table = flat_params.reshape(owners, -1)
    members = []
    offset = 0
    for extent, length in zip(member_extents(), member_sizes()):
        width = length // owners
        members.append(table[:, offset : offset + width].reshape(extent))
        offset = offset + width
    return members


def join_table(members, owners):
    return jnp.concatenate([member.reshape(owners, -1) for member in members], axis=1)


def layer_norm(values, norm_gain, norm_shift):
    center = values - jnp.mean(values, axis=-1, keepdims=True)
    spread = jnp.mean(center * center, axis=-1, keepdims=True)
    return center * lax.rsqrt(spread + norm_epsilon) * norm_gain + norm_shift


def pack_layout(lengths_row, row_count):
    ends_at = jnp.cumsum(lengths_row)
    position = jnp.arange(row_count, dtype=jnp.int32)
    segment = jnp.sum((position[:, None] >= ends_at[None, :]).astype(jnp.int32), axis=1)
    validity = (position < ends_at[-1]).astype(jnp.float32)
    return (segment, validity)


def cross_rows(left_side, right_side):
    return lax.dot_general(
        left_side, right_side, (((0,), (0,)), ((), ())), preferred_element_type=jnp.float32
    )


def times_transposed(left_side, right_side):
    return lax.dot_general(
        left_side, right_side, (((1,), (1,)), ((), ())), preferred_element_type=jnp.float32
    )


def on_device(tokens, cotangent, crop_lengths, master, first_moment, second_moment, outer_momentum):
    row_count = tokens.shape[0]
    pair_count = HEADS // 2
    score_scale = HEAD_DIM ** (-0.5)
    owners = lax.axis_size("tok")
    segment, validity = pack_layout(crop_lengths[0], row_count)
    allowed = segment[:, None] == segment[None, :]
    master_low = master.astype(jnp.bfloat16)
    gathered = split_params(lax.all_gather(master_low, "tok", axis=0, tiled=True), owners)
    w_qkv, w_proj, w_fc1, w_fc2 = gathered[:4]
    (
        gain_one,
        shift_one,
        query_bias,
        value_bias,
        proj_bias,
        scale_one,
        gain_two,
        shift_two,
        fc1_bias,
        fc2_bias,
        scale_two,
    ) = [member.astype(jnp.float32) for member in gathered[4:]]

    def to_pairs(block_cols):
        return jnp.moveaxis(block_cols.reshape(row_count, pair_count, 2 * HEAD_DIM), 1, 0)

    def from_pairs(paired):
        return jnp.moveaxis(paired, 0, 1).reshape(row_count, D)

    normed = layer_norm(tokens, gain_one, shift_one).astype(jnp.bfloat16)
    qkv_bias = jnp.concatenate([query_bias, jnp.zeros_like(query_bias), value_bias])
    projected = (jnp.dot(normed, w_qkv, preferred_element_type=jnp.float32) + qkv_bias).astype(
        jnp.bfloat16
    )
    query_pairs = to_pairs(projected[:, :D])
    key_pairs = to_pairs(projected[:, D : 2 * D])
    value_pairs = to_pairs(projected[:, 2 * D :])

    def forward_pair(pair_item):
        queries, keys_pair, values_pair = [
            member.reshape(row_count, 2, HEAD_DIM) for member in pair_item
        ]
        raw_scores = jnp.einsum(
            "qhd,khd->hqk", queries, keys_pair, preferred_element_type=jnp.float32
        )
        scores = jnp.where(allowed[None], raw_scores * score_scale, -1e30)
        largest = jnp.max(scores, axis=-1, keepdims=True)
        weights_exp = jnp.exp(scores - largest)
        totals = jnp.sum(weights_exp, axis=-1, keepdims=True)
        weights_low = (weights_exp / totals).astype(jnp.bfloat16)
        attended_pair = jnp.einsum(
            "hqk,khd->qhd", weights_low, values_pair, preferred_element_type=jnp.float32
        )
        return (attended_pair.reshape(row_count, 2 * HEAD_DIM), (largest + jnp.log(totals))[..., 0])

    attended_pairs, log_totals = lax.map(forward_pair, (query_pairs, key_pairs, value_pairs))
    attended = from_pairs(attended_pairs).astype(jnp.bfloat16)
    branch_one = jnp.dot(attended, w_proj, preferred_element_type=jnp.float32) + proj_bias
    middle = tokens + scale_one * branch_one
    normed_two = layer_norm(middle, gain_two, shift_two).astype(jnp.bfloat16)
    hidden_pre = jnp.dot(normed_two, w_fc1, preferred_element_type=jnp.float32) + fc1_bias
    hidden = jax.nn.gelu(hidden_pre, approximate=False).astype(jnp.bfloat16)
    branch_two = jnp.dot(hidden, w_fc2, preferred_element_type=jnp.float32) + fc2_bias
    block_output = middle + scale_two * branch_two
    back_out = cotangent * validity[:, None]
    grad_branch_two = (scale_two * back_out).astype(jnp.bfloat16)
    grad_scale_two = jnp.sum(back_out * branch_two, axis=0)
    grad_fc2_bias = jnp.sum(grad_branch_two.astype(jnp.float32), axis=0)
    grad_w_fc2 = cross_rows(hidden, grad_branch_two)
    grad_hidden = times_transposed(grad_branch_two, w_fc2)
    gelu_pull = jax.vjp(lambda values: jax.nn.gelu(values, approximate=False), hidden_pre)[1]
    grad_pre = gelu_pull(grad_hidden)[0].astype(jnp.bfloat16)
    grad_fc1_bias = jnp.sum(grad_pre.astype(jnp.float32), axis=0)
    grad_w_fc1 = cross_rows(normed_two, grad_pre)
    grad_normed_two = times_transposed(grad_pre, w_fc1)
    norm_pull = jax.vjp(layer_norm, middle, gain_two, shift_two)[1]
    grad_middle_part, grad_gain_two, grad_shift_two = norm_pull(grad_normed_two)
    grad_middle = back_out + grad_middle_part
    grad_scale_one = jnp.sum(grad_middle * branch_one, axis=0)
    grad_branch_one = (scale_one * grad_middle).astype(jnp.bfloat16)
    grad_proj_bias = jnp.sum(grad_branch_one.astype(jnp.float32), axis=0)
    grad_w_proj = cross_rows(attended, grad_branch_one)
    grad_attended = times_transposed(grad_branch_one, w_proj).astype(jnp.bfloat16)

    def backward_pair(pair_item):
        queries, keys_pair, values_pair, grad_pair = [
            member.reshape(row_count, 2, HEAD_DIM) for member in pair_item[:4]
        ]
        log_total = pair_item[4]
        raw_scores = jnp.einsum(
            "qhd,khd->hqk", queries, keys_pair, preferred_element_type=jnp.float32
        )
        scores = jnp.where(allowed[None], raw_scores * score_scale, -1e30)
        weights_soft = jnp.exp(scores - log_total[..., None])
        grad_values = jnp.einsum(
            "hqk,qhd->khd",
            weights_soft.astype(jnp.bfloat16),
            grad_pair,
            preferred_element_type=jnp.float32,
        )
        grad_weights = jnp.einsum(
            "qhd,khd->hqk", grad_pair, values_pair, preferred_element_type=jnp.float32
        )
        row_dot = jnp.sum(weights_soft * grad_weights, axis=-1, keepdims=True)
        grad_scores = (weights_soft * (grad_weights - row_dot)).astype(jnp.bfloat16)
        grad_queries = (
            jnp.einsum("hqk,khd->qhd", grad_scores, keys_pair, preferred_element_type=jnp.float32)
            * score_scale
        )
        grad_keys = (
            jnp.einsum("hqk,qhd->khd", grad_scores, queries, preferred_element_type=jnp.float32)
            * score_scale
        )
        return (
            grad_queries.reshape(row_count, 2 * HEAD_DIM),
            grad_keys.reshape(row_count, 2 * HEAD_DIM),
            grad_values.reshape(row_count, 2 * HEAD_DIM),
        )

    grad_q_pairs, grad_k_pairs, grad_v_pairs = lax.map(
        backward_pair, (query_pairs, key_pairs, value_pairs, to_pairs(grad_attended), log_totals)
    )
    grad_projected = jnp.concatenate(
        [from_pairs(grad_q_pairs), from_pairs(grad_k_pairs), from_pairs(grad_v_pairs)], axis=1
    ).astype(jnp.bfloat16)
    grad_query_bias = jnp.sum(grad_projected[:, :D].astype(jnp.float32), axis=0)
    grad_value_bias = jnp.sum(grad_projected[:, 2 * D :].astype(jnp.float32), axis=0)
    grad_w_qkv = cross_rows(normed, grad_projected)
    grad_normed = times_transposed(grad_projected, w_qkv)
    first_pull = jax.vjp(layer_norm, tokens, gain_one, shift_one)[1]
    grad_tokens_part, grad_gain_one, grad_shift_one = first_pull(grad_normed)
    input_grad = grad_middle + grad_tokens_part
    all_members = [
        grad_w_qkv,
        grad_w_proj,
        grad_w_fc1,
        grad_w_fc2,
        grad_gain_one,
        grad_shift_one,
        grad_query_bias,
        grad_value_bias,
        grad_proj_bias,
        grad_scale_one,
        grad_gain_two,
        grad_shift_two,
        grad_fc1_bias,
        grad_fc2_bias,
        grad_scale_two,
    ]
    received = lax.all_to_all(
        join_table(all_members, owners).astype(jnp.bfloat16),
        "tok",
        split_axis=0,
        concat_axis=0,
        tiled=True,
    ).astype(jnp.float32)
    summed = jnp.sum(received, axis=0)
    matrix_width = (4 * D * D + 2 * D * MLP) // owners
    vector_part = summed[matrix_width:] / (owners * row_count) ** 0.5
    square_total = lax.psum(jnp.sum(summed * summed), "tok")
    norm_value = jnp.sqrt(square_total)
    clipped = summed * (clip_limit / (norm_value + 1e-06))
    moment_one = beta_first * first_moment[0] + (1.0 - beta_first) * clipped
    moment_two = beta_second * second_moment[0] + (1.0 - beta_second) * clipped * clipped
    corrected_one = moment_one / (1.0 - beta_first**adam_count)
    corrected_two = moment_two / (1.0 - beta_second**adam_count)
    shard_size = master.shape[0]
    local_index = jnp.arange(shard_size, dtype=jnp.int32)
    decay_mask = (local_index < matrix_width).astype(jnp.float32)
    step_rate = base_rate * rate_scale
    updated = master - step_rate * (
        corrected_one / (jnp.sqrt(corrected_two) + adam_epsilon)
        + weight_decay * decay_mask * master
    )
    mean_difference = lax.psum((master - updated).astype(jnp.bfloat16), "grp").astype(
        jnp.float32
    ) / lax.axis_size("grp")
    outer_new = outer_beta * outer_momentum + mean_difference
    new_weights = master - outer_rate * (mean_difference + outer_beta * outer_new)
    return (
        block_output,
        input_grad,
        norm_value.reshape(1),
        vector_part[None],
        moment_one[None],
        moment_two[None],
        mean_difference,
        outer_new,
        new_weights,
    )


def rows_at(ref, start, count):
    return ref.at[pl.ds(pl.multiple_of(start, 16), count), :]


TILE = 256


def nn(a, b):
    return lax.dot_general(a, b, (((1,), (0,)), ((), ())), preferred_element_type=F32)


def nt(a, b):
    return lax.dot_general(a, b, (((1,), (1,)), ((), ())), preferred_element_type=F32)


def tn(a, b):
    return lax.dot_general(a, b, (((0,), (0,)), ((), ())), preferred_element_type=F32)


def normalize(values):
    center = values - jnp.mean(values, axis=-1, keepdims=True)
    spread = jnp.mean(center * center, axis=-1, keepdims=True)
    inverse = lax.rsqrt(spread + norm_epsilon)
    return center * inverse, inverse


def norm_pull(grad, normal, inverse, gain):
    scaled = grad * gain
    return inverse * (
        scaled
        - jnp.mean(scaled, axis=-1, keepdims=True)
        - normal * jnp.mean(scaled * normal, axis=-1, keepdims=True)
    )


def gelu_and_slope(x):
    phi = 0.5 * (1.0 + lax.erf(x * 0.7071067811865476))
    return x * phi, phi + x * jnp.exp(-0.5 * x * x) * 0.3989422804014327


def col_sum(x):
    return jnp.sum(x, axis=0, keepdims=True)


def mlp_kernel(tok, cot, valid, att, wa, wb, wc, vec, fb1, bo, gm, gatt, gout, gproj, vg, vg1, hid, gpre, n2, gb2, gb1, slope, wp, sem):
    load = pltpu.make_async_copy(wa.at[3], wp, sem.at[0])
    load.start()
    vg[...] = jnp.zeros_like(vg)
    vg1[...] = jnp.zeros_like(vg1)
    rows = tok.shape[0]
    load.wait()

    def row(j):
        return vec[j : j + 1, :]

    def tile(i, _):
        at = pl.ds(pl.multiple_of(i * TILE, TILE), TILE)
        branch_one = nn(att[at, :], wp[...]) + row(4)
        middle = tok[at, :] + row(5) * branch_one
        normal, inverse = normalize(middle)
        n2[at, :] = (normal * row(6) + row(7)).astype(BF16)

        def forward(q, _):
            low = pl.ds(pl.multiple_of(q * D, D), D)
            pre = nn(n2[at, :], wb[q]) + fb1[0:1, low]
            h, s = gelu_and_slope(pre)
            hid[at, low] = h.astype(BF16)
            slope[:, low] = s
            return 0
        lax.fori_loop(0, 4, forward, 0)
        branch_two = nn(hid[at, :], wc[...]) + row(12)
        bo[at, :] = middle + row(13) * branch_two
        back = cot[at, :] * valid[at, 0:1]
        low_back = (row(13) * back).astype(BF16)
        gb2[at, :] = low_back
        vg[13:14, :] += col_sum(back * branch_two)
        vg[12:13, :] += col_sum(low_back.astype(F32))

        def backward(q, total):
            low = pl.ds(pl.multiple_of(q * D, D), D)
            grad_hidden = nt(gb2[at, :], wc[low, :])
            grad = grad_hidden * slope[:, low]
            grad = grad.astype(BF16)
            gpre[at, low] = grad
            vg1[0:1, low] += col_sum(grad.astype(F32))
            return total + nt(grad, wb[q])
        grad_n2 = lax.fori_loop(0, 4, backward, jnp.zeros((TILE, D), F32))
        vg[6:7, :] += col_sum(grad_n2 * normal)
        vg[7:8, :] += col_sum(grad_n2)
        grad_mid = back + norm_pull(grad_n2, normal, inverse, row(6))
        gm[at, :] = grad_mid
        vg[5:6, :] += col_sum(grad_mid * branch_one)
        low_one = (row(5) * grad_mid).astype(BF16)
        gb1[at, :] = low_one
        vg[4:5, :] += col_sum(low_one.astype(F32))
        gatt[at, :] = nt(low_one, wp[...]).astype(BF16)
        return 0
    lax.fori_loop(0, rows // TILE, tile, 0)

    def fc2(t, _):
        low = pl.ds(pl.multiple_of(t * 384, 128), 384)
        gout[1, t] = tn(hid[:, low], gb2[...]).astype(BF16).reshape(4, 96, D)
        return 0
    lax.fori_loop(0, 8, fc2, 0)

    def fc1(q, _):
        def part(m, _):
            low = pl.ds(pl.multiple_of(q * D + m * 384, 128), 384)
            col = pl.ds(pl.multiple_of(m * 384, 128), 384)
            gout[0, :, q, :, col] = tn(n2[...], gpre[:, low]).astype(BF16).reshape(8, 96, 384)
            return 0
        return lax.fori_loop(0, 2, part, 0)
    lax.fori_loop(0, 4, fc1, 0)

    def proj(m, _):
        col = pl.ds(pl.multiple_of(m * 384, 128), 384)
        gproj[:, :, col] = tn(att[...], gb1[:, col]).astype(BF16).reshape(8, 96, 384)
        return 0
    lax.fori_loop(0, 2, proj, 0)


def mlp_block(tok, cot, valid, att, wa, wb, wc, vec, fb1):
    vm = pl.BlockSpec(memory_space=pltpu.VMEM)
    rows = tok.shape[0]
    S = jax.ShapeDtypeStruct
    return pl.pallas_call(
        mlp_kernel,
        name="mlp_block",
        out_shape=[
            S((rows, D), F32), S((rows, D), F32), S((rows, D), BF16),
            S((2, 8, 4, 96, D), BF16), S((8, 96, D), BF16), S((16, D), F32), S((8, MLP), F32),
        ],
        in_specs=[vm] * 4 + [ANY] + [vm] * 4,
        out_specs=[vm] * 7,
        scratch_shapes=[
            pltpu.VMEM((rows, MLP), BF16), pltpu.VMEM((rows, MLP), BF16),
            pltpu.VMEM((rows, D), BF16), pltpu.VMEM((rows, D), BF16), pltpu.VMEM((rows, D), BF16),
            pltpu.VMEM((TILE, MLP), F32), pltpu.VMEM((D, D), BF16), DMA((1,)),
        ],
        compiler_params=pltpu.CompilerParams(vmem_limit_bytes=62 * 2**20),
    )(tok, cot, valid, att, wa, wb, wc, vec, fb1)


QT = 256


def fill_bias(lens, bias):
    rows = bias.shape[0]
    column = lax.broadcasted_iota(jnp.int32, (rows, 128), 0)
    line = lax.broadcasted_iota(jnp.int32, (8, rows), 1)
    seg_col, seg_line = jnp.zeros((rows, 128), jnp.int32), jnp.zeros((8, rows), jnp.int32)
    end = jnp.int32(0)
    for j in range(lens.shape[1]):
        end = end + lens[0, j]
        seg_col = seg_col + (column >= end).astype(jnp.int32)
        seg_line = seg_line + (line >= end).astype(jnp.int32)

    for i in range(rows // 128):
        same = seg_col[i * 128 : (i + 1) * 128, 0:1] == seg_line[0:1, :]
        bias[pl.ds(i * 128, 128), :] = jnp.where(same, 0.0, -1e30).astype(F32)


def head_part(block, h):
    lane = lax.broadcasted_iota(jnp.int32, (1, 128), 1)
    keep = lane < 64 if h == 0 else lane >= 64
    return jnp.where(keep, block, jnp.zeros_like(block))


def first_half(a, b):
    lane = lax.broadcasted_iota(jnp.int32, (1, 128), 1)
    return jnp.where(lane < 64, a, b)


def norm_rows(tok, vec, normed):
    def tile(i, _):
        at = pl.ds(pl.multiple_of(i * QT, QT), QT)
        normal, _inverse = normalize(tok[at, :])
        normed[at, :] = (normal * vec[0:1, :] + vec[1:2, :]).astype(BF16)
        return 0
    lax.fori_loop(0, tok.shape[0] // QT, tile, 0)


def project_in(vec, wa, normed, proj):
    def block(i, _):
        at = pl.ds(pl.multiple_of(i * QT, QT), QT)
        proj[0, at, :] = (nn(normed[at, :], wa[0]) + vec[2:3, :]).astype(BF16)
        proj[1, at, :] = nn(normed[at, :], wa[1]).astype(BF16)
        proj[2, at, :] = (nn(normed[at, :], wa[2]) + vec[3:4, :]).astype(BF16)
        return 0
    lax.fori_loop(0, normed.shape[0] // QT, block, 0)


def attend(p, proj, bias, att, lse):
    rows = bias.shape[0]
    cols = pl.ds(pl.multiple_of(p * 128, 128), 128)

    def tile(i, _):
        at = pl.ds(pl.multiple_of(i * QT, QT), QT)
        q = proj[0, at, cols] * jnp.asarray(0.125, BF16)
        k, v = proj[1, :, cols], proj[2, :, cols]
        lane = lax.broadcasted_iota(jnp.int32, (1, 128), 1)
        outs = []
        logs = lse[at, :]
        for h in (0, 1):
            scores = nt(head_part(q, h), k) + bias[at, :]
            largest = jnp.max(scores, axis=-1, keepdims=True)
            weights = jnp.exp(scores - largest)
            total = jnp.sum(weights, axis=-1, keepdims=True)
            low = (weights * (1.0 / total)).astype(BF16)
            outs.append(nn(low, v))
            logs = jnp.where(lane == 2 * p + h, largest + jnp.log(total), logs)
        lse[at, :] = logs
        att[at, cols] = first_half(*outs).astype(BF16)
        return 0
    lax.fori_loop(0, rows // QT, tile, 0)


def attend_back(p, proj, gatt, bias, lse_t):
    rows = bias.shape[0]
    cols = pl.ds(pl.multiple_of(p * 128, 128), 128)
    k, v = proj[1, :, cols], proj[2, :, cols]

    def tile(i, carry):
        dk, dv = carry
        at = pl.ds(pl.multiple_of(i * QT, QT), QT)
        q = proj[0, at, cols]
        g = gatt[at, cols]
        scaled = q * jnp.asarray(0.125, BF16)
        dks, dvs, dqs = [], [], []
        for h in (0, 1):
            scores = nt(k, head_part(scaled, h)) + bias[:, at]
            probs = jnp.exp(scores - lse_t[pl.ds(2 * p + h, 1), at])
            grad = nt(v, head_part(g, h))
            dot = jnp.sum(probs * grad, axis=0, keepdims=True)
            low = (probs * (grad - dot)).astype(BF16)
            dvs.append(nn(probs.astype(BF16), g))
            dks.append(nn(low, scaled))
            dqs.append(tn(low, k))
        proj[0, at, cols] = (first_half(*dqs) * 0.125).astype(BF16)
        return dk + first_half(*dks), dv + first_half(*dvs)
    zero = jnp.zeros((rows, 128), F32)
    dk, dv = lax.fori_loop(0, rows // QT, tile, (zero, zero))
    proj[1, :, cols] = dk.astype(BF16)
    proj[2, :, cols] = dv.astype(BF16)


def weight_grads(normed, gproj, gout):
    def block(q, _):
        def part(m, _):
            col = pl.ds(pl.multiple_of(m * 384, 128), 384)
            gout[:, q, :, col] = tn(normed[...], gproj[q, :, col]).astype(BF16).reshape(8, ROWS, 384)
            return 0
        return lax.fori_loop(0, 2, part, 0)
    lax.fori_loop(0, 3, block, 0)


def row_grads(wide, total, vec, wa, gproj, vg):
    vg[...] = jnp.zeros_like(vg)

    def tile(i, _):
        at = pl.ds(pl.multiple_of(i * QT, QT), QT)
        grad = nt(gproj[0, at, :], wa[0]) + nt(gproj[1, at, :], wa[1]) + nt(gproj[2, at, :], wa[2])
        normal, inverse = normalize(wide[at, :D])
        vg[0:1, :] += col_sum(grad * normal)
        vg[1:2, :] += col_sum(grad)
        vg[2:3, :] += col_sum(gproj[0, at, :].astype(F32))
        vg[3:4, :] += col_sum(gproj[2, at, :].astype(F32))
        total[at, :] = total[at, :] + norm_pull(grad, normal, inverse, vec[0:1, :])
        return 0
    lax.fori_loop(0, total.shape[0] // QT, tile, 0)


def convert_piece(w, lin, piece):
    if w == 2:
        for q in range(4):
            for m in range(6):
                piece[q, :, 128 * m : 128 * m + 128] = lin[pl.ds(4608 + 576 * q + m, ROWS, stride=6), :].astype(BF16)
        return
    for q in range(4):
        for m in range(6):
            if w == 1:
                at = pl.ds(2304 + 6 * q + m, ROWS, stride=24)
            elif q == 3:
                at = pl.ds(1728 + m, ROWS, stride=6)
            else:
                at = pl.ds(6 * q + m, ROWS, stride=18)
            piece[q, :, 128 * m : 128 * m + 128] = lin[at, :].astype(BF16)


def weight_strip(w, ref, t):
    if w == 2:
        return ref.at[t]
    return ref.at[:, pl.ds(pl.multiple_of(t * ROWS, 16), ROWS), :]


def weight_block(w, ref, t, q, half=None):
    lead, count = (0, ROWS) if half is None else (48 * half, 48)
    if w == 2:
        return ref.at[t, q, pl.ds(lead, count), :]
    return ref.at[q, pl.ds(pl.multiple_of(t * ROWS + lead, 16), count), :]


def front_kernel(
    lens, lin, pv, tok,
    wa, wb, wc, vec, fb1, normed, proj, att, lse,
    pieces, wv, wa_in, bias,
    ls, zs, zr, xs, xr, ys, yr, ds, dr, cs, cr, vs, vr,
):
    g, t, z, c, gx, gy = place()
    fulls = (wa, wb, wc)
    peers = [lax.rem(t + k, 8) for k in range(1, 8)]
    barrier = pltpu.get_barrier_semaphore()
    for target in [(g, p) for p in peers] + [(gx, t), (gy, t)]:
        pl.semaphore_signal(barrier, inc=1, device_id=target, device_id_type=MESH_ID)
    convert_piece(0, lin, pieces.at[0])
    pl.semaphore_wait(barrier, 9)
    other = t + 1 - 2 * c

    def z_copy(w, d, s):
        step = 1 if d == 0 else -1
        src_t = t - 2 * step * s
        src = pieces.at[w, g] if s == 0 else weight_block(w, fulls[w], src_t, g)
        ok = (z - s >= 0) & (z + 1 < NZ) if d == 0 else (z + s < NZ) & (z - 1 >= 0)
        return ok, remote(src, weight_block(w, fulls[w], src_t, g), zs.at[w, d, s], zr.at[w, d, s], (g, t + 2 * step))

    def from_t(d, s):
        return t - 2 * (s + 1) if d == 0 else t + 2 * (s + 1)

    def here(d, s):
        return z - s - 1 >= 0 if d == 0 else z + s + 1 < NZ

    def z_wait(w, d, s):
        blk = weight_block(w, fulls[w], from_t(d, s), g)
        remote(blk, blk, zs.at[w, d, s], zr.at[w, d, s], (g, other)).wait_recv()

    def side_copy(w, d, s, axis):
        blk = weight_block(w, fulls[w], from_t(d, s), g)
        sems = (xs, xr) if axis == 0 else (ys, yr)
        return remote(blk, blk, sems[0].at[w, d, s], sems[1].at[w, d, s], (gx if axis == 0 else gy, t))

    def side_wait(w, d, s, axis):
        blk = weight_block(w, fulls[w], from_t(d, s), gx if axis == 0 else gy)
        sems = (xs, xr) if axis == 0 else (ys, yr)
        remote(blk, blk, sems[0].at[w, d, s], sems[1].at[w, d, s], (gx, t)).wait_recv()

    def diag_copy(w, d, s, axis):
        blk = weight_block(w, fulls[w], from_t(d, s), gx if axis == 0 else gy, axis)
        return remote(blk, blk, ds.at[w, d, s, axis], dr.at[w, d, s, axis], (gy if axis == 0 else gx, t))

    def diag_wait(w, d, s, axis):
        blk = weight_block(w, fulls[w], from_t(d, s), 3 - g, axis)
        remote(blk, blk, ds.at[w, d, s, axis], dr.at[w, d, s, axis], (gx, t)).wait_recv()

    def core_copy(w, d, s):
        blk = weight_strip(w, fulls[w], from_t(d, s))
        return remote(blk, blk, cs.at[w, d, s], cr.at[w, d, s], (g, other))

    def core_wait(w, d, s):
        blk = weight_strip(w, fulls[w], from_t(d, s) + 1 - 2 * c)
        remote(blk, blk, cs.at[w, d, s], cr.at[w, d, s], (g, other)).wait_recv()

    def own_copy(w):
        return remote(pieces.at[w], weight_strip(w, fulls[w], t), cs.at[w, 2, 0], cr.at[w, 2, 0], (g, other))

    def own_wait(w):
        blk = weight_strip(w, fulls[w], other)
        remote(blk, blk, cs.at[w, 2, 0], cr.at[w, 2, 0], (g, other)).wait_recv()

    def own_local(w):
        return pltpu.make_async_copy(pieces.at[w], weight_strip(w, fulls[w], t), ls.at[w])

    def both(s, fn):
        for d in (0, 1):
            @pl.when(here(d, s))
            def _():
                fn(d)

    def start_z(w, s):
        for d in (0, 1):
            ok, copy = z_copy(w, d, s)

            @pl.when(ok)
            def _():
                copy.start()

    def arrive(n):
        w, s = divmod(n, 3)
        both(s, lambda d: z_wait(w, d, s))
        if s < 2:
            start_z(w, s + 1)

        def sides(d):
            side_copy(w, d, s, 0).start()
            side_copy(w, d, s, 1).start()
        both(s, sides)
        if s == 0 and w < 2:
            start_z(w + 1, 0)
            own_copy(w + 1).start()

    def cross(n):
        w, s = divmod(n, 3)

        def fn(d):
            for axis in (0, 1):
                side_wait(w, d, s, axis)
                diag_copy(w, d, s, axis).start()
        both(s, fn)

    def finish(n):
        w, s = divmod(n, 3)

        def fn(d):
            diag_wait(w, d, s, 0)
            diag_wait(w, d, s, 1)
            core_copy(w, d, s).start()
        both(s, fn)

    def drain(w):
        own_wait(w)
        own_local(w).wait()
        for s in range(3):
            both(s, lambda d: core_wait(w, d, s))

    start_z(0, 0)
    own_copy(0).start()
    own_local(0).start()
    local_v = pltpu.make_async_copy(pv, wv.at[t], ls.at[3])
    local_v.start()
    v_copies = [remote(pv, wv.at[t], vs.at[k], vr.at[k], (g, peers[k])) for k in range(7)]
    for copy in v_copies:
        copy.start()
    for w in (1, 2):
        convert_piece(w, lin, pieces.at[w])
        own_local(w).start()
    fill_bias(lens, bias)
    lse[...] = jnp.zeros_like(lse)
    arrive(0)
    local_v.wait()
    for k in range(7):
        remote(pv, wv.at[lax.rem(t + 7 - k, 8)], vs.at[k], vr.at[k], (g, peers[k])).wait_recv()
    for k in range(8):
        vec[:, ROWS * k : ROWS * k + ROWS] = wv[k, :, :ROWS]
        for j in range(4):
            lead = 4 * ROWS * k + ROWS * j
            fb1[0:1, lead : lead + ROWS] = wv[k, 8 + j : 9 + j, :ROWS]
    arrive(1)
    cross(0)
    norm_rows(tok, vec, normed)
    arrive(2)
    cross(1)
    finish(0)
    arrive(3)
    cross(2)
    finish(1)
    finish(2)
    drain(0)
    load = pltpu.make_async_copy(wa.at[pl.ds(0, 3)], wa_in, ls.at[4])
    load.start()
    load.wait()
    project_in(vec, wa_in, normed, proj)
    arrive(4)
    cross(3)
    events = [
        [(arrive, 5), (arrive, 6), (cross, 4), (finish, 3)],
        [(arrive, 7), (cross, 5), (finish, 4)],
        [(arrive, 8), (cross, 6), (finish, 5)],
        [(cross, 7), (finish, 6)],
        [(cross, 8), (finish, 7)],
        [(finish, 8)],
    ]
    for p in range(6):
        attend(p, proj, bias, att, lse)
        for event, n in events[p]:
            event(n)
    drain(1)
    drain(2)
    for copy in v_copies:
        copy.wait_send()
    for w in range(3):
        own_copy(w).wait_send()
        for s in range(3):
            for d in (0, 1):
                ok, copy = z_copy(w, d, s)

                @pl.when(ok)
                def _():
                    copy.wait_send()

            def sent(d):
                side_copy(w, d, s, 0).wait_send()
                side_copy(w, d, s, 1).wait_send()
                diag_copy(w, d, s, 0).wait_send()
                diag_copy(w, d, s, 1).wait_send()
                core_copy(w, d, s).wait_send()
            both(s, sent)


def front(lens, lin, pv, tok):
    vm = pl.BlockSpec(memory_space=pltpu.VMEM)
    rows = tok.shape[0]
    S = jax.ShapeDtypeStruct
    return pl.pallas_call(
        front_kernel,
        name="front",
        out_shape=[
            S((4, D, D), BF16), S((4, D, D), BF16), S((8, 4, ROWS, D), BF16),
            S((16, D), F32), S((8, MLP), F32),
            S((rows, D), BF16), S((3, rows, D), BF16), S((rows, D), BF16), S((rows, 128), F32),
        ],
        in_specs=[pl.BlockSpec(memory_space=pltpu.SMEM)] + [vm] * 3,
        out_specs=[ANY] * 3 + [vm] * 6,
        scratch_shapes=[
            pltpu.VMEM((3, 4, ROWS, D), BF16),
            pltpu.VMEM((8, 16, 128), F32),
            pltpu.VMEM((3, D, D), BF16),
            pltpu.VMEM((rows, rows), F32),
            DMA((5,)),
            DMA((3, 2, 3)), DMA((3, 2, 3)),
            DMA((3, 2, 3)), DMA((3, 2, 3)),
            DMA((3, 2, 3)), DMA((3, 2, 3)),
            DMA((3, 2, 3, 2)), DMA((3, 2, 3, 2)),
            DMA((3, 3, 3)), DMA((3, 3, 3)),
            DMA((7,)), DMA((7,)),
        ],
        compiler_params=pltpu.CompilerParams(collective_id=0, has_side_effects=True, vmem_limit_bytes=60 * 2**20),
    )(lens, lin, pv, tok)


ORDER = (2, 1, 0)


def back_kernel(
    lens, vec, vg_in, vg1, tok, gm, wa, normed_in, proj_in, gatt_in, lse_in, gbc, gp,
    gin, lin, sv, sq,
    bias, tall, wa_v, normed, proj, gatt, lse_t, gout, own, core, zbuf, vg, gv, vbuf, qbuf,
    ls, os, cs, cr, zs, zr, vs, vr, qs, qr,
):
    g, t, z, c, gx, gy = place()
    peers = [lax.rem(t + k, 8) for k in range(1, 8)]
    rows = tok.shape[0]
    other = t + 1 - 2 * c
    loads = [
        pltpu.make_async_copy(src, dst, ls.at[i])
        for i, (src, dst) in enumerate(
            [
                (proj_in, proj), (gatt_in, gatt), (wa.at[pl.ds(0, 3)], wa_v), (normed_in, normed),
                (gp, gout.at[:, 3]), (gm, tall),
            ]
        )
    ]
    for copy in loads:
        copy.start()
    greet([(g, p) for p in peers], 7)

    def own_at(w, k):
        return gout.at[2 * k + c] if w == 0 else own.at[w - 1, k]

    def core_copy(w, k):
        src = gout.at[2 * k + 1 - c] if w == 0 else gbc.at[w - 1, 2 * k + 1 - c]
        return remote(src, core.at[w, k], cs.at[w, k], cr.at[w, k], (g, other))

    def load(w, k):
        return pltpu.make_async_copy(gbc.at[w - 1, 2 * k + c], own.at[w - 1, k], os.at[w, k])

    def begin(w):
        for k in (3, 0, 2, 1):
            core_copy(w, k).start()
            if w:
                load(w, k).start()

    def slot(d, k):
        return k - 1 if d == 0 else k

    def total_of(w, k, q, at, extra):
        mine = own_at(w, k)
        total = mine[q, at, :].astype(F32) + core[w, k, q, at, :].astype(F32)
        for d in extra:
            total = total + zbuf[d, w, slot(d, k), q, at, :].astype(F32)
        return total

    def add_rows(w, k, h, extra):
        for q in (2 * h, 2 * h + 1):
            def body(i, _):
                at = pl.ds(pl.multiple_of(i * 32, 32), 32)
                own_at(w, k)[q, at, :] = total_of(w, k, q, at, extra).astype(BF16)
                return 0
            lax.fori_loop(0, ROWS // 32, body, 0)

    def lay_out(w, k, h, extra):
        for q in (2 * h, 2 * h + 1):
            if w == 2:
                base, stride = 4608 + 576 * q, 6
            elif w == 1:
                base, stride = 2304 + 6 * q, 24
            else:
                base, stride = (1728, 6) if q == 3 else (6 * q, 18)

            def body(i, _):
                at = pl.ds(pl.multiple_of(i * 32, 32), 32)
                total = total_of(w, k, q, at, extra)
                for m in range(6):
                    lin[pl.ds(base + m + i * (32 * stride), 32, stride=stride), :] = total[:, 128 * m : 128 * m + 128]
                return 0
            lax.fori_loop(0, ROWS // 32, body, 0)

    def z_copy(w, d, k, h):
        step = 2 if d == 0 else -2
        at = pl.ds(2 * h, 2)
        return remote(
            own_at(w, k).at[at], zbuf.at[d, w, slot(d, k), at], zs.at[w, d, k, h], zr.at[w, d, k, h], (g, t + step)
        )

    def ready(w, k):
        if w:
            load(w, k).wait()
        core_copy(w, k).wait_recv()

    def pass_on(i, d, j, h):
        w = ORDER[i]
        reach = NZ - 1 - z if d == 0 else z
        k = z + j if d == 0 else z - j
        first = z == 0 if d == 0 else z == NZ - 1

        @pl.when(j <= reach)
        def _():
            if h == 0:
                ready(w, k)

            @pl.when(first)
            def _():
                add_rows(w, k, h, ())

            @pl.when(jnp.logical_not(first))
            def _():
                z_copy(w, d, k, h).wait_recv()
                add_rows(w, k, h, (d,))

            if i > 0:
                @pl.when(j == reach)
                def _():
                    z_copy(ORDER[i - 1], d, z + 1 if d == 0 else z - 1, h).wait_send()
            if j < NZ - 1:
                @pl.when(j < reach)
                def _():
                    z_copy(w, d, k + 1 if d == 0 else k - 1, h).wait_send()
            z_copy(w, d, k, h).start()

    def settle(i):
        w = ORDER[i]
        ready(w, z)
        for h in (0, 1):
            for cond, dirs in ((z == 0, (1,)), (z == NZ - 1, (0,)), ((z > 0) & (z < NZ - 1), (0, 1))):
                @pl.when(cond)
                def _():
                    for d in dirs:
                        z_copy(w, d, z, h).wait_recv()
                    lay_out(w, z, h, dirs)

    steps = [(i, j, h) for i in range(3) for j in (3, 2, 1) for h in (0, 1)]

    def run(lo, hi):
        for i, j, h in steps[lo:hi]:
            pass_on(i, 0, j, h)
            pass_on(i, 1, j, h)

    begin(2)
    begin(1)
    fill_bias(lens, bias)
    lse_t[...] = lse_in[...].T
    for n in (0, 1):
        loads[n].wait()
    run(0, 1)
    done = 1
    for p, count in enumerate((2, 1, 2, 1, 2, 1)):
        attend_back(p, proj, gatt, bias, lse_t)
        run(done, done + count)
        done += count
    for n in (2, 3, 4, 5):
        loads[n].wait()
    tok_load = pltpu.make_async_copy(tok, bias.at[:, pl.ds(0, D)], ls.at[6])
    tok_load.start()
    weight_grads(normed, proj, gout)
    begin(0)
    run(10, 11)
    tok_load.wait()
    row_grads(bias, tall, vec, wa_v, proj, vg)
    store = pltpu.make_async_copy(tall, gin, ls.at[7])
    store.start()
    vg[...] += vg_in[...]
    for k in range(8):
        gv[k, :, :ROWS] = vg[:, ROWS * k : ROWS * k + ROWS]
        for j in range(4):
            lead = 4 * ROWS * k + ROWS * j
            gv[k, 8 + j : 9 + j, :ROWS] = vg1[0:1, lead : lead + ROWS]
    v_copies = [remote(gv.at[peers[k]], vbuf.at[k], vs.at[k], vr.at[k], (g, peers[k])) for k in range(7)]
    for copy in v_copies:
        copy.start()
    run(11, 12)
    settle(0)
    run(12, 18)
    settle(1)
    for k in range(7):
        v_copies[k].wait_recv()
    total = gv[t]
    for k in range(7):
        total = total + vbuf[k]
    lane = lax.broadcasted_iota(jnp.int32, (16, 128), 1)
    line = lax.broadcasted_iota(jnp.int32, (16, 128), 0)
    total = jnp.where((lane < ROWS) & (line < 14), total, 0.0)
    sv[...] = total
    settle(2)

    def square(i, acc):
        v = lin[pl.ds(pl.multiple_of(i * 64, 64), 64), :]
        return acc + v * v
    acc = lax.fori_loop(0, 108, square, jnp.zeros((64, 128), F32))
    qbuf[7] = jnp.full((8, 128), jnp.sum(acc) + jnp.sum(total * total), F32)
    q_copies = [remote(qbuf.at[7], qbuf.at[k], qs.at[k], qr.at[k], (g, peers[k])) for k in range(7)]
    for copy in q_copies:
        copy.start()
    for w in range(3):
        for k in range(NZ):
            core_copy(w, k).wait_send()
    for h in (0, 1):
        @pl.when(z < NZ - 1)
        def _():
            z_copy(0, 0, z + 1, h).wait_send()

        @pl.when(z > 0)
        def _():
            z_copy(0, 1, z - 1, h).wait_send()
    store.wait()
    for k in range(7):
        q_copies[k].wait_recv()
    acc = qbuf[7]
    for k in range(7):
        acc = acc + qbuf[k]
    sq[...] = acc
    for k in range(7):
        q_copies[k].wait_send()
        v_copies[k].wait_send()


def back(lens, vec, vg, vg1, tok, gm, wa, normed, proj, gatt, lse, gbc, gp):
    vm = pl.BlockSpec(memory_space=pltpu.VMEM)
    rows = tok.shape[0]
    S = jax.ShapeDtypeStruct
    return pl.pallas_call(
        back_kernel,
        name="back",
        out_shape=[S((rows, D), F32), S((6912, 128), F32), S((16, 128), F32), S((8, 128), F32)],
        in_specs=[pl.BlockSpec(memory_space=pltpu.SMEM)] + [vm] * 3 + [ANY] * 6 + [vm] + [ANY] * 2,
        out_specs=[ANY] + [vm] * 3,
        scratch_shapes=[
            pltpu.VMEM((rows, rows), F32),
            pltpu.VMEM((rows, D), F32),
            pltpu.VMEM((3, D, D), BF16),
            pltpu.VMEM((rows, D), BF16),
            pltpu.VMEM((3, rows, D), BF16),
            pltpu.VMEM((rows, D), BF16),
            pltpu.VMEM((128, rows), F32),
            pltpu.VMEM((8, 4, ROWS, D), BF16),
            pltpu.VMEM((2, NZ, 4, ROWS, D), BF16),
            pltpu.VMEM((3, NZ, 4, ROWS, D), BF16),
            pltpu.VMEM((2, 3, NZ - 1, 4, ROWS, D), BF16),
            pltpu.VMEM((16, D), F32),
            pltpu.VMEM((8, 16, 128), F32),
            pltpu.VMEM((7, 16, 128), F32),
            pltpu.VMEM((8, 8, 128), F32),
            DMA((8,)), DMA((3, NZ)), DMA((3, NZ)), DMA((3, NZ)),
            DMA((3, 2, NZ, 2)), DMA((3, 2, NZ, 2)),
            DMA((7,)), DMA((7,)), DMA((7,)), DMA((7,)),
        ],
        compiler_params=pltpu.CompilerParams(
            collective_id=1, has_side_effects=True, vmem_limit_bytes=62 * 2**20
        ),
    )(lens, vec, vg, vg1, tok, gm, wa, normed, proj, gatt, lse, gbc, gp)


SUM_ROWS = 7040
SUM_H, SUM_Q, SUM_E = SUM_ROWS // 2, SUM_ROWS // 4, SUM_ROWS // 8


def mean_kernel(diff, out, part, mid, buf, ss, rs):
    g, t, z, c, gx, gy = place()
    greet([(gx, t), (gy, t)], 2)
    xi, yi = lax.rem(g, 2), lax.div(g, 2)
    hop = [((gx, t), (gy, t)), ((gy, t), (gx, t))]
    mine = [(xi, yi), (yi, xi)]

    def copies(h):
        a, b = mine[h]
        base = h * SUM_H
        sent = rows_at(diff, base + (1 - a) * SUM_Q, SUM_Q)
        one = remote(sent, part.at[h], ss.at[h, 0], rs.at[h, 0], hop[h][0])
        two = remote(rows_at(mid.at[h], (1 - b) * SUM_E, SUM_E), buf.at[h], ss.at[h, 1], rs.at[h, 1], hop[h][1])
        done = rows_at(out, base + a * SUM_Q + b * SUM_E, SUM_E)
        three = remote(done, done, ss.at[h, 2], rs.at[h, 2], hop[h][1])
        whole = rows_at(out, base + a * SUM_Q, SUM_Q)
        four = remote(whole, whole, ss.at[h, 3], rs.at[h, 3], hop[h][0])
        return one, two, three, four

    steps = [copies(0), copies(1)]
    chunk = 80

    def at(lo, i):
        return pl.ds(pl.multiple_of(lo + i * chunk, 16), chunk)

    for h in (0, 1):
        steps[h][0].start()
    for h in (0, 1):
        a, b = mine[h]
        steps[h][0].wait_recv()
        lo, src = (1 - b) * SUM_E, h * SUM_H + a * SUM_Q + (1 - b) * SUM_E

        def first(i, _):
            total = diff[at(src, i), :].astype(jnp.float32) + part[h, at(lo, i), :].astype(jnp.float32)
            mid[h, at(lo, i), :] = total.astype(jnp.bfloat16)
            return 0
        lax.fori_loop(0, SUM_E // chunk, first, 0)
        steps[h][1].start()
    for h in (0, 1):
        a, b = mine[h]
        steps[h][1].wait_recv()
        lo, src = b * SUM_E, h * SUM_H + a * SUM_Q + b * SUM_E

        def second(i, _):
            total = diff[at(src, i), :].astype(jnp.float32) + part[h, at(lo, i), :].astype(jnp.float32)
            total = total + buf[h, at(0, i), :].astype(jnp.float32)
            out[at(src, i), :] = (total * 0.25).astype(jnp.bfloat16)
            return 0
        lax.fori_loop(0, SUM_E // chunk, second, 0)
        steps[h][2].start()
    for h in (0, 1):
        a, b = mine[h]
        other = rows_at(out, h * SUM_H + a * SUM_Q + (1 - b) * SUM_E, SUM_E)
        remote(other, other, ss.at[h, 2], rs.at[h, 2], hop[h][1]).wait_recv()
        steps[h][2].wait_send()
        steps[h][3].start()
    for h in (0, 1):
        a, b = mine[h]
        other = rows_at(out, h * SUM_H + (1 - a) * SUM_Q, SUM_Q)
        remote(other, other, ss.at[h, 3], rs.at[h, 3], hop[h][0]).wait_recv()
        steps[h][0].wait_send()
        steps[h][1].wait_send()
        steps[h][3].wait_send()


def mean_groups(diff):
    vm = pl.BlockSpec(memory_space=pltpu.VMEM)
    return pl.pallas_call(
        mean_kernel,
        name="mean_groups",
        out_shape=jax.ShapeDtypeStruct((SUM_ROWS, 128), jnp.bfloat16),
        in_specs=[vm],
        out_specs=vm,
        scratch_shapes=[
            pltpu.VMEM((2, SUM_Q, 128), jnp.bfloat16),
            pltpu.VMEM((2, SUM_Q, 128), jnp.bfloat16),
            pltpu.VMEM((2, SUM_E, 128), jnp.bfloat16),
            DMA((2, 4)), DMA((2, 4)),
        ],
        compiler_params=pltpu.CompilerParams(collective_id=2, has_side_effects=True),
    )(diff)


MATRIX_WIDTH = (4 * D * D + 2 * D * MLP) // 8


def optimizer(summed, norm_value, master, first_moment, second_moment, outer_momentum):
    clipped = summed * (clip_limit / (norm_value + 1e-06))
    moment_one = beta_first * first_moment[0] + (1.0 - beta_first) * clipped
    moment_two = beta_second * second_moment[0] + (1.0 - beta_second) * clipped * clipped
    corrected_one = moment_one / (1.0 - beta_first**adam_count)
    corrected_two = moment_two / (1.0 - beta_second**adam_count)
    decay_mask = (jnp.arange(master.shape[0], dtype=jnp.int32) < MATRIX_WIDTH).astype(F32)
    step_rate = base_rate * rate_scale
    difference = step_rate * (
        corrected_one / (jnp.sqrt(corrected_two) + adam_epsilon)
        + weight_decay * decay_mask * master
    )
    low = jnp.pad(difference.astype(BF16), (0, SUM_ROWS * 128 - master.shape[0]))
    mean_difference = mean_groups(low.reshape(SUM_ROWS, 128)).reshape(-1)[: master.shape[0]]
    mean_difference = mean_difference.astype(F32)
    outer_new = outer_beta * outer_momentum + mean_difference
    new_weights = master - outer_rate * (mean_difference + outer_beta * outer_new)
    return moment_one, moment_two, mean_difference, outer_new, new_weights


def on_small_slice(tokens, cotangent, crop_lengths, master, first_moment, second_moment, outer_momentum):
    row_count = tokens.shape[0]
    _segment, validity = pack_layout(crop_lengths[0], row_count)
    valid = jnp.broadcast_to(validity[:, None], (row_count, 128))
    lin = master[:MATRIX_WIDTH].reshape(-1, 128)
    vector = master[MATRIX_WIDTH:].astype(BF16).astype(F32).reshape(14, ROWS)
    piece = jnp.pad(vector, ((0, 2), (0, 128 - ROWS)))
    wa, wb, wc, vec, fb1, normed, projected, attended, lse = front(crop_lengths, lin, piece, tokens)
    block_output, grad_middle, grad_attended, gbc, gproj, vg, vg1 = mlp_block(
        tokens, cotangent, valid, attended, wa, wb, wc.reshape(MLP, D), vec, fb1
    )
    input_grad, grad_lin, sv, sq = back(
        crop_lengths, vec, vg, vg1, tokens, grad_middle, wa, normed, projected, grad_attended, lse, gbc, gproj
    )
    summed = jnp.concatenate([grad_lin.reshape(-1), sv[:14, :ROWS].reshape(-1)])
    norm_value = jnp.sqrt(sq[0, 0])
    vector_part = summed[MATRIX_WIDTH:] / (8 * row_count) ** 0.5
    moment_one, moment_two, mean_difference, outer_new, new_weights = optimizer(
        summed, norm_value, master, first_moment, second_moment, outer_momentum
    )
    return (
        block_output,
        input_grad,
        norm_value.reshape(1),
        vector_part[None],
        moment_one[None],
        moment_two[None],
        mean_difference,
        outer_new,
        new_weights,
    )


def solution(mesh):
    small = mesh.shape["grp"] == 4 and mesh.shape["tok"] == 8
    return jax.shard_map(
        on_small_slice if small else on_device,
        mesh=mesh,
        in_specs=(
            P(("grp", "tok"), None),
            P(("grp", "tok"), None),
            P(("grp", "tok"), None),
            P("tok"),
            P("grp", "tok"),
            P("grp", "tok"),
            P("tok"),
        ),
        out_specs=(
            P(("grp", "tok"), None),
            P(("grp", "tok"), None),
            P("grp"),
            P("grp", "tok"),
            P("grp", "tok"),
            P("grp", "tok"),
            P("tok"),
            P("tok"),
            P("tok"),
        ),
        check_vma=False,
    )
```

```python
import jax
import jax.numpy as jnp
from jax import lax
from jax.experimental import pallas as pl
from jax.experimental.pallas import tpu as pltpu
from jax.sharding import PartitionSpec as P

D = 768
MLP = 3072
HEADS = 12
HEAD_DIM = 64
ROWS = D // 8
ANY = pl.BlockSpec(memory_space=pl.ANY)
DMA = pltpu.SemaphoreType.DMA
MESH_ID = pl.DeviceIdType.MESH
NZ = 4
F32, BF16 = jnp.float32, jnp.bfloat16


def place():
    g = lax.axis_index("grp")
    t = lax.axis_index("tok")
    z, c = lax.div(t, 2), lax.rem(t, 2)
    gx = g + 1 - 2 * lax.rem(g, 2)
    gy = g + 2 - 4 * lax.div(g, 2)
    return g, t, z, c, gx, gy


def greet(targets, count):
    barrier = pltpu.get_barrier_semaphore()
    for target in targets:
        pl.semaphore_signal(barrier, inc=1, device_id=target, device_id_type=MESH_ID)
    pl.semaphore_wait(barrier, count)


def remote(src, dst, send, recv, target):
    return pltpu.make_async_remote_copy(
        src_ref=src, dst_ref=dst, send_sem=send, recv_sem=recv,
        device_id=target, device_id_type=MESH_ID,
    )


clip_limit = 3.0
beta_first = 0.9
beta_second = 0.999
adam_epsilon = 1e-08
weight_decay = 0.04
adam_count = 10.0
base_rate = 0.075
rate_scale = 0.9**6
outer_rate = 0.7
outer_beta = 0.9
norm_epsilon = 1e-06


def member_extents():
    return [(D, 3 * D), (D, D), (D, MLP), (MLP, D)] + [(D,)] * 8 + [(MLP,), (D,), (D,)]


def member_sizes():
    sizes_list = []
    for extent in member_extents():
        length = 1
        for member in extent:
            length = length * member
        sizes_list.append(length)
    return sizes_list


def split_params(flat_params, owners):
    table = flat_params.reshape(owners, -1)
    members = []
    offset = 0
    for extent, length in zip(member_extents(), member_sizes()):
        width = length // owners
        members.append(table[:, offset : offset + width].reshape(extent))
        offset = offset + width
    return members


def join_table(members, owners):
    return jnp.concatenate([member.reshape(owners, -1) for member in members], axis=1)


def layer_norm(values, norm_gain, norm_shift):
    center = values - jnp.mean(values, axis=-1, keepdims=True)
    spread = jnp.mean(center * center, axis=-1, keepdims=True)
    return center * lax.rsqrt(spread + norm_epsilon) * norm_gain + norm_shift


def pack_layout(lengths_row, row_count):
    ends_at = jnp.cumsum(lengths_row)
    position = jnp.arange(row_count, dtype=jnp.int32)
    segment = jnp.sum((position[:, None] >= ends_at[None, :]).astype(jnp.int32), axis=1)
    validity = (position < ends_at[-1]).astype(jnp.float32)
    return (segment, validity)


def cross_rows(left_side, right_side):
    return lax.dot_general(
        left_side, right_side, (((0,), (0,)), ((), ())), preferred_element_type=jnp.float32
    )


def times_transposed(left_side, right_side):
    return lax.dot_general(
        left_side, right_side, (((1,), (1,)), ((), ())), preferred_element_type=jnp.float32
    )


def on_device(tokens, cotangent, crop_lengths, master, first_moment, second_moment, outer_momentum):
    row_count = tokens.shape[0]
    pair_count = HEADS // 2
    score_scale = HEAD_DIM ** (-0.5)
    owners = lax.axis_size("tok")
    segment, validity = pack_layout(crop_lengths[0], row_count)
    allowed = segment[:, None] == segment[None, :]
    master_low = master.astype(jnp.bfloat16)
    gathered = split_params(lax.all_gather(master_low, "tok", axis=0, tiled=True), owners)
    w_qkv, w_proj, w_fc1, w_fc2 = gathered[:4]
    (
        gain_one,
        shift_one,
        query_bias,
        value_bias,
        proj_bias,
        scale_one,
        gain_two,
        shift_two,
        fc1_bias,
        fc2_bias,
        scale_two,
    ) = [member.astype(jnp.float32) for member in gathered[4:]]

    def to_pairs(block_cols):
        return jnp.moveaxis(block_cols.reshape(row_count, pair_count, 2 * HEAD_DIM), 1, 0)

    def from_pairs(paired):
        return jnp.moveaxis(paired, 0, 1).reshape(row_count, D)

    normed = layer_norm(tokens, gain_one, shift_one).astype(jnp.bfloat16)
    qkv_bias = jnp.concatenate([query_bias, jnp.zeros_like(query_bias), value_bias])
    projected = (jnp.dot(normed, w_qkv, preferred_element_type=jnp.float32) + qkv_bias).astype(
        jnp.bfloat16
    )
    query_pairs = to_pairs(projected[:, :D])
    key_pairs = to_pairs(projected[:, D : 2 * D])
    value_pairs = to_pairs(projected[:, 2 * D :])

    def forward_pair(pair_item):
        queries, keys_pair, values_pair = [
            member.reshape(row_count, 2, HEAD_DIM) for member in pair_item
        ]
        raw_scores = jnp.einsum(
            "qhd,khd->hqk", queries, keys_pair, preferred_element_type=jnp.float32
        )
        scores = jnp.where(allowed[None], raw_scores * score_scale, -1e30)
        largest = jnp.max(scores, axis=-1, keepdims=True)
        weights_exp = jnp.exp(scores - largest)
        totals = jnp.sum(weights_exp, axis=-1, keepdims=True)
        weights_low = (weights_exp / totals).astype(jnp.bfloat16)
        attended_pair = jnp.einsum(
            "hqk,khd->qhd", weights_low, values_pair, preferred_element_type=jnp.float32
        )
        return (attended_pair.reshape(row_count, 2 * HEAD_DIM), (largest + jnp.log(totals))[..., 0])

    attended_pairs, log_totals = lax.map(forward_pair, (query_pairs, key_pairs, value_pairs))
    attended = from_pairs(attended_pairs).astype(jnp.bfloat16)
    branch_one = jnp.dot(attended, w_proj, preferred_element_type=jnp.float32) + proj_bias
    middle = tokens + scale_one * branch_one
    normed_two = layer_norm(middle, gain_two, shift_two).astype(jnp.bfloat16)
    hidden_pre = jnp.dot(normed_two, w_fc1, preferred_element_type=jnp.float32) + fc1_bias
    hidden = jax.nn.gelu(hidden_pre, approximate=False).astype(jnp.bfloat16)
    branch_two = jnp.dot(hidden, w_fc2, preferred_element_type=jnp.float32) + fc2_bias
    block_output = middle + scale_two * branch_two
    back_out = cotangent * validity[:, None]
    grad_branch_two = (scale_two * back_out).astype(jnp.bfloat16)
    grad_scale_two = jnp.sum(back_out * branch_two, axis=0)
    grad_fc2_bias = jnp.sum(grad_branch_two.astype(jnp.float32), axis=0)
    grad_w_fc2 = cross_rows(hidden, grad_branch_two)
    grad_hidden = times_transposed(grad_branch_two, w_fc2)
    gelu_pull = jax.vjp(lambda values: jax.nn.gelu(values, approximate=False), hidden_pre)[1]
    grad_pre = gelu_pull(grad_hidden)[0].astype(jnp.bfloat16)
    grad_fc1_bias = jnp.sum(grad_pre.astype(jnp.float32), axis=0)
    grad_w_fc1 = cross_rows(normed_two, grad_pre)
    grad_normed_two = times_transposed(grad_pre, w_fc1)
    norm_pull = jax.vjp(layer_norm, middle, gain_two, shift_two)[1]
    grad_middle_part, grad_gain_two, grad_shift_two = norm_pull(grad_normed_two)
    grad_middle = back_out + grad_middle_part
    grad_scale_one = jnp.sum(grad_middle * branch_one, axis=0)
    grad_branch_one = (scale_one * grad_middle).astype(jnp.bfloat16)
    grad_proj_bias = jnp.sum(grad_branch_one.astype(jnp.float32), axis=0)
    grad_w_proj = cross_rows(attended, grad_branch_one)
    grad_attended = times_transposed(grad_branch_one, w_proj).astype(jnp.bfloat16)

    def backward_pair(pair_item):
        queries, keys_pair, values_pair, grad_pair = [
            member.reshape(row_count, 2, HEAD_DIM) for member in pair_item[:4]
        ]
        log_total = pair_item[4]
        raw_scores = jnp.einsum(
            "qhd,khd->hqk", queries, keys_pair, preferred_element_type=jnp.float32
        )
        scores = jnp.where(allowed[None], raw_scores * score_scale, -1e30)
        weights_soft = jnp.exp(scores - log_total[..., None])
        grad_values = jnp.einsum(
            "hqk,qhd->khd",
            weights_soft.astype(jnp.bfloat16),
            grad_pair,
            preferred_element_type=jnp.float32,
        )
        grad_weights = jnp.einsum(
            "qhd,khd->hqk", grad_pair, values_pair, preferred_element_type=jnp.float32
        )
        row_dot = jnp.sum(weights_soft * grad_weights, axis=-1, keepdims=True)
        grad_scores = (weights_soft * (grad_weights - row_dot)).astype(jnp.bfloat16)
        grad_queries = (
            jnp.einsum("hqk,khd->qhd", grad_scores, keys_pair, preferred_element_type=jnp.float32)
            * score_scale
        )
        grad_keys = (
            jnp.einsum("hqk,qhd->khd", grad_scores, queries, preferred_element_type=jnp.float32)
            * score_scale
        )
        return (
            grad_queries.reshape(row_count, 2 * HEAD_DIM),
            grad_keys.reshape(row_count, 2 * HEAD_DIM),
            grad_values.reshape(row_count, 2 * HEAD_DIM),
        )

    grad_q_pairs, grad_k_pairs, grad_v_pairs = lax.map(
        backward_pair, (query_pairs, key_pairs, value_pairs, to_pairs(grad_attended), log_totals)
    )
    grad_projected = jnp.concatenate(
        [from_pairs(grad_q_pairs), from_pairs(grad_k_pairs), from_pairs(grad_v_pairs)], axis=1
    ).astype(jnp.bfloat16)
    grad_query_bias = jnp.sum(grad_projected[:, :D].astype(jnp.float32), axis=0)
    grad_value_bias = jnp.sum(grad_projected[:, 2 * D :].astype(jnp.float32), axis=0)
    grad_w_qkv = cross_rows(normed, grad_projected)
    grad_normed = times_transposed(grad_projected, w_qkv)
    first_pull = jax.vjp(layer_norm, tokens, gain_one, shift_one)[1]
    grad_tokens_part, grad_gain_one, grad_shift_one = first_pull(grad_normed)
    input_grad = grad_middle + grad_tokens_part
    all_members = [
        grad_w_qkv,
        grad_w_proj,
        grad_w_fc1,
        grad_w_fc2,
        grad_gain_one,
        grad_shift_one,
        grad_query_bias,
        grad_value_bias,
        grad_proj_bias,
        grad_scale_one,
        grad_gain_two,
        grad_shift_two,
        grad_fc1_bias,
        grad_fc2_bias,
        grad_scale_two,
    ]
    received = lax.all_to_all(
        join_table(all_members, owners).astype(jnp.bfloat16),
        "tok",
        split_axis=0,
        concat_axis=0,
        tiled=True,
    ).astype(jnp.float32)
    summed = jnp.sum(received, axis=0)
    matrix_width = (4 * D * D + 2 * D * MLP) // owners
    vector_part = summed[matrix_width:] / (owners * row_count) ** 0.5
    square_total = lax.psum(jnp.sum(summed * summed), "tok")
    norm_value = jnp.sqrt(square_total)
    clipped = summed * (clip_limit / (norm_value + 1e-06))
    moment_one = beta_first * first_moment[0] + (1.0 - beta_first) * clipped
    moment_two = beta_second * second_moment[0] + (1.0 - beta_second) * clipped * clipped
    corrected_one = moment_one / (1.0 - beta_first**adam_count)
    corrected_two = moment_two / (1.0 - beta_second**adam_count)
    shard_size = master.shape[0]
    local_index = jnp.arange(shard_size, dtype=jnp.int32)
    decay_mask = (local_index < matrix_width).astype(jnp.float32)
    step_rate = base_rate * rate_scale
    updated = master - step_rate * (
        corrected_one / (jnp.sqrt(corrected_two) + adam_epsilon)
        + weight_decay * decay_mask * master
    )
    mean_difference = lax.psum((master - updated).astype(jnp.bfloat16), "grp").astype(
        jnp.float32
    ) / lax.axis_size("grp")
    outer_new = outer_beta * outer_momentum + mean_difference
    new_weights = master - outer_rate * (mean_difference + outer_beta * outer_new)
    return (
        block_output,
        input_grad,
        norm_value.reshape(1),
        vector_part[None],
        moment_one[None],
        moment_two[None],
        mean_difference,
        outer_new,
        new_weights,
    )


def rows_at(ref, start, count):
    return ref.at[pl.ds(pl.multiple_of(start, 16), count), :]


TILE = 256


def nn(a, b):
    return lax.dot_general(a, b, (((1,), (0,)), ((), ())), preferred_element_type=F32)


def nt(a, b):
    return lax.dot_general(a, b, (((1,), (1,)), ((), ())), preferred_element_type=F32)


def tn(a, b):
    return lax.dot_general(a, b, (((0,), (0,)), ((), ())), preferred_element_type=F32)


def normalize(values):
    center = values - jnp.mean(values, axis=-1, keepdims=True)
    spread = jnp.mean(center * center, axis=-1, keepdims=True)
    inverse = lax.rsqrt(spread + norm_epsilon)
    return center * inverse, inverse


def norm_pull(grad, normal, inverse, gain):
    scaled = grad * gain
    return inverse * (
        scaled
        - jnp.mean(scaled, axis=-1, keepdims=True)
        - normal * jnp.mean(scaled * normal, axis=-1, keepdims=True)
    )


def gelu_and_slope(x):
    phi = 0.5 * (1.0 + lax.erf(x * 0.7071067811865476))
    return x * phi, phi + x * jnp.exp(-0.5 * x * x) * 0.3989422804014327


def col_sum(x):
    return jnp.sum(x, axis=0, keepdims=True)


def mlp_kernel(tok, cot, valid, att, wa, wb, wc, vec, fb1, bo, gm, gatt, gout, gproj, vg, vg1, hid, gpre, n2, gb2, gb1, slope, wp, sem):
    load = pltpu.make_async_copy(wa.at[3], wp, sem.at[0])
    load.start()
    vg[...] = jnp.zeros_like(vg)
    vg1[...] = jnp.zeros_like(vg1)
    rows = tok.shape[0]
    load.wait()

    def row(j):
        return vec[j : j + 1, :]

    def tile(i, _):
        at = pl.ds(pl.multiple_of(i * TILE, TILE), TILE)
        branch_one = nn(att[at, :], wp[...]) + row(4)
        middle = tok[at, :] + row(5) * branch_one
        normal, inverse = normalize(middle)
        n2[at, :] = (normal * row(6) + row(7)).astype(BF16)

        def forward(q, _):
            low = pl.ds(pl.multiple_of(q * D, D), D)
            pre = nn(n2[at, :], wb[q]) + fb1[0:1, low]
            h, s = gelu_and_slope(pre)
            hid[at, low] = h.astype(BF16)
            slope[:, low] = s
            return 0
        lax.fori_loop(0, 4, forward, 0)
        branch_two = nn(hid[at, :], wc[...]) + row(12)
        bo[at, :] = middle + row(13) * branch_two
        back = cot[at, :] * valid[at, 0:1]
        low_back = (row(13) * back).astype(BF16)
        gb2[at, :] = low_back
        vg[13:14, :] += col_sum(back * branch_two)
        vg[12:13, :] += col_sum(low_back.astype(F32))

        def backward(q, total):
            low = pl.ds(pl.multiple_of(q * D, D), D)
            grad_hidden = nt(gb2[at, :], wc[low, :])
            grad = grad_hidden * slope[:, low]
            grad = grad.astype(BF16)
            gpre[at, low] = grad
            vg1[0:1, low] += col_sum(grad.astype(F32))
            return total + nt(grad, wb[q])
        grad_n2 = lax.fori_loop(0, 4, backward, jnp.zeros((TILE, D), F32))
        vg[6:7, :] += col_sum(grad_n2 * normal)
        vg[7:8, :] += col_sum(grad_n2)
        grad_mid = back + norm_pull(grad_n2, normal, inverse, row(6))
        gm[at, :] = grad_mid
        vg[5:6, :] += col_sum(grad_mid * branch_one)
        low_one = (row(5) * grad_mid).astype(BF16)
        gb1[at, :] = low_one
        vg[4:5, :] += col_sum(low_one.astype(F32))
        gatt[at, :] = nt(low_one, wp[...]).astype(BF16)
        return 0
    lax.fori_loop(0, rows // TILE, tile, 0)

    def fc2(t, _):
        low = pl.ds(pl.multiple_of(t * 384, 128), 384)
        gout[1, t] = tn(hid[:, low], gb2[...]).astype(BF16).reshape(4, 96, D)
        return 0
    lax.fori_loop(0, 8, fc2, 0)

    def fc1(q, _):
        def part(m, _):
            low = pl.ds(pl.multiple_of(q * D + m * 384, 128), 384)
            col = pl.ds(pl.multiple_of(m * 384, 128), 384)
            gout[0, :, q, :, col] = tn(n2[...], gpre[:, low]).astype(BF16).reshape(8, 96, 384)
            return 0
        return lax.fori_loop(0, 2, part, 0)
    lax.fori_loop(0, 4, fc1, 0)

    def proj(m, _):
        col = pl.ds(pl.multiple_of(m * 384, 128), 384)
        gproj[:, :, col] = tn(att[...], gb1[:, col]).astype(BF16).reshape(8, 96, 384)
        return 0
    lax.fori_loop(0, 2, proj, 0)


def mlp_block(tok, cot, valid, att, wa, wb, wc, vec, fb1):
    vm = pl.BlockSpec(memory_space=pltpu.VMEM)
    rows = tok.shape[0]
    S = jax.ShapeDtypeStruct
    return pl.pallas_call(
        mlp_kernel,
        name="mlp_block",
        out_shape=[
            S((rows, D), F32), S((rows, D), F32), S((rows, D), BF16),
            S((2, 8, 4, 96, D), BF16), S((8, 96, D), BF16), S((16, D), F32), S((8, MLP), F32),
        ],
        in_specs=[vm] * 4 + [ANY] + [vm] * 4,
        out_specs=[vm] * 7,
        scratch_shapes=[
            pltpu.VMEM((rows, MLP), BF16), pltpu.VMEM((rows, MLP), BF16),
            pltpu.VMEM((rows, D), BF16), pltpu.VMEM((rows, D), BF16), pltpu.VMEM((rows, D), BF16),
            pltpu.VMEM((TILE, MLP), F32), pltpu.VMEM((D, D), BF16), DMA((1,)),
        ],
        compiler_params=pltpu.CompilerParams(vmem_limit_bytes=62 * 2**20),
    )(tok, cot, valid, att, wa, wb, wc, vec, fb1)


QT = 256


def fill_bias(lens, bias):
    rows = bias.shape[0]
    column = lax.broadcasted_iota(jnp.int32, (rows, 128), 0)
    line = lax.broadcasted_iota(jnp.int32, (8, rows), 1)
    seg_col, seg_line = jnp.zeros((rows, 128), jnp.int32), jnp.zeros((8, rows), jnp.int32)
    end = jnp.int32(0)
    for j in range(lens.shape[1]):
        end = end + lens[0, j]
        seg_col = seg_col + (column >= end).astype(jnp.int32)
        seg_line = seg_line + (line >= end).astype(jnp.int32)

    for i in range(rows // 128):
        same = seg_col[i * 128 : (i + 1) * 128, 0:1] == seg_line[0:1, :]
        bias[pl.ds(i * 128, 128), :] = jnp.where(same, 0.0, -1e30).astype(F32)


def head_part(block, h):
    lane = lax.broadcasted_iota(jnp.int32, (1, 128), 1)
    keep = lane < 64 if h == 0 else lane >= 64
    return jnp.where(keep, block, jnp.zeros_like(block))


def first_half(a, b):
    lane = lax.broadcasted_iota(jnp.int32, (1, 128), 1)
    return jnp.where(lane < 64, a, b)


def norm_rows(tok, vec, normed):
    def tile(i, _):
        at = pl.ds(pl.multiple_of(i * QT, QT), QT)
        normal, _inverse = normalize(tok[at, :])
        normed[at, :] = (normal * vec[0:1, :] + vec[1:2, :]).astype(BF16)
        return 0
    lax.fori_loop(0, tok.shape[0] // QT, tile, 0)


def project_in(vec, wa, normed, proj):
    def block(i, _):
        at = pl.ds(pl.multiple_of(i * QT, QT), QT)
        proj[0, at, :] = (nn(normed[at, :], wa[0]) + vec[2:3, :]).astype(BF16)
        proj[1, at, :] = nn(normed[at, :], wa[1]).astype(BF16)
        proj[2, at, :] = (nn(normed[at, :], wa[2]) + vec[3:4, :]).astype(BF16)
        return 0
    lax.fori_loop(0, normed.shape[0] // QT, block, 0)


def attend(p, proj, bias, att, lse):
    rows = bias.shape[0]
    cols = pl.ds(pl.multiple_of(p * 128, 128), 128)

    def tile(i, _):
        at = pl.ds(pl.multiple_of(i * QT, QT), QT)
        q = proj[0, at, cols] * jnp.asarray(0.125, BF16)
        k, v = proj[1, :, cols], proj[2, :, cols]
        lane = lax.broadcasted_iota(jnp.int32, (1, 128), 1)
        outs = []
        logs = lse[at, :]
        for h in (0, 1):
            scores = nt(head_part(q, h), k) + bias[at, :]
            largest = jnp.max(scores, axis=-1, keepdims=True)
            weights = jnp.exp(scores - largest)
            total = jnp.sum(weights, axis=-1, keepdims=True)
            low = (weights * (1.0 / total)).astype(BF16)
            outs.append(nn(low, v))
            logs = jnp.where(lane == 2 * p + h, largest + jnp.log(total), logs)
        lse[at, :] = logs
        att[at, cols] = first_half(*outs).astype(BF16)
        return 0
    lax.fori_loop(0, rows // QT, tile, 0)


def attend_back(p, proj, gatt, bias, lse_t):
    rows = bias.shape[0]
    cols = pl.ds(pl.multiple_of(p * 128, 128), 128)
    k, v = proj[1, :, cols], proj[2, :, cols]

    def tile(i, carry):
        dk, dv = carry
        at = pl.ds(pl.multiple_of(i * QT, QT), QT)
        q = proj[0, at, cols]
        g = gatt[at, cols]
        scaled = q * jnp.asarray(0.125, BF16)
        dks, dvs, dqs = [], [], []
        for h in (0, 1):
            scores = nt(k, head_part(scaled, h)) + bias[:, at]
            probs = jnp.exp(scores - lse_t[pl.ds(2 * p + h, 1), at])
            grad = nt(v, head_part(g, h))
            dot = jnp.sum(probs * grad, axis=0, keepdims=True)
            low = (probs * (grad - dot)).astype(BF16)
            dvs.append(nn(probs.astype(BF16), g))
            dks.append(nn(low, scaled))
            dqs.append(tn(low, k))
        proj[0, at, cols] = (first_half(*dqs) * 0.125).astype(BF16)
        return dk + first_half(*dks), dv + first_half(*dvs)
    zero = jnp.zeros((rows, 128), F32)
    dk, dv = lax.fori_loop(0, rows // QT, tile, (zero, zero))
    proj[1, :, cols] = dk.astype(BF16)
    proj[2, :, cols] = dv.astype(BF16)


def weight_grads(normed, gproj, gout):
    def block(q, _):
        def part(m, _):
            col = pl.ds(pl.multiple_of(m * 384, 128), 384)
            gout[:, q, :, col] = tn(normed[...], gproj[q, :, col]).astype(BF16).reshape(8, ROWS, 384)
            return 0
        return lax.fori_loop(0, 2, part, 0)
    lax.fori_loop(0, 3, block, 0)


def row_grads(wide, total, vec, wa, gproj, vg):
    vg[...] = jnp.zeros_like(vg)

    def tile(i, _):
        at = pl.ds(pl.multiple_of(i * QT, QT), QT)
        grad = nt(gproj[0, at, :], wa[0]) + nt(gproj[1, at, :], wa[1]) + nt(gproj[2, at, :], wa[2])
        normal, inverse = normalize(wide[at, :D])
        vg[0:1, :] += col_sum(grad * normal)
        vg[1:2, :] += col_sum(grad)
        vg[2:3, :] += col_sum(gproj[0, at, :].astype(F32))
        vg[3:4, :] += col_sum(gproj[2, at, :].astype(F32))
        total[at, :] = total[at, :] + norm_pull(grad, normal, inverse, vec[0:1, :])
        return 0
    lax.fori_loop(0, total.shape[0] // QT, tile, 0)


def convert_piece(w, lin, piece):
    if w == 2:
        for q in range(4):
            for m in range(6):
                piece[q, :, 128 * m : 128 * m + 128] = lin[pl.ds(4608 + 576 * q + m, ROWS, stride=6), :].astype(BF16)
        return
    for q in range(4):
        for m in range(6):
            if w == 1:
                at = pl.ds(2304 + 6 * q + m, ROWS, stride=24)
            elif q == 3:
                at = pl.ds(1728 + m, ROWS, stride=6)
            else:
                at = pl.ds(6 * q + m, ROWS, stride=18)
            piece[q, :, 128 * m : 128 * m + 128] = lin[at, :].astype(BF16)


def weight_strip(w, ref, t):
    if w == 2:
        return ref.at[t]
    return ref.at[:, pl.ds(pl.multiple_of(t * ROWS, 16), ROWS), :]


def weight_block(w, ref, t, q, half=None):
    lead, count = (0, ROWS) if half is None else (48 * half, 48)
    if w == 2:
        return ref.at[t, q, pl.ds(lead, count), :]
    return ref.at[q, pl.ds(pl.multiple_of(t * ROWS + lead, 16), count), :]


def front_kernel(
    lens, lin, pv, tok,
    wa, wb, wc, vec, fb1, normed, proj, att, lse,
    pieces, wv, wa_in, bias,
    ls, zs, zr, xs, xr, ys, yr, ds, dr, cs, cr, vs, vr,
):
    g, t, z, c, gx, gy = place()
    fulls = (wa, wb, wc)
    peers = [lax.rem(t + k, 8) for k in range(1, 8)]
    barrier = pltpu.get_barrier_semaphore()
    for target in [(g, p) for p in peers] + [(gx, t), (gy, t)]:
        pl.semaphore_signal(barrier, inc=1, device_id=target, device_id_type=MESH_ID)
    convert_piece(0, lin, pieces.at[0])
    pl.semaphore_wait(barrier, 9)
    other = t + 1 - 2 * c

    def z_copy(w, d, s):
        step = 1 if d == 0 else -1
        src_t = t - 2 * step * s
        src = pieces.at[w, g] if s == 0 else weight_block(w, fulls[w], src_t, g)
        ok = (z - s >= 0) & (z + 1 < NZ) if d == 0 else (z + s < NZ) & (z - 1 >= 0)
        return ok, remote(src, weight_block(w, fulls[w], src_t, g), zs.at[w, d, s], zr.at[w, d, s], (g, t + 2 * step))

    def from_t(d, s):
        return t - 2 * (s + 1) if d == 0 else t + 2 * (s + 1)

    def here(d, s):
        return z - s - 1 >= 0 if d == 0 else z + s + 1 < NZ

    def z_wait(w, d, s):
        blk = weight_block(w, fulls[w], from_t(d, s), g)
        remote(blk, blk, zs.at[w, d, s], zr.at[w, d, s], (g, other)).wait_recv()

    def side_copy(w, d, s, axis):
        blk = weight_block(w, fulls[w], from_t(d, s), g)
        sems = (xs, xr) if axis == 0 else (ys, yr)
        return remote(blk, blk, sems[0].at[w, d, s], sems[1].at[w, d, s], (gx if axis == 0 else gy, t))

    def side_wait(w, d, s, axis):
        blk = weight_block(w, fulls[w], from_t(d, s), gx if axis == 0 else gy)
        sems = (xs, xr) if axis == 0 else (ys, yr)
        remote(blk, blk, sems[0].at[w, d, s], sems[1].at[w, d, s], (gx, t)).wait_recv()

    def diag_copy(w, d, s, axis):
        blk = weight_block(w, fulls[w], from_t(d, s), gx if axis == 0 else gy, axis)
        return remote(blk, blk, ds.at[w, d, s, axis], dr.at[w, d, s, axis], (gy if axis == 0 else gx, t))

    def diag_wait(w, d, s, axis):
        blk = weight_block(w, fulls[w], from_t(d, s), 3 - g, axis)
        remote(blk, blk, ds.at[w, d, s, axis], dr.at[w, d, s, axis], (gx, t)).wait_recv()

    def core_copy(w, d, s):
        blk = weight_strip(w, fulls[w], from_t(d, s))
        return remote(blk, blk, cs.at[w, d, s], cr.at[w, d, s], (g, other))

    def core_wait(w, d, s):
        blk = weight_strip(w, fulls[w], from_t(d, s) + 1 - 2 * c)
        remote(blk, blk, cs.at[w, d, s], cr.at[w, d, s], (g, other)).wait_recv()

    def own_copy(w):
        return remote(pieces.at[w], weight_strip(w, fulls[w], t), cs.at[w, 2, 0], cr.at[w, 2, 0], (g, other))

    def own_wait(w):
        blk = weight_strip(w, fulls[w], other)
        remote(blk, blk, cs.at[w, 2, 0], cr.at[w, 2, 0], (g, other)).wait_recv()

    def own_local(w):
        return pltpu.make_async_copy(pieces.at[w], weight_strip(w, fulls[w], t), ls.at[w])

    def both(s, fn):
        for d in (0, 1):
            @pl.when(here(d, s))
            def _():
                fn(d)

    def start_z(w, s):
        for d in (0, 1):
            ok, copy = z_copy(w, d, s)

            @pl.when(ok)
            def _():
                copy.start()

    def arrive(n):
        w, s = divmod(n, 3)
        both(s, lambda d: z_wait(w, d, s))
        if s < 2:
            start_z(w, s + 1)

        def sides(d):
            side_copy(w, d, s, 0).start()
            side_copy(w, d, s, 1).start()
        both(s, sides)
        if s == 0 and w < 2:
            start_z(w + 1, 0)
            own_copy(w + 1).start()

    def cross(n):
        w, s = divmod(n, 3)

        def fn(d):
            for axis in (0, 1):
                side_wait(w, d, s, axis)
                diag_copy(w, d, s, axis).start()
        both(s, fn)

    def finish(n):
        w, s = divmod(n, 3)

        def fn(d):
            diag_wait(w, d, s, 0)
            diag_wait(w, d, s, 1)
            core_copy(w, d, s).start()
        both(s, fn)

    def drain(w):
        own_wait(w)
        own_local(w).wait()
        for s in range(3):
            both(s, lambda d: core_wait(w, d, s))

    start_z(0, 0)
    own_copy(0).start()
    own_local(0).start()
    local_v = pltpu.make_async_copy(pv, wv.at[t], ls.at[3])
    local_v.start()
    v_copies = [remote(pv, wv.at[t], vs.at[k], vr.at[k], (g, peers[k])) for k in range(7)]
    for copy in v_copies:
        copy.start()
    for w in (1, 2):
        convert_piece(w, lin, pieces.at[w])
        own_local(w).start()
    fill_bias(lens, bias)
    lse[...] = jnp.zeros_like(lse)
    arrive(0)
    local_v.wait()
    for k in range(7):
        remote(pv, wv.at[lax.rem(t + 7 - k, 8)], vs.at[k], vr.at[k], (g, peers[k])).wait_recv()
    for k in range(8):
        vec[:, ROWS * k : ROWS * k + ROWS] = wv[k, :, :ROWS]
        for j in range(4):
            lead = 4 * ROWS * k + ROWS * j
            fb1[0:1, lead : lead + ROWS] = wv[k, 8 + j : 9 + j, :ROWS]
    arrive(1)
    cross(0)
    norm_rows(tok, vec, normed)
    arrive(2)
    cross(1)
    finish(0)
    arrive(3)
    cross(2)
    finish(1)
    finish(2)
    drain(0)
    load = pltpu.make_async_copy(wa.at[pl.ds(0, 3)], wa_in, ls.at[4])
    load.start()
    load.wait()
    project_in(vec, wa_in, normed, proj)
    arrive(4)
    cross(3)
    events = [
        [(arrive, 5), (arrive, 6), (cross, 4), (finish, 3)],
        [(arrive, 7), (cross, 5), (finish, 4)],
        [(arrive, 8), (cross, 6), (finish, 5)],
        [(cross, 7), (finish, 6)],
        [(cross, 8), (finish, 7)],
        [(finish, 8)],
    ]
    for p in range(6):
        attend(p, proj, bias, att, lse)
        for event, n in events[p]:
            event(n)
    drain(1)
    drain(2)
    for copy in v_copies:
        copy.wait_send()
    for w in range(3):
        own_copy(w).wait_send()
        for s in range(3):
            for d in (0, 1):
                ok, copy = z_copy(w, d, s)

                @pl.when(ok)
                def _():
                    copy.wait_send()

            def sent(d):
                side_copy(w, d, s, 0).wait_send()
                side_copy(w, d, s, 1).wait_send()
                diag_copy(w, d, s, 0).wait_send()
                diag_copy(w, d, s, 1).wait_send()
                core_copy(w, d, s).wait_send()
            both(s, sent)


def front(lens, lin, pv, tok):
    vm = pl.BlockSpec(memory_space=pltpu.VMEM)
    rows = tok.shape[0]
    S = jax.ShapeDtypeStruct
    return pl.pallas_call(
        front_kernel,
        name="front",
        out_shape=[
            S((4, D, D), BF16), S((4, D, D), BF16), S((8, 4, ROWS, D), BF16),
            S((16, D), F32), S((8, MLP), F32),
            S((rows, D), BF16), S((3, rows, D), BF16), S((rows, D), BF16), S((rows, 128), F32),
        ],
        in_specs=[pl.BlockSpec(memory_space=pltpu.SMEM)] + [vm] * 3,
        out_specs=[ANY] * 3 + [vm] * 6,
        scratch_shapes=[
            pltpu.VMEM((3, 4, ROWS, D), BF16),
            pltpu.VMEM((8, 16, 128), F32),
            pltpu.VMEM((3, D, D), BF16),
            pltpu.VMEM((rows, rows), F32),
            DMA((5,)),
            DMA((3, 2, 3)), DMA((3, 2, 3)),
            DMA((3, 2, 3)), DMA((3, 2, 3)),
            DMA((3, 2, 3)), DMA((3, 2, 3)),
            DMA((3, 2, 3, 2)), DMA((3, 2, 3, 2)),
            DMA((3, 3, 3)), DMA((3, 3, 3)),
            DMA((7,)), DMA((7,)),
        ],
        compiler_params=pltpu.CompilerParams(collective_id=0, has_side_effects=True, vmem_limit_bytes=60 * 2**20),
    )(lens, lin, pv, tok)


ORDER = (2, 1, 0)


def back_kernel(
    lens, vec, vg_in, vg1, tok, gm, wa, normed_in, proj_in, gatt_in, lse_in, gbc, gp,
    gin, lin, sv, sq,
    bias, tall, wa_v, normed, proj, gatt, lse_t, gout, own, core, zbuf, vg, gv, vbuf, qbuf,
    ls, os, cs, cr, zs, zr, vs, vr, qs, qr,
):
    g, t, z, c, gx, gy = place()
    peers = [lax.rem(t + k, 8) for k in range(1, 8)]
    rows = tok.shape[0]
    other = t + 1 - 2 * c
    loads = [
        pltpu.make_async_copy(src, dst, ls.at[i])
        for i, (src, dst) in enumerate(
            [
                (proj_in, proj), (gatt_in, gatt), (wa.at[pl.ds(0, 3)], wa_v), (normed_in, normed),
                (gp, gout.at[:, 3]), (gm, tall),
            ]
        )
    ]
    for copy in loads:
        copy.start()
    greet([(g, p) for p in peers], 7)

    def own_at(w, k):
        return gout.at[2 * k + c] if w == 0 else own.at[w - 1, k]

    def core_copy(w, k):
        src = gout.at[2 * k + 1 - c] if w == 0 else gbc.at[w - 1, 2 * k + 1 - c]
        return remote(src, core.at[w, k], cs.at[w, k], cr.at[w, k], (g, other))

    def load(w, k):
        return pltpu.make_async_copy(gbc.at[w - 1, 2 * k + c], own.at[w - 1, k], os.at[w, k])

    def begin(w):
        for k in (3, 0, 2, 1):
            core_copy(w, k).start()
            if w:
                load(w, k).start()

    def slot(d, k):
        return k - 1 if d == 0 else k

    def total_of(w, k, q, at, extra):
        mine = own_at(w, k)
        total = mine[q, at, :].astype(F32) + core[w, k, q, at, :].astype(F32)
        for d in extra:
            total = total + zbuf[d, w, slot(d, k), q, at, :].astype(F32)
        return total

    def add_rows(w, k, h, extra):
        for q in (2 * h, 2 * h + 1):
            def body(i, _):
                at = pl.ds(pl.multiple_of(i * 32, 32), 32)
                own_at(w, k)[q, at, :] = total_of(w, k, q, at, extra).astype(BF16)
                return 0
            lax.fori_loop(0, ROWS // 32, body, 0)

    def lay_out(w, k, h, extra):
        for q in (2 * h, 2 * h + 1):
            if w == 2:
                base, stride = 4608 + 576 * q, 6
            elif w == 1:
                base, stride = 2304 + 6 * q, 24
            else:
                base, stride = (1728, 6) if q == 3 else (6 * q, 18)

            def body(i, _):
                at = pl.ds(pl.multiple_of(i * 32, 32), 32)
                total = total_of(w, k, q, at, extra)
                for m in range(6):
                    lin[pl.ds(base + m + i * (32 * stride), 32, stride=stride), :] = total[:, 128 * m : 128 * m + 128]
                return 0
            lax.fori_loop(0, ROWS // 32, body, 0)

    def z_copy(w, d, k, h):
        step = 2 if d == 0 else -2
        at = pl.ds(2 * h, 2)
        return remote(
            own_at(w, k).at[at], zbuf.at[d, w, slot(d, k), at], zs.at[w, d, k, h], zr.at[w, d, k, h], (g, t + step)
        )

    def ready(w, k):
        if w:
            load(w, k).wait()
        core_copy(w, k).wait_recv()

    def pass_on(i, d, j, h):
        w = ORDER[i]
        reach = NZ - 1 - z if d == 0 else z
        k = z + j if d == 0 else z - j
        first = z == 0 if d == 0 else z == NZ - 1

        @pl.when(j <= reach)
        def _():
            if h == 0:
                ready(w, k)

            @pl.when(first)
            def _():
                add_rows(w, k, h, ())

            @pl.when(jnp.logical_not(first))
            def _():
                z_copy(w, d, k, h).wait_recv()
                add_rows(w, k, h, (d,))

            if i > 0:
                @pl.when(j == reach)
                def _():
                    z_copy(ORDER[i - 1], d, z + 1 if d == 0 else z - 1, h).wait_send()
            if j < NZ - 1:
                @pl.when(j < reach)
                def _():
                    z_copy(w, d, k + 1 if d == 0 else k - 1, h).wait_send()
            z_copy(w, d, k, h).start()

    def settle(i):
        w = ORDER[i]
        ready(w, z)
        for h in (0, 1):
            for cond, dirs in ((z == 0, (1,)), (z == NZ - 1, (0,)), ((z > 0) & (z < NZ - 1), (0, 1))):
                @pl.when(cond)
                def _():
                    for d in dirs:
                        z_copy(w, d, z, h).wait_recv()
                    lay_out(w, z, h, dirs)

    steps = [(i, j, h) for i in range(3) for j in (3, 2, 1) for h in (0, 1)]

    def run(lo, hi):
        for i, j, h in steps[lo:hi]:
            pass_on(i, 0, j, h)
            pass_on(i, 1, j, h)

    begin(2)
    begin(1)
    fill_bias(lens, bias)
    lse_t[...] = lse_in[...].T
    for n in (0, 1):
        loads[n].wait()
    run(0, 1)
    done = 1
    for p, count in enumerate((2, 1, 2, 1, 2, 1)):
        attend_back(p, proj, gatt, bias, lse_t)
        run(done, done + count)
        done += count
    for n in (2, 3, 4, 5):
        loads[n].wait()
    tok_load = pltpu.make_async_copy(tok, bias.at[:, pl.ds(0, D)], ls.at[6])
    tok_load.start()
    weight_grads(normed, proj, gout)
    begin(0)
    run(10, 11)
    tok_load.wait()
    row_grads(bias, tall, vec, wa_v, proj, vg)
    store = pltpu.make_async_copy(tall, gin, ls.at[7])
    store.start()
    vg[...] += vg_in[...]
    for k in range(8):
        gv[k, :, :ROWS] = vg[:, ROWS * k : ROWS * k + ROWS]
        for j in range(4):
            lead = 4 * ROWS * k + ROWS * j
            gv[k, 8 + j : 9 + j, :ROWS] = vg1[0:1, lead : lead + ROWS]
    v_copies = [remote(gv.at[peers[k]], vbuf.at[k], vs.at[k], vr.at[k], (g, peers[k])) for k in range(7)]
    for copy in v_copies:
        copy.start()
    run(11, 12)
    settle(0)
    run(12, 18)
    settle(1)
    for k in range(7):
        v_copies[k].wait_recv()
    total = gv[t]
    for k in range(7):
        total = total + vbuf[k]
    lane = lax.broadcasted_iota(jnp.int32, (16, 128), 1)
    line = lax.broadcasted_iota(jnp.int32, (16, 128), 0)
    total = jnp.where((lane < ROWS) & (line < 14), total, 0.0)
    sv[...] = total
    settle(2)

    def square(i, acc):
        v = lin[pl.ds(pl.multiple_of(i * 64, 64), 64), :]
        return acc + v * v
    acc = lax.fori_loop(0, 108, square, jnp.zeros((64, 128), F32))
    qbuf[7] = jnp.full((8, 128), jnp.sum(acc) + jnp.sum(total * total), F32)
    q_copies = [remote(qbuf.at[7], qbuf.at[k], qs.at[k], qr.at[k], (g, peers[k])) for k in range(7)]
    for copy in q_copies:
        copy.start()
    for w in range(3):
        for k in range(NZ):
            core_copy(w, k).wait_send()
    for h in (0, 1):
        @pl.when(z < NZ - 1)
        def _():
            z_copy(0, 0, z + 1, h).wait_send()

        @pl.when(z > 0)
        def _():
            z_copy(0, 1, z - 1, h).wait_send()
    store.wait()
    for k in range(7):
        q_copies[k].wait_recv()
    acc = qbuf[7]
    for k in range(7):
        acc = acc + qbuf[k]
    sq[...] = acc
    for k in range(7):
        q_copies[k].wait_send()
        v_copies[k].wait_send()


def back(lens, vec, vg, vg1, tok, gm, wa, normed, proj, gatt, lse, gbc, gp):
    vm = pl.BlockSpec(memory_space=pltpu.VMEM)
    rows = tok.shape[0]
    S = jax.ShapeDtypeStruct
    return pl.pallas_call(
        back_kernel,
        name="back",
        out_shape=[S((rows, D), F32), S((6912, 128), F32), S((16, 128), F32), S((8, 128), F32)],
        in_specs=[pl.BlockSpec(memory_space=pltpu.SMEM)] + [vm] * 3 + [ANY] * 6 + [vm] + [ANY] * 2,
        out_specs=[ANY] + [vm] * 3,
        scratch_shapes=[
            pltpu.VMEM((rows, rows), F32),
            pltpu.VMEM((rows, D), F32),
            pltpu.VMEM((3, D, D), BF16),
            pltpu.VMEM((rows, D), BF16),
            pltpu.VMEM((3, rows, D), BF16),
            pltpu.VMEM((rows, D), BF16),
            pltpu.VMEM((128, rows), F32),
            pltpu.VMEM((8, 4, ROWS, D), BF16),
            pltpu.VMEM((2, NZ, 4, ROWS, D), BF16),
            pltpu.VMEM((3, NZ, 4, ROWS, D), BF16),
            pltpu.VMEM((2, 3, NZ - 1, 4, ROWS, D), BF16),
            pltpu.VMEM((16, D), F32),
            pltpu.VMEM((8, 16, 128), F32),
            pltpu.VMEM((7, 16, 128), F32),
            pltpu.VMEM((8, 8, 128), F32),
            DMA((8,)), DMA((3, NZ)), DMA((3, NZ)), DMA((3, NZ)),
            DMA((3, 2, NZ, 2)), DMA((3, 2, NZ, 2)),
            DMA((7,)), DMA((7,)), DMA((7,)), DMA((7,)),
        ],
        compiler_params=pltpu.CompilerParams(
            collective_id=1, has_side_effects=True, vmem_limit_bytes=62 * 2**20
        ),
    )(lens, vec, vg, vg1, tok, gm, wa, normed, proj, gatt, lse, gbc, gp)


PARTS = 6912
SUM_H, SUM_Q, SUM_E = PARTS // 2, PARTS // 4, PARTS // 8
MATRIX_WIDTH = PARTS * 128
VECTOR_WIDTH = 14 * ROWS


def finish_kernel(
    grad, sv, sq, master, first, second, outer,
    first_new, second_new, mean_out, outer_new, weights_new, vector_out, norm_out,
    b_master, b_first, b_second, b_outer, b_mean, diff, mean, part, mid, buf, tail_grad, tail, ls, os, ss, rs, ts, tr,
):
    g, t, z, c, gx, gy = place()
    pairs = [(master, b_master.at[0]), (first, b_first), (second, b_second), (outer, b_outer.at[0])]
    loads = [pltpu.make_async_copy(src, dst, ls.at[i]) for i, (src, dst) in enumerate(pairs)]
    for copy in loads:
        copy.start()
    peers = [gx, gy, 3 - g]
    barrier = pltpu.get_barrier_semaphore()
    for peer in peers:
        pl.semaphore_signal(barrier, inc=1, device_id=(peer, t), device_id_type=MESH_ID)
    norm = jnp.sqrt(sq[0:1, 0:1])
    norm_out[...] = jnp.broadcast_to(norm, (8, 128))
    scale = clip_limit / (norm + 1e-06)
    for j in range(14):
        tail_grad[0:1, ROWS * j : ROWS * j + ROWS] = sv[j : j + 1, :ROWS]
    vector_out[...] = tail_grad[...] / jnp.sqrt(F32(8 * 1024))
    xi, yi = lax.rem(g, 2), lax.div(g, 2)
    hop = [((gx, t), (gy, t)), ((gy, t), (gx, t))]
    mine = [(xi, yi), (yi, xi)]

    def line(at):
        return pl.ds(pl.multiple_of(at.start * 128, 1024), at.size * 128)

    step_rate = base_rate * rate_scale

    def adam(value, old_first, old_second, weight, decay):
        clipped = value * scale
        new_first = beta_first * old_first + (1.0 - beta_first) * clipped
        new_second = beta_second * old_second + (1.0 - beta_second) * clipped * clipped
        root = jnp.sqrt(new_second * (1.0 / (1.0 - beta_second**adam_count))) + adam_epsilon
        ahead = new_first * (1.0 / (1.0 - beta_first**adam_count)) / root
        if decay:
            ahead = ahead + weight_decay * weight
        return new_first, new_second, step_rate * ahead

    def nesterov(weight, momentum, average):
        new_momentum = outer_beta * momentum + average
        return new_momentum, weight - outer_rate * (average + outer_beta * new_momentum)

    def rows_loop(lo, count, fn):
        chunk = 48

        def body(i, _):
            fn(pl.ds(pl.multiple_of(lo + i * chunk, 16), chunk), pl.ds(pl.multiple_of(i * chunk, 16), chunk))
            return 0
        lax.fori_loop(0, count // chunk, body, 0)

    def adam_rows(lo, count):
        def fn(at, _):
            flat = line(at)
            b_first[:, flat], b_second[:, flat], ahead = adam(
                grad[at, :].reshape(1, -1), b_first[:, flat], b_second[:, flat], b_master[:, flat], True
            )
            diff[at, :] = ahead.reshape(-1, 128).astype(BF16)
        rows_loop(lo, count, fn)

    def outer_rows(lo, count):
        def fn(at, _):
            flat = line(at)
            average = mean[at, :].astype(F32).reshape(1, -1)
            b_mean[:, flat] = average
            b_outer[:, flat], b_master[:, flat] = nesterov(b_master[:, flat], b_outer[:, flat], average)
        rows_loop(lo, count, fn)

    def copies(h):
        a, b = mine[h]
        base = h * SUM_H
        sent = rows_at(diff, base + (1 - a) * SUM_Q, SUM_Q)
        one = remote(sent, part.at[h], ss.at[h, 0], rs.at[h, 0], hop[h][0])
        two = remote(rows_at(mid.at[h], (1 - b) * SUM_E, SUM_E), buf.at[h], ss.at[h, 1], rs.at[h, 1], hop[h][1])
        done = rows_at(mean, base + a * SUM_Q + b * SUM_E, SUM_E)
        three = remote(done, done, ss.at[h, 2], rs.at[h, 2], hop[h][1])
        whole = rows_at(mean, base + a * SUM_Q, SUM_Q)
        four = remote(whole, whole, ss.at[h, 3], rs.at[h, 3], hop[h][0])
        return one, two, three, four

    steps = [copies(0), copies(1)]
    for copy in loads[:3]:
        copy.wait()
    for h in (0, 1):
        adam_rows(h * SUM_H + (1 - mine[h][0]) * SUM_Q, SUM_Q)
        if h == 0:
            pl.semaphore_wait(barrier, 3)
        steps[h][0].start()
    at_tail = pl.ds(MATRIX_WIDTH, VECTOR_WIDTH)
    new_first, new_second, ahead = adam(tail_grad[...], b_first[:, at_tail], b_second[:, at_tail], None, False)
    b_first[:, at_tail] = new_first
    b_second[:, at_tail] = new_second
    tail[3, :, :] = jnp.zeros((1, 1408), F32)
    tail[3, :, pl.ds(0, VECTOR_WIDTH)] = ahead
    t_copies = [remote(tail.at[3], tail.at[k], ts.at[k], tr.at[k], (peers[k], t)) for k in range(3)]
    for copy in t_copies:
        copy.start()
    for h in (0, 1):
        adam_rows(h * SUM_H + mine[h][0] * SUM_Q, SUM_Q)
    stores = [pltpu.make_async_copy(b_first, first_new, os.at[0]), pltpu.make_async_copy(b_second, second_new, os.at[1])]
    for copy in stores:
        copy.start()
    for h in (0, 1):
        a, b = mine[h]
        steps[h][0].wait_recv()
        lo = (1 - b) * SUM_E
        src = h * SUM_H + a * SUM_Q + lo

        def fn(at, local):
            here = pl.ds(pl.multiple_of(lo + local.start, 16), local.size)
            mid[h, here, :] = (diff[at, :].astype(F32) + part[h, here, :].astype(F32)).astype(BF16)
        rows_loop(src, SUM_E, fn)
        steps[h][1].start()
    loads[3].wait()
    for h in (0, 1):
        a, b = mine[h]
        steps[h][1].wait_recv()
        lo = b * SUM_E
        src = h * SUM_H + a * SUM_Q + lo

        def fn(at, local):
            here = pl.ds(pl.multiple_of(lo + local.start, 16), local.size)
            total = diff[at, :].astype(F32) + part[h, here, :].astype(F32) + buf[h, local, :].astype(F32)
            mean[at, :] = (total * 0.25).astype(BF16)
        rows_loop(src, SUM_E, fn)
        steps[h][2].start()
    for copy in t_copies:
        copy.wait_recv()
    total = tail[3] + tail[0] + tail[1] + tail[2]
    average = total[:, :VECTOR_WIDTH] * 0.25
    b_mean[:, at_tail] = average
    new_momentum, new_weights = nesterov(b_master[:, at_tail], b_outer[:, at_tail], average)
    b_outer[:, at_tail] = new_momentum
    b_master[:, at_tail] = new_weights
    for h in (0, 1):
        a, b = mine[h]
        outer_rows(h * SUM_H + a * SUM_Q + b * SUM_E, SUM_E)
    for h in (0, 1):
        a, b = mine[h]
        rest = h * SUM_H + a * SUM_Q + (1 - b) * SUM_E
        other = rows_at(mean, rest, SUM_E)
        remote(other, other, ss.at[h, 2], rs.at[h, 2], hop[h][1]).wait_recv()
        steps[h][2].wait_send()
        steps[h][3].start()
        outer_rows(rest, SUM_E)
    for h in (0, 1):
        a, b = mine[h]
        rest = h * SUM_H + (1 - a) * SUM_Q
        other = rows_at(mean, rest, SUM_Q)
        remote(other, other, ss.at[h, 3], rs.at[h, 3], hop[h][0]).wait_recv()
        outer_rows(rest, SUM_Q)
    last = [
        pltpu.make_async_copy(b_mean.at[0], mean_out, os.at[2]),
        pltpu.make_async_copy(b_outer.at[0], outer_new, os.at[3]),
        pltpu.make_async_copy(b_master.at[0], weights_new, os.at[4]),
    ]
    for copy in last:
        copy.start()
    for h in (0, 1):
        steps[h][0].wait_send()
        steps[h][1].wait_send()
        steps[h][3].wait_send()
    for copy in t_copies:
        copy.wait_send()
    for copy in stores + last:
        copy.wait()


def finish(grad, sv, sq, master, first, second, outer):
    vm = pl.BlockSpec(memory_space=pltpu.VMEM)
    S = jax.ShapeDtypeStruct
    n = master.shape[0]
    flat = pltpu.VMEM((1, n), F32)
    return pl.pallas_call(
        finish_kernel,
        name="finish",
        out_shape=[S((1, n), F32)] * 2 + [S((n,), F32)] * 3 + [S((1, VECTOR_WIDTH), F32), S((8, 128), F32)],
        in_specs=[vm] * 3 + [ANY] * 4,
        out_specs=[ANY] * 5 + [vm] * 2,
        scratch_shapes=[flat] * 5
        + [
            pltpu.VMEM((PARTS, 128), BF16),
            pltpu.VMEM((PARTS, 128), BF16),
            pltpu.VMEM((2, SUM_Q, 128), BF16),
            pltpu.VMEM((2, SUM_Q, 128), BF16),
            pltpu.VMEM((2, SUM_E, 128), BF16),
            pltpu.VMEM((1, VECTOR_WIDTH), F32),
            pltpu.VMEM((4, 1, 1408), F32),
            DMA((4,)), DMA((5,)), DMA((2, 4)), DMA((2, 4)), DMA((3,)), DMA((3,)),
        ],
        compiler_params=pltpu.CompilerParams(collective_id=2, has_side_effects=True, vmem_limit_bytes=60 * 2**20),
    )(grad, sv, sq, master, first, second, outer)


def on_small_slice(tokens, cotangent, crop_lengths, master, first_moment, second_moment, outer_momentum):
    row_count = tokens.shape[0]
    _segment, validity = pack_layout(crop_lengths[0], row_count)
    valid = jnp.broadcast_to(validity[:, None], (row_count, 128))
    lin = master[:MATRIX_WIDTH].reshape(-1, 128)
    vector = master[MATRIX_WIDTH:].astype(BF16).astype(F32).reshape(14, ROWS)
    piece = jnp.pad(vector, ((0, 2), (0, 128 - ROWS)))
    wa, wb, wc, vec, fb1, normed, projected, attended, lse = front(crop_lengths, lin, piece, tokens)
    block_output, grad_middle, grad_attended, gbc, gproj, vg, vg1 = mlp_block(
        tokens, cotangent, valid, attended, wa, wb, wc.reshape(MLP, D), vec, fb1
    )
    input_grad, grad_lin, sv, sq = back(
        crop_lengths, vec, vg, vg1, tokens, grad_middle, wa, normed, projected, grad_attended, lse, gbc, gproj
    )
    moment_one, moment_two, mean_difference, outer_new, new_weights, vector_part, norm = finish(
        grad_lin, sv, sq, master, first_moment, second_moment, outer_momentum
    )
    return (
        block_output,
        input_grad,
        norm[0, :1],
        vector_part,
        moment_one,
        moment_two,
        mean_difference,
        outer_new,
        new_weights,
    )


def solution(mesh):
    small = mesh.shape["grp"] == 4 and mesh.shape["tok"] == 8
    return jax.shard_map(
        on_small_slice if small else on_device,
        mesh=mesh,
        in_specs=(
            P(("grp", "tok"), None),
            P(("grp", "tok"), None),
            P(("grp", "tok"), None),
            P("tok"),
            P("grp", "tok"),
            P("grp", "tok"),
            P("tok"),
        ),
        out_specs=(
            P(("grp", "tok"), None),
            P(("grp", "tok"), None),
            P("grp"),
            P("grp", "tok"),
            P("grp", "tok"),
            P("grp", "tok"),
            P("tok"),
            P("tok"),
            P("tok"),
        ),
        check_vma=False,
    )
```

```python
import jax
import jax.numpy as jnp
from jax import lax
from jax.experimental import pallas as pl
from jax.experimental.pallas import tpu as pltpu
from jax.sharding import PartitionSpec as P

D = 768
MLP = 3072
HEADS = 12
HEAD_DIM = 64
ROWS = D // 8
ANY = pl.BlockSpec(memory_space=pl.ANY)
DMA = pltpu.SemaphoreType.DMA
MESH_ID = pl.DeviceIdType.MESH
NZ = 4
F32, BF16 = jnp.float32, jnp.bfloat16


def place():
    g = lax.axis_index("grp")
    t = lax.axis_index("tok")
    z, c = lax.div(t, 2), lax.rem(t, 2)
    gx = g + 1 - 2 * lax.rem(g, 2)
    gy = g + 2 - 4 * lax.div(g, 2)
    return g, t, z, c, gx, gy


def greet(targets, count):
    barrier = pltpu.get_barrier_semaphore()
    for target in targets:
        pl.semaphore_signal(barrier, inc=1, device_id=target, device_id_type=MESH_ID)
    pl.semaphore_wait(barrier, count)


def remote(src, dst, send, recv, target):
    return pltpu.make_async_remote_copy(
        src_ref=src, dst_ref=dst, send_sem=send, recv_sem=recv,
        device_id=target, device_id_type=MESH_ID,
    )


clip_limit = 3.0
beta_first = 0.9
beta_second = 0.999
adam_epsilon = 1e-08
weight_decay = 0.04
adam_count = 10.0
base_rate = 0.075
rate_scale = 0.9**6
outer_rate = 0.7
outer_beta = 0.9
norm_epsilon = 1e-06


def member_extents():
    return [(D, 3 * D), (D, D), (D, MLP), (MLP, D)] + [(D,)] * 8 + [(MLP,), (D,), (D,)]


def member_sizes():
    sizes_list = []
    for extent in member_extents():
        length = 1
        for member in extent:
            length = length * member
        sizes_list.append(length)
    return sizes_list


def split_params(flat_params, owners):
    table = flat_params.reshape(owners, -1)
    members = []
    offset = 0
    for extent, length in zip(member_extents(), member_sizes()):
        width = length // owners
        members.append(table[:, offset : offset + width].reshape(extent))
        offset = offset + width
    return members


def join_table(members, owners):
    return jnp.concatenate([member.reshape(owners, -1) for member in members], axis=1)


def layer_norm(values, norm_gain, norm_shift):
    center = values - jnp.mean(values, axis=-1, keepdims=True)
    spread = jnp.mean(center * center, axis=-1, keepdims=True)
    return center * lax.rsqrt(spread + norm_epsilon) * norm_gain + norm_shift


def pack_layout(lengths_row, row_count):
    ends_at = jnp.cumsum(lengths_row)
    position = jnp.arange(row_count, dtype=jnp.int32)
    segment = jnp.sum((position[:, None] >= ends_at[None, :]).astype(jnp.int32), axis=1)
    validity = (position < ends_at[-1]).astype(jnp.float32)
    return (segment, validity)


def cross_rows(left_side, right_side):
    return lax.dot_general(
        left_side, right_side, (((0,), (0,)), ((), ())), preferred_element_type=jnp.float32
    )


def times_transposed(left_side, right_side):
    return lax.dot_general(
        left_side, right_side, (((1,), (1,)), ((), ())), preferred_element_type=jnp.float32
    )


def on_device(tokens, cotangent, crop_lengths, master, first_moment, second_moment, outer_momentum):
    row_count = tokens.shape[0]
    pair_count = HEADS // 2
    score_scale = HEAD_DIM ** (-0.5)
    owners = lax.axis_size("tok")
    segment, validity = pack_layout(crop_lengths[0], row_count)
    allowed = segment[:, None] == segment[None, :]
    master_low = master.astype(jnp.bfloat16)
    gathered = split_params(lax.all_gather(master_low, "tok", axis=0, tiled=True), owners)
    w_qkv, w_proj, w_fc1, w_fc2 = gathered[:4]
    (
        gain_one,
        shift_one,
        query_bias,
        value_bias,
        proj_bias,
        scale_one,
        gain_two,
        shift_two,
        fc1_bias,
        fc2_bias,
        scale_two,
    ) = [member.astype(jnp.float32) for member in gathered[4:]]

    def to_pairs(block_cols):
        return jnp.moveaxis(block_cols.reshape(row_count, pair_count, 2 * HEAD_DIM), 1, 0)

    def from_pairs(paired):
        return jnp.moveaxis(paired, 0, 1).reshape(row_count, D)

    normed = layer_norm(tokens, gain_one, shift_one).astype(jnp.bfloat16)
    qkv_bias = jnp.concatenate([query_bias, jnp.zeros_like(query_bias), value_bias])
    projected = (jnp.dot(normed, w_qkv, preferred_element_type=jnp.float32) + qkv_bias).astype(
        jnp.bfloat16
    )
    query_pairs = to_pairs(projected[:, :D])
    key_pairs = to_pairs(projected[:, D : 2 * D])
    value_pairs = to_pairs(projected[:, 2 * D :])

    def forward_pair(pair_item):
        queries, keys_pair, values_pair = [
            member.reshape(row_count, 2, HEAD_DIM) for member in pair_item
        ]
        raw_scores = jnp.einsum(
            "qhd,khd->hqk", queries, keys_pair, preferred_element_type=jnp.float32
        )
        scores = jnp.where(allowed[None], raw_scores * score_scale, -1e30)
        largest = jnp.max(scores, axis=-1, keepdims=True)
        weights_exp = jnp.exp(scores - largest)
        totals = jnp.sum(weights_exp, axis=-1, keepdims=True)
        weights_low = (weights_exp / totals).astype(jnp.bfloat16)
        attended_pair = jnp.einsum(
            "hqk,khd->qhd", weights_low, values_pair, preferred_element_type=jnp.float32
        )
        return (attended_pair.reshape(row_count, 2 * HEAD_DIM), (largest + jnp.log(totals))[..., 0])

    attended_pairs, log_totals = lax.map(forward_pair, (query_pairs, key_pairs, value_pairs))
    attended = from_pairs(attended_pairs).astype(jnp.bfloat16)
    branch_one = jnp.dot(attended, w_proj, preferred_element_type=jnp.float32) + proj_bias
    middle = tokens + scale_one * branch_one
    normed_two = layer_norm(middle, gain_two, shift_two).astype(jnp.bfloat16)
    hidden_pre = jnp.dot(normed_two, w_fc1, preferred_element_type=jnp.float32) + fc1_bias
    hidden = jax.nn.gelu(hidden_pre, approximate=False).astype(jnp.bfloat16)
    branch_two = jnp.dot(hidden, w_fc2, preferred_element_type=jnp.float32) + fc2_bias
    block_output = middle + scale_two * branch_two
    back_out = cotangent * validity[:, None]
    grad_branch_two = (scale_two * back_out).astype(jnp.bfloat16)
    grad_scale_two = jnp.sum(back_out * branch_two, axis=0)
    grad_fc2_bias = jnp.sum(grad_branch_two.astype(jnp.float32), axis=0)
    grad_w_fc2 = cross_rows(hidden, grad_branch_two)
    grad_hidden = times_transposed(grad_branch_two, w_fc2)
    gelu_pull = jax.vjp(lambda values: jax.nn.gelu(values, approximate=False), hidden_pre)[1]
    grad_pre = gelu_pull(grad_hidden)[0].astype(jnp.bfloat16)
    grad_fc1_bias = jnp.sum(grad_pre.astype(jnp.float32), axis=0)
    grad_w_fc1 = cross_rows(normed_two, grad_pre)
    grad_normed_two = times_transposed(grad_pre, w_fc1)
    norm_pull = jax.vjp(layer_norm, middle, gain_two, shift_two)[1]
    grad_middle_part, grad_gain_two, grad_shift_two = norm_pull(grad_normed_two)
    grad_middle = back_out + grad_middle_part
    grad_scale_one = jnp.sum(grad_middle * branch_one, axis=0)
    grad_branch_one = (scale_one * grad_middle).astype(jnp.bfloat16)
    grad_proj_bias = jnp.sum(grad_branch_one.astype(jnp.float32), axis=0)
    grad_w_proj = cross_rows(attended, grad_branch_one)
    grad_attended = times_transposed(grad_branch_one, w_proj).astype(jnp.bfloat16)

    def backward_pair(pair_item):
        queries, keys_pair, values_pair, grad_pair = [
            member.reshape(row_count, 2, HEAD_DIM) for member in pair_item[:4]
        ]
        log_total = pair_item[4]
        raw_scores = jnp.einsum(
            "qhd,khd->hqk", queries, keys_pair, preferred_element_type=jnp.float32
        )
        scores = jnp.where(allowed[None], raw_scores * score_scale, -1e30)
        weights_soft = jnp.exp(scores - log_total[..., None])
        grad_values = jnp.einsum(
            "hqk,qhd->khd",
            weights_soft.astype(jnp.bfloat16),
            grad_pair,
            preferred_element_type=jnp.float32,
        )
        grad_weights = jnp.einsum(
            "qhd,khd->hqk", grad_pair, values_pair, preferred_element_type=jnp.float32
        )
        row_dot = jnp.sum(weights_soft * grad_weights, axis=-1, keepdims=True)
        grad_scores = (weights_soft * (grad_weights - row_dot)).astype(jnp.bfloat16)
        grad_queries = (
            jnp.einsum("hqk,khd->qhd", grad_scores, keys_pair, preferred_element_type=jnp.float32)
            * score_scale
        )
        grad_keys = (
            jnp.einsum("hqk,qhd->khd", grad_scores, queries, preferred_element_type=jnp.float32)
            * score_scale
        )
        return (
            grad_queries.reshape(row_count, 2 * HEAD_DIM),
            grad_keys.reshape(row_count, 2 * HEAD_DIM),
            grad_values.reshape(row_count, 2 * HEAD_DIM),
        )

    grad_q_pairs, grad_k_pairs, grad_v_pairs = lax.map(
        backward_pair, (query_pairs, key_pairs, value_pairs, to_pairs(grad_attended), log_totals)
    )
    grad_projected = jnp.concatenate(
        [from_pairs(grad_q_pairs), from_pairs(grad_k_pairs), from_pairs(grad_v_pairs)], axis=1
    ).astype(jnp.bfloat16)
    grad_query_bias = jnp.sum(grad_projected[:, :D].astype(jnp.float32), axis=0)
    grad_value_bias = jnp.sum(grad_projected[:, 2 * D :].astype(jnp.float32), axis=0)
    grad_w_qkv = cross_rows(normed, grad_projected)
    grad_normed = times_transposed(grad_projected, w_qkv)
    first_pull = jax.vjp(layer_norm, tokens, gain_one, shift_one)[1]
    grad_tokens_part, grad_gain_one, grad_shift_one = first_pull(grad_normed)
    input_grad = grad_middle + grad_tokens_part
    all_members = [
        grad_w_qkv,
        grad_w_proj,
        grad_w_fc1,
        grad_w_fc2,
        grad_gain_one,
        grad_shift_one,
        grad_query_bias,
        grad_value_bias,
        grad_proj_bias,
        grad_scale_one,
        grad_gain_two,
        grad_shift_two,
        grad_fc1_bias,
        grad_fc2_bias,
        grad_scale_two,
    ]
    received = lax.all_to_all(
        join_table(all_members, owners).astype(jnp.bfloat16),
        "tok",
        split_axis=0,
        concat_axis=0,
        tiled=True,
    ).astype(jnp.float32)
    summed = jnp.sum(received, axis=0)
    matrix_width = (4 * D * D + 2 * D * MLP) // owners
    vector_part = summed[matrix_width:] / (owners * row_count) ** 0.5
    square_total = lax.psum(jnp.sum(summed * summed), "tok")
    norm_value = jnp.sqrt(square_total)
    clipped = summed * (clip_limit / (norm_value + 1e-06))
    moment_one = beta_first * first_moment[0] + (1.0 - beta_first) * clipped
    moment_two = beta_second * second_moment[0] + (1.0 - beta_second) * clipped * clipped
    corrected_one = moment_one / (1.0 - beta_first**adam_count)
    corrected_two = moment_two / (1.0 - beta_second**adam_count)
    shard_size = master.shape[0]
    local_index = jnp.arange(shard_size, dtype=jnp.int32)
    decay_mask = (local_index < matrix_width).astype(jnp.float32)
    step_rate = base_rate * rate_scale
    updated = master - step_rate * (
        corrected_one / (jnp.sqrt(corrected_two) + adam_epsilon)
        + weight_decay * decay_mask * master
    )
    mean_difference = lax.psum((master - updated).astype(jnp.bfloat16), "grp").astype(
        jnp.float32
    ) / lax.axis_size("grp")
    outer_new = outer_beta * outer_momentum + mean_difference
    new_weights = master - outer_rate * (mean_difference + outer_beta * outer_new)
    return (
        block_output,
        input_grad,
        norm_value.reshape(1),
        vector_part[None],
        moment_one[None],
        moment_two[None],
        mean_difference,
        outer_new,
        new_weights,
    )


def rows_at(ref, start, count):
    return ref.at[pl.ds(pl.multiple_of(start, 16), count), :]

TILE = 256


def nn(a, b):
    return lax.dot_general(a, b, (((1,), (0,)), ((), ())), preferred_element_type=F32)


def nt(a, b):
    return lax.dot_general(a, b, (((1,), (1,)), ((), ())), preferred_element_type=F32)


def tn(a, b):
    return lax.dot_general(a, b, (((0,), (0,)), ((), ())), preferred_element_type=F32)


def normalize(values):
    center = values - jnp.mean(values, axis=-1, keepdims=True)
    spread = jnp.mean(center * center, axis=-1, keepdims=True)
    inverse = lax.rsqrt(spread + norm_epsilon)
    return center * inverse, inverse


def norm_pull(grad, normal, inverse, gain):
    scaled = grad * gain
    return inverse * (
        scaled
        - jnp.mean(scaled, axis=-1, keepdims=True)
        - normal * jnp.mean(scaled * normal, axis=-1, keepdims=True)
    )


def gelu_and_slope(x):
    phi = 0.5 * (1.0 + lax.erf(x * 0.7071067811865476))
    return x * phi, phi + x * jnp.exp(-0.5 * x * x) * 0.3989422804014327


def col_sum(x):
    return jnp.sum(x, axis=0, keepdims=True)


QT = 256
LONG, SHORT = 261, 54
TILES = (
    (0, 272, 0, 384, 0, 261),
    (256, 272, 256, 384, 261, 522),
    (512, 288, 512, 384, 522, 792),
    (784, 240, 768, 256, 792, 1024),
)


def find_places(lens, line, column):
    crops = lens.shape[1]
    longs, shorts, begin = jnp.int32(0), jnp.int32(0), jnp.int32(0)
    at_line = lax.broadcasted_iota(jnp.int32, line.shape, 1)
    at_column = lax.broadcasted_iota(jnp.int32, column.shape, 0)
    new_line, new_column = at_line, at_column
    for j in range(crops):
        size = lens[0, j]
        is_long = (size == LONG).astype(jnp.int32)
        place_at = is_long * (longs * LONG) + (1 - is_long) * (2 * LONG + shorts * SHORT)
        shift = place_at - begin
        new_line = jnp.where((at_line >= begin) & (at_line < begin + size), at_line + shift, new_line)
        new_column = jnp.where((at_column >= begin) & (at_column < begin + size), at_column + shift, new_column)
        longs, shorts, begin = longs + is_long, shorts + 1 - is_long, begin + size
    line[...] = new_line
    column[...] = new_column


def to_places(line, first, count):
    rows = lax.broadcasted_iota(jnp.int32, (count, line.shape[1]), 0) + first
    return (rows == line[0:1, :]).astype(F32).astype(BF16)


def from_places(column, first, count):
    lanes = lax.broadcasted_iota(jnp.int32, (count, column.shape[0]), 1)
    return (lanes == column[pl.ds(first, count), 0:1]).astype(F32).astype(BF16)


def fill_bias(bias):
    def crop(at):
        found = jnp.zeros(at.shape, jnp.int32)
        for end in [LONG] + [2 * LONG + SHORT * j for j in range(9)]:
            found = found + (at >= end).astype(jnp.int32)
        return found

    for i, (row, rows, col, cols, low, high) in enumerate(TILES):
        at_row = lax.broadcasted_iota(jnp.int32, (rows, 1), 0) + row
        at_col = lax.broadcasted_iota(jnp.int32, (1, cols), 1) + col
        same = crop(at_row) == jnp.where((at_col >= low) & (at_col < high), crop(at_col), -1)
        bias[i, :rows, :cols] = jnp.where(same, 0.0, -1e30).astype(F32)


def head_part(block, h):
    lane = lax.broadcasted_iota(jnp.int32, (1, 128), 1)
    keep = lane < 64 if h == 0 else lane >= 64
    return jnp.where(keep, block, jnp.zeros_like(block))


def first_half(a, b):
    lane = lax.broadcasted_iota(jnp.int32, (1, 128), 1)
    return jnp.where(lane < 64, a, b)


def rows_from(tile, new, old):
    row, rows, low = tile[0], tile[1], tile[4]
    if row == low:
        return new
    return jnp.where(lax.broadcasted_iota(jnp.int32, (rows, 1), 0) + row >= low, new, old)


def norm_rows(tok, vec, normed):
    def tile(i, _):
        at = pl.ds(pl.multiple_of(i * QT, QT), QT)
        normal, _inverse = normalize(tok[at, :])
        normed[at, :] = (normal * vec[0:1, :] + vec[1:2, :]).astype(BF16)
        return 0
    lax.fori_loop(0, tok.shape[0] // QT, tile, 0)


def project_in(vec, wa, normed, proj):
    def block(i, _):
        at = pl.ds(pl.multiple_of(i * QT, QT), QT)
        proj[0, at, :] = (nn(normed[at, :], wa[0]) + vec[2:3, :]).astype(BF16)
        proj[1, at, :] = nn(normed[at, :], wa[1]).astype(BF16)
        proj[2, at, :] = (nn(normed[at, :], wa[2]) + vec[3:4, :]).astype(BF16)
        return 0
    lax.fori_loop(0, normed.shape[0] // QT, block, 0)


def move_rows(one_hot, src, dst):
    def block(i, _):
        first = pl.multiple_of(i * QT, QT)
        dst[pl.ds(first, QT), :] = nn(one_hot(first, QT), src[...]).astype(BF16)
        return 0
    lax.fori_loop(0, src.shape[0] // QT, block, 0)


def attend(p, proj, bias, att, lse):
    cols = pl.ds(pl.multiple_of(p * 128, 128), 128)
    lane = lax.broadcasted_iota(jnp.int32, (1, 128), 1)
    for i, tile in enumerate(TILES):
        row, rows, col, wide = tile[:4]
        at, keys = pl.ds(row, rows), pl.ds(col, wide)
        q = proj[0, at, cols] * jnp.asarray(0.125, BF16)
        k, v = proj[1, keys, cols], proj[2, keys, cols]
        outs = []
        logs = lse[at, :]
        for h in (0, 1):
            scores = nt(head_part(q, h), k) + bias[i, :rows, :wide]
            largest = jnp.max(scores, axis=-1, keepdims=True)
            weights = jnp.exp(scores - largest)
            total = jnp.sum(weights, axis=-1, keepdims=True)
            low = (weights * (1.0 / total)).astype(BF16)
            outs.append(nn(low, v))
            logs = jnp.where(lane == 2 * p + h, largest + jnp.log(total), logs)
        lse[at, :] = rows_from(tile, logs, lse[at, :])
        att[at, cols] = rows_from(tile, first_half(*outs), att[at, cols].astype(F32)).astype(BF16)


def attend_back(p, proj, gatt, bias, lse_t, dq):
    cols = pl.ds(pl.multiple_of(p * 128, 128), 128)
    dq[...] = jnp.zeros_like(dq)
    dks, dvs = [], []
    for i, tile in enumerate(TILES):
        row, rows, col, wide = tile[:4]
        at, queries = pl.ds(row, rows), pl.ds(col, wide)
        k, v = proj[1, at, cols], proj[2, at, cols]
        g = gatt[queries, cols]
        scaled = proj[0, queries, cols] * jnp.asarray(0.125, BF16)
        dk, dv, dqs = [], [], []
        for h in (0, 1):
            scores = nt(head_part(k, h), scaled) + bias[i, :rows, :wide]
            probs = jnp.exp(scores - lse_t[pl.ds(2 * p + h, 1), queries])
            grad = nt(head_part(v, h), g)
            dot = jnp.sum(probs * grad, axis=0, keepdims=True)
            low = (probs * (grad - dot)).astype(BF16)
            dv.append(nn(probs.astype(BF16), g))
            dk.append(nn(low, scaled))
            dqs.append(tn(low, k))
        dq[queries, :] += first_half(*dqs) * 0.125
        dks.append(first_half(*dk))
        dvs.append(first_half(*dv))
    for i, tile in enumerate(TILES):
        at = pl.ds(tile[0], tile[1])
        proj[1, at, cols] = rows_from(tile, dks[i], proj[1, at, cols].astype(F32)).astype(BF16)
        proj[2, at, cols] = rows_from(tile, dvs[i], proj[2, at, cols].astype(F32)).astype(BF16)
    proj[0, :, cols] = dq[...].astype(BF16)


def weight_grads(normed, gproj, gout):
    def block(q, _):
        def part(m, _):
            col = pl.ds(pl.multiple_of(m * 384, 128), 384)
            gout[:, q, :, col] = tn(normed[...], gproj[q, :, col]).astype(BF16).reshape(8, ROWS, 384)
            return 0
        return lax.fori_loop(0, 2, part, 0)
    lax.fori_loop(0, 3, block, 0)


def row_grads(column, wide, total, vec, wa, gproj, vg):

    def tile(i, _):
        first = pl.multiple_of(i * QT, QT)
        at = pl.ds(first, QT)
        back = from_places(column, first, QT)
        parts = [nn(back, gproj[j]).astype(BF16) for j in range(3)]
        grad = nt(parts[0], wa[0]) + nt(parts[1], wa[1]) + nt(parts[2], wa[2])
        normal, inverse = normalize(wide[at, :D])
        vg[0:1, :] += col_sum(grad * normal)
        vg[1:2, :] += col_sum(grad)
        vg[2:3, :] += col_sum(parts[0].astype(F32))
        vg[3:4, :] += col_sum(parts[2].astype(F32))
        total[at, :] = total[at, :] + norm_pull(grad, normal, inverse, vec[0:1, :])
        return 0
    lax.fori_loop(0, total.shape[0] // QT, tile, 0)


def convert_piece(w, lin, piece):
    if w == 2:
        for q in range(4):
            for m in range(6):
                piece[q, :, 128 * m : 128 * m + 128] = lin[pl.ds(4608 + 576 * q + m, ROWS, stride=6), :].astype(BF16)
        return
    for q in range(4):
        for m in range(6):
            if w == 1:
                at = pl.ds(2304 + 6 * q + m, ROWS, stride=24)
            elif q == 3:
                at = pl.ds(1728 + m, ROWS, stride=6)
            else:
                at = pl.ds(6 * q + m, ROWS, stride=18)
            piece[q, :, 128 * m : 128 * m + 128] = lin[at, :].astype(BF16)


def weight_strip(w, ref, t):
    if w == 2:
        return ref.at[t]
    return ref.at[:, pl.ds(pl.multiple_of(t * ROWS, 16), ROWS), :]


def weight_block(w, ref, t, q, half=None):
    lead, count = (0, ROWS) if half is None else (48 * half, 48)
    if w == 2:
        return ref.at[t, q, pl.ds(lead, count), :]
    return ref.at[q, pl.ds(pl.multiple_of(t * ROWS + lead, 16), count), :]


def front_kernel(
    lens, lin, pv, tok,
    wa, wb, wc, vec, fb1, normed, proj, att, lse_out,
    pieces, wv, wa_in, bias, line, column, att_in, lse,
    ls, zs, zr, xs, xr, ys, yr, ds, dr, cs, cr, vs, vr,
):
    g, t, z, c, gx, gy = place()
    fulls = (wa, wb, wc)
    peers = [lax.rem(t + k, 8) for k in range(1, 8)]
    barrier = pltpu.get_barrier_semaphore()
    for target in [(g, p) for p in peers] + [(gx, t), (gy, t)]:
        pl.semaphore_signal(barrier, inc=1, device_id=target, device_id_type=MESH_ID)
    convert_piece(0, lin, pieces.at[0])
    pl.semaphore_wait(barrier, 9)
    other = t + 1 - 2 * c

    def z_copy(w, d, s):
        step = 1 if d == 0 else -1
        src_t = t - 2 * step * s
        src = pieces.at[w, g] if s == 0 else weight_block(w, fulls[w], src_t, g)
        ok = (z - s >= 0) & (z + 1 < NZ) if d == 0 else (z + s < NZ) & (z - 1 >= 0)
        return ok, remote(src, weight_block(w, fulls[w], src_t, g), zs.at[w, d, s], zr.at[w, d, s], (g, t + 2 * step))

    def from_t(d, s):
        return t - 2 * (s + 1) if d == 0 else t + 2 * (s + 1)

    def here(d, s):
        return z - s - 1 >= 0 if d == 0 else z + s + 1 < NZ

    def z_wait(w, d, s):
        blk = weight_block(w, fulls[w], from_t(d, s), g)
        remote(blk, blk, zs.at[w, d, s], zr.at[w, d, s], (g, other)).wait_recv()

    def side_copy(w, d, s, axis):
        blk = weight_block(w, fulls[w], from_t(d, s), g)
        sems = (xs, xr) if axis == 0 else (ys, yr)
        return remote(blk, blk, sems[0].at[w, d, s], sems[1].at[w, d, s], (gx if axis == 0 else gy, t))

    def side_wait(w, d, s, axis):
        blk = weight_block(w, fulls[w], from_t(d, s), gx if axis == 0 else gy)
        sems = (xs, xr) if axis == 0 else (ys, yr)
        remote(blk, blk, sems[0].at[w, d, s], sems[1].at[w, d, s], (gx, t)).wait_recv()

    def diag_copy(w, d, s, axis):
        blk = weight_block(w, fulls[w], from_t(d, s), gx if axis == 0 else gy, axis)
        return remote(blk, blk, ds.at[w, d, s, axis], dr.at[w, d, s, axis], (gy if axis == 0 else gx, t))

    def diag_wait(w, d, s, axis):
        blk = weight_block(w, fulls[w], from_t(d, s), 3 - g, axis)
        remote(blk, blk, ds.at[w, d, s, axis], dr.at[w, d, s, axis], (gx, t)).wait_recv()

    def core_copy(w, d, s):
        blk = weight_strip(w, fulls[w], from_t(d, s))
        return remote(blk, blk, cs.at[w, d, s], cr.at[w, d, s], (g, other))

    def core_wait(w, d, s):
        blk = weight_strip(w, fulls[w], from_t(d, s) + 1 - 2 * c)
        remote(blk, blk, cs.at[w, d, s], cr.at[w, d, s], (g, other)).wait_recv()

    def own_copy(w):
        return remote(pieces.at[w], weight_strip(w, fulls[w], t), cs.at[w, 2, 0], cr.at[w, 2, 0], (g, other))

    def own_wait(w):
        blk = weight_strip(w, fulls[w], other)
        remote(blk, blk, cs.at[w, 2, 0], cr.at[w, 2, 0], (g, other)).wait_recv()

    def own_local(w):
        return pltpu.make_async_copy(pieces.at[w], weight_strip(w, fulls[w], t), ls.at[w])

    def both(s, fn):
        for d in (0, 1):
            @pl.when(here(d, s))
            def _():
                fn(d)

    def start_z(w, s):
        for d in (0, 1):
            ok, copy = z_copy(w, d, s)

            @pl.when(ok)
            def _():
                copy.start()

    def arrive(n):
        w, s = divmod(n, 3)
        both(s, lambda d: z_wait(w, d, s))
        if s < 2:
            start_z(w, s + 1)

        def sides(d):
            side_copy(w, d, s, 0).start()
            side_copy(w, d, s, 1).start()
        both(s, sides)
        if s == 0 and w < 2:
            start_z(w + 1, 0)
            own_copy(w + 1).start()

    def cross(n):
        w, s = divmod(n, 3)

        def fn(d):
            for axis in (0, 1):
                side_wait(w, d, s, axis)
                diag_copy(w, d, s, axis).start()
        both(s, fn)

    def finish(n):
        w, s = divmod(n, 3)

        def fn(d):
            diag_wait(w, d, s, 0)
            diag_wait(w, d, s, 1)
            core_copy(w, d, s).start()
        both(s, fn)

    def drain(w):
        own_wait(w)
        own_local(w).wait()
        for s in range(3):
            both(s, lambda d: core_wait(w, d, s))

    start_z(0, 0)
    own_copy(0).start()
    own_local(0).start()
    local_v = pltpu.make_async_copy(pv, wv.at[t], ls.at[3])
    local_v.start()
    v_copies = [remote(pv, wv.at[t], vs.at[k], vr.at[k], (g, peers[k])) for k in range(7)]
    for copy in v_copies:
        copy.start()
    for w in (1, 2):
        convert_piece(w, lin, pieces.at[w])
        own_local(w).start()
    fill_bias(bias)
    find_places(lens, line, column)
    att_in[...] = jnp.zeros_like(att_in)
    lse[...] = jnp.zeros_like(lse)
    arrive(0)
    local_v.wait()
    for k in range(7):
        remote(pv, wv.at[lax.rem(t + 7 - k, 8)], vs.at[k], vr.at[k], (g, peers[k])).wait_recv()
    for k in range(8):
        vec[:, ROWS * k : ROWS * k + ROWS] = wv[k, :, :ROWS]
        for j in range(4):
            lead = 4 * ROWS * k + ROWS * j
            fb1[0:1, lead : lead + ROWS] = wv[k, 8 + j : 9 + j, :ROWS]
    arrive(1)
    cross(0)
    norm_rows(tok, vec, att)
    move_rows(lambda first, count: to_places(line, first, count), att, normed)
    arrive(2)
    cross(1)
    finish(0)
    arrive(3)
    cross(2)
    finish(1)
    finish(2)
    drain(0)
    load = pltpu.make_async_copy(wa.at[pl.ds(0, 3)], wa_in, ls.at[4])
    load.start()
    load.wait()
    project_in(vec, wa_in, normed, proj)
    arrive(4)
    cross(3)
    events = [
        [(arrive, 5), (arrive, 6), (cross, 4), (finish, 3)],
        [(arrive, 7), (cross, 5), (finish, 4)],
        [(arrive, 8), (cross, 6), (finish, 5)],
        [(cross, 7), (finish, 6)],
        [(cross, 8), (finish, 7)],
        [(finish, 8)],
    ]
    for p in range(6):
        attend(p, proj, bias, att_in, lse)
        for event, n in events[p]:
            event(n)
    move_rows(lambda first, count: from_places(column, first, count), att_in, att)
    lse_out[...] = lse[...].T[:16]
    drain(1)
    drain(2)
    for copy in v_copies:
        copy.wait_send()
    for w in range(3):
        own_copy(w).wait_send()
        for s in range(3):
            for d in (0, 1):
                ok, copy = z_copy(w, d, s)

                @pl.when(ok)
                def _():
                    copy.wait_send()

            def sent(d):
                side_copy(w, d, s, 0).wait_send()
                side_copy(w, d, s, 1).wait_send()
                diag_copy(w, d, s, 0).wait_send()
                diag_copy(w, d, s, 1).wait_send()
                core_copy(w, d, s).wait_send()
            both(s, sent)


def front(lens, lin, pv, tok):
    vm = pl.BlockSpec(memory_space=pltpu.VMEM)
    rows = tok.shape[0]
    S = jax.ShapeDtypeStruct
    return pl.pallas_call(
        front_kernel,
        name="front",
        out_shape=[
            S((4, D, D), BF16), S((4, D, D), BF16), S((8, 4, ROWS, D), BF16),
            S((16, D), F32), S((8, MLP), F32),
            S((rows, D), BF16), S((3, rows, D), BF16), S((rows, D), BF16), S((16, rows), F32),
        ],
        in_specs=[pl.BlockSpec(memory_space=pltpu.SMEM)] + [vm] * 3,
        out_specs=[ANY] * 3 + [vm] * 6,
        scratch_shapes=[
            pltpu.VMEM((3, 4, ROWS, D), BF16),
            pltpu.VMEM((8, 16, 128), F32),
            pltpu.VMEM((3, D, D), BF16),
            pltpu.VMEM((4, 288, 384), F32),
            pltpu.VMEM((8, rows), jnp.int32),
            pltpu.VMEM((rows, 128), jnp.int32),
            pltpu.VMEM((rows, D), BF16),
            pltpu.VMEM((rows, 128), F32),
            DMA((5,)),
            DMA((3, 2, 3)), DMA((3, 2, 3)),
            DMA((3, 2, 3)), DMA((3, 2, 3)),
            DMA((3, 2, 3)), DMA((3, 2, 3)),
            DMA((3, 2, 3, 2)), DMA((3, 2, 3, 2)),
            DMA((3, 3, 3)), DMA((3, 3, 3)),
            DMA((7,)), DMA((7,)),
        ],
        compiler_params=pltpu.CompilerParams(collective_id=0, has_side_effects=True, vmem_limit_bytes=60 * 2**20),
    )(lens, lin, pv, tok)


def valid_rows(lens, first, count):
    total = jnp.int32(0)
    for j in range(lens.shape[1]):
        total = total + lens[0, j]
    at = lax.broadcasted_iota(jnp.int32, (count, 1), 0) + first
    return (at < total).astype(F32)


def forward_kernel(
    lens, tok_in, cot_in, att_in, wa, wb_in, wc_in, vec, fb1,
    bo_out, slope_out, n2_out, gc_out, vg,
    tok, cot, att, wp, wb, wc, bo, slope, n2, hid, gb2, gc, ls, os,
):
    pairs = [(att_in, att), (wa.at[3], wp), (tok_in, tok), (wb_in, wb), (wc_in, wc), (cot_in, cot)]
    loads = [pltpu.make_async_copy(src, dst, ls.at[i]) for i, (src, dst) in enumerate(pairs)]
    for copy in loads:
        copy.start()
    vg[...] = jnp.zeros_like(vg)
    rows = tok.shape[0]

    def row(j):
        return vec[j : j + 1, :]

    def stores(i):
        at = pl.ds(i * TILE, TILE)
        trio = [(bo, bo_out), (slope, slope_out), (n2, n2_out)]
        return [pltpu.make_async_copy(a.at[at, :], b.at[at, :], os.at[i, n]) for n, (a, b) in enumerate(trio)]

    for copy in loads[:3]:
        copy.wait()
    for i in range(rows // TILE):
        at = pl.ds(i * TILE, TILE)
        middle = tok[at, :] + row(5) * (nn(att[at, :], wp[...]) + row(4))
        normal, _inverse = normalize(middle)
        bo[at, :] = middle
        n2[at, :] = (normal * row(6) + row(7)).astype(BF16)
        if i == 0:
            loads[3].wait()

        def hidden(q, _):
            low = pl.ds(pl.multiple_of(q * D, D), D)
            pre = nn(n2[at, :], wb[q]) + fb1[0:1, low]
            h, s = gelu_and_slope(pre)
            hid[at, low] = h.astype(BF16)
            slope[at, low] = s.astype(BF16)
            return 0
        lax.fori_loop(0, 4, hidden, 0)
        if i == 0:
            loads[4].wait()
            loads[5].wait()
        branch_two = nn(hid[at, :], wc[...]) + row(12)
        bo[at, :] += row(13) * branch_two
        back = cot[at, :] * valid_rows(lens, i * TILE, TILE)
        low_back = (row(13) * back).astype(BF16)
        gb2[at, :] = low_back
        vg[13:14, :] += col_sum(back * branch_two)
        vg[12:13, :] += col_sum(low_back.astype(F32))
        for copy in stores(i):
            copy.start()

    def fc2(t, _):
        low = pl.ds(pl.multiple_of(t * 384, 128), 384)
        gc[t] = tn(hid[:, low], gb2[...]).astype(BF16).reshape(4, ROWS, D)
        return 0
    lax.fori_loop(0, 8, fc2, 0)
    store = pltpu.make_async_copy(gc, gc_out, os.at[4, 0])
    store.start()
    for i in range(rows // TILE):
        for copy in stores(i):
            copy.wait()
    store.wait()


def forward(lens, tok, cot, att, wa, wb, wc, vec, fb1):
    vm = pl.BlockSpec(memory_space=pltpu.VMEM)
    rows = tok.shape[0]
    S = jax.ShapeDtypeStruct
    V = pltpu.VMEM
    return pl.pallas_call(
        forward_kernel,
        name="mlp_forward",
        out_shape=[S((rows, D), F32), S((rows, MLP), BF16), S((rows, D), BF16), S((8, 4, ROWS, D), BF16), S((16, D), F32)],
        in_specs=[pl.BlockSpec(memory_space=pltpu.SMEM)] + [ANY] * 6 + [vm] * 2,
        out_specs=[ANY] * 4 + [vm],
        scratch_shapes=[
            V((rows, D), F32), V((rows, D), F32), V((rows, D), BF16), V((D, D), BF16),
            V((4, D, D), BF16), V((MLP, D), BF16), V((rows, D), F32), V((rows, MLP), BF16),
            V((rows, D), BF16), V((rows, MLP), BF16), V((rows, D), BF16), V((8, 4, ROWS, D), BF16),
            DMA((6,)), DMA((5, 3)),
        ],
        compiler_params=pltpu.CompilerParams(vmem_limit_bytes=62 * 2**20),
    )(lens, tok, cot, att, wa, wb, wc, vec, fb1)


ORDER = (2, 1, 0)


def back_kernel(
    lens, vec, vg_in, tok, cot, wa, wb_in, wc_in, att_in, slope_in, n2_in, normed_in, proj_in, lse_in, gc,
    gin, lin_out, sv, sq,
    line, column, wide, tall, gatt, gout, gb, own, core, zbuf, vg, vg1, gv, vbuf, qbuf,
    ls, os, cs, cr, zs, zr, vs, vr, qs, qr,
):
    g, t, z, c, gx, gy = place()
    peers = [lax.rem(t + k, 8) for k in range(1, 8)]
    rows = tok.shape[0]
    other = t + 1 - 2 * c

    def local(pairs, first):
        return [pltpu.make_async_copy(src, dst, ls.at[first + i]) for i, (src, dst) in enumerate(pairs)]

    loads = local([(tok, wide), (cot, tall)], 0)
    for copy in loads:
        copy.start()
    greet([(g, p) for p in peers], 7)

    def own_at(w, k):
        return (gout.at[2 * k + c], gb.at[2 * k + c], own.at[k])[w]

    def core_copy(w, k):
        return remote((gout, gb, gc)[w].at[2 * k + 1 - c], core.at[w, k], cs.at[w, k], cr.at[w, k], (g, other))

    def load(k):
        return pltpu.make_async_copy(gc.at[2 * k + c], own.at[k], os.at[k])

    def begin(w):
        for k in (3, 0, 2, 1):
            core_copy(w, k).start()
            if w == 2:
                load(k).start()

    def slot(d, k, to):
        return k - to if d == 0 else 4 - (to - k)

    def total_of(w, k, q, at, extra):
        mine = own_at(w, k)
        total = mine[q, at, :].astype(F32) + core[w, k, q, at, :].astype(F32)
        for d in extra:
            total = total + zbuf[w, slot(d, k, z), q, at, :].astype(F32)
        return total

    def add_rows(w, k, h, extra):
        for q in (2 * h, 2 * h + 1):
            def body(i, _):
                at = pl.ds(pl.multiple_of(i * 32, 32), 32)
                own_at(w, k)[q, at, :] = total_of(w, k, q, at, extra).astype(BF16)
                return 0
            lax.fori_loop(0, ROWS // 32, body, 0)

    def lay_out(lin, w, k, h, extra):
        for q in (2 * h, 2 * h + 1):
            if w == 2:
                base, stride = 4608 + 576 * q, 6
            elif w == 1:
                base, stride = 2304 + 6 * q, 24
            else:
                base, stride = (1728, 6) if q == 3 else (6 * q, 18)

            def body(i, _):
                at = pl.ds(pl.multiple_of(i * 32, 32), 32)
                total = total_of(w, k, q, at, extra)
                for m in range(6):
                    lin[pl.ds(base + m + i * (32 * stride), 32, stride=stride), :] = total[:, 128 * m : 128 * m + 128]
                return 0
            lax.fori_loop(0, ROWS // 32, body, 0)

    def z_copy(w, d, k, h):
        step = 1 if d == 0 else -1
        at = pl.ds(2 * h, 2)
        return remote(
            own_at(w, k).at[at],
            zbuf.at[w, slot(d, k, z + step), at],
            zs.at[w, d, k, h],
            zr.at[w, d, k, h],
            (g, t + 2 * step),
        )

    def z_wait(w, d, k, h):
        here = zbuf.at[w, slot(d, k, z), pl.ds(2 * h, 2)]
        remote(here, here, zs.at[w, d, k, h], zr.at[w, d, k, h], (g, other)).wait_recv()

    def ready(w, k):
        if w == 2:
            load(k).wait()
        core_copy(w, k).wait_recv()

    def pass_on(i, d, j, h):
        w = ORDER[i]
        reach = NZ - 1 - z if d == 0 else z
        k = z + j if d == 0 else z - j
        first = z == 0 if d == 0 else z == NZ - 1

        @pl.when(j <= reach)
        def _():
            if h == 0:
                ready(w, k)

            @pl.when(first)
            def _():
                add_rows(w, k, h, ())

            @pl.when(jnp.logical_not(first))
            def _():
                z_wait(w, d, k, h)
                add_rows(w, k, h, (d,))

            if i > 0:
                @pl.when(j == reach)
                def _():
                    z_copy(ORDER[i - 1], d, z + 1 if d == 0 else z - 1, h).wait_send()
            if j < NZ - 1:
                @pl.when(j < reach)
                def _():
                    z_copy(w, d, k + 1 if d == 0 else k - 1, h).wait_send()
            z_copy(w, d, k, h).start()

    def settle(lin, i):
        w = ORDER[i]
        ready(w, z)
        for h in (0, 1):
            for cond, dirs in ((z == 0, (1,)), (z == NZ - 1, (0,)), ((z > 0) & (z < NZ - 1), (0, 1))):
                @pl.when(cond)
                def _():
                    for d in dirs:
                        z_wait(w, d, z, h)
                    lay_out(lin, w, z, h, dirs)

    steps = [(i, j, h) for i in range(3) for j in (3, 2, 1) for h in (0, 1)]

    def run(lo, hi):
        for i, j, h in steps[lo:hi]:
            pass_on(i, 0, j, h)
            pass_on(i, 1, j, h)

    begin(2)
    find_places(lens, line, column)
    vg[...] = vg_in[...]
    vg1[...] = jnp.zeros_like(vg1)

    def mlp_part(wp, wb, wc, grads, n2, att, gb1):
        inner = local(
            [(att_in, att), (wa.at[3], wp), (wc_in, wc), (slope_in, grads), (wb_in, wb), (n2_in, n2)], 2
        )
        for copy in inner:
            copy.start()
        run(0, 2)
        for copy in loads + inner:
            copy.wait()

        def row(j):
            return vec[j : j + 1, :]

        def tile(i):
            at = pl.ds(i * TILE, TILE)
            branch_one = nn(att[at, :], wp[...]) + row(4)
            normal, inverse = normalize(wide[at, :] + row(5) * branch_one)
            tall[at, :] = tall[at, :] * valid_rows(lens, i * TILE, TILE)
            low_back = (row(13) * tall[at, :]).astype(BF16)

            def backward(q, total):
                low = pl.ds(pl.multiple_of(q * D, D), D)
                grad = nt(low_back, wc[low, :]) * grads[at, low].astype(F32)
                grad = grad.astype(BF16)
                grads[at, low] = grad
                vg1[0:1, low] += col_sum(grad.astype(F32))
                return total + nt(grad, wb[q])
            grad_n2 = lax.fori_loop(0, 4, backward, jnp.zeros((TILE, D), F32))
            vg[6:7, :] += col_sum(grad_n2 * normal)
            vg[7:8, :] += col_sum(grad_n2)
            grad_mid = tall[at, :] + norm_pull(grad_n2, normal, inverse, row(6))
            tall[at, :] = grad_mid
            vg[5:6, :] += col_sum(grad_mid * branch_one)
            low_one = (row(5) * grad_mid).astype(BF16)
            gb1[at, :] = low_one
            vg[4:5, :] += col_sum(low_one.astype(F32))
            gatt[at, :] = nt(low_one, wp[...]).astype(BF16)

        for i in range(rows // TILE):
            tile(i)
            run(2 + i, 3 + i)

        def fc1(q, _):
            def part(m, _):
                low = pl.ds(pl.multiple_of(q * D + m * 384, 128), 384)
                col = pl.ds(pl.multiple_of(m * 384, 128), 384)
                gb[:, q, :, col] = tn(n2[...], grads[:, low]).astype(BF16).reshape(8, ROWS, 384)
                return 0
            return lax.fori_loop(0, 2, part, 0)
        lax.fori_loop(0, 4, fc1, 0)
        begin(1)

        def proj_part(m, _):
            col = pl.ds(pl.multiple_of(m * 384, 128), 384)
            gout[:, 3, :, col] = tn(att[...], gb1[:, col]).astype(BF16).reshape(8, ROWS, 384)
            return 0
        lax.fori_loop(0, 2, proj_part, 0)

    pl.run_scoped(
        mlp_part,
        pltpu.VMEM((D, D), BF16),
        pltpu.VMEM((4, D, D), BF16),
        pltpu.VMEM((MLP, D), BF16),
        pltpu.VMEM((rows, MLP), BF16),
        pltpu.VMEM((rows, D), BF16),
        pltpu.VMEM((rows, D), BF16),
        pltpu.VMEM((rows, D), BF16),
    )
    v_copies = [remote(gv.at[peers[k]], vbuf.at[k], vs.at[k], vr.at[k], (g, peers[k])) for k in range(7)]
    q_copies = [remote(qbuf.at[7], qbuf.at[k], qs.at[k], qr.at[k], (g, peers[k])) for k in range(7)]

    def attention_part(lin, bias, lse_t, gatt_at, dq, wa_v, normed, proj):
        inner = local([(proj_in, proj), (lse_in, lse_t), (wa.at[pl.ds(0, 3)], wa_v), (normed_in, normed)], 8)
        for copy in inner:
            copy.start()
        run(6, 7)
        fill_bias(bias)
        move_rows(lambda first, count: to_places(line, first, count), gatt, gatt_at)
        for copy in inner:
            copy.wait()
        for p in range(6):
            attend_back(p, proj, gatt_at, bias, lse_t, dq)
            if p == 0:
                settle(lin, 0)
            if p < 5:
                run(7 + p, 8 + p)
        weight_grads(normed, proj, gout)
        begin(0)
        row_grads(column, wide, tall, vec, wa_v, proj, vg)
        store = pltpu.make_async_copy(tall, gin, ls.at[12])
        store.start()
        for k in range(8):
            gv[k, :, :ROWS] = vg[:, ROWS * k : ROWS * k + ROWS]
            for j in range(4):
                lead = 4 * ROWS * k + ROWS * j
                gv[k, 8 + j : 9 + j, :ROWS] = vg1[0:1, lead : lead + ROWS]
        run(12, 13)
        for copy in v_copies:
            copy.start()
        settle(lin, 1)
        run(13, 18)
        for k in range(7):
            v_copies[k].wait_recv()
        total = gv[t]
        for k in range(7):
            total = total + vbuf[k]
        lane = lax.broadcasted_iota(jnp.int32, (16, 128), 1)
        across = lax.broadcasted_iota(jnp.int32, (16, 128), 0)
        total = jnp.where((lane < ROWS) & (across < 14), total, 0.0)
        sv[...] = total
        settle(lin, 2)
        lin_store = pltpu.make_async_copy(lin, lin_out, ls.at[13])
        lin_store.start()

        def square(i, acc):
            v = lin[pl.ds(pl.multiple_of(i * 64, 64), 64), :]
            return acc + v * v
        acc = lax.fori_loop(0, 108, square, jnp.zeros((64, 128), F32))
        qbuf[7] = jnp.full((8, 128), jnp.sum(acc) + jnp.sum(total * total), F32)
        for copy in q_copies:
            copy.start()
        store.wait()
        lin_store.wait()

    pl.run_scoped(
        attention_part,
        pltpu.VMEM((6912, 128), F32),
        pltpu.VMEM((4, 288, 384), F32),
        pltpu.VMEM((16, rows), F32),
        pltpu.VMEM((rows, D), BF16),
        pltpu.VMEM((rows, 128), F32),
        pltpu.VMEM((3, D, D), BF16),
        pltpu.VMEM((rows, D), BF16),
        pltpu.VMEM((3, rows, D), BF16),
    )
    for w in range(3):
        for k in range(NZ):
            core_copy(w, k).wait_send()
    for h in (0, 1):
        @pl.when(z < NZ - 1)
        def _():
            z_copy(0, 0, z + 1, h).wait_send()

        @pl.when(z > 0)
        def _():
            z_copy(0, 1, z - 1, h).wait_send()
    for k in range(7):
        q_copies[k].wait_recv()
    acc = qbuf[7]
    for k in range(7):
        acc = acc + qbuf[k]
    sq[...] = acc
    for k in range(7):
        q_copies[k].wait_send()
        v_copies[k].wait_send()


def back(lens, vec, vg, tok, cot, wa, wb, wc, att, slope, n2, normed, proj, lse_t, gc):
    vm = pl.BlockSpec(memory_space=pltpu.VMEM)
    rows = tok.shape[0]
    S = jax.ShapeDtypeStruct
    V = pltpu.VMEM
    return pl.pallas_call(
        back_kernel,
        name="back",
        out_shape=[S((rows, D), F32), S((6912, 128), F32), S((16, 128), F32), S((8, 128), F32)],
        in_specs=[pl.BlockSpec(memory_space=pltpu.SMEM)] + [vm] * 2 + [ANY] * 12,
        out_specs=[ANY] * 2 + [vm] * 2,
        scratch_shapes=[
            V((8, rows), jnp.int32),
            V((rows, 128), jnp.int32),
            V((rows, D), F32),
            V((rows, D), F32),
            V((rows, D), BF16),
            V((8, 4, ROWS, D), BF16),
            V((8, 4, ROWS, D), BF16),
            V((NZ, 4, ROWS, D), BF16),
            V((3, NZ, 4, ROWS, D), BF16),
            V((3, 5, 4, ROWS, D), BF16),
            V((16, D), F32),
            V((8, MLP), F32),
            V((8, 16, 128), F32),
            V((7, 16, 128), F32),
            V((8, 8, 128), F32),
            DMA((14,)), DMA((NZ,)), DMA((3, NZ)), DMA((3, NZ)),
            DMA((3, 2, NZ, 2)), DMA((3, 2, NZ, 2)),
            DMA((7,)), DMA((7,)), DMA((7,)), DMA((7,)),
        ],
        compiler_params=pltpu.CompilerParams(
            collective_id=1, has_side_effects=True, vmem_limit_bytes=63 * 2**20
        ),
    )(lens, vec, vg, tok, cot, wa, wb, wc, att, slope, n2, normed, proj, lse_t, gc)


PARTS = 6912
SUM_H, SUM_Q, SUM_E = PARTS // 2, PARTS // 4, PARTS // 8
MATRIX_WIDTH = PARTS * 128
VECTOR_WIDTH = 14 * ROWS


def finish_kernel(
    grad, sv, sq, master, first, second, outer,
    first_new, second_new, mean_out, outer_new, weights_new, vector_out, norm_out,
    b_master, b_first, b_second, b_outer, b_mean, diff, mean, part, mid, buf, tail_grad, tail, ls, os, ss, rs, ts, tr,
):
    g, t, z, c, gx, gy = place()
    pairs = [(master, b_master.at[0]), (first, b_first), (second, b_second), (outer, b_outer.at[0])]
    loads = [pltpu.make_async_copy(src, dst, ls.at[i]) for i, (src, dst) in enumerate(pairs)]
    for copy in loads:
        copy.start()
    peers = [gx, gy, 3 - g]
    barrier = pltpu.get_barrier_semaphore()
    for peer in peers:
        pl.semaphore_signal(barrier, inc=1, device_id=(peer, t), device_id_type=MESH_ID)
    norm = jnp.sqrt(sq[0:1, 0:1])
    norm_out[...] = jnp.broadcast_to(norm, (8, 128))
    scale = clip_limit / (norm + 1e-06)
    for j in range(14):
        tail_grad[0:1, ROWS * j : ROWS * j + ROWS] = sv[j : j + 1, :ROWS]
    vector_out[...] = tail_grad[...] / jnp.sqrt(F32(8 * 1024))
    xi, yi = lax.rem(g, 2), lax.div(g, 2)
    hop = [((gx, t), (gy, t)), ((gy, t), (gx, t))]
    mine = [(xi, yi), (yi, xi)]

    def line(at):
        return pl.ds(pl.multiple_of(at.start * 128, 1024), at.size * 128)

    step_rate = base_rate * rate_scale

    def adam(value, old_first, old_second, weight, decay):
        clipped = value * scale
        new_first = beta_first * old_first + (1.0 - beta_first) * clipped
        new_second = beta_second * old_second + (1.0 - beta_second) * clipped * clipped
        root = jnp.sqrt(new_second * (1.0 / (1.0 - beta_second**adam_count))) + adam_epsilon
        ahead = new_first * (1.0 / (1.0 - beta_first**adam_count)) / root
        if decay:
            ahead = ahead + weight_decay * weight
        return new_first, new_second, step_rate * ahead

    def nesterov(weight, momentum, average):
        new_momentum = outer_beta * momentum + average
        return new_momentum, weight - outer_rate * (average + outer_beta * new_momentum)

    def rows_loop(lo, count, fn):
        chunk = 48

        def body(i, _):
            fn(pl.ds(pl.multiple_of(lo + i * chunk, 16), chunk), pl.ds(pl.multiple_of(i * chunk, 16), chunk))
            return 0
        lax.fori_loop(0, count // chunk, body, 0)

    def adam_rows(lo, count):
        def fn(at, _):
            flat = line(at)
            b_first[:, flat], b_second[:, flat], ahead = adam(
                grad[at, :].reshape(1, -1), b_first[:, flat], b_second[:, flat], b_master[:, flat], True
            )
            diff[at, :] = ahead.reshape(-1, 128).astype(BF16)
        rows_loop(lo, count, fn)

    def outer_rows(lo, count):
        def fn(at, _):
            flat = line(at)
            average = mean[at, :].astype(F32).reshape(1, -1)
            b_mean[:, flat] = average
            b_outer[:, flat], b_master[:, flat] = nesterov(b_master[:, flat], b_outer[:, flat], average)
        rows_loop(lo, count, fn)

    def copies(h):
        a, b = mine[h]
        base = h * SUM_H
        sent = rows_at(diff, base + (1 - a) * SUM_Q, SUM_Q)
        one = remote(sent, part.at[h], ss.at[h, 0], rs.at[h, 0], hop[h][0])
        two = remote(rows_at(mid.at[h], (1 - b) * SUM_E, SUM_E), buf.at[h], ss.at[h, 1], rs.at[h, 1], hop[h][1])
        done = rows_at(mean, base + a * SUM_Q + b * SUM_E, SUM_E)
        three = remote(done, done, ss.at[h, 2], rs.at[h, 2], hop[h][1])
        whole = rows_at(mean, base + a * SUM_Q, SUM_Q)
        four = remote(whole, whole, ss.at[h, 3], rs.at[h, 3], hop[h][0])
        return one, two, three, four

    steps = [copies(0), copies(1)]
    for copy in loads[:3]:
        copy.wait()
    for h in (0, 1):
        adam_rows(h * SUM_H + (1 - mine[h][0]) * SUM_Q, SUM_Q)
        if h == 0:
            pl.semaphore_wait(barrier, 3)
        steps[h][0].start()
    at_tail = pl.ds(MATRIX_WIDTH, VECTOR_WIDTH)
    new_first, new_second, ahead = adam(tail_grad[...], b_first[:, at_tail], b_second[:, at_tail], None, False)
    b_first[:, at_tail] = new_first
    b_second[:, at_tail] = new_second
    tail[3, :, :] = jnp.zeros((1, 1408), F32)
    tail[3, :, pl.ds(0, VECTOR_WIDTH)] = ahead
    t_copies = [remote(tail.at[3], tail.at[k], ts.at[k], tr.at[k], (peers[k], t)) for k in range(3)]
    for copy in t_copies:
        copy.start()
    for h in (0, 1):
        adam_rows(h * SUM_H + mine[h][0] * SUM_Q, SUM_Q)
    stores = [pltpu.make_async_copy(b_first, first_new, os.at[0]), pltpu.make_async_copy(b_second, second_new, os.at[1])]
    for copy in stores:
        copy.start()
    for h in (0, 1):
        a, b = mine[h]
        steps[h][0].wait_recv()
        lo = (1 - b) * SUM_E
        src = h * SUM_H + a * SUM_Q + lo

        def fn(at, local):
            here = pl.ds(pl.multiple_of(lo + local.start, 16), local.size)
            mid[h, here, :] = (diff[at, :].astype(F32) + part[h, here, :].astype(F32)).astype(BF16)
        rows_loop(src, SUM_E, fn)
        steps[h][1].start()
    loads[3].wait()
    for h in (0, 1):
        a, b = mine[h]
        steps[h][1].wait_recv()
        lo = b * SUM_E
        src = h * SUM_H + a * SUM_Q + lo

        def fn(at, local):
            here = pl.ds(pl.multiple_of(lo + local.start, 16), local.size)
            total = diff[at, :].astype(F32) + part[h, here, :].astype(F32) + buf[h, local, :].astype(F32)
            mean[at, :] = (total * 0.25).astype(BF16)
        rows_loop(src, SUM_E, fn)
        steps[h][2].start()
    for copy in t_copies:
        copy.wait_recv()
    total = tail[3] + tail[0] + tail[1] + tail[2]
    average = total[:, :VECTOR_WIDTH] * 0.25
    b_mean[:, at_tail] = average
    new_momentum, new_weights = nesterov(b_master[:, at_tail], b_outer[:, at_tail], average)
    b_outer[:, at_tail] = new_momentum
    b_master[:, at_tail] = new_weights
    for h in (0, 1):
        a, b = mine[h]
        outer_rows(h * SUM_H + a * SUM_Q + b * SUM_E, SUM_E)
    for h in (0, 1):
        a, b = mine[h]
        rest = h * SUM_H + a * SUM_Q + (1 - b) * SUM_E
        other = rows_at(mean, rest, SUM_E)
        remote(other, other, ss.at[h, 2], rs.at[h, 2], hop[h][1]).wait_recv()
        steps[h][2].wait_send()
        steps[h][3].start()
        outer_rows(rest, SUM_E)
    for h in (0, 1):
        a, b = mine[h]
        rest = h * SUM_H + (1 - a) * SUM_Q
        other = rows_at(mean, rest, SUM_Q)
        remote(other, other, ss.at[h, 3], rs.at[h, 3], hop[h][0]).wait_recv()
        outer_rows(rest, SUM_Q)
    last = [
        pltpu.make_async_copy(b_mean.at[0], mean_out, os.at[2]),
        pltpu.make_async_copy(b_outer.at[0], outer_new, os.at[3]),
        pltpu.make_async_copy(b_master.at[0], weights_new, os.at[4]),
    ]
    for copy in last:
        copy.start()
    for h in (0, 1):
        steps[h][0].wait_send()
        steps[h][1].wait_send()
        steps[h][3].wait_send()
    for copy in t_copies:
        copy.wait_send()
    for copy in stores + last:
        copy.wait()


def finish(grad, sv, sq, master, first, second, outer):
    vm = pl.BlockSpec(memory_space=pltpu.VMEM)
    S = jax.ShapeDtypeStruct
    n = master.shape[0]
    flat = pltpu.VMEM((1, n), F32)
    return pl.pallas_call(
        finish_kernel,
        name="finish",
        out_shape=[S((1, n), F32)] * 2 + [S((n,), F32)] * 3 + [S((1, VECTOR_WIDTH), F32), S((8, 128), F32)],
        in_specs=[vm] * 3 + [ANY] * 4,
        out_specs=[ANY] * 5 + [vm] * 2,
        scratch_shapes=[flat] * 5
        + [
            pltpu.VMEM((PARTS, 128), BF16),
            pltpu.VMEM((PARTS, 128), BF16),
            pltpu.VMEM((2, SUM_Q, 128), BF16),
            pltpu.VMEM((2, SUM_Q, 128), BF16),
            pltpu.VMEM((2, SUM_E, 128), BF16),
            pltpu.VMEM((1, VECTOR_WIDTH), F32),
            pltpu.VMEM((4, 1, 1408), F32),
            DMA((4,)), DMA((5,)), DMA((2, 4)), DMA((2, 4)), DMA((3,)), DMA((3,)),
        ],
        compiler_params=pltpu.CompilerParams(collective_id=2, has_side_effects=True, vmem_limit_bytes=60 * 2**20),
    )(grad, sv, sq, master, first, second, outer)


def on_small_slice(tokens, cotangent, crop_lengths, master, first_moment, second_moment, outer_momentum):
    lin = master[:MATRIX_WIDTH].reshape(-1, 128)
    vector = master[MATRIX_WIDTH:].astype(BF16).astype(F32).reshape(14, ROWS)
    piece = jnp.pad(vector, ((0, 2), (0, 128 - ROWS)))
    wa, wb, wc, vec, fb1, normed, projected, attended, lse = front(crop_lengths, lin, piece, tokens)
    block_output, slope, normed_two, grad_fc2, vg = forward(
        crop_lengths, tokens, cotangent, attended, wa, wb, wc.reshape(MLP, D), vec, fb1
    )
    input_grad, grad_lin, sv, sq = back(
        crop_lengths, vec, vg, tokens, cotangent, wa, wb, wc.reshape(MLP, D), attended, slope, normed_two, normed,
        projected, lse, grad_fc2
    )
    moment_one, moment_two, mean_difference, outer_new, new_weights, vector_part, norm = finish(
        grad_lin, sv, sq, master, first_moment, second_moment, outer_momentum
    )
    return (
        block_output,
        input_grad,
        norm[0, :1],
        vector_part,
        moment_one,
        moment_two,
        mean_difference,
        outer_new,
        new_weights,
    )


def solution(mesh):
    small = mesh.shape["grp"] == 4 and mesh.shape["tok"] == 8
    return jax.shard_map(
        on_small_slice if small else on_device,
        mesh=mesh,
        in_specs=(
            P(("grp", "tok"), None),
            P(("grp", "tok"), None),
            P(("grp", "tok"), None),
            P("tok"),
            P("grp", "tok"),
            P("grp", "tok"),
            P("tok"),
        ),
        out_specs=(
            P(("grp", "tok"), None),
            P(("grp", "tok"), None),
            P("grp"),
            P("grp", "tok"),
            P("grp", "tok"),
            P("grp", "tok"),
            P("tok"),
            P("tok"),
            P("tok"),
        ),
        check_vma=False,
    )
```

```python
import jax
import jax.numpy as jnp
from jax import lax
from jax.experimental import pallas as pl
from jax.experimental.pallas import tpu as pltpu
from jax.sharding import PartitionSpec as P

D = 768
MLP = 3072
HEADS = 12
HEAD_DIM = 64
ROWS = D // 8
ANY = pl.BlockSpec(memory_space=pl.ANY)
DMA = pltpu.SemaphoreType.DMA
MESH_ID = pl.DeviceIdType.MESH
NZ = 4
F32, BF16 = jnp.float32, jnp.bfloat16


def place():
    g = lax.axis_index("grp")
    t = lax.axis_index("tok")
    z, c = lax.div(t, 2), lax.rem(t, 2)
    gx = g + 1 - 2 * lax.rem(g, 2)
    gy = g + 2 - 4 * lax.div(g, 2)
    return g, t, z, c, gx, gy


def greet(targets, count):
    barrier = pltpu.get_barrier_semaphore()
    for target in targets:
        pl.semaphore_signal(barrier, inc=1, device_id=target, device_id_type=MESH_ID)
    pl.semaphore_wait(barrier, count)


def remote(src, dst, send, recv, target):
    return pltpu.make_async_remote_copy(
        src_ref=src, dst_ref=dst, send_sem=send, recv_sem=recv,
        device_id=target, device_id_type=MESH_ID,
    )


clip_limit = 3.0
beta_first = 0.9
beta_second = 0.999
adam_epsilon = 1e-08
weight_decay = 0.04
adam_count = 10.0
base_rate = 0.075
rate_scale = 0.9**6
outer_rate = 0.7
outer_beta = 0.9
norm_epsilon = 1e-06


def member_extents():
    return [(D, 3 * D), (D, D), (D, MLP), (MLP, D)] + [(D,)] * 8 + [(MLP,), (D,), (D,)]


def member_sizes():
    sizes_list = []
    for extent in member_extents():
        length = 1
        for member in extent:
            length = length * member
        sizes_list.append(length)
    return sizes_list


def split_params(flat_params, owners):
    table = flat_params.reshape(owners, -1)
    members = []
    offset = 0
    for extent, length in zip(member_extents(), member_sizes()):
        width = length // owners
        members.append(table[:, offset : offset + width].reshape(extent))
        offset = offset + width
    return members


def join_table(members, owners):
    return jnp.concatenate([member.reshape(owners, -1) for member in members], axis=1)


def layer_norm(values, norm_gain, norm_shift):
    center = values - jnp.mean(values, axis=-1, keepdims=True)
    spread = jnp.mean(center * center, axis=-1, keepdims=True)
    return center * lax.rsqrt(spread + norm_epsilon) * norm_gain + norm_shift


def pack_layout(lengths_row, row_count):
    ends_at = jnp.cumsum(lengths_row)
    position = jnp.arange(row_count, dtype=jnp.int32)
    segment = jnp.sum((position[:, None] >= ends_at[None, :]).astype(jnp.int32), axis=1)
    validity = (position < ends_at[-1]).astype(jnp.float32)
    return (segment, validity)


def cross_rows(left_side, right_side):
    return lax.dot_general(
        left_side, right_side, (((0,), (0,)), ((), ())), preferred_element_type=jnp.float32
    )


def times_transposed(left_side, right_side):
    return lax.dot_general(
        left_side, right_side, (((1,), (1,)), ((), ())), preferred_element_type=jnp.float32
    )


def on_device(tokens, cotangent, crop_lengths, master, first_moment, second_moment, outer_momentum):
    row_count = tokens.shape[0]
    pair_count = HEADS // 2
    score_scale = HEAD_DIM ** (-0.5)
    owners = lax.axis_size("tok")
    segment, validity = pack_layout(crop_lengths[0], row_count)
    allowed = segment[:, None] == segment[None, :]
    master_low = master.astype(jnp.bfloat16)
    gathered = split_params(lax.all_gather(master_low, "tok", axis=0, tiled=True), owners)
    w_qkv, w_proj, w_fc1, w_fc2 = gathered[:4]
    (
        gain_one,
        shift_one,
        query_bias,
        value_bias,
        proj_bias,
        scale_one,
        gain_two,
        shift_two,
        fc1_bias,
        fc2_bias,
        scale_two,
    ) = [member.astype(jnp.float32) for member in gathered[4:]]

    def to_pairs(block_cols):
        return jnp.moveaxis(block_cols.reshape(row_count, pair_count, 2 * HEAD_DIM), 1, 0)

    def from_pairs(paired):
        return jnp.moveaxis(paired, 0, 1).reshape(row_count, D)

    normed = layer_norm(tokens, gain_one, shift_one).astype(jnp.bfloat16)
    qkv_bias = jnp.concatenate([query_bias, jnp.zeros_like(query_bias), value_bias])
    projected = (jnp.dot(normed, w_qkv, preferred_element_type=jnp.float32) + qkv_bias).astype(
        jnp.bfloat16
    )
    query_pairs = to_pairs(projected[:, :D])
    key_pairs = to_pairs(projected[:, D : 2 * D])
    value_pairs = to_pairs(projected[:, 2 * D :])

    def forward_pair(pair_item):
        queries, keys_pair, values_pair = [
            member.reshape(row_count, 2, HEAD_DIM) for member in pair_item
        ]
        raw_scores = jnp.einsum(
            "qhd,khd->hqk", queries, keys_pair, preferred_element_type=jnp.float32
        )
        scores = jnp.where(allowed[None], raw_scores * score_scale, -1e30)
        largest = jnp.max(scores, axis=-1, keepdims=True)
        weights_exp = jnp.exp(scores - largest)
        totals = jnp.sum(weights_exp, axis=-1, keepdims=True)
        weights_low = (weights_exp / totals).astype(jnp.bfloat16)
        attended_pair = jnp.einsum(
            "hqk,khd->qhd", weights_low, values_pair, preferred_element_type=jnp.float32
        )
        return (attended_pair.reshape(row_count, 2 * HEAD_DIM), (largest + jnp.log(totals))[..., 0])

    attended_pairs, log_totals = lax.map(forward_pair, (query_pairs, key_pairs, value_pairs))
    attended = from_pairs(attended_pairs).astype(jnp.bfloat16)
    branch_one = jnp.dot(attended, w_proj, preferred_element_type=jnp.float32) + proj_bias
    middle = tokens + scale_one * branch_one
    normed_two = layer_norm(middle, gain_two, shift_two).astype(jnp.bfloat16)
    hidden_pre = jnp.dot(normed_two, w_fc1, preferred_element_type=jnp.float32) + fc1_bias
    hidden = jax.nn.gelu(hidden_pre, approximate=False).astype(jnp.bfloat16)
    branch_two = jnp.dot(hidden, w_fc2, preferred_element_type=jnp.float32) + fc2_bias
    block_output = middle + scale_two * branch_two
    back_out = cotangent * validity[:, None]
    grad_branch_two = (scale_two * back_out).astype(jnp.bfloat16)
    grad_scale_two = jnp.sum(back_out * branch_two, axis=0)
    grad_fc2_bias = jnp.sum(grad_branch_two.astype(jnp.float32), axis=0)
    grad_w_fc2 = cross_rows(hidden, grad_branch_two)
    grad_hidden = times_transposed(grad_branch_two, w_fc2)
    gelu_pull = jax.vjp(lambda values: jax.nn.gelu(values, approximate=False), hidden_pre)[1]
    grad_pre = gelu_pull(grad_hidden)[0].astype(jnp.bfloat16)
    grad_fc1_bias = jnp.sum(grad_pre.astype(jnp.float32), axis=0)
    grad_w_fc1 = cross_rows(normed_two, grad_pre)
    grad_normed_two = times_transposed(grad_pre, w_fc1)
    norm_pull = jax.vjp(layer_norm, middle, gain_two, shift_two)[1]
    grad_middle_part, grad_gain_two, grad_shift_two = norm_pull(grad_normed_two)
    grad_middle = back_out + grad_middle_part
    grad_scale_one = jnp.sum(grad_middle * branch_one, axis=0)
    grad_branch_one = (scale_one * grad_middle).astype(jnp.bfloat16)
    grad_proj_bias = jnp.sum(grad_branch_one.astype(jnp.float32), axis=0)
    grad_w_proj = cross_rows(attended, grad_branch_one)
    grad_attended = times_transposed(grad_branch_one, w_proj).astype(jnp.bfloat16)

    def backward_pair(pair_item):
        queries, keys_pair, values_pair, grad_pair = [
            member.reshape(row_count, 2, HEAD_DIM) for member in pair_item[:4]
        ]
        log_total = pair_item[4]
        raw_scores = jnp.einsum(
            "qhd,khd->hqk", queries, keys_pair, preferred_element_type=jnp.float32
        )
        scores = jnp.where(allowed[None], raw_scores * score_scale, -1e30)
        weights_soft = jnp.exp(scores - log_total[..., None])
        grad_values = jnp.einsum(
            "hqk,qhd->khd",
            weights_soft.astype(jnp.bfloat16),
            grad_pair,
            preferred_element_type=jnp.float32,
        )
        grad_weights = jnp.einsum(
            "qhd,khd->hqk", grad_pair, values_pair, preferred_element_type=jnp.float32
        )
        row_dot = jnp.sum(weights_soft * grad_weights, axis=-1, keepdims=True)
        grad_scores = (weights_soft * (grad_weights - row_dot)).astype(jnp.bfloat16)
        grad_queries = (
            jnp.einsum("hqk,khd->qhd", grad_scores, keys_pair, preferred_element_type=jnp.float32)
            * score_scale
        )
        grad_keys = (
            jnp.einsum("hqk,qhd->khd", grad_scores, queries, preferred_element_type=jnp.float32)
            * score_scale
        )
        return (
            grad_queries.reshape(row_count, 2 * HEAD_DIM),
            grad_keys.reshape(row_count, 2 * HEAD_DIM),
            grad_values.reshape(row_count, 2 * HEAD_DIM),
        )

    grad_q_pairs, grad_k_pairs, grad_v_pairs = lax.map(
        backward_pair, (query_pairs, key_pairs, value_pairs, to_pairs(grad_attended), log_totals)
    )
    grad_projected = jnp.concatenate(
        [from_pairs(grad_q_pairs), from_pairs(grad_k_pairs), from_pairs(grad_v_pairs)], axis=1
    ).astype(jnp.bfloat16)
    grad_query_bias = jnp.sum(grad_projected[:, :D].astype(jnp.float32), axis=0)
    grad_value_bias = jnp.sum(grad_projected[:, 2 * D :].astype(jnp.float32), axis=0)
    grad_w_qkv = cross_rows(normed, grad_projected)
    grad_normed = times_transposed(grad_projected, w_qkv)
    first_pull = jax.vjp(layer_norm, tokens, gain_one, shift_one)[1]
    grad_tokens_part, grad_gain_one, grad_shift_one = first_pull(grad_normed)
    input_grad = grad_middle + grad_tokens_part
    all_members = [
        grad_w_qkv,
        grad_w_proj,
        grad_w_fc1,
        grad_w_fc2,
        grad_gain_one,
        grad_shift_one,
        grad_query_bias,
        grad_value_bias,
        grad_proj_bias,
        grad_scale_one,
        grad_gain_two,
        grad_shift_two,
        grad_fc1_bias,
        grad_fc2_bias,
        grad_scale_two,
    ]
    received = lax.all_to_all(
        join_table(all_members, owners).astype(jnp.bfloat16),
        "tok",
        split_axis=0,
        concat_axis=0,
        tiled=True,
    ).astype(jnp.float32)
    summed = jnp.sum(received, axis=0)
    matrix_width = (4 * D * D + 2 * D * MLP) // owners
    vector_part = summed[matrix_width:] / (owners * row_count) ** 0.5
    square_total = lax.psum(jnp.sum(summed * summed), "tok")
    norm_value = jnp.sqrt(square_total)
    clipped = summed * (clip_limit / (norm_value + 1e-06))
    moment_one = beta_first * first_moment[0] + (1.0 - beta_first) * clipped
    moment_two = beta_second * second_moment[0] + (1.0 - beta_second) * clipped * clipped
    corrected_one = moment_one / (1.0 - beta_first**adam_count)
    corrected_two = moment_two / (1.0 - beta_second**adam_count)
    shard_size = master.shape[0]
    local_index = jnp.arange(shard_size, dtype=jnp.int32)
    decay_mask = (local_index < matrix_width).astype(jnp.float32)
    step_rate = base_rate * rate_scale
    updated = master - step_rate * (
        corrected_one / (jnp.sqrt(corrected_two) + adam_epsilon)
        + weight_decay * decay_mask * master
    )
    mean_difference = lax.psum((master - updated).astype(jnp.bfloat16), "grp").astype(
        jnp.float32
    ) / lax.axis_size("grp")
    outer_new = outer_beta * outer_momentum + mean_difference
    new_weights = master - outer_rate * (mean_difference + outer_beta * outer_new)
    return (
        block_output,
        input_grad,
        norm_value.reshape(1),
        vector_part[None],
        moment_one[None],
        moment_two[None],
        mean_difference,
        outer_new,
        new_weights,
    )


def rows_at(ref, start, count):
    return ref.at[pl.ds(pl.multiple_of(start, 16), count), :]


TILE = 256


def nn(a, b):
    return lax.dot_general(a, b, (((1,), (0,)), ((), ())), preferred_element_type=F32)


def nt(a, b):
    return lax.dot_general(a, b, (((1,), (1,)), ((), ())), preferred_element_type=F32)


def tn(a, b):
    return lax.dot_general(a, b, (((0,), (0,)), ((), ())), preferred_element_type=F32)


def normalize(values):
    center = values - jnp.mean(values, axis=-1, keepdims=True)
    spread = jnp.mean(center * center, axis=-1, keepdims=True)
    inverse = lax.rsqrt(spread + norm_epsilon)
    return center * inverse, inverse


def norm_pull(grad, normal, inverse, gain):
    scaled = grad * gain
    return inverse * (
        scaled
        - jnp.mean(scaled, axis=-1, keepdims=True)
        - normal * jnp.mean(scaled * normal, axis=-1, keepdims=True)
    )


def gelu_and_slope(x):
    phi = 0.5 * (1.0 + lax.erf(x * 0.7071067811865476))
    return x * phi, phi + x * jnp.exp(-0.5 * x * x) * 0.3989422804014327


def col_sum(x):
    return jnp.sum(x, axis=0, keepdims=True)


QT = 256
LONG, SHORT = 261, 54
TILES = (
    (0, 272, 0, 384, 0, 261),
    (256, 272, 256, 384, 261, 522),
    (512, 288, 512, 384, 522, 792),
    (784, 240, 768, 256, 792, 1024),
)


def find_places(lens, line, column):
    crops = lens.shape[1]
    longs, shorts, begin = jnp.int32(0), jnp.int32(0), jnp.int32(0)
    at_line = lax.broadcasted_iota(jnp.int32, line.shape, 1)
    at_column = lax.broadcasted_iota(jnp.int32, column.shape, 0)
    new_line, new_column = at_line, at_column
    for j in range(crops):
        size = lens[0, j]
        is_long = (size == LONG).astype(jnp.int32)
        place_at = is_long * (longs * LONG) + (1 - is_long) * (2 * LONG + shorts * SHORT)
        shift = place_at - begin
        new_line = jnp.where((at_line >= begin) & (at_line < begin + size), at_line + shift, new_line)
        new_column = jnp.where((at_column >= begin) & (at_column < begin + size), at_column + shift, new_column)
        longs, shorts, begin = longs + is_long, shorts + 1 - is_long, begin + size
    line[...] = new_line
    column[...] = new_column


def to_places(line, first, count):
    rows = lax.broadcasted_iota(jnp.int32, (count, line.shape[1]), 0) + first
    return (rows == line[0:1, :]).astype(F32).astype(BF16)


def from_places(column, first, count):
    lanes = lax.broadcasted_iota(jnp.int32, (count, column.shape[0]), 1)
    return (lanes == column[pl.ds(first, count), 0:1]).astype(F32).astype(BF16)


def fill_bias(bias):
    def crop(at):
        found = jnp.zeros(at.shape, jnp.int32)
        for end in [LONG] + [2 * LONG + SHORT * j for j in range(9)]:
            found = found + (at >= end).astype(jnp.int32)
        return found

    for i, (row, rows, col, cols, low, high) in enumerate(TILES):
        at_row = lax.broadcasted_iota(jnp.int32, (rows, 1), 0) + row
        at_col = lax.broadcasted_iota(jnp.int32, (1, cols), 1) + col
        same = crop(at_row) == jnp.where((at_col >= low) & (at_col < high), crop(at_col), -1)
        bias[i, :rows, :cols] = jnp.where(same, 0.0, -1e30).astype(F32)


def head_part(block, h):
    lane = lax.broadcasted_iota(jnp.int32, (1, 128), 1)
    keep = lane < 64 if h == 0 else lane >= 64
    return jnp.where(keep, block, jnp.zeros_like(block))


def first_half(a, b):
    lane = lax.broadcasted_iota(jnp.int32, (1, 128), 1)
    return jnp.where(lane < 64, a, b)


def rows_from(tile, new, old):
    row, rows, low = tile[0], tile[1], tile[4]
    if row == low:
        return new
    return jnp.where(lax.broadcasted_iota(jnp.int32, (rows, 1), 0) + row >= low, new, old)


def norm_rows(tok, vec, normed):
    def tile(i, _):
        at = pl.ds(pl.multiple_of(i * QT, QT), QT)
        normal, _inverse = normalize(tok[at, :])
        normed[at, :] = (normal * vec[0:1, :] + vec[1:2, :]).astype(BF16)
        return 0
    lax.fori_loop(0, tok.shape[0] // QT, tile, 0)


def project_in(vec, wa, normed, proj):
    def block(i, _):
        at = pl.ds(pl.multiple_of(i * QT, QT), QT)
        proj[0, at, :] = (nn(normed[at, :], wa[0]) + vec[2:3, :]).astype(BF16)
        proj[1, at, :] = nn(normed[at, :], wa[1]).astype(BF16)
        proj[2, at, :] = (nn(normed[at, :], wa[2]) + vec[3:4, :]).astype(BF16)
        return 0
    lax.fori_loop(0, normed.shape[0] // QT, block, 0)


def move_rows(one_hot, src, dst):
    def block(i, _):
        first = pl.multiple_of(i * QT, QT)
        dst[pl.ds(first, QT), :] = nn(one_hot(first, QT), src[...]).astype(BF16)
        return 0
    lax.fori_loop(0, src.shape[0] // QT, block, 0)


def attend(p, proj, bias, att, lse):
    cols = pl.ds(pl.multiple_of(p * 128, 128), 128)
    lane = lax.broadcasted_iota(jnp.int32, (1, 128), 1)
    for i, tile in enumerate(TILES):
        row, rows, col, wide = tile[:4]
        at, keys = pl.ds(row, rows), pl.ds(col, wide)
        q = proj[0, at, cols] * jnp.asarray(0.125, BF16)
        k, v = proj[1, keys, cols], proj[2, keys, cols]
        outs = []
        logs = lse[at, :]
        for h in (0, 1):
            scores = nt(head_part(q, h), k) + bias[i, :rows, :wide]
            largest = jnp.max(scores, axis=-1, keepdims=True)
            weights = jnp.exp(scores - largest)
            total = jnp.sum(weights, axis=-1, keepdims=True)
            low = (weights * (1.0 / total)).astype(BF16)
            outs.append(nn(low, v))
            logs = jnp.where(lane == 2 * p + h, largest + jnp.log(total), logs)
        lse[at, :] = rows_from(tile, logs, lse[at, :])
        att[at, cols] = rows_from(tile, first_half(*outs), att[at, cols].astype(F32)).astype(BF16)


def attend_back(p, proj, gatt, bias, lse_t, dq):
    cols = pl.ds(pl.multiple_of(p * 128, 128), 128)
    dq[...] = jnp.zeros_like(dq)
    dks, dvs = [], []
    for i, tile in enumerate(TILES):
        row, rows, col, wide = tile[:4]
        at, queries = pl.ds(row, rows), pl.ds(col, wide)
        k, v = proj[1, at, cols], proj[2, at, cols]
        g = gatt[queries, cols]
        scaled = proj[0, queries, cols] * jnp.asarray(0.125, BF16)
        dk, dv, dqs = [], [], []
        for h in (0, 1):
            scores = nt(head_part(k, h), scaled) + bias[i, :rows, :wide]
            probs = jnp.exp(scores - lse_t[pl.ds(2 * p + h, 1), queries])
            grad = nt(head_part(v, h), g)
            dot = jnp.sum(probs * grad, axis=0, keepdims=True)
            low = (probs * (grad - dot)).astype(BF16)
            dv.append(nn(probs.astype(BF16), g))
            dk.append(nn(low, scaled))
            dqs.append(tn(low, k))
        dq[queries, :] += first_half(*dqs) * 0.125
        dks.append(first_half(*dk))
        dvs.append(first_half(*dv))
    for i, tile in enumerate(TILES):
        at = pl.ds(tile[0], tile[1])
        proj[1, at, cols] = rows_from(tile, dks[i], proj[1, at, cols].astype(F32)).astype(BF16)
        proj[2, at, cols] = rows_from(tile, dvs[i], proj[2, at, cols].astype(F32)).astype(BF16)
    proj[0, :, cols] = dq[...].astype(BF16)


def weight_grads(normed, gproj, gout):
    def block(q, _):
        def part(m, _):
            col = pl.ds(pl.multiple_of(m * 384, 128), 384)
            gout[:, q, :, col] = tn(normed[...], gproj[q, :, col]).astype(BF16).reshape(8, ROWS, 384)
            return 0
        return lax.fori_loop(0, 2, part, 0)
    lax.fori_loop(0, 3, block, 0)


def row_grads(column, wide, total, vec, wa, gproj, vg):

    def tile(i, _):
        first = pl.multiple_of(i * QT, QT)
        at = pl.ds(first, QT)
        back = from_places(column, first, QT)
        parts = [nn(back, gproj[j]).astype(BF16) for j in range(3)]
        grad = nt(parts[0], wa[0]) + nt(parts[1], wa[1]) + nt(parts[2], wa[2])
        normal, inverse = normalize(wide[at, :D])
        vg[0:1, :] += col_sum(grad * normal)
        vg[1:2, :] += col_sum(grad)
        vg[2:3, :] += col_sum(parts[0].astype(F32))
        vg[3:4, :] += col_sum(parts[2].astype(F32))
        total[at, :] = total[at, :] + norm_pull(grad, normal, inverse, vec[0:1, :])
        return 0
    lax.fori_loop(0, total.shape[0] // QT, tile, 0)


def convert_piece(w, lin, piece):
    if w == 2:
        for q in range(4):
            for m in range(6):
                piece[q, :, 128 * m : 128 * m + 128] = lin[pl.ds(4608 + 576 * q + m, ROWS, stride=6), :].astype(BF16)
        return
    for q in range(4):
        for m in range(6):
            if w == 1:
                at = pl.ds(2304 + 6 * q + m, ROWS, stride=24)
            elif q == 3:
                at = pl.ds(1728 + m, ROWS, stride=6)
            else:
                at = pl.ds(6 * q + m, ROWS, stride=18)
            piece[q, :, 128 * m : 128 * m + 128] = lin[at, :].astype(BF16)


def to_rows(flat, lin, first, count):
    def body(i, _):
        at = first + i * 48
        value = flat[:, pl.ds(pl.multiple_of(at * 128, 6144), 6144)]
        lin[pl.ds(pl.multiple_of(at, 48), 48), :] = value.reshape(48, 128)
        return 0
    lax.fori_loop(0, count // 48, body, 0)


def weight_strip(w, ref, t):
    if w == 2:
        return ref.at[t]
    return ref.at[:, pl.ds(pl.multiple_of(t * ROWS, 16), ROWS), :]


def weight_block(w, ref, t, q, lead=0, count=ROWS):
    if w == 2:
        return ref.at[t, q, pl.ds(lead, count), :]
    return ref.at[q, pl.ds(pl.multiple_of(t * ROWS + lead, 16), count), :]


def front_kernel(
    lens, master, tok,
    wa, wb, wc, vec, fb1, normed, proj, att, lse_out,
    flat, lin, pv, pieces, wv, wa_in, bias, line, column, att_in, lse,
    ls, zs, zr, xs, xr, ys, yr, ds, dr, cs, cr, vs, vr, es, er,
):
    weights_in = pltpu.make_async_copy(master, flat.at[0], ls.at[5])
    weights_in.start()
    g, t, z, c, gx, gy = place()
    fulls = (wa, wb, wc)
    peers = [lax.rem(t + k, 8) for k in range(1, 8)]
    barrier = pltpu.get_barrier_semaphore()
    for target in [(g, p) for p in peers] + [(gx, t), (gy, t)]:
        pl.semaphore_signal(barrier, inc=1, device_id=target, device_id_type=MESH_ID)
    weights_in.wait()
    to_rows(flat, lin, 0, 2304)
    convert_piece(0, lin, pieces.at[0])
    pv[...] = jnp.zeros_like(pv)
    for j in range(14):
        low = flat[:, pl.ds(6912 * 128 + ROWS * j, ROWS)].astype(BF16)
        pv[j : j + 1, :ROWS] = low.astype(F32)
    pl.semaphore_wait(barrier, 9)
    other = t + 1 - 2 * c

    def z_copy(w, d, s):
        step = 1 if d == 0 else -1
        src_t = t - 2 * step * s
        src = pieces.at[w, g] if s == 0 else weight_block(w, fulls[w], src_t, g)
        ok = (z - s >= 0) & (z + 1 < NZ) if d == 0 else (z + s < NZ) & (z - 1 >= 0)
        return ok, remote(src, weight_block(w, fulls[w], src_t, g), zs.at[w, d, s], zr.at[w, d, s], (g, t + 2 * step))

    def extra_copy(w, d, s):
        step = 1 if d == 0 else -1
        src_t = t - 2 * step * s
        src = pieces.at[w, 3 - g, pl.ds(0, 32)] if s == 0 else weight_block(w, fulls[w], src_t, 3 - g, 0, 32)
        ok = (z - s >= 0) & (z + 1 < NZ) if d == 0 else (z + s < NZ) & (z - 1 >= 0)
        dst = weight_block(w, fulls[w], src_t, 3 - g, 0, 32)
        return ok, remote(src, dst, es.at[w, d, s], er.at[w, d, s], (g, t + 2 * step))

    def extra_wait(w, d, s):
        blk = weight_block(w, fulls[w], from_t(d, s), 3 - g, 0, 32)
        remote(blk, blk, es.at[w, d, s], er.at[w, d, s], (g, other)).wait_recv()

    def from_t(d, s):
        return t - 2 * (s + 1) if d == 0 else t + 2 * (s + 1)

    def here(d, s):
        return z - s - 1 >= 0 if d == 0 else z + s + 1 < NZ

    def z_wait(w, d, s):
        blk = weight_block(w, fulls[w], from_t(d, s), g)
        remote(blk, blk, zs.at[w, d, s], zr.at[w, d, s], (g, other)).wait_recv()

    def side_copy(w, d, s, axis):
        blk = weight_block(w, fulls[w], from_t(d, s), g)
        sems = (xs, xr) if axis == 0 else (ys, yr)
        return remote(blk, blk, sems[0].at[w, d, s], sems[1].at[w, d, s], (gx if axis == 0 else gy, t))

    def side_wait(w, d, s, axis):
        blk = weight_block(w, fulls[w], from_t(d, s), gx if axis == 0 else gy)
        sems = (xs, xr) if axis == 0 else (ys, yr)
        remote(blk, blk, sems[0].at[w, d, s], sems[1].at[w, d, s], (gx, t)).wait_recv()

    def diag_copy(w, d, s, axis):
        blk = weight_block(w, fulls[w], from_t(d, s), gx if axis == 0 else gy, 32 + 32 * axis, 32)
        return remote(blk, blk, ds.at[w, d, s, axis], dr.at[w, d, s, axis], (gy if axis == 0 else gx, t))

    def diag_wait(w, d, s, axis):
        blk = weight_block(w, fulls[w], from_t(d, s), 3 - g, 32 + 32 * axis, 32)
        remote(blk, blk, ds.at[w, d, s, axis], dr.at[w, d, s, axis], (gx, t)).wait_recv()

    def core_copy(w, d, s):
        blk = weight_strip(w, fulls[w], from_t(d, s))
        return remote(blk, blk, cs.at[w, d, s], cr.at[w, d, s], (g, other))

    def core_wait(w, d, s):
        blk = weight_strip(w, fulls[w], from_t(d, s) + 1 - 2 * c)
        remote(blk, blk, cs.at[w, d, s], cr.at[w, d, s], (g, other)).wait_recv()

    def own_copy(w):
        return remote(pieces.at[w], weight_strip(w, fulls[w], t), cs.at[w, 2, 0], cr.at[w, 2, 0], (g, other))

    def own_wait(w):
        blk = weight_strip(w, fulls[w], other)
        remote(blk, blk, cs.at[w, 2, 0], cr.at[w, 2, 0], (g, other)).wait_recv()

    def own_local(w):
        return pltpu.make_async_copy(pieces.at[w], weight_strip(w, fulls[w], t), ls.at[w])

    def both(s, fn):
        for d in (0, 1):
            @pl.when(here(d, s))
            def _():
                fn(d)

    def start_z(w, s, kind=None):
        for d in (0, 1):
            ok, copy = (kind or z_copy)(w, d, s)

            @pl.when(ok)
            def _():
                copy.start()

    def arrive(n):
        w, s = divmod(n, 3)
        both(s, lambda d: z_wait(w, d, s))
        if s < 2:
            start_z(w, s + 1)

        def sides(d):
            side_copy(w, d, s, 0).start()
            side_copy(w, d, s, 1).start()
        both(s, sides)
        if s == 0 and w < 2:
            start_z(w + 1, 0)
            own_copy(w + 1).start()
            start_z(w + 1, 0, extra_copy)

    def cross(n):
        w, s = divmod(n, 3)

        def fn(d):
            for axis in (0, 1):
                side_wait(w, d, s, axis)
                diag_copy(w, d, s, axis).start()
            extra_wait(w, d, s)
        both(s, fn)
        if s < 2:
            start_z(w, s + 1, extra_copy)

    def finish(n):
        w, s = divmod(n, 3)

        def fn(d):
            diag_wait(w, d, s, 0)
            diag_wait(w, d, s, 1)
            core_copy(w, d, s).start()
        both(s, fn)

    def drain(w):
        own_wait(w)
        own_local(w).wait()
        for s in range(3):
            both(s, lambda d: core_wait(w, d, s))

    start_z(0, 0)
    own_copy(0).start()
    start_z(0, 0, extra_copy)
    own_local(0).start()
    local_v = pltpu.make_async_copy(pv, wv.at[t], ls.at[3])
    local_v.start()
    v_copies = [remote(pv, wv.at[t], vs.at[k], vr.at[k], (g, peers[k])) for k in range(7)]
    for copy in v_copies:
        copy.start()
    to_rows(flat, lin, 2304, 4608)
    for w in (1, 2):
        convert_piece(w, lin, pieces.at[w])
        own_local(w).start()
    fill_bias(bias)
    find_places(lens, line, column)
    att_in[...] = jnp.zeros_like(att_in)
    lse[...] = jnp.zeros_like(lse)
    arrive(0)
    local_v.wait()
    for k in range(7):
        remote(pv, wv.at[lax.rem(t + 7 - k, 8)], vs.at[k], vr.at[k], (g, peers[k])).wait_recv()
    for k in range(8):
        vec[:, ROWS * k : ROWS * k + ROWS] = wv[k, :, :ROWS]
        for j in range(4):
            lead = 4 * ROWS * k + ROWS * j
            fb1[0:1, lead : lead + ROWS] = wv[k, 8 + j : 9 + j, :ROWS]
    arrive(1)
    cross(0)
    norm_rows(tok, vec, att)
    move_rows(lambda first, count: to_places(line, first, count), att, normed)
    arrive(2)
    cross(1)
    finish(0)
    arrive(3)
    cross(2)
    finish(1)
    finish(2)
    drain(0)
    load = pltpu.make_async_copy(wa.at[pl.ds(0, 3)], wa_in, ls.at[4])
    load.start()
    load.wait()
    project_in(vec, wa_in, normed, proj)
    arrive(4)
    cross(3)
    events = [
        [(arrive, 5), (arrive, 6), (cross, 4), (finish, 3)],
        [(arrive, 7), (cross, 5), (finish, 4)],
        [(arrive, 8), (cross, 6), (finish, 5)],
        [(cross, 7), (finish, 6)],
        [(cross, 8), (finish, 7)],
        [(finish, 8)],
    ]
    for p in range(6):
        attend(p, proj, bias, att_in, lse)
        for event, n in events[p]:
            event(n)
    move_rows(lambda first, count: from_places(column, first, count), att_in, att)
    lse_out[...] = lse[...].T[:16]
    drain(1)
    drain(2)
    for copy in v_copies:
        copy.wait_send()
    for w in range(3):
        own_copy(w).wait_send()
        for s in range(3):
            for d in (0, 1):
                for kind in (z_copy, extra_copy):
                    ok, copy = kind(w, d, s)

                    @pl.when(ok)
                    def _():
                        copy.wait_send()

            def sent(d):
                side_copy(w, d, s, 0).wait_send()
                side_copy(w, d, s, 1).wait_send()
                diag_copy(w, d, s, 0).wait_send()
                diag_copy(w, d, s, 1).wait_send()
                core_copy(w, d, s).wait_send()
            both(s, sent)


def front(lens, master, tok):
    vm = pl.BlockSpec(memory_space=pltpu.VMEM)
    rows = tok.shape[0]
    S = jax.ShapeDtypeStruct
    return pl.pallas_call(
        front_kernel,
        name="front",
        out_shape=[
            S((4, D, D), BF16), S((4, D, D), BF16), S((8, 4, ROWS, D), BF16),
            S((16, D), F32), S((8, MLP), F32),
            S((rows, D), BF16), S((3, rows, D), BF16), S((rows, D), BF16), S((16, rows), F32),
        ],
        in_specs=[pl.BlockSpec(memory_space=pltpu.SMEM)] + [ANY, vm],
        out_specs=[ANY] * 3 + [vm] * 6,
        scratch_shapes=[
            pltpu.VMEM((1, master.shape[0]), F32),
            pltpu.VMEM((6912, 128), F32),
            pltpu.VMEM((16, 128), F32),
            pltpu.VMEM((3, 4, ROWS, D), BF16),
            pltpu.VMEM((8, 16, 128), F32),
            pltpu.VMEM((3, D, D), BF16),
            pltpu.VMEM((4, 288, 384), F32),
            pltpu.VMEM((8, rows), jnp.int32),
            pltpu.VMEM((rows, 128), jnp.int32),
            pltpu.VMEM((rows, D), BF16),
            pltpu.VMEM((rows, 128), F32),
            DMA((6,)),
            DMA((3, 2, 3)), DMA((3, 2, 3)),
            DMA((3, 2, 3)), DMA((3, 2, 3)),
            DMA((3, 2, 3)), DMA((3, 2, 3)),
            DMA((3, 2, 3, 2)), DMA((3, 2, 3, 2)),
            DMA((3, 3, 3)), DMA((3, 3, 3)),
            DMA((7,)), DMA((7,)),
            DMA((3, 2, 3)), DMA((3, 2, 3)),
        ],
        compiler_params=pltpu.CompilerParams(collective_id=0, has_side_effects=True, vmem_limit_bytes=60 * 2**20),
    )(lens, master, tok)


def valid_rows(lens, first, count):
    total = jnp.int32(0)
    for j in range(lens.shape[1]):
        total = total + lens[0, j]
    at = lax.broadcasted_iota(jnp.int32, (count, 1), 0) + first
    return (at < total).astype(F32)


def forward_kernel(
    lens, tok_in, cot_in, att_in, wa, wb_in, wc_in, vec, fb1,
    bo_out, slope_out, n2_out, gc_out, vg,
    tok, cot, att, wp, wb, wc, bo, slope, n2, hid, gb2, gc, ls, os,
):
    pairs = [(att_in, att), (wa.at[3], wp), (tok_in, tok), (wb_in, wb), (wc_in, wc), (cot_in, cot)]
    loads = [pltpu.make_async_copy(src, dst, ls.at[i]) for i, (src, dst) in enumerate(pairs)]
    for copy in loads:
        copy.start()
    vg[...] = jnp.zeros_like(vg)
    rows = tok.shape[0]

    def row(j):
        return vec[j : j + 1, :]

    def stores(i):
        at = pl.ds(i * TILE, TILE)
        trio = [(bo, bo_out), (slope, slope_out), (n2, n2_out)]
        return [pltpu.make_async_copy(a.at[at, :], b.at[at, :], os.at[i, n]) for n, (a, b) in enumerate(trio)]

    for copy in loads[:3]:
        copy.wait()
    for i in range(rows // TILE):
        at = pl.ds(i * TILE, TILE)
        middle = tok[at, :] + row(5) * (nn(att[at, :], wp[...]) + row(4))
        normal, _inverse = normalize(middle)
        bo[at, :] = middle
        n2[at, :] = (normal * row(6) + row(7)).astype(BF16)
        if i == 0:
            loads[3].wait()

        def hidden(q, _):
            low = pl.ds(pl.multiple_of(q * D, D), D)
            pre = nn(n2[at, :], wb[q]) + fb1[0:1, low]
            h, s = gelu_and_slope(pre)
            hid[at, low] = h.astype(BF16)
            slope[at, low] = s.astype(BF16)
            return 0
        lax.fori_loop(0, 4, hidden, 0)
        if i == 0:
            loads[4].wait()
            loads[5].wait()
        branch_two = nn(hid[at, :], wc[...]) + row(12)
        bo[at, :] += row(13) * branch_two
        back = cot[at, :] * valid_rows(lens, i * TILE, TILE)
        low_back = (row(13) * back).astype(BF16)
        gb2[at, :] = low_back
        vg[13:14, :] += col_sum(back * branch_two)
        vg[12:13, :] += col_sum(low_back.astype(F32))
        for copy in stores(i):
            copy.start()

    def fc2(t, _):
        low = pl.ds(pl.multiple_of(t * 384, 128), 384)
        gc[t] = tn(hid[:, low], gb2[...]).astype(BF16).reshape(4, ROWS, D)
        return 0
    lax.fori_loop(0, 8, fc2, 0)
    store = pltpu.make_async_copy(gc, gc_out, os.at[4, 0])
    store.start()
    for i in range(rows // TILE):
        for copy in stores(i):
            copy.wait()
    store.wait()


def forward(lens, tok, cot, att, wa, wb, wc, vec, fb1):
    vm = pl.BlockSpec(memory_space=pltpu.VMEM)
    rows = tok.shape[0]
    S = jax.ShapeDtypeStruct
    V = pltpu.VMEM
    return pl.pallas_call(
        forward_kernel,
        name="mlp_forward",
        out_shape=[S((rows, D), F32), S((rows, MLP), BF16), S((rows, D), BF16), S((8, 4, ROWS, D), BF16), S((16, D), F32)],
        in_specs=[pl.BlockSpec(memory_space=pltpu.SMEM)] + [ANY] * 6 + [vm] * 2,
        out_specs=[ANY] * 4 + [vm],
        scratch_shapes=[
            V((rows, D), F32), V((rows, D), F32), V((rows, D), BF16), V((D, D), BF16),
            V((4, D, D), BF16), V((MLP, D), BF16), V((rows, D), F32), V((rows, MLP), BF16),
            V((rows, D), BF16), V((rows, MLP), BF16), V((rows, D), BF16), V((8, 4, ROWS, D), BF16),
            DMA((6,)), DMA((5, 3)),
        ],
        compiler_params=pltpu.CompilerParams(vmem_limit_bytes=62 * 2**20),
    )(lens, tok, cot, att, wa, wb, wc, vec, fb1)


ORDER = (2, 1, 0)


def back_kernel(
    lens, vec, vg_in, tok, cot, wa, wb_in, wc_in, att_in, slope_in, n2_in, normed_in, proj_in, lse_in, gc,
    gin, lin_out, sv, sq,
    line, column, wide, tall, gatt, gout, gb, own, core, zbuf, vg, vg1, gv, vbuf, qbuf,
    ls, os, cs, cr, zs, zr, vs, vr, qs, qr,
):
    g, t, z, c, gx, gy = place()
    peers = [lax.rem(t + k, 8) for k in range(1, 8)]
    rows = tok.shape[0]
    other = t + 1 - 2 * c

    def local(pairs, first):
        return [pltpu.make_async_copy(src, dst, ls.at[first + i]) for i, (src, dst) in enumerate(pairs)]

    loads = local([(tok, wide), (cot, tall)], 0)
    for copy in loads:
        copy.start()
    greet([(g, p) for p in peers], 7)

    def own_at(w, k):
        return (gout.at[2 * k + c], gb.at[2 * k + c], own.at[k])[w]

    def core_copy(w, k):
        return remote((gout, gb, gc)[w].at[2 * k + 1 - c], core.at[w, k], cs.at[w, k], cr.at[w, k], (g, other))

    def load(k):
        return pltpu.make_async_copy(gc.at[2 * k + c], own.at[k], os.at[k])

    def begin(w):
        for k in (3, 0, 2, 1):
            core_copy(w, k).start()
            if w == 2:
                load(k).start()

    def slot(d, k, to):
        return k - to if d == 0 else 4 - (to - k)

    def total_of(w, k, q, at, extra):
        mine = own_at(w, k)
        total = mine[q, at, :].astype(F32) + core[w, k, q, at, :].astype(F32)
        for d in extra:
            total = total + zbuf[w, slot(d, k, z), q, at, :].astype(F32)
        return total

    def add_rows(w, k, h, extra):
        for q in (2 * h, 2 * h + 1):
            def body(i, _):
                at = pl.ds(pl.multiple_of(i * 32, 32), 32)
                own_at(w, k)[q, at, :] = total_of(w, k, q, at, extra).astype(BF16)
                return 0
            lax.fori_loop(0, ROWS // 32, body, 0)

    def lay_out(lin, w, k, h, extra):
        for q in (2 * h, 2 * h + 1):
            if w == 2:
                base, stride = 4608 + 576 * q, 6
            elif w == 1:
                base, stride = 2304 + 6 * q, 24
            else:
                base, stride = (1728, 6) if q == 3 else (6 * q, 18)

            def body(i, _):
                at = pl.ds(pl.multiple_of(i * 32, 32), 32)
                total = total_of(w, k, q, at, extra)
                for m in range(6):
                    lin[pl.ds(base + m + i * (32 * stride), 32, stride=stride), :] = total[:, 128 * m : 128 * m + 128]
                return 0
            lax.fori_loop(0, ROWS // 32, body, 0)

    def z_copy(w, d, k, h):
        step = 1 if d == 0 else -1
        at = pl.ds(2 * h, 2)
        return remote(
            own_at(w, k).at[at],
            zbuf.at[w, slot(d, k, z + step), at],
            zs.at[w, d, k, h],
            zr.at[w, d, k, h],
            (g, t + 2 * step),
        )

    def z_wait(w, d, k, h):
        here = zbuf.at[w, slot(d, k, z), pl.ds(2 * h, 2)]
        remote(here, here, zs.at[w, d, k, h], zr.at[w, d, k, h], (g, other)).wait_recv()

    def ready(w, k):
        if w == 2:
            load(k).wait()
        core_copy(w, k).wait_recv()

    def pass_on(i, d, j, h):
        w = ORDER[i]
        reach = NZ - 1 - z if d == 0 else z
        k = z + j if d == 0 else z - j
        first = z == 0 if d == 0 else z == NZ - 1

        @pl.when(j <= reach)
        def _():
            if h == 0:
                ready(w, k)

            @pl.when(first)
            def _():
                add_rows(w, k, h, ())

            @pl.when(jnp.logical_not(first))
            def _():
                z_wait(w, d, k, h)
                add_rows(w, k, h, (d,))

            if i > 0:
                @pl.when(j == reach)
                def _():
                    z_copy(ORDER[i - 1], d, z + 1 if d == 0 else z - 1, h).wait_send()
            if j < NZ - 1:
                @pl.when(j < reach)
                def _():
                    z_copy(w, d, k + 1 if d == 0 else k - 1, h).wait_send()
            z_copy(w, d, k, h).start()

    def settle(lin, i):
        w = ORDER[i]
        ready(w, z)
        for h in (0, 1):
            for cond, dirs in ((z == 0, (1,)), (z == NZ - 1, (0,)), ((z > 0) & (z < NZ - 1), (0, 1))):
                @pl.when(cond)
                def _():
                    for d in dirs:
                        z_wait(w, d, z, h)
                    lay_out(lin, w, z, h, dirs)

    steps = [(i, j, h) for i in range(3) for j in (3, 2, 1) for h in (0, 1)]

    def run(lo, hi):
        for i, j, h in steps[lo:hi]:
            pass_on(i, 0, j, h)
            pass_on(i, 1, j, h)

    begin(2)
    find_places(lens, line, column)
    vg[...] = vg_in[...]
    vg1[...] = jnp.zeros_like(vg1)

    def mlp_part(wp, wb, wc, grads, n2, att, gb1):
        inner = local(
            [(att_in, att), (wa.at[3], wp), (wc_in, wc), (slope_in, grads), (wb_in, wb), (n2_in, n2)], 2
        )
        for copy in inner:
            copy.start()
        run(0, 2)
        for copy in loads + inner:
            copy.wait()

        def row(j):
            return vec[j : j + 1, :]

        def tile(i):
            at = pl.ds(i * TILE, TILE)
            branch_one = nn(att[at, :], wp[...]) + row(4)
            normal, inverse = normalize(wide[at, :] + row(5) * branch_one)
            tall[at, :] = tall[at, :] * valid_rows(lens, i * TILE, TILE)
            low_back = (row(13) * tall[at, :]).astype(BF16)

            def backward(q, total):
                low = pl.ds(pl.multiple_of(q * D, D), D)
                grad = nt(low_back, wc[low, :]) * grads[at, low].astype(F32)
                grad = grad.astype(BF16)
                grads[at, low] = grad
                vg1[0:1, low] += col_sum(grad.astype(F32))
                return total + nt(grad, wb[q])
            grad_n2 = lax.fori_loop(0, 4, backward, jnp.zeros((TILE, D), F32))
            vg[6:7, :] += col_sum(grad_n2 * normal)
            vg[7:8, :] += col_sum(grad_n2)
            grad_mid = tall[at, :] + norm_pull(grad_n2, normal, inverse, row(6))
            tall[at, :] = grad_mid
            vg[5:6, :] += col_sum(grad_mid * branch_one)
            low_one = (row(5) * grad_mid).astype(BF16)
            gb1[at, :] = low_one
            vg[4:5, :] += col_sum(low_one.astype(F32))
            gatt[at, :] = nt(low_one, wp[...]).astype(BF16)

        for i in range(rows // TILE):
            tile(i)
            run(2 + i, 3 + i)

        def fc1(q, _):
            def part(m, _):
                low = pl.ds(pl.multiple_of(q * D + m * 384, 128), 384)
                col = pl.ds(pl.multiple_of(m * 384, 128), 384)
                gb[:, q, :, col] = tn(n2[...], grads[:, low]).astype(BF16).reshape(8, ROWS, 384)
                return 0
            return lax.fori_loop(0, 2, part, 0)
        lax.fori_loop(0, 4, fc1, 0)
        begin(1)

        def proj_part(m, _):
            col = pl.ds(pl.multiple_of(m * 384, 128), 384)
            gout[:, 3, :, col] = tn(att[...], gb1[:, col]).astype(BF16).reshape(8, ROWS, 384)
            return 0
        lax.fori_loop(0, 2, proj_part, 0)

    pl.run_scoped(
        mlp_part,
        pltpu.VMEM((D, D), BF16),
        pltpu.VMEM((4, D, D), BF16),
        pltpu.VMEM((MLP, D), BF16),
        pltpu.VMEM((rows, MLP), BF16),
        pltpu.VMEM((rows, D), BF16),
        pltpu.VMEM((rows, D), BF16),
        pltpu.VMEM((rows, D), BF16),
    )
    v_copies = [remote(gv.at[peers[k]], vbuf.at[k], vs.at[k], vr.at[k], (g, peers[k])) for k in range(7)]
    q_copies = [remote(qbuf.at[7], qbuf.at[k], qs.at[k], qr.at[k], (g, peers[k])) for k in range(7)]

    def attention_part(lin, bias, lse_t, gatt_at, dq, wa_v, normed, proj):
        inner = local([(proj_in, proj), (lse_in, lse_t), (wa.at[pl.ds(0, 3)], wa_v), (normed_in, normed)], 8)
        for copy in inner:
            copy.start()
        run(6, 7)
        fill_bias(bias)
        move_rows(lambda first, count: to_places(line, first, count), gatt, gatt_at)
        for copy in inner:
            copy.wait()
        for p in range(6):
            attend_back(p, proj, gatt_at, bias, lse_t, dq)
            if p == 0:
                settle(lin, 0)
            if p < 5:
                run(7 + p, 8 + p)
        weight_grads(normed, proj, gout)
        begin(0)
        run(12, 14)
        row_grads(column, wide, tall, vec, wa_v, proj, vg)
        store = pltpu.make_async_copy(tall, gin, ls.at[12])
        store.start()
        for k in range(8):
            gv[k, :, :ROWS] = vg[:, ROWS * k : ROWS * k + ROWS]
            for j in range(4):
                lead = 4 * ROWS * k + ROWS * j
                gv[k, 8 + j : 9 + j, :ROWS] = vg1[0:1, lead : lead + ROWS]
        for copy in v_copies:
            copy.start()
        run(14, 15)
        settle(lin, 1)
        run(15, 18)
        for k in range(7):
            v_copies[k].wait_recv()
        total = gv[t]
        for k in range(7):
            total = total + vbuf[k]
        lane = lax.broadcasted_iota(jnp.int32, (16, 128), 1)
        across = lax.broadcasted_iota(jnp.int32, (16, 128), 0)
        total = jnp.where((lane < ROWS) & (across < 14), total, 0.0)
        sv[...] = total

        def square(i, acc):
            v = lin[pl.ds(pl.multiple_of(i * 64, 64), 64), :]
            return acc + v * v
        acc = lax.fori_loop(36, 108, square, jnp.zeros((64, 128), F32))
        settle(lin, 2)
        lin_store = pltpu.make_async_copy(lin, lin_out, ls.at[13])
        lin_store.start()

        acc = lax.fori_loop(0, 36, square, acc)
        qbuf[7] = jnp.full((8, 128), jnp.sum(acc) + jnp.sum(total * total), F32)
        for copy in q_copies:
            copy.start()
        store.wait()
        lin_store.wait()

    pl.run_scoped(
        attention_part,
        pltpu.VMEM((6912, 128), F32),
        pltpu.VMEM((4, 288, 384), F32),
        pltpu.VMEM((16, rows), F32),
        pltpu.VMEM((rows, D), BF16),
        pltpu.VMEM((rows, 128), F32),
        pltpu.VMEM((3, D, D), BF16),
        pltpu.VMEM((rows, D), BF16),
        pltpu.VMEM((3, rows, D), BF16),
    )
    for w in range(3):
        for k in range(NZ):
            core_copy(w, k).wait_send()
    for h in (0, 1):
        @pl.when(z < NZ - 1)
        def _():
            z_copy(0, 0, z + 1, h).wait_send()

        @pl.when(z > 0)
        def _():
            z_copy(0, 1, z - 1, h).wait_send()
    for k in range(7):
        q_copies[k].wait_recv()
    acc = qbuf[7]
    for k in range(7):
        acc = acc + qbuf[k]
    sq[...] = acc
    for k in range(7):
        q_copies[k].wait_send()
        v_copies[k].wait_send()


def back(lens, vec, vg, tok, cot, wa, wb, wc, att, slope, n2, normed, proj, lse_t, gc):
    vm = pl.BlockSpec(memory_space=pltpu.VMEM)
    rows = tok.shape[0]
    S = jax.ShapeDtypeStruct
    V = pltpu.VMEM
    return pl.pallas_call(
        back_kernel,
        name="back",
        out_shape=[S((rows, D), F32), S((6912, 128), F32), S((16, 128), F32), S((8, 128), F32)],
        in_specs=[pl.BlockSpec(memory_space=pltpu.SMEM)] + [vm] * 2 + [ANY] * 12,
        out_specs=[ANY] * 2 + [vm] * 2,
        scratch_shapes=[
            V((8, rows), jnp.int32),
            V((rows, 128), jnp.int32),
            V((rows, D), F32),
            V((rows, D), F32),
            V((rows, D), BF16),
            V((8, 4, ROWS, D), BF16),
            V((8, 4, ROWS, D), BF16),
            V((NZ, 4, ROWS, D), BF16),
            V((3, NZ, 4, ROWS, D), BF16),
            V((3, 5, 4, ROWS, D), BF16),
            V((16, D), F32),
            V((8, MLP), F32),
            V((8, 16, 128), F32),
            V((7, 16, 128), F32),
            V((8, 8, 128), F32),
            DMA((14,)), DMA((NZ,)), DMA((3, NZ)), DMA((3, NZ)),
            DMA((3, 2, NZ, 2)), DMA((3, 2, NZ, 2)),
            DMA((7,)), DMA((7,)), DMA((7,)), DMA((7,)),
        ],
        compiler_params=pltpu.CompilerParams(
            collective_id=1, has_side_effects=True, vmem_limit_bytes=63 * 2**20
        ),
    )(lens, vec, vg, tok, cot, wa, wb, wc, att, slope, n2, normed, proj, lse_t, gc)


PARTS = 6912
SUM_H, SUM_Q, SUM_E = PARTS // 2, PARTS // 4, PARTS // 8
MATRIX_WIDTH = PARTS * 128
VECTOR_WIDTH = 14 * ROWS
BLOCKS = 4
BLOCK = MATRIX_WIDTH // BLOCKS
CHUNK = 6144


def adam_kernel(grad, sv, sq, master, first, second, first_new, second_new, diff, tail, vector_out, norm_out, tail_grad):
    i = pl.program_id(0)
    norm = jnp.sqrt(sq[0:1, 0:1])
    scale = clip_limit / (norm + 1e-06)
    step_rate = base_rate * rate_scale

    def adam(value, old_first, old_second, weight):
        clipped = value * scale
        new_first = beta_first * old_first + (1.0 - beta_first) * clipped
        new_second = beta_second * old_second + (1.0 - beta_second) * clipped * clipped
        root = jnp.sqrt(new_second * (1.0 / (1.0 - beta_second**adam_count))) + adam_epsilon
        ahead = new_first * (1.0 / (1.0 - beta_first**adam_count)) / root
        if weight is not None:
            ahead = ahead + weight_decay * weight
        return new_first, new_second, step_rate * ahead

    @pl.when(i < BLOCKS)
    def _():
        def body(n, _):
            flat = pl.ds(pl.multiple_of(n * CHUNK, CHUNK), CHUNK)
            at = pl.ds(pl.multiple_of(n * (CHUNK // 128), CHUNK // 128), CHUNK // 128)
            first_new[:, flat], second_new[:, flat], ahead = adam(
                grad[at, :].reshape(1, CHUNK), first[:, flat], second[:, flat], master[flat].reshape(1, CHUNK)
            )
            diff[at, :] = ahead.reshape(CHUNK // 128, 128).astype(BF16)
            return 0
        lax.fori_loop(0, BLOCK // CHUNK, body, 0, unroll=12)

    @pl.when(i == BLOCKS)
    def _():
        norm_out[...] = jnp.broadcast_to(norm, (8, 128))
        for j in range(14):
            tail_grad[0:1, ROWS * j : ROWS * j + ROWS] = sv[j : j + 1, :ROWS]
        vector_out[...] = tail_grad[...] / jnp.sqrt(F32(8 * 1024))
        at = pl.ds(0, VECTOR_WIDTH)
        first_new[:, at], second_new[:, at], ahead = adam(tail_grad[...], first[:, at], second[:, at], None)
        tail[...] = jnp.zeros_like(tail)
        tail[:, at] = ahead


def adam_step(grad, sv, sq, master, first, second):
    S = jax.ShapeDtypeStruct
    n = master.shape[0]

    def whole(shape):
        return pl.BlockSpec(shape, lambda i: (0, 0))

    line = pl.BlockSpec((1, BLOCK), lambda i: (0, i))
    rows = pl.BlockSpec((PARTS // BLOCKS, 128), lambda i: (jnp.minimum(i, BLOCKS - 1), 0))
    return pl.pallas_call(
        adam_kernel,
        name="adam",
        grid=(BLOCKS + 1,),
        out_shape=[
            S((1, n), F32), S((1, n), F32), S((PARTS, 128), BF16), S((1, 1408), F32), S((1, VECTOR_WIDTH), F32), S((8, 128), F32)
        ],
        in_specs=[rows, whole((16, 128)), whole((8, 128)), pl.BlockSpec((BLOCK,), lambda i: (i,)), line, line],
        out_specs=[line, line, rows, whole((1, 1408)), whole((1, VECTOR_WIDTH)), whole((8, 128))],
        scratch_shapes=[pltpu.VMEM((1, VECTOR_WIDTH), F32)],
    )(grad, sv, sq, master, first, second)


def outer_kernel(mean, tail, master, momentum, mean_out, momentum_out, weights_out):
    i = pl.program_id(0)

    def step(flat, average):
        new_momentum = outer_beta * momentum[flat] + average
        mean_out[flat] = average
        momentum_out[flat] = new_momentum
        weights_out[flat] = master[flat] - outer_rate * (average + outer_beta * new_momentum)

    @pl.when(i < BLOCKS)
    def _():
        def body(n, _):
            flat = pl.ds(pl.multiple_of(n * CHUNK, CHUNK), CHUNK)
            at = pl.ds(pl.multiple_of(n * (CHUNK // 128), CHUNK // 128), CHUNK // 128)
            step(flat, mean[at, :].astype(F32).reshape(CHUNK))
            return 0
        lax.fori_loop(0, BLOCK // CHUNK, body, 0, unroll=12)

    @pl.when(i == BLOCKS)
    def _():
        step(pl.ds(0, 1408), tail[0, :])


def outer_step(mean, tail, master, momentum):
    n = master.shape[0]
    line = pl.BlockSpec((BLOCK,), lambda i: (i,))
    return pl.pallas_call(
        outer_kernel,
        name="outer",
        grid=(BLOCKS + 1,),
        out_shape=[jax.ShapeDtypeStruct((n,), F32)] * 3,
        in_specs=[
            pl.BlockSpec((PARTS // BLOCKS, 128), lambda i: (jnp.minimum(i, BLOCKS - 1), 0)),
            pl.BlockSpec((1, 1408), lambda i: (0, 0)), line, line,
        ],
        out_specs=[line] * 3,
    )(mean, tail, master, momentum)


def mean_kernel(diff, tail, mean, tail_mean, part, mid, buf, tails, ss, rs, ts, tr):
    g, t, z, c, gx, gy = place()
    peers = [gx, gy, 3 - g]
    greet([(peer, t) for peer in peers], 3)
    xi, yi = lax.rem(g, 2), lax.div(g, 2)
    hop = [((gx, t), (gy, t)), ((gy, t), (gx, t))]
    mine = [(xi, yi), (yi, xi)]

    def at(h, i, j):
        return h * SUM_H + i * SUM_Q + j * SUM_E

    def to_sum(h, e):
        a, b = mine[h]
        j = 1 - b if e == 0 else b
        src = rows_at(diff, at(h, 1 - a, j), SUM_E)
        return remote(src, part.at[h, e], ss.at[h, e], rs.at[h, e], hop[h][0])

    def over(h):
        return remote(mid.at[h], buf.at[h], ss.at[h, 2], rs.at[h, 2], hop[h][1])

    def share(h, e):
        a, b = mine[h]
        block = rows_at(mean, at(h, a, 1 - b if e == 2 else b), SUM_E)
        return remote(block, block, ss.at[h, 3 + e], rs.at[h, 3 + e], hop[h][1 if e == 0 else 0])

    def landed(h, e):
        a, b = mine[h]
        block = rows_at(mean, at(h, a, 1 - b) if e == 0 else at(h, 1 - a, 1 - b if e == 2 else b), SUM_E)
        remote(block, block, ss.at[h, 3 + e], rs.at[h, 3 + e], hop[h][0]).wait_recv()

    def add(fn):
        def body(i, _):
            fn(pl.multiple_of(i * 96, 96))
            return 0
        lax.fori_loop(0, SUM_E // 96, body, 0)

    for e in (0, 1):
        for h in (0, 1):
            to_sum(h, e).start()
    t_copies = [remote(tail, tails.at[k], ts.at[k], tr.at[k], (peers[k], t)) for k in range(3)]
    for copy in t_copies:
        copy.start()
    for h in (0, 1):
        a, b = mine[h]
        to_sum(h, 0).wait_recv()

        def first(i):
            total = diff[pl.ds(pl.multiple_of(at(h, a, 1 - b) + i, 32), 96), :].astype(F32)
            mid[h, pl.ds(i, 96), :] = (total + part[h, 0, pl.ds(i, 96), :].astype(F32)).astype(BF16)
        add(first)
        over(h).start()
    for h in (0, 1):
        a, b = mine[h]
        to_sum(h, 1).wait_recv()
        over(h).wait_recv()

        def second(i):
            here = pl.ds(pl.multiple_of(at(h, a, b) + i, 32), 96)
            local = pl.ds(i, 96)
            total = diff[here, :].astype(F32) + part[h, 1, local, :].astype(F32) + buf[h, local, :].astype(F32)
            mean[here, :] = (total * 0.25).astype(BF16)
        add(second)
        share(h, 0).start()
        share(h, 1).start()
    for copy in t_copies:
        copy.wait_recv()
    tail_mean[...] = (tail[...] + tails[0] + tails[1] + tails[2]) * 0.25
    for h in (0, 1):
        landed(h, 0)
        share(h, 2).start()
    for h in (0, 1):
        landed(h, 1)
        landed(h, 2)
        for e in (0, 1):
            to_sum(h, e).wait_send()
        over(h).wait_send()
        for e in range(3):
            share(h, e).wait_send()
    for copy in t_copies:
        copy.wait_send()


def mean_groups(diff, tail):
    vm = pl.BlockSpec(memory_space=pltpu.VMEM)
    S = jax.ShapeDtypeStruct
    V = pltpu.VMEM
    return pl.pallas_call(
        mean_kernel,
        name="mean_groups",
        out_shape=[S((PARTS, 128), BF16), S((1, 1408), F32)],
        in_specs=[vm] * 2,
        out_specs=[vm] * 2,
        scratch_shapes=[
            V((2, 2, SUM_E, 128), BF16), V((2, SUM_E, 128), BF16), V((2, SUM_E, 128), BF16), V((3, 1, 1408), F32),
            DMA((2, 6)), DMA((2, 6)), DMA((3,)), DMA((3,)),
        ],
        compiler_params=pltpu.CompilerParams(collective_id=2, has_side_effects=True),
    )(diff, tail)


def on_small_slice(tokens, cotangent, crop_lengths, master, first_moment, second_moment, outer_momentum):
    wa, wb, wc, vec, fb1, normed, projected, attended, lse = front(crop_lengths, master, tokens)
    block_output, slope, normed_two, grad_fc2, vg = forward(
        crop_lengths, tokens, cotangent, attended, wa, wb, wc.reshape(MLP, D), vec, fb1
    )
    input_grad, grad_lin, sv, sq = back(
        crop_lengths, vec, vg, tokens, cotangent, wa, wb, wc.reshape(MLP, D), attended, slope, normed_two, normed,
        projected, lse, grad_fc2
    )
    moment_one, moment_two, difference, tail, vector_part, norm = adam_step(
        grad_lin, sv, sq, master, first_moment, second_moment
    )
    mean, tail_mean = mean_groups(difference, tail)
    mean_difference, outer_new, new_weights = outer_step(mean, tail_mean, master, outer_momentum)
    return (
        block_output,
        input_grad,
        norm[0, :1],
        vector_part,
        moment_one,
        moment_two,
        mean_difference,
        outer_new,
        new_weights,
    )


def solution(mesh):
    small = mesh.shape["grp"] == 4 and mesh.shape["tok"] == 8
    return jax.shard_map(
        on_small_slice if small else on_device,
        mesh=mesh,
        in_specs=(
            P(("grp", "tok"), None),
            P(("grp", "tok"), None),
            P(("grp", "tok"), None),
            P("tok"),
            P("grp", "tok"),
            P("grp", "tok"),
            P("tok"),
        ),
        out_specs=(
            P(("grp", "tok"), None),
            P(("grp", "tok"), None),
            P("grp"),
            P("grp", "tok"),
            P("grp", "tok"),
            P("grp", "tok"),
            P("tok"),
            P("tok"),
            P("tok"),
        ),
        check_vma=False,
    )
```

```python
import jax
import jax.numpy as jnp
from jax import lax
from jax.experimental import pallas as pl
from jax.experimental.pallas import tpu as pltpu
from jax.sharding import PartitionSpec as P

D = 768
MLP = 3072
HEADS = 12
HEAD_DIM = 64
ROWS = D // 8
ANY = pl.BlockSpec(memory_space=pl.ANY)
DMA = pltpu.SemaphoreType.DMA
MESH_ID = pl.DeviceIdType.MESH
NZ = 4
F32, BF16 = jnp.float32, jnp.bfloat16


def place():
    g = lax.axis_index("grp")
    t = lax.axis_index("tok")
    z, c = lax.div(t, 2), lax.rem(t, 2)
    gx = g + 1 - 2 * lax.rem(g, 2)
    gy = g + 2 - 4 * lax.div(g, 2)
    return g, t, z, c, gx, gy


def greet(targets, count):
    barrier = pltpu.get_barrier_semaphore()
    for target in targets:
        pl.semaphore_signal(barrier, inc=1, device_id=target, device_id_type=MESH_ID)
    pl.semaphore_wait(barrier, count)


def remote(src, dst, send, recv, target):
    return pltpu.make_async_remote_copy(
        src_ref=src, dst_ref=dst, send_sem=send, recv_sem=recv,
        device_id=target, device_id_type=MESH_ID,
    )


clip_limit = 3.0
beta_first = 0.9
beta_second = 0.999
adam_epsilon = 1e-08
weight_decay = 0.04
adam_count = 10.0
base_rate = 0.075
rate_scale = 0.9**6
outer_rate = 0.7
outer_beta = 0.9
norm_epsilon = 1e-06


def member_extents():
    return [(D, 3 * D), (D, D), (D, MLP), (MLP, D)] + [(D,)] * 8 + [(MLP,), (D,), (D,)]


def member_sizes():
    sizes_list = []
    for extent in member_extents():
        length = 1
        for member in extent:
            length = length * member
        sizes_list.append(length)
    return sizes_list


def split_params(flat_params, owners):
    table = flat_params.reshape(owners, -1)
    members = []
    offset = 0
    for extent, length in zip(member_extents(), member_sizes()):
        width = length // owners
        members.append(table[:, offset : offset + width].reshape(extent))
        offset = offset + width
    return members


def join_table(members, owners):
    return jnp.concatenate([member.reshape(owners, -1) for member in members], axis=1)


def layer_norm(values, norm_gain, norm_shift):
    center = values - jnp.mean(values, axis=-1, keepdims=True)
    spread = jnp.mean(center * center, axis=-1, keepdims=True)
    return center * lax.rsqrt(spread + norm_epsilon) * norm_gain + norm_shift


def pack_layout(lengths_row, row_count):
    ends_at = jnp.cumsum(lengths_row)
    position = jnp.arange(row_count, dtype=jnp.int32)
    segment = jnp.sum((position[:, None] >= ends_at[None, :]).astype(jnp.int32), axis=1)
    validity = (position < ends_at[-1]).astype(jnp.float32)
    return (segment, validity)


def cross_rows(left_side, right_side):
    return lax.dot_general(
        left_side, right_side, (((0,), (0,)), ((), ())), preferred_element_type=jnp.float32
    )


def times_transposed(left_side, right_side):
    return lax.dot_general(
        left_side, right_side, (((1,), (1,)), ((), ())), preferred_element_type=jnp.float32
    )


def on_device(tokens, cotangent, crop_lengths, master, first_moment, second_moment, outer_momentum):
    row_count = tokens.shape[0]
    pair_count = HEADS // 2
    score_scale = HEAD_DIM ** (-0.5)
    owners = lax.axis_size("tok")
    segment, validity = pack_layout(crop_lengths[0], row_count)
    allowed = segment[:, None] == segment[None, :]
    master_low = master.astype(jnp.bfloat16)
    gathered = split_params(lax.all_gather(master_low, "tok", axis=0, tiled=True), owners)
    w_qkv, w_proj, w_fc1, w_fc2 = gathered[:4]
    (
        gain_one,
        shift_one,
        query_bias,
        value_bias,
        proj_bias,
        scale_one,
        gain_two,
        shift_two,
        fc1_bias,
        fc2_bias,
        scale_two,
    ) = [member.astype(jnp.float32) for member in gathered[4:]]

    def to_pairs(block_cols):
        return jnp.moveaxis(block_cols.reshape(row_count, pair_count, 2 * HEAD_DIM), 1, 0)

    def from_pairs(paired):
        return jnp.moveaxis(paired, 0, 1).reshape(row_count, D)

    normed = layer_norm(tokens, gain_one, shift_one).astype(jnp.bfloat16)
    qkv_bias = jnp.concatenate([query_bias, jnp.zeros_like(query_bias), value_bias])
    projected = (jnp.dot(normed, w_qkv, preferred_element_type=jnp.float32) + qkv_bias).astype(
        jnp.bfloat16
    )
    query_pairs = to_pairs(projected[:, :D])
    key_pairs = to_pairs(projected[:, D : 2 * D])
    value_pairs = to_pairs(projected[:, 2 * D :])

    def forward_pair(pair_item):
        queries, keys_pair, values_pair = [
            member.reshape(row_count, 2, HEAD_DIM) for member in pair_item
        ]
        raw_scores = jnp.einsum(
            "qhd,khd->hqk", queries, keys_pair, preferred_element_type=jnp.float32
        )
        scores = jnp.where(allowed[None], raw_scores * score_scale, -1e30)
        largest = jnp.max(scores, axis=-1, keepdims=True)
        weights_exp = jnp.exp(scores - largest)
        totals = jnp.sum(weights_exp, axis=-1, keepdims=True)
        weights_low = (weights_exp / totals).astype(jnp.bfloat16)
        attended_pair = jnp.einsum(
            "hqk,khd->qhd", weights_low, values_pair, preferred_element_type=jnp.float32
        )
        return (attended_pair.reshape(row_count, 2 * HEAD_DIM), (largest + jnp.log(totals))[..., 0])

    attended_pairs, log_totals = lax.map(forward_pair, (query_pairs, key_pairs, value_pairs))
    attended = from_pairs(attended_pairs).astype(jnp.bfloat16)
    branch_one = jnp.dot(attended, w_proj, preferred_element_type=jnp.float32) + proj_bias
    middle = tokens + scale_one * branch_one
    normed_two = layer_norm(middle, gain_two, shift_two).astype(jnp.bfloat16)
    hidden_pre = jnp.dot(normed_two, w_fc1, preferred_element_type=jnp.float32) + fc1_bias
    hidden = jax.nn.gelu(hidden_pre, approximate=False).astype(jnp.bfloat16)
    branch_two = jnp.dot(hidden, w_fc2, preferred_element_type=jnp.float32) + fc2_bias
    block_output = middle + scale_two * branch_two
    back_out = cotangent * validity[:, None]
    grad_branch_two = (scale_two * back_out).astype(jnp.bfloat16)
    grad_scale_two = jnp.sum(back_out * branch_two, axis=0)
    grad_fc2_bias = jnp.sum(grad_branch_two.astype(jnp.float32), axis=0)
    grad_w_fc2 = cross_rows(hidden, grad_branch_two)
    grad_hidden = times_transposed(grad_branch_two, w_fc2)
    gelu_pull = jax.vjp(lambda values: jax.nn.gelu(values, approximate=False), hidden_pre)[1]
    grad_pre = gelu_pull(grad_hidden)[0].astype(jnp.bfloat16)
    grad_fc1_bias = jnp.sum(grad_pre.astype(jnp.float32), axis=0)
    grad_w_fc1 = cross_rows(normed_two, grad_pre)
    grad_normed_two = times_transposed(grad_pre, w_fc1)
    norm_pull = jax.vjp(layer_norm, middle, gain_two, shift_two)[1]
    grad_middle_part, grad_gain_two, grad_shift_two = norm_pull(grad_normed_two)
    grad_middle = back_out + grad_middle_part
    grad_scale_one = jnp.sum(grad_middle * branch_one, axis=0)
    grad_branch_one = (scale_one * grad_middle).astype(jnp.bfloat16)
    grad_proj_bias = jnp.sum(grad_branch_one.astype(jnp.float32), axis=0)
    grad_w_proj = cross_rows(attended, grad_branch_one)
    grad_attended = times_transposed(grad_branch_one, w_proj).astype(jnp.bfloat16)

    def backward_pair(pair_item):
        queries, keys_pair, values_pair, grad_pair = [
            member.reshape(row_count, 2, HEAD_DIM) for member in pair_item[:4]
        ]
        log_total = pair_item[4]
        raw_scores = jnp.einsum(
            "qhd,khd->hqk", queries, keys_pair, preferred_element_type=jnp.float32
        )
        scores = jnp.where(allowed[None], raw_scores * score_scale, -1e30)
        weights_soft = jnp.exp(scores - log_total[..., None])
        grad_values = jnp.einsum(
            "hqk,qhd->khd",
            weights_soft.astype(jnp.bfloat16),
            grad_pair,
            preferred_element_type=jnp.float32,
        )
        grad_weights = jnp.einsum(
            "qhd,khd->hqk", grad_pair, values_pair, preferred_element_type=jnp.float32
        )
        row_dot = jnp.sum(weights_soft * grad_weights, axis=-1, keepdims=True)
        grad_scores = (weights_soft * (grad_weights - row_dot)).astype(jnp.bfloat16)
        grad_queries = (
            jnp.einsum("hqk,khd->qhd", grad_scores, keys_pair, preferred_element_type=jnp.float32)
            * score_scale
        )
        grad_keys = (
            jnp.einsum("hqk,qhd->khd", grad_scores, queries, preferred_element_type=jnp.float32)
            * score_scale
        )
        return (
            grad_queries.reshape(row_count, 2 * HEAD_DIM),
            grad_keys.reshape(row_count, 2 * HEAD_DIM),
            grad_values.reshape(row_count, 2 * HEAD_DIM),
        )

    grad_q_pairs, grad_k_pairs, grad_v_pairs = lax.map(
        backward_pair, (query_pairs, key_pairs, value_pairs, to_pairs(grad_attended), log_totals)
    )
    grad_projected = jnp.concatenate(
        [from_pairs(grad_q_pairs), from_pairs(grad_k_pairs), from_pairs(grad_v_pairs)], axis=1
    ).astype(jnp.bfloat16)
    grad_query_bias = jnp.sum(grad_projected[:, :D].astype(jnp.float32), axis=0)
    grad_value_bias = jnp.sum(grad_projected[:, 2 * D :].astype(jnp.float32), axis=0)
    grad_w_qkv = cross_rows(normed, grad_projected)
    grad_normed = times_transposed(grad_projected, w_qkv)
    first_pull = jax.vjp(layer_norm, tokens, gain_one, shift_one)[1]
    grad_tokens_part, grad_gain_one, grad_shift_one = first_pull(grad_normed)
    input_grad = grad_middle + grad_tokens_part
    all_members = [
        grad_w_qkv,
        grad_w_proj,
        grad_w_fc1,
        grad_w_fc2,
        grad_gain_one,
        grad_shift_one,
        grad_query_bias,
        grad_value_bias,
        grad_proj_bias,
        grad_scale_one,
        grad_gain_two,
        grad_shift_two,
        grad_fc1_bias,
        grad_fc2_bias,
        grad_scale_two,
    ]
    received = lax.all_to_all(
        join_table(all_members, owners).astype(jnp.bfloat16),
        "tok",
        split_axis=0,
        concat_axis=0,
        tiled=True,
    ).astype(jnp.float32)
    summed = jnp.sum(received, axis=0)
    matrix_width = (4 * D * D + 2 * D * MLP) // owners
    vector_part = summed[matrix_width:] / (owners * row_count) ** 0.5
    square_total = lax.psum(jnp.sum(summed * summed), "tok")
    norm_value = jnp.sqrt(square_total)
    clipped = summed * (clip_limit / (norm_value + 1e-06))
    moment_one = beta_first * first_moment[0] + (1.0 - beta_first) * clipped
    moment_two = beta_second * second_moment[0] + (1.0 - beta_second) * clipped * clipped
    corrected_one = moment_one / (1.0 - beta_first**adam_count)
    corrected_two = moment_two / (1.0 - beta_second**adam_count)
    shard_size = master.shape[0]
    local_index = jnp.arange(shard_size, dtype=jnp.int32)
    decay_mask = (local_index < matrix_width).astype(jnp.float32)
    step_rate = base_rate * rate_scale
    updated = master - step_rate * (
        corrected_one / (jnp.sqrt(corrected_two) + adam_epsilon)
        + weight_decay * decay_mask * master
    )
    mean_difference = lax.psum((master - updated).astype(jnp.bfloat16), "grp").astype(
        jnp.float32
    ) / lax.axis_size("grp")
    outer_new = outer_beta * outer_momentum + mean_difference
    new_weights = master - outer_rate * (mean_difference + outer_beta * outer_new)
    return (
        block_output,
        input_grad,
        norm_value.reshape(1),
        vector_part[None],
        moment_one[None],
        moment_two[None],
        mean_difference,
        outer_new,
        new_weights,
    )


def rows_at(ref, start, count):
    return ref.at[pl.ds(pl.multiple_of(start, 16), count), :]


TILE = 512


def nn(a, b):
    return lax.dot_general(a, b, (((1,), (0,)), ((), ())), preferred_element_type=F32)


def nt(a, b):
    return lax.dot_general(a, b, (((1,), (1,)), ((), ())), preferred_element_type=F32)


def tn(a, b):
    return lax.dot_general(a, b, (((0,), (0,)), ((), ())), preferred_element_type=F32)


def normalize(values):
    center = values - jnp.mean(values, axis=-1, keepdims=True)
    spread = jnp.mean(center * center, axis=-1, keepdims=True)
    inverse = lax.rsqrt(spread + norm_epsilon)
    return center * inverse, inverse


def norm_pull(grad, normal, inverse, gain):
    scaled = grad * gain
    return inverse * (
        scaled
        - jnp.mean(scaled, axis=-1, keepdims=True)
        - normal * jnp.mean(scaled * normal, axis=-1, keepdims=True)
    )


def gelu_and_slope(x):
    phi = 0.5 * (1.0 + lax.erf(x * 0.7071067811865476))
    return x * phi, phi + x * jnp.exp(-0.5 * x * x) * 0.3989422804014327


def col_sum(x):
    return jnp.sum(x, axis=0, keepdims=True)


QT = 256
LONG, SHORT = 261, 54
TILES = (
    (0, 272, 0, 384, 0, 261),
    (256, 272, 256, 384, 261, 522),
    (512, 288, 512, 384, 522, 792),
    (784, 240, 768, 256, 792, 1024),
)


def find_places(lens, line, column):
    crops = lens.shape[1]
    longs, shorts, begin = jnp.int32(0), jnp.int32(0), jnp.int32(0)
    at_line = lax.broadcasted_iota(jnp.int32, line.shape, 1)
    at_column = lax.broadcasted_iota(jnp.int32, column.shape, 0)
    new_line, new_column = at_line, at_column
    for j in range(crops):
        size = lens[0, j]
        is_long = (size == LONG).astype(jnp.int32)
        place_at = is_long * (longs * LONG) + (1 - is_long) * (2 * LONG + shorts * SHORT)
        shift = place_at - begin
        new_line = jnp.where((at_line >= begin) & (at_line < begin + size), at_line + shift, new_line)
        new_column = jnp.where((at_column >= begin) & (at_column < begin + size), at_column + shift, new_column)
        longs, shorts, begin = longs + is_long, shorts + 1 - is_long, begin + size
    line[...] = new_line
    column[...] = new_column


def to_places(line, first, count):
    rows = lax.broadcasted_iota(jnp.int32, (count, line.shape[1]), 0) + first
    return (rows == line[0:1, :]).astype(F32).astype(BF16)


def from_places(column, first, count):
    lanes = lax.broadcasted_iota(jnp.int32, (count, column.shape[0]), 1)
    return (lanes == column[pl.ds(first, count), 0:1]).astype(F32).astype(BF16)


def fill_bias(bias):
    def crop(at):
        found = jnp.zeros(at.shape, jnp.int32)
        for end in [LONG] + [2 * LONG + SHORT * j for j in range(9)]:
            found = found + (at >= end).astype(jnp.int32)
        return found

    for i, (row, rows, col, cols, low, high) in enumerate(TILES):
        at_row = lax.broadcasted_iota(jnp.int32, (rows, 1), 0) + row
        at_col = lax.broadcasted_iota(jnp.int32, (1, cols), 1) + col
        same = crop(at_row) == jnp.where((at_col >= low) & (at_col < high), crop(at_col), -1)
        bias[i, :rows, :cols] = jnp.where(same, 0.0, -1e30).astype(F32)


def head_part(block, h):
    lane = lax.broadcasted_iota(jnp.int32, (1, 128), 1)
    keep = lane < 64 if h == 0 else lane >= 64
    return jnp.where(keep, block, jnp.zeros_like(block))


def first_half(a, b):
    lane = lax.broadcasted_iota(jnp.int32, (1, 128), 1)
    return jnp.where(lane < 64, a, b)


def rows_from(tile, new, old):
    row, rows, low = tile[0], tile[1], tile[4]
    if row == low:
        return new
    return jnp.where(lax.broadcasted_iota(jnp.int32, (rows, 1), 0) + row >= low, new, old)


def norm_rows(tok, vec, normed):
    def tile(i, _):
        at = pl.ds(pl.multiple_of(i * QT, QT), QT)
        normal, _inverse = normalize(tok[at, :])
        normed[at, :] = (normal * vec[0:1, :] + vec[1:2, :]).astype(BF16)
        return 0
    lax.fori_loop(0, tok.shape[0] // QT, tile, 0)


def project_in(vec, wa, normed, proj):
    def block(i, _):
        at = pl.ds(pl.multiple_of(i * QT, QT), QT)
        proj[0, at, :] = (nn(normed[at, :], wa[0]) + vec[2:3, :]).astype(BF16)
        proj[1, at, :] = nn(normed[at, :], wa[1]).astype(BF16)
        proj[2, at, :] = (nn(normed[at, :], wa[2]) + vec[3:4, :]).astype(BF16)
        return 0
    lax.fori_loop(0, normed.shape[0] // QT, block, 0)


def move_rows(one_hot, src, dst):
    def block(i, _):
        first = pl.multiple_of(i * QT, QT)
        dst[pl.ds(first, QT), :] = nn(one_hot(first, QT), src[...]).astype(BF16)
        return 0
    lax.fori_loop(0, src.shape[0] // QT, block, 0)


def attend(p, proj, bias, att, lse):
    cols = pl.ds(pl.multiple_of(p * 128, 128), 128)
    lane = lax.broadcasted_iota(jnp.int32, (1, 128), 1)
    for i, tile in enumerate(TILES):
        row, rows, col, wide = tile[:4]
        at, keys = pl.ds(row, rows), pl.ds(col, wide)
        q = proj[0, at, cols] * jnp.asarray(0.125, BF16)
        k, v = proj[1, keys, cols], proj[2, keys, cols]
        outs = []
        logs = lse[at, :]
        for h in (0, 1):
            scores = nt(head_part(q, h), k) + bias[i, :rows, :wide]
            largest = jnp.max(scores, axis=-1, keepdims=True)
            weights = jnp.exp(scores - largest)
            total = jnp.sum(weights, axis=-1, keepdims=True)
            low = (weights * (1.0 / total)).astype(BF16)
            outs.append(nn(low, v))
            logs = jnp.where(lane == 2 * p + h, largest + jnp.log(total), logs)
        lse[at, :] = rows_from(tile, logs, lse[at, :])
        att[at, cols] = rows_from(tile, first_half(*outs), att[at, cols].astype(F32)).astype(BF16)


def attend_back(p, proj, gatt, bias, lse_t, dq):
    cols = pl.ds(pl.multiple_of(p * 128, 128), 128)
    dq[...] = jnp.zeros_like(dq)
    dks, dvs = [], []
    for i, tile in enumerate(TILES):
        row, rows, col, wide = tile[:4]
        at, queries = pl.ds(row, rows), pl.ds(col, wide)
        k, v = proj[1, at, cols], proj[2, at, cols]
        g = gatt[queries, cols]
        scaled = proj[0, queries, cols] * jnp.asarray(0.125, BF16)
        dk, dv, dqs = [], [], []
        for h in (0, 1):
            scores = nt(head_part(k, h), scaled) + bias[i, :rows, :wide]
            probs = jnp.exp(scores - lse_t[pl.ds(2 * p + h, 1), queries])
            grad = nt(head_part(v, h), g)
            dot = jnp.sum(probs * grad, axis=0, keepdims=True)
            low = (probs * (grad - dot)).astype(BF16)
            dv.append(nn(probs.astype(BF16), g))
            dk.append(nn(low, scaled))
            dqs.append(tn(low, k))
        dq[queries, :] += first_half(*dqs) * 0.125
        dks.append(first_half(*dk))
        dvs.append(first_half(*dv))
    for i, tile in enumerate(TILES):
        at = pl.ds(tile[0], tile[1])
        proj[1, at, cols] = rows_from(tile, dks[i], proj[1, at, cols].astype(F32)).astype(BF16)
        proj[2, at, cols] = rows_from(tile, dvs[i], proj[2, at, cols].astype(F32)).astype(BF16)
    proj[0, :, cols] = dq[...].astype(BF16)


def weight_grads(normed, gproj, gout):
    def block(q, _):
        def part(m, _):
            col = pl.ds(pl.multiple_of(m * 384, 128), 384)
            gout[:, q, :, col] = tn(normed[...], gproj[q, :, col]).astype(BF16).reshape(8, ROWS, 384)
            return 0
        return lax.fori_loop(0, 2, part, 0)
    lax.fori_loop(0, 3, block, 0)


def row_grads(column, wide, total, vec, wa, gproj, vg):

    def tile(i, _):
        first = pl.multiple_of(i * QT, QT)
        at = pl.ds(first, QT)
        back = from_places(column, first, QT)
        parts = [nn(back, gproj[j]).astype(BF16) for j in range(3)]
        grad = nt(parts[0], wa[0]) + nt(parts[1], wa[1]) + nt(parts[2], wa[2])
        normal, inverse = normalize(wide[at, :D])
        vg[0:1, :] += col_sum(grad * normal)
        vg[1:2, :] += col_sum(grad)
        vg[2:3, :] += col_sum(parts[0].astype(F32))
        vg[3:4, :] += col_sum(parts[2].astype(F32))
        total[at, :] = total[at, :] + norm_pull(grad, normal, inverse, vec[0:1, :])
        return 0
    lax.fori_loop(0, total.shape[0] // QT, tile, 0)


def convert_piece(w, lin, piece):
    if w == 2:
        for q in range(4):
            for m in range(6):
                piece[q, :, 128 * m : 128 * m + 128] = lin[pl.ds(4608 + 576 * q + m, ROWS, stride=6), :].astype(BF16)
        return
    for q in range(4):
        for m in range(6):
            if w == 1:
                at = pl.ds(2304 + 6 * q + m, ROWS, stride=24)
            elif q == 3:
                at = pl.ds(1728 + m, ROWS, stride=6)
            else:
                at = pl.ds(6 * q + m, ROWS, stride=18)
            piece[q, :, 128 * m : 128 * m + 128] = lin[at, :].astype(BF16)


def to_rows(flat, lin, first, count):
    def body(i, _):
        at = first + i * 48
        value = flat[:, pl.ds(pl.multiple_of(at * 128, 6144), 6144)]
        lin[pl.ds(pl.multiple_of(at, 48), 48), :] = value.reshape(48, 128)
        return 0
    lax.fori_loop(0, count // 48, body, 0)


def weight_strip(w, ref, t):
    if w == 2:
        return ref.at[t]
    return ref.at[:, pl.ds(pl.multiple_of(t * ROWS, 16), ROWS), :]


def weight_block(w, ref, t, q, lead=0, count=ROWS):
    if w == 2:
        return ref.at[t, q, pl.ds(lead, count), :]
    return ref.at[q, pl.ds(pl.multiple_of(t * ROWS + lead, 16), count), :]


def front_kernel(
    lens, master, tok,
    wa, wb, wc, vec, fb1, normed, proj, att, lse_out,
    flat, lin, pv, pieces, wv, wa_in, bias, line, column, att_in, lse,
    ls, zs, zr, xs, xr, ys, yr, ds, dr, cs, cr, vs, vr, es, er,
):
    weights_in = pltpu.make_async_copy(master, flat.at[0], ls.at[5])
    weights_in.start()
    g, t, z, c, gx, gy = place()
    fulls = (wa, wb, wc)
    peers = [lax.rem(t + k, 8) for k in range(1, 8)]
    barrier = pltpu.get_barrier_semaphore()
    for target in [(g, p) for p in peers] + [(gx, t), (gy, t)]:
        pl.semaphore_signal(barrier, inc=1, device_id=target, device_id_type=MESH_ID)
    weights_in.wait()
    to_rows(flat, lin, 0, 2304)
    convert_piece(0, lin, pieces.at[0])
    pv[...] = jnp.zeros_like(pv)
    for j in range(14):
        low = flat[:, pl.ds(6912 * 128 + ROWS * j, ROWS)].astype(BF16)
        pv[j : j + 1, :ROWS] = low.astype(F32)
    pl.semaphore_wait(barrier, 9)
    other = t + 1 - 2 * c

    def z_copy(w, d, s):
        step = 1 if d == 0 else -1
        src_t = t - 2 * step * s
        src = pieces.at[w, g] if s == 0 else weight_block(w, fulls[w], src_t, g)
        ok = (z - s >= 0) & (z + 1 < NZ) if d == 0 else (z + s < NZ) & (z - 1 >= 0)
        return ok, remote(src, weight_block(w, fulls[w], src_t, g), zs.at[w, d, s], zr.at[w, d, s], (g, t + 2 * step))

    def extra_copy(w, d, s):
        step = 1 if d == 0 else -1
        src_t = t - 2 * step * s
        src = pieces.at[w, 3 - g, pl.ds(0, 32)] if s == 0 else weight_block(w, fulls[w], src_t, 3 - g, 0, 32)
        ok = (z - s >= 0) & (z + 1 < NZ) if d == 0 else (z + s < NZ) & (z - 1 >= 0)
        dst = weight_block(w, fulls[w], src_t, 3 - g, 0, 32)
        return ok, remote(src, dst, es.at[w, d, s], er.at[w, d, s], (g, t + 2 * step))

    def extra_wait(w, d, s):
        blk = weight_block(w, fulls[w], from_t(d, s), 3 - g, 0, 32)
        remote(blk, blk, es.at[w, d, s], er.at[w, d, s], (g, other)).wait_recv()

    def from_t(d, s):
        return t - 2 * (s + 1) if d == 0 else t + 2 * (s + 1)

    def here(d, s):
        return z - s - 1 >= 0 if d == 0 else z + s + 1 < NZ

    def z_wait(w, d, s):
        blk = weight_block(w, fulls[w], from_t(d, s), g)
        remote(blk, blk, zs.at[w, d, s], zr.at[w, d, s], (g, other)).wait_recv()

    def side_copy(w, d, s, axis):
        blk = weight_block(w, fulls[w], from_t(d, s), g)
        sems = (xs, xr) if axis == 0 else (ys, yr)
        return remote(blk, blk, sems[0].at[w, d, s], sems[1].at[w, d, s], (gx if axis == 0 else gy, t))

    def side_wait(w, d, s, axis):
        blk = weight_block(w, fulls[w], from_t(d, s), gx if axis == 0 else gy)
        sems = (xs, xr) if axis == 0 else (ys, yr)
        remote(blk, blk, sems[0].at[w, d, s], sems[1].at[w, d, s], (gx, t)).wait_recv()

    def diag_copy(w, d, s, axis):
        blk = weight_block(w, fulls[w], from_t(d, s), gx if axis == 0 else gy, 32 + 32 * axis, 32)
        return remote(blk, blk, ds.at[w, d, s, axis], dr.at[w, d, s, axis], (gy if axis == 0 else gx, t))

    def diag_wait(w, d, s, axis):
        blk = weight_block(w, fulls[w], from_t(d, s), 3 - g, 32 + 32 * axis, 32)
        remote(blk, blk, ds.at[w, d, s, axis], dr.at[w, d, s, axis], (gx, t)).wait_recv()

    def core_copy(w, d, s):
        blk = weight_strip(w, fulls[w], from_t(d, s))
        return remote(blk, blk, cs.at[w, d, s], cr.at[w, d, s], (g, other))

    def core_wait(w, d, s):
        blk = weight_strip(w, fulls[w], from_t(d, s) + 1 - 2 * c)
        remote(blk, blk, cs.at[w, d, s], cr.at[w, d, s], (g, other)).wait_recv()

    def own_copy(w):
        return remote(pieces.at[w], weight_strip(w, fulls[w], t), cs.at[w, 2, 0], cr.at[w, 2, 0], (g, other))

    def own_wait(w):
        blk = weight_strip(w, fulls[w], other)
        remote(blk, blk, cs.at[w, 2, 0], cr.at[w, 2, 0], (g, other)).wait_recv()

    def own_local(w):
        return pltpu.make_async_copy(pieces.at[w], weight_strip(w, fulls[w], t), ls.at[w])

    def both(s, fn):
        for d in (0, 1):
            @pl.when(here(d, s))
            def _():
                fn(d)

    def start_z(w, s, kind=None):
        for d in (0, 1):
            ok, copy = (kind or z_copy)(w, d, s)

            @pl.when(ok)
            def _():
                copy.start()

    def arrive(n):
        w, s = divmod(n, 3)
        both(s, lambda d: z_wait(w, d, s))
        if s < 2:
            start_z(w, s + 1)

        def sides(d):
            side_copy(w, d, s, 0).start()
            side_copy(w, d, s, 1).start()
        both(s, sides)
        if s == 0 and w < 2:
            start_z(w + 1, 0)
            own_copy(w + 1).start()
            start_z(w + 1, 0, extra_copy)

    def cross(n):
        w, s = divmod(n, 3)

        def fn(d):
            for axis in (0, 1):
                side_wait(w, d, s, axis)
                diag_copy(w, d, s, axis).start()
            extra_wait(w, d, s)
        both(s, fn)
        if s < 2:
            start_z(w, s + 1, extra_copy)

    def finish(n):
        w, s = divmod(n, 3)

        def fn(d):
            diag_wait(w, d, s, 0)
            diag_wait(w, d, s, 1)
            core_copy(w, d, s).start()
        both(s, fn)

    def drain(w):
        own_wait(w)
        own_local(w).wait()
        for s in range(3):
            both(s, lambda d: core_wait(w, d, s))

    start_z(0, 0)
    own_copy(0).start()
    start_z(0, 0, extra_copy)
    own_local(0).start()
    local_v = pltpu.make_async_copy(pv, wv.at[t], ls.at[3])
    local_v.start()
    v_copies = [remote(pv, wv.at[t], vs.at[k], vr.at[k], (g, peers[k])) for k in range(7)]
    for copy in v_copies:
        copy.start()
    to_rows(flat, lin, 2304, 4608)
    for w in (1, 2):
        convert_piece(w, lin, pieces.at[w])
        own_local(w).start()
    fill_bias(bias)
    find_places(lens, line, column)
    att_in[...] = jnp.zeros_like(att_in)
    lse[...] = jnp.zeros_like(lse)
    arrive(0)
    local_v.wait()
    for k in range(7):
        remote(pv, wv.at[lax.rem(t + 7 - k, 8)], vs.at[k], vr.at[k], (g, peers[k])).wait_recv()
    for k in range(8):
        vec[:, ROWS * k : ROWS * k + ROWS] = wv[k, :, :ROWS]
        for j in range(4):
            lead = 4 * ROWS * k + ROWS * j
            fb1[0:1, lead : lead + ROWS] = wv[k, 8 + j : 9 + j, :ROWS]
    arrive(1)
    cross(0)
    norm_rows(tok, vec, att)
    move_rows(lambda first, count: to_places(line, first, count), att, normed)
    arrive(2)
    cross(1)
    finish(0)
    arrive(3)
    cross(2)
    finish(1)
    finish(2)
    drain(0)
    load = pltpu.make_async_copy(wa.at[pl.ds(0, 3)], wa_in, ls.at[4])
    load.start()
    load.wait()
    project_in(vec, wa_in, normed, proj)
    arrive(4)
    cross(3)
    events = [
        [(arrive, 5), (arrive, 6), (cross, 4), (finish, 3)],
        [(arrive, 7), (cross, 5), (finish, 4)],
        [(arrive, 8), (cross, 6), (finish, 5)],
        [(cross, 7), (finish, 6)],
        [(cross, 8), (finish, 7)],
        [(finish, 8)],
    ]
    for p in range(6):
        attend(p, proj, bias, att_in, lse)
        for event, n in events[p]:
            event(n)
    move_rows(lambda first, count: from_places(column, first, count), att_in, att)
    lse_out[...] = lse[...].T[:16]
    drain(1)
    drain(2)
    for copy in v_copies:
        copy.wait_send()
    for w in range(3):
        own_copy(w).wait_send()
        for s in range(3):
            for d in (0, 1):
                for kind in (z_copy, extra_copy):
                    ok, copy = kind(w, d, s)

                    @pl.when(ok)
                    def _():
                        copy.wait_send()

            def sent(d):
                side_copy(w, d, s, 0).wait_send()
                side_copy(w, d, s, 1).wait_send()
                diag_copy(w, d, s, 0).wait_send()
                diag_copy(w, d, s, 1).wait_send()
                core_copy(w, d, s).wait_send()
            both(s, sent)


def front(lens, master, tok):
    vm = pl.BlockSpec(memory_space=pltpu.VMEM)
    rows = tok.shape[0]
    S = jax.ShapeDtypeStruct
    return pl.pallas_call(
        front_kernel,
        name="front",
        out_shape=[
            S((4, D, D), BF16), S((4, D, D), BF16), S((8, 4, ROWS, D), BF16),
            S((16, D), F32), S((8, MLP), F32),
            S((rows, D), BF16), S((3, rows, D), BF16), S((rows, D), BF16), S((16, rows), F32),
        ],
        in_specs=[pl.BlockSpec(memory_space=pltpu.SMEM)] + [ANY, vm],
        out_specs=[ANY] * 3 + [vm] * 6,
        scratch_shapes=[
            pltpu.VMEM((1, master.shape[0]), F32),
            pltpu.VMEM((6912, 128), F32),
            pltpu.VMEM((16, 128), F32),
            pltpu.VMEM((3, 4, ROWS, D), BF16),
            pltpu.VMEM((8, 16, 128), F32),
            pltpu.VMEM((3, D, D), BF16),
            pltpu.VMEM((4, 288, 384), F32),
            pltpu.VMEM((8, rows), jnp.int32),
            pltpu.VMEM((rows, 128), jnp.int32),
            pltpu.VMEM((rows, D), BF16),
            pltpu.VMEM((rows, 128), F32),
            DMA((6,)),
            DMA((3, 2, 3)), DMA((3, 2, 3)),
            DMA((3, 2, 3)), DMA((3, 2, 3)),
            DMA((3, 2, 3)), DMA((3, 2, 3)),
            DMA((3, 2, 3, 2)), DMA((3, 2, 3, 2)),
            DMA((3, 3, 3)), DMA((3, 3, 3)),
            DMA((7,)), DMA((7,)),
            DMA((3, 2, 3)), DMA((3, 2, 3)),
        ],
        compiler_params=pltpu.CompilerParams(collective_id=0, has_side_effects=True, vmem_limit_bytes=60 * 2**20),
    )(lens, master, tok)


def valid_rows(lens, first, count):
    total = jnp.int32(0)
    for j in range(lens.shape[1]):
        total = total + lens[0, j]
    at = lax.broadcasted_iota(jnp.int32, (count, 1), 0) + first
    return (at < total).astype(F32)


def forward_kernel(
    lens, tok_in, cot_in, att_in, wa, wb_in, wc_in, vec, fb1,
    bo_out, slope_out, n2_out, hid_out, vg,
    tok, cot, att, wp, wb, wc, bo, slope, n2, hid, ls, os,
):
    pairs = [(att_in, att), (wa.at[3], wp), (tok_in, tok), (wb_in, wb), (wc_in, wc), (cot_in, cot)]
    loads = [pltpu.make_async_copy(src, dst, ls.at[i]) for i, (src, dst) in enumerate(pairs)]
    for copy in loads:
        copy.start()
    vg[...] = jnp.zeros_like(vg)
    rows = tok.shape[0]

    def row(j):
        return vec[j : j + 1, :]

    def stores(i):
        at = pl.ds(i * TILE, TILE)
        trio = [(slope, slope_out), (n2, n2_out), (hid, hid_out), (bo, bo_out)]
        return [pltpu.make_async_copy(a.at[at, :], b.at[at, :], os.at[i, n]) for n, (a, b) in enumerate(trio)]

    for copy in loads[:3]:
        copy.wait()
    for i in range(rows // TILE):
        at = pl.ds(i * TILE, TILE)
        middle = tok[at, :] + row(5) * (nn(att[at, :], wp[...]) + row(4))
        normal, _inverse = normalize(middle)
        bo[at, :] = middle
        n2[at, :] = (normal * row(6) + row(7)).astype(BF16)
        if i == 0:
            loads[3].wait()

        def hidden(q, _):
            low = pl.ds(pl.multiple_of(q * D, D), D)
            pre = nn(n2[at, :], wb[q]) + fb1[0:1, low]
            h, s = gelu_and_slope(pre)
            hid[at, low] = h.astype(BF16)
            slope[at, low] = s.astype(BF16)
            return 0
        lax.fori_loop(0, 4, hidden, 0)
        if i == 0:
            loads[4].wait()
            loads[5].wait()
        for copy in stores(i)[:3]:
            copy.start()
        branch_two = nn(hid[at, :], wc[...]) + row(12)
        bo[at, :] += row(13) * branch_two
        back = cot[at, :] * valid_rows(lens, i * TILE, TILE)
        low_back = (row(13) * back).astype(BF16)
        vg[13:14, :] += col_sum(back * branch_two)
        vg[12:13, :] += col_sum(low_back.astype(F32))
        stores(i)[3].start()
    for i in range(rows // TILE):
        for copy in stores(i):
            copy.wait()


def forward(lens, tok, cot, att, wa, wb, wc, vec, fb1):
    vm = pl.BlockSpec(memory_space=pltpu.VMEM)
    rows = tok.shape[0]
    S = jax.ShapeDtypeStruct
    V = pltpu.VMEM
    return pl.pallas_call(
        forward_kernel,
        name="mlp_forward",
        out_shape=[S((rows, D), F32), S((rows, MLP), BF16), S((rows, D), BF16), S((rows, MLP), BF16), S((16, D), F32)],
        in_specs=[pl.BlockSpec(memory_space=pltpu.SMEM)] + [ANY] * 6 + [vm] * 2,
        out_specs=[ANY] * 4 + [vm],
        scratch_shapes=[
            V((rows, D), F32), V((rows, D), F32), V((rows, D), BF16), V((D, D), BF16),
            V((4, D, D), BF16), V((MLP, D), BF16), V((rows, D), F32), V((rows, MLP), BF16),
            V((rows, D), BF16), V((rows, MLP), BF16),
            DMA((6,)), DMA((4, 4)),
        ],
        compiler_params=pltpu.CompilerParams(vmem_limit_bytes=62 * 2**20),
    )(lens, tok, cot, att, wa, wb, wc, vec, fb1)


ORDER = (2, 1, 0)
FIRST = (3, 0, 2, 1)


def back_kernel(
    lens, vec, vg_in, tok, cot, wa, wb_in, wc_in, att_in, slope_in, hid_in, n2_in, normed_in, proj_in, lse_in,
    gin, lin_out, sv, sq,
    line, column, wide, tall, gatt, gout, gb, own, core, zbuf, vg, vg1, gv, vbuf, qbuf,
    ls, hs, cs, cr, zs, zr, vs, vr, qs, qr,
):
    g, t, z, c, gx, gy = place()
    peers = [lax.rem(t + k, 8) for k in range(1, 8)]
    rows = tok.shape[0]
    other = t + 1 - 2 * c

    def local(pairs, first):
        return [pltpu.make_async_copy(src, dst, ls.at[first + i]) for i, (src, dst) in enumerate(pairs)]

    loads = local([(tok, wide), (cot, tall)], 0)
    for copy in loads:
        copy.start()
    greet([(g, p) for p in peers], 7)

    def own_at(w, k):
        return own.at[k] if w == 2 else (gout, gb)[w].at[2 * k + c]

    def core_copy(w, k):
        return remote((gout, gb, gout)[w].at[2 * k + 1 - c], core.at[w, k], cs.at[w, k], cr.at[w, k], (g, other))

    def begin(w):
        for k in FIRST:
            core_copy(w, k).start()

    def slot(d, k, to):
        return k - to if d == 0 else 4 - (to - k)

    def total_of(w, k, q, at, extra):
        mine = own_at(w, k)
        total = mine[q, at, :].astype(F32) + core[w, k, q, at, :].astype(F32)
        for d in extra:
            total = total + zbuf[w, slot(d, k, z), q, at, :].astype(F32)
        return total

    def add_rows(w, k, h, extra):
        for q in (2 * h, 2 * h + 1):
            def body(i, _):
                at = pl.ds(pl.multiple_of(i * 32, 32), 32)
                own_at(w, k)[q, at, :] = total_of(w, k, q, at, extra).astype(BF16)
                return 0
            lax.fori_loop(0, ROWS // 32, body, 0)

    def lay_out(lin, w, k, h, extra):
        for q in (2 * h, 2 * h + 1):
            if w == 2:
                base, stride = 4608 + 576 * q, 6
            elif w == 1:
                base, stride = 2304 + 6 * q, 24
            else:
                base, stride = (1728, 6) if q == 3 else (6 * q, 18)

            def body(i, _):
                at = pl.ds(pl.multiple_of(i * 32, 32), 32)
                total = total_of(w, k, q, at, extra)
                for m in range(6):
                    lin[pl.ds(base + m + i * (32 * stride), 32, stride=stride), :] = total[:, 128 * m : 128 * m + 128]
                return 0
            lax.fori_loop(0, ROWS // 32, body, 0)

    def z_copy(w, d, k, h):
        step = 1 if d == 0 else -1
        at = pl.ds(2 * h, 2)
        return remote(
            own_at(w, k).at[at],
            zbuf.at[w, slot(d, k, z + step), at],
            zs.at[w, d, k, h],
            zr.at[w, d, k, h],
            (g, t + 2 * step),
        )

    def z_wait(w, d, k, h):
        here = zbuf.at[w, slot(d, k, z), pl.ds(2 * h, 2)]
        remote(here, here, zs.at[w, d, k, h], zr.at[w, d, k, h], (g, other)).wait_recv()

    def ready(w, k):
        core_copy(w, k).wait_recv()

    def pass_on(i, d, j, h):
        w = ORDER[i]
        reach = NZ - 1 - z if d == 0 else z
        k = z + j if d == 0 else z - j
        first = z == 0 if d == 0 else z == NZ - 1

        @pl.when(j <= reach)
        def _():
            if h == 0:
                ready(w, k)

            @pl.when(first)
            def _():
                add_rows(w, k, h, ())

            @pl.when(jnp.logical_not(first))
            def _():
                z_wait(w, d, k, h)
                add_rows(w, k, h, (d,))

            if i > 0:
                @pl.when(j == reach)
                def _():
                    z_copy(ORDER[i - 1], d, z + 1 if d == 0 else z - 1, h).wait_send()
            if j < NZ - 1:
                @pl.when(j < reach)
                def _():
                    z_copy(w, d, k + 1 if d == 0 else k - 1, h).wait_send()
            z_copy(w, d, k, h).start()

    def settle(lin, i):
        w = ORDER[i]
        ready(w, z)
        for h in (0, 1):
            for cond, dirs in ((z == 0, (1,)), (z == NZ - 1, (0,)), ((z > 0) & (z < NZ - 1), (0, 1))):
                @pl.when(cond)
                def _():
                    for d in dirs:
                        z_wait(w, d, z, h)
                    lay_out(lin, w, z, h, dirs)

    steps = [(i, j, h) for i in range(3) for j in (3, 2, 1) for h in (0, 1)]

    def run(lo, hi):
        for i, j, h in steps[lo:hi]:
            pass_on(i, 0, j, h)
            pass_on(i, 1, j, h)

    find_places(lens, line, column)
    vg[...] = vg_in[...]
    vg1[...] = jnp.zeros_like(vg1)

    def mlp_part(wp, wb, wc, grads, n2, att, gb1):
        inner = local([(att_in, att), (wa.at[3], wp), (wc_in, wc), (wb_in, wb), (n2_in, n2)], 2)

        def hidden_load(q):
            low = pl.ds(q * D, D)
            return pltpu.make_async_copy(hid_in.at[:, low], grads.at[:, low], hs.at[q])

        def slope_load(i):
            at = pl.ds(i * TILE, TILE)
            return pltpu.make_async_copy(slope_in.at[at, :], grads.at[at, :], hs.at[4 + i])

        for q in FIRST:
            hidden_load(q).start()
        for copy in inner:
            copy.start()

        def row(j):
            return vec[j : j + 1, :]

        for copy in loads:
            copy.wait()
        for i in range(rows // TILE):
            at = pl.ds(i * TILE, TILE)
            tall[at, :] = tall[at, :] * valid_rows(lens, i * TILE, TILE)
            gb1[at, :] = (row(13) * tall[at, :]).astype(BF16)
        for q in FIRST:
            hidden_load(q).wait()

            for t_at, dst in ((2 * q + 1 - c, gout.at[2 * q + 1 - c]), (2 * q + c, own.at[q])):
                low = pl.ds(pl.multiple_of(t_at * 384, 128), 384)
                dst[...] = tn(grads[:, low], gb1[...]).astype(BF16).reshape(4, ROWS, D)
            core_copy(2, q).start()
        for i in range(rows // TILE):
            slope_load(i).start()
        run(0, 2)
        for copy in inner:
            copy.wait()

        def tile(i):
            at = pl.ds(i * TILE, TILE)
            slope_load(i).wait()
            branch_one = nn(att[at, :], wp[...]) + row(4)
            normal, inverse = normalize(wide[at, :] + row(5) * branch_one)
            low_back = gb1[at, :]

            def backward(q, total):
                low = pl.ds(pl.multiple_of(q * D, D), D)
                grad = nt(low_back, wc[low, :]) * grads[at, low].astype(F32)
                grad = grad.astype(BF16)
                grads[at, low] = grad
                vg1[0:1, low] += col_sum(grad.astype(F32))
                return total + nt(grad, wb[q])
            grad_n2 = lax.fori_loop(0, 4, backward, jnp.zeros((TILE, D), F32))
            vg[6:7, :] += col_sum(grad_n2 * normal)
            vg[7:8, :] += col_sum(grad_n2)
            grad_mid = tall[at, :] + norm_pull(grad_n2, normal, inverse, row(6))
            tall[at, :] = grad_mid
            vg[5:6, :] += col_sum(grad_mid * branch_one)
            low_one = (row(5) * grad_mid).astype(BF16)
            gb1[at, :] = low_one
            vg[4:5, :] += col_sum(low_one.astype(F32))
            gatt[at, :] = nt(low_one, wp[...]).astype(BF16)

        for i in range(rows // TILE):
            tile(i)
            run(2 + 2 * i, 4 + 2 * i)

        def fc1(q, _):
            def part(m, _):
                low = pl.ds(pl.multiple_of(q * D + m * 384, 128), 384)
                col = pl.ds(pl.multiple_of(m * 384, 128), 384)
                gb[:, q, :, col] = tn(n2[...], grads[:, low]).astype(BF16).reshape(8, ROWS, 384)
                return 0
            return lax.fori_loop(0, 2, part, 0)
        lax.fori_loop(0, 4, fc1, 0)
        begin(1)

        for q in FIRST:
            core_copy(2, q).wait_send()

        def proj_part(m, _):
            col = pl.ds(pl.multiple_of(m * 384, 128), 384)
            gout[:, 3, :, col] = tn(att[...], gb1[:, col]).astype(BF16).reshape(8, ROWS, 384)
            return 0
        lax.fori_loop(0, 2, proj_part, 0)

    pl.run_scoped(
        mlp_part,
        pltpu.VMEM((D, D), BF16),
        pltpu.VMEM((4, D, D), BF16),
        pltpu.VMEM((MLP, D), BF16),
        pltpu.VMEM((rows, MLP), BF16),
        pltpu.VMEM((rows, D), BF16),
        pltpu.VMEM((rows, D), BF16),
        pltpu.VMEM((rows, D), BF16),
    )
    v_copies = [remote(gv.at[peers[k]], vbuf.at[k], vs.at[k], vr.at[k], (g, peers[k])) for k in range(7)]
    q_copies = [remote(qbuf.at[7], qbuf.at[k], qs.at[k], qr.at[k], (g, peers[k])) for k in range(7)]

    def attention_part(lin, bias, lse_t, gatt_at, dq, wa_v, normed, proj):
        inner = local([(proj_in, proj), (lse_in, lse_t), (wa.at[pl.ds(0, 3)], wa_v), (normed_in, normed)], 8)
        for copy in inner:
            copy.start()
        run(6, 7)
        fill_bias(bias)
        move_rows(lambda first, count: to_places(line, first, count), gatt, gatt_at)
        for copy in inner:
            copy.wait()
        for p in range(6):
            attend_back(p, proj, gatt_at, bias, lse_t, dq)
            if p == 0:
                settle(lin, 0)
            if p < 5:
                run(7 + p, 8 + p)
        weight_grads(normed, proj, gout)
        begin(0)
        run(12, 14)
        row_grads(column, wide, tall, vec, wa_v, proj, vg)
        store = pltpu.make_async_copy(tall, gin, ls.at[12])
        store.start()
        for k in range(8):
            gv[k, :, :ROWS] = vg[:, ROWS * k : ROWS * k + ROWS]
            for j in range(4):
                lead = 4 * ROWS * k + ROWS * j
                gv[k, 8 + j : 9 + j, :ROWS] = vg1[0:1, lead : lead + ROWS]
        for copy in v_copies:
            copy.start()
        run(14, 15)
        settle(lin, 1)
        run(15, 18)
        for k in range(7):
            v_copies[k].wait_recv()
        total = gv[t]
        for k in range(7):
            total = total + vbuf[k]
        lane = lax.broadcasted_iota(jnp.int32, (16, 128), 1)
        across = lax.broadcasted_iota(jnp.int32, (16, 128), 0)
        total = jnp.where((lane < ROWS) & (across < 14), total, 0.0)
        sv[...] = total

        def square(i, acc):
            v = lin[pl.ds(pl.multiple_of(i * 64, 64), 64), :]
            return acc + v * v
        acc = lax.fori_loop(36, 108, square, jnp.zeros((64, 128), F32))
        settle(lin, 2)
        lin_store = pltpu.make_async_copy(lin, lin_out, ls.at[13])
        lin_store.start()

        acc = lax.fori_loop(0, 36, square, acc)
        qbuf[7] = jnp.full((8, 128), jnp.sum(acc) + jnp.sum(total * total), F32)
        for copy in q_copies:
            copy.start()
        store.wait()
        lin_store.wait()

    pl.run_scoped(
        attention_part,
        pltpu.VMEM((6912, 128), F32),
        pltpu.VMEM((4, 288, 384), F32),
        pltpu.VMEM((16, rows), F32),
        pltpu.VMEM((rows, D), BF16),
        pltpu.VMEM((rows, 128), F32),
        pltpu.VMEM((3, D, D), BF16),
        pltpu.VMEM((rows, D), BF16),
        pltpu.VMEM((3, rows, D), BF16),
    )
    for w in range(2):
        for k in range(NZ):
            core_copy(w, k).wait_send()
    for h in (0, 1):
        @pl.when(z < NZ - 1)
        def _():
            z_copy(0, 0, z + 1, h).wait_send()

        @pl.when(z > 0)
        def _():
            z_copy(0, 1, z - 1, h).wait_send()
    for k in range(7):
        q_copies[k].wait_recv()
    acc = qbuf[7]
    for k in range(7):
        acc = acc + qbuf[k]
    sq[...] = acc
    for k in range(7):
        q_copies[k].wait_send()
        v_copies[k].wait_send()


def back(lens, vec, vg, tok, cot, wa, wb, wc, att, slope, hid, n2, normed, proj, lse_t):
    vm = pl.BlockSpec(memory_space=pltpu.VMEM)
    rows = tok.shape[0]
    S = jax.ShapeDtypeStruct
    V = pltpu.VMEM
    return pl.pallas_call(
        back_kernel,
        name="back",
        out_shape=[S((rows, D), F32), S((6912, 128), F32), S((16, 128), F32), S((8, 128), F32)],
        in_specs=[pl.BlockSpec(memory_space=pltpu.SMEM)] + [vm] * 2 + [ANY] * 12,
        out_specs=[ANY] * 2 + [vm] * 2,
        scratch_shapes=[
            V((8, rows), jnp.int32),
            V((rows, 128), jnp.int32),
            V((rows, D), F32),
            V((rows, D), F32),
            V((rows, D), BF16),
            V((8, 4, ROWS, D), BF16),
            V((8, 4, ROWS, D), BF16),
            V((NZ, 4, ROWS, D), BF16),
            V((3, NZ, 4, ROWS, D), BF16),
            V((3, 5, 4, ROWS, D), BF16),
            V((16, D), F32),
            V((8, MLP), F32),
            V((8, 16, 128), F32),
            V((7, 16, 128), F32),
            V((8, 8, 128), F32),
            DMA((14,)), DMA((8,)), DMA((3, NZ)), DMA((3, NZ)),
            DMA((3, 2, NZ, 2)), DMA((3, 2, NZ, 2)),
            DMA((7,)), DMA((7,)), DMA((7,)), DMA((7,)),
        ],
        compiler_params=pltpu.CompilerParams(
            collective_id=1, has_side_effects=True, vmem_limit_bytes=63 * 2**20
        ),
    )(lens, vec, vg, tok, cot, wa, wb, wc, att, slope, hid, n2, normed, proj, lse_t)


PARTS = 6912
SUM_H, SUM_Q, SUM_E = PARTS // 2, PARTS // 4, PARTS // 8
MATRIX_WIDTH = PARTS * 128
VECTOR_WIDTH = 14 * ROWS
BLOCKS = 4
BLOCK = MATRIX_WIDTH // BLOCKS
CHUNK = 6144


def adam_kernel(grad, sv, sq, master, first, second, first_new, second_new, diff, tail, vector_out, norm_out, tail_grad):
    i = pl.program_id(0)
    norm = jnp.sqrt(sq[0:1, 0:1])
    scale = clip_limit / (norm + 1e-06)
    step_rate = base_rate * rate_scale

    def adam(value, old_first, old_second, weight):
        clipped = value * scale
        new_first = beta_first * old_first + (1.0 - beta_first) * clipped
        new_second = beta_second * old_second + (1.0 - beta_second) * clipped * clipped
        root = jnp.sqrt(new_second * (1.0 / (1.0 - beta_second**adam_count))) + adam_epsilon
        ahead = new_first * (1.0 / (1.0 - beta_first**adam_count)) / root
        if weight is not None:
            ahead = ahead + weight_decay * weight
        return new_first, new_second, step_rate * ahead

    @pl.when(i < BLOCKS)
    def _():
        def body(n, _):
            flat = pl.ds(pl.multiple_of(n * CHUNK, CHUNK), CHUNK)
            at = pl.ds(pl.multiple_of(n * (CHUNK // 128), CHUNK // 128), CHUNK // 128)
            first_new[:, flat], second_new[:, flat], ahead = adam(
                grad[at, :].reshape(1, CHUNK), first[:, flat], second[:, flat], master[flat].reshape(1, CHUNK)
            )
            diff[at, :] = ahead.reshape(CHUNK // 128, 128).astype(BF16)
            return 0
        lax.fori_loop(0, BLOCK // CHUNK, body, 0, unroll=12)

    @pl.when(i == BLOCKS)
    def _():
        norm_out[...] = norm
        for j in range(14):
            tail_grad[0:1, ROWS * j : ROWS * j + ROWS] = sv[j : j + 1, :ROWS]
        vector_out[...] = tail_grad[...] / jnp.sqrt(F32(8 * 1024))
        at = pl.ds(0, VECTOR_WIDTH)
        first_new[:, at], second_new[:, at], ahead = adam(tail_grad[...], first[:, at], second[:, at], None)
        tail[...] = jnp.zeros_like(tail)
        tail[:, at] = ahead


def adam_step(grad, sv, sq, master, first, second):
    S = jax.ShapeDtypeStruct
    n = master.shape[0]

    def whole(shape):
        return pl.BlockSpec(shape, lambda i: (0, 0))

    line = pl.BlockSpec((1, BLOCK), lambda i: (0, i))
    rows = pl.BlockSpec((PARTS // BLOCKS, 128), lambda i: (jnp.minimum(i, BLOCKS - 1), 0))
    return pl.pallas_call(
        adam_kernel,
        name="adam",
        grid=(BLOCKS + 1,),
        out_shape=[
            S((1, n), F32), S((1, n), F32), S((PARTS, 128), BF16), S((1, 1408), F32), S((1, VECTOR_WIDTH), F32), S((1, 1), F32)
        ],
        in_specs=[rows, whole((16, 128)), whole((8, 128)), pl.BlockSpec((BLOCK,), lambda i: (i,)), line, line],
        out_specs=[line, line, rows, whole((1, 1408)), whole((1, VECTOR_WIDTH)), whole((1, 1))],
        scratch_shapes=[pltpu.VMEM((1, VECTOR_WIDTH), F32)],
    )(grad, sv, sq, master, first, second)


def outer_kernel(mean, tail, master, momentum, mean_out, momentum_out, weights_out):
    i = pl.program_id(0)

    def step(flat, average):
        new_momentum = outer_beta * momentum[flat] + average
        mean_out[flat] = average
        momentum_out[flat] = new_momentum
        weights_out[flat] = master[flat] - outer_rate * (average + outer_beta * new_momentum)

    @pl.when(i < BLOCKS)
    def _():
        def body(n, _):
            flat = pl.ds(pl.multiple_of(n * CHUNK, CHUNK), CHUNK)
            at = pl.ds(pl.multiple_of(n * (CHUNK // 128), CHUNK // 128), CHUNK // 128)
            step(flat, mean[at, :].astype(F32).reshape(CHUNK))
            return 0
        lax.fori_loop(0, BLOCK // CHUNK, body, 0, unroll=12)

    @pl.when(i == BLOCKS)
    def _():
        step(pl.ds(0, 1408), tail[0, :])


def outer_step(mean, tail, master, momentum):
    n = master.shape[0]
    line = pl.BlockSpec((BLOCK,), lambda i: (i,))
    return pl.pallas_call(
        outer_kernel,
        name="outer",
        grid=(BLOCKS + 1,),
        out_shape=[jax.ShapeDtypeStruct((n,), F32)] * 3,
        in_specs=[
            pl.BlockSpec((PARTS // BLOCKS, 128), lambda i: (jnp.minimum(i, BLOCKS - 1), 0)),
            pl.BlockSpec((1, 1408), lambda i: (0, 0)), line, line,
        ],
        out_specs=[line] * 3,
    )(mean, tail, master, momentum)


def mean_kernel(diff, tail, mean, tail_mean, part, mid, buf, tails, ss, rs, ts, tr):
    g, t, z, c, gx, gy = place()
    peers = [gx, gy, 3 - g]
    greet([(peer, t) for peer in peers], 3)
    xi, yi = lax.rem(g, 2), lax.div(g, 2)
    hop = [((gx, t), (gy, t)), ((gy, t), (gx, t))]
    mine = [(xi, yi), (yi, xi)]

    def at(h, i, j):
        return h * SUM_H + i * SUM_Q + j * SUM_E

    def to_sum(h, e):
        a, b = mine[h]
        j = 1 - b if e == 0 else b
        src = rows_at(diff, at(h, 1 - a, j), SUM_E)
        return remote(src, part.at[h, e], ss.at[h, e], rs.at[h, e], hop[h][0])

    def over(h):
        return remote(mid.at[h], buf.at[h], ss.at[h, 2], rs.at[h, 2], hop[h][1])

    def share(h, e):
        a, b = mine[h]
        block = rows_at(mean, at(h, a, 1 - b if e == 2 else b), SUM_E)
        return remote(block, block, ss.at[h, 3 + e], rs.at[h, 3 + e], hop[h][1 if e == 0 else 0])

    def landed(h, e):
        a, b = mine[h]
        block = rows_at(mean, at(h, a, 1 - b) if e == 0 else at(h, 1 - a, 1 - b if e == 2 else b), SUM_E)
        remote(block, block, ss.at[h, 3 + e], rs.at[h, 3 + e], hop[h][0]).wait_recv()

    def add(fn):
        def body(i, _):
            fn(pl.multiple_of(i * 96, 96))
            return 0
        lax.fori_loop(0, SUM_E // 96, body, 0)

    for e in (0, 1):
        for h in (0, 1):
            to_sum(h, e).start()
    t_copies = [remote(tail, tails.at[k], ts.at[k], tr.at[k], (peers[k], t)) for k in range(3)]
    for copy in t_copies:
        copy.start()
    for h in (0, 1):
        a, b = mine[h]
        to_sum(h, 0).wait_recv()

        def first(i):
            total = diff[pl.ds(pl.multiple_of(at(h, a, 1 - b) + i, 32), 96), :].astype(F32)
            mid[h, pl.ds(i, 96), :] = (total + part[h, 0, pl.ds(i, 96), :].astype(F32)).astype(BF16)
        add(first)
        over(h).start()
    for h in (0, 1):
        a, b = mine[h]
        to_sum(h, 1).wait_recv()
        over(h).wait_recv()

        def second(i):
            here = pl.ds(pl.multiple_of(at(h, a, b) + i, 32), 96)
            local = pl.ds(i, 96)
            total = diff[here, :].astype(F32) + part[h, 1, local, :].astype(F32) + buf[h, local, :].astype(F32)
            mean[here, :] = (total * 0.25).astype(BF16)
        add(second)
        share(h, 0).start()
        share(h, 1).start()
    for copy in t_copies:
        copy.wait_recv()
    tail_mean[...] = (tail[...] + tails[0] + tails[1] + tails[2]) * 0.25
    for h in (0, 1):
        landed(h, 0)
        share(h, 2).start()
    for h in (0, 1):
        landed(h, 1)
        landed(h, 2)
        for e in (0, 1):
            to_sum(h, e).wait_send()
        over(h).wait_send()
        for e in range(3):
            share(h, e).wait_send()
    for copy in t_copies:
        copy.wait_send()


def mean_groups(diff, tail):
    vm = pl.BlockSpec(memory_space=pltpu.VMEM)
    S = jax.ShapeDtypeStruct
    V = pltpu.VMEM
    return pl.pallas_call(
        mean_kernel,
        name="mean_groups",
        out_shape=[S((PARTS, 128), BF16), S((1, 1408), F32)],
        in_specs=[vm] * 2,
        out_specs=[vm] * 2,
        scratch_shapes=[
            V((2, 2, SUM_E, 128), BF16), V((2, SUM_E, 128), BF16), V((2, SUM_E, 128), BF16), V((3, 1, 1408), F32),
            DMA((2, 6)), DMA((2, 6)), DMA((3,)), DMA((3,)),
        ],
        compiler_params=pltpu.CompilerParams(collective_id=2, has_side_effects=True),
    )(diff, tail)


def on_small_slice(tokens, cotangent, crop_lengths, master, first_moment, second_moment, outer_momentum):
    wa, wb, wc, vec, fb1, normed, projected, attended, lse = front(crop_lengths, master, tokens)
    block_output, slope, normed_two, hidden, vg = forward(
        crop_lengths, tokens, cotangent, attended, wa, wb, wc.reshape(MLP, D), vec, fb1
    )
    input_grad, grad_lin, sv, sq = back(
        crop_lengths, vec, vg, tokens, cotangent, wa, wb, wc.reshape(MLP, D), attended, slope, hidden, normed_two,
        normed, projected, lse
    )
    moment_one, moment_two, difference, tail, vector_part, norm = adam_step(
        grad_lin, sv, sq, master, first_moment, second_moment
    )
    mean, tail_mean = mean_groups(difference, tail)
    mean_difference, outer_new, new_weights = outer_step(mean, tail_mean, master, outer_momentum)
    return (
        block_output,
        input_grad,
        norm.reshape(1),
        vector_part,
        moment_one,
        moment_two,
        mean_difference,
        outer_new,
        new_weights,
    )


def solution(mesh):
    small = mesh.shape["grp"] == 4 and mesh.shape["tok"] == 8
    return jax.shard_map(
        on_small_slice if small else on_device,
        mesh=mesh,
        in_specs=(
            P(("grp", "tok"), None),
            P(("grp", "tok"), None),
            P(("grp", "tok"), None),
            P("tok"),
            P("grp", "tok"),
            P("grp", "tok"),
            P("tok"),
        ),
        out_specs=(
            P(("grp", "tok"), None),
            P(("grp", "tok"), None),
            P("grp"),
            P("grp", "tok"),
            P("grp", "tok"),
            P("grp", "tok"),
            P("tok"),
            P("tok"),
            P("tok"),
        ),
        check_vma=False,
    )
```

```python
import jax
import jax.numpy as jnp
from jax import lax
from jax.experimental import pallas as pl
from jax.experimental.pallas import tpu as pltpu
from jax.sharding import PartitionSpec as P

D = 768
MLP = 3072
HEADS = 12
HEAD_DIM = 64
ROWS = D // 8
ANY = pl.BlockSpec(memory_space=pl.ANY)
DMA = pltpu.SemaphoreType.DMA
MESH_ID = pl.DeviceIdType.MESH
NZ = 4
F32, BF16 = jnp.float32, jnp.bfloat16


def place():
    g = lax.axis_index("grp")
    t = lax.axis_index("tok")
    z, c = lax.div(t, 2), lax.rem(t, 2)
    gx = g + 1 - 2 * lax.rem(g, 2)
    gy = g + 2 - 4 * lax.div(g, 2)
    return g, t, z, c, gx, gy


def greet(targets, count):
    barrier = pltpu.get_barrier_semaphore()
    for target in targets:
        pl.semaphore_signal(barrier, inc=1, device_id=target, device_id_type=MESH_ID)
    pl.semaphore_wait(barrier, count)


def remote(src, dst, send, recv, target):
    return pltpu.make_async_remote_copy(
        src_ref=src, dst_ref=dst, send_sem=send, recv_sem=recv,
        device_id=target, device_id_type=MESH_ID,
    )


clip_limit = 3.0
beta_first = 0.9
beta_second = 0.999
adam_epsilon = 1e-08
weight_decay = 0.04
adam_count = 10.0
base_rate = 0.075
rate_scale = 0.9**6
outer_rate = 0.7
outer_beta = 0.9
norm_epsilon = 1e-06


def member_extents():
    return [(D, 3 * D), (D, D), (D, MLP), (MLP, D)] + [(D,)] * 8 + [(MLP,), (D,), (D,)]


def member_sizes():
    sizes_list = []
    for extent in member_extents():
        length = 1
        for member in extent:
            length = length * member
        sizes_list.append(length)
    return sizes_list


def split_params(flat_params, owners):
    table = flat_params.reshape(owners, -1)
    members = []
    offset = 0
    for extent, length in zip(member_extents(), member_sizes()):
        width = length // owners
        members.append(table[:, offset : offset + width].reshape(extent))
        offset = offset + width
    return members


def join_table(members, owners):
    return jnp.concatenate([member.reshape(owners, -1) for member in members], axis=1)


def layer_norm(values, norm_gain, norm_shift):
    center = values - jnp.mean(values, axis=-1, keepdims=True)
    spread = jnp.mean(center * center, axis=-1, keepdims=True)
    return center * lax.rsqrt(spread + norm_epsilon) * norm_gain + norm_shift


def pack_layout(lengths_row, row_count):
    ends_at = jnp.cumsum(lengths_row)
    position = jnp.arange(row_count, dtype=jnp.int32)
    segment = jnp.sum((position[:, None] >= ends_at[None, :]).astype(jnp.int32), axis=1)
    validity = (position < ends_at[-1]).astype(jnp.float32)
    return (segment, validity)


def cross_rows(left_side, right_side):
    return lax.dot_general(
        left_side, right_side, (((0,), (0,)), ((), ())), preferred_element_type=jnp.float32
    )


def times_transposed(left_side, right_side):
    return lax.dot_general(
        left_side, right_side, (((1,), (1,)), ((), ())), preferred_element_type=jnp.float32
    )


def on_device(tokens, cotangent, crop_lengths, master, first_moment, second_moment, outer_momentum):
    row_count = tokens.shape[0]
    pair_count = HEADS // 2
    score_scale = HEAD_DIM ** (-0.5)
    owners = lax.axis_size("tok")
    segment, validity = pack_layout(crop_lengths[0], row_count)
    allowed = segment[:, None] == segment[None, :]
    master_low = master.astype(jnp.bfloat16)
    gathered = split_params(lax.all_gather(master_low, "tok", axis=0, tiled=True), owners)
    w_qkv, w_proj, w_fc1, w_fc2 = gathered[:4]
    (
        gain_one,
        shift_one,
        query_bias,
        value_bias,
        proj_bias,
        scale_one,
        gain_two,
        shift_two,
        fc1_bias,
        fc2_bias,
        scale_two,
    ) = [member.astype(jnp.float32) for member in gathered[4:]]

    def to_pairs(block_cols):
        return jnp.moveaxis(block_cols.reshape(row_count, pair_count, 2 * HEAD_DIM), 1, 0)

    def from_pairs(paired):
        return jnp.moveaxis(paired, 0, 1).reshape(row_count, D)

    normed = layer_norm(tokens, gain_one, shift_one).astype(jnp.bfloat16)
    qkv_bias = jnp.concatenate([query_bias, jnp.zeros_like(query_bias), value_bias])
    projected = (jnp.dot(normed, w_qkv, preferred_element_type=jnp.float32) + qkv_bias).astype(
        jnp.bfloat16
    )
    query_pairs = to_pairs(projected[:, :D])
    key_pairs = to_pairs(projected[:, D : 2 * D])
    value_pairs = to_pairs(projected[:, 2 * D :])

    def forward_pair(pair_item):
        queries, keys_pair, values_pair = [
            member.reshape(row_count, 2, HEAD_DIM) for member in pair_item
        ]
        raw_scores = jnp.einsum(
            "qhd,khd->hqk", queries, keys_pair, preferred_element_type=jnp.float32
        )
        scores = jnp.where(allowed[None], raw_scores * score_scale, -1e30)
        largest = jnp.max(scores, axis=-1, keepdims=True)
        weights_exp = jnp.exp(scores - largest)
        totals = jnp.sum(weights_exp, axis=-1, keepdims=True)
        weights_low = (weights_exp / totals).astype(jnp.bfloat16)
        attended_pair = jnp.einsum(
            "hqk,khd->qhd", weights_low, values_pair, preferred_element_type=jnp.float32
        )
        return (attended_pair.reshape(row_count, 2 * HEAD_DIM), (largest + jnp.log(totals))[..., 0])

    attended_pairs, log_totals = lax.map(forward_pair, (query_pairs, key_pairs, value_pairs))
    attended = from_pairs(attended_pairs).astype(jnp.bfloat16)
    branch_one = jnp.dot(attended, w_proj, preferred_element_type=jnp.float32) + proj_bias
    middle = tokens + scale_one * branch_one
    normed_two = layer_norm(middle, gain_two, shift_two).astype(jnp.bfloat16)
    hidden_pre = jnp.dot(normed_two, w_fc1, preferred_element_type=jnp.float32) + fc1_bias
    hidden = jax.nn.gelu(hidden_pre, approximate=False).astype(jnp.bfloat16)
    branch_two = jnp.dot(hidden, w_fc2, preferred_element_type=jnp.float32) + fc2_bias
    block_output = middle + scale_two * branch_two
    back_out = cotangent * validity[:, None]
    grad_branch_two = (scale_two * back_out).astype(jnp.bfloat16)
    grad_scale_two = jnp.sum(back_out * branch_two, axis=0)
    grad_fc2_bias = jnp.sum(grad_branch_two.astype(jnp.float32), axis=0)
    grad_w_fc2 = cross_rows(hidden, grad_branch_two)
    grad_hidden = times_transposed(grad_branch_two, w_fc2)
    gelu_pull = jax.vjp(lambda values: jax.nn.gelu(values, approximate=False), hidden_pre)[1]
    grad_pre = gelu_pull(grad_hidden)[0].astype(jnp.bfloat16)
    grad_fc1_bias = jnp.sum(grad_pre.astype(jnp.float32), axis=0)
    grad_w_fc1 = cross_rows(normed_two, grad_pre)
    grad_normed_two = times_transposed(grad_pre, w_fc1)
    norm_pull = jax.vjp(layer_norm, middle, gain_two, shift_two)[1]
    grad_middle_part, grad_gain_two, grad_shift_two = norm_pull(grad_normed_two)
    grad_middle = back_out + grad_middle_part
    grad_scale_one = jnp.sum(grad_middle * branch_one, axis=0)
    grad_branch_one = (scale_one * grad_middle).astype(jnp.bfloat16)
    grad_proj_bias = jnp.sum(grad_branch_one.astype(jnp.float32), axis=0)
    grad_w_proj = cross_rows(attended, grad_branch_one)
    grad_attended = times_transposed(grad_branch_one, w_proj).astype(jnp.bfloat16)

    def backward_pair(pair_item):
        queries, keys_pair, values_pair, grad_pair = [
            member.reshape(row_count, 2, HEAD_DIM) for member in pair_item[:4]
        ]
        log_total = pair_item[4]
        raw_scores = jnp.einsum(
            "qhd,khd->hqk", queries, keys_pair, preferred_element_type=jnp.float32
        )
        scores = jnp.where(allowed[None], raw_scores * score_scale, -1e30)
        weights_soft = jnp.exp(scores - log_total[..., None])
        grad_values = jnp.einsum(
            "hqk,qhd->khd",
            weights_soft.astype(jnp.bfloat16),
            grad_pair,
            preferred_element_type=jnp.float32,
        )
        grad_weights = jnp.einsum(
            "qhd,khd->hqk", grad_pair, values_pair, preferred_element_type=jnp.float32
        )
        row_dot = jnp.sum(weights_soft * grad_weights, axis=-1, keepdims=True)
        grad_scores = (weights_soft * (grad_weights - row_dot)).astype(jnp.bfloat16)
        grad_queries = (
            jnp.einsum("hqk,khd->qhd", grad_scores, keys_pair, preferred_element_type=jnp.float32)
            * score_scale
        )
        grad_keys = (
            jnp.einsum("hqk,qhd->khd", grad_scores, queries, preferred_element_type=jnp.float32)
            * score_scale
        )
        return (
            grad_queries.reshape(row_count, 2 * HEAD_DIM),
            grad_keys.reshape(row_count, 2 * HEAD_DIM),
            grad_values.reshape(row_count, 2 * HEAD_DIM),
        )

    grad_q_pairs, grad_k_pairs, grad_v_pairs = lax.map(
        backward_pair, (query_pairs, key_pairs, value_pairs, to_pairs(grad_attended), log_totals)
    )
    grad_projected = jnp.concatenate(
        [from_pairs(grad_q_pairs), from_pairs(grad_k_pairs), from_pairs(grad_v_pairs)], axis=1
    ).astype(jnp.bfloat16)
    grad_query_bias = jnp.sum(grad_projected[:, :D].astype(jnp.float32), axis=0)
    grad_value_bias = jnp.sum(grad_projected[:, 2 * D :].astype(jnp.float32), axis=0)
    grad_w_qkv = cross_rows(normed, grad_projected)
    grad_normed = times_transposed(grad_projected, w_qkv)
    first_pull = jax.vjp(layer_norm, tokens, gain_one, shift_one)[1]
    grad_tokens_part, grad_gain_one, grad_shift_one = first_pull(grad_normed)
    input_grad = grad_middle + grad_tokens_part
    all_members = [
        grad_w_qkv,
        grad_w_proj,
        grad_w_fc1,
        grad_w_fc2,
        grad_gain_one,
        grad_shift_one,
        grad_query_bias,
        grad_value_bias,
        grad_proj_bias,
        grad_scale_one,
        grad_gain_two,
        grad_shift_two,
        grad_fc1_bias,
        grad_fc2_bias,
        grad_scale_two,
    ]
    received = lax.all_to_all(
        join_table(all_members, owners).astype(jnp.bfloat16),
        "tok",
        split_axis=0,
        concat_axis=0,
        tiled=True,
    ).astype(jnp.float32)
    summed = jnp.sum(received, axis=0)
    matrix_width = (4 * D * D + 2 * D * MLP) // owners
    vector_part = summed[matrix_width:] / (owners * row_count) ** 0.5
    square_total = lax.psum(jnp.sum(summed * summed), "tok")
    norm_value = jnp.sqrt(square_total)
    clipped = summed * (clip_limit / (norm_value + 1e-06))
    moment_one = beta_first * first_moment[0] + (1.0 - beta_first) * clipped
    moment_two = beta_second * second_moment[0] + (1.0 - beta_second) * clipped * clipped
    corrected_one = moment_one / (1.0 - beta_first**adam_count)
    corrected_two = moment_two / (1.0 - beta_second**adam_count)
    shard_size = master.shape[0]
    local_index = jnp.arange(shard_size, dtype=jnp.int32)
    decay_mask = (local_index < matrix_width).astype(jnp.float32)
    step_rate = base_rate * rate_scale
    updated = master - step_rate * (
        corrected_one / (jnp.sqrt(corrected_two) + adam_epsilon)
        + weight_decay * decay_mask * master
    )
    mean_difference = lax.psum((master - updated).astype(jnp.bfloat16), "grp").astype(
        jnp.float32
    ) / lax.axis_size("grp")
    outer_new = outer_beta * outer_momentum + mean_difference
    new_weights = master - outer_rate * (mean_difference + outer_beta * outer_new)
    return (
        block_output,
        input_grad,
        norm_value.reshape(1),
        vector_part[None],
        moment_one[None],
        moment_two[None],
        mean_difference,
        outer_new,
        new_weights,
    )


def rows_at(ref, start, count):
    return ref.at[pl.ds(pl.multiple_of(start, 16), count), :]


TILE = 512


def nn(a, b):
    return lax.dot_general(a, b, (((1,), (0,)), ((), ())), preferred_element_type=F32)


def nt(a, b):
    return lax.dot_general(a, b, (((1,), (1,)), ((), ())), preferred_element_type=F32)


def tn(a, b):
    return lax.dot_general(a, b, (((0,), (0,)), ((), ())), preferred_element_type=F32)


def normalize(values):
    center = values - jnp.mean(values, axis=-1, keepdims=True)
    spread = jnp.mean(center * center, axis=-1, keepdims=True)
    inverse = lax.rsqrt(spread + norm_epsilon)
    return center * inverse, inverse


def norm_pull(grad, normal, inverse, gain):
    scaled = grad * gain
    return inverse * (
        scaled
        - jnp.mean(scaled, axis=-1, keepdims=True)
        - normal * jnp.mean(scaled * normal, axis=-1, keepdims=True)
    )


def gelu_and_slope(x):
    phi = 0.5 * (1.0 + lax.erf(x * 0.7071067811865476))
    return x * phi, phi + x * jnp.exp(-0.5 * x * x) * 0.3989422804014327


def col_sum(x):
    return jnp.sum(x, axis=0, keepdims=True)


QT = 256
LONG, SHORT = 261, 54
TILES = (
    (0, 272, 0, 384, 0, 261),
    (256, 272, 256, 384, 261, 522),
    (512, 288, 512, 384, 522, 792),
    (784, 240, 768, 256, 792, 1024),
)


def find_places(lens, line, column):
    crops = lens.shape[1]
    longs, shorts, begin = jnp.int32(0), jnp.int32(0), jnp.int32(0)
    at_line = lax.broadcasted_iota(jnp.int32, line.shape, 1)
    at_column = lax.broadcasted_iota(jnp.int32, column.shape, 0)
    new_line, new_column = at_line, at_column
    for j in range(crops):
        size = lens[0, j]
        is_long = (size == LONG).astype(jnp.int32)
        place_at = is_long * (longs * LONG) + (1 - is_long) * (2 * LONG + shorts * SHORT)
        shift = place_at - begin
        new_line = jnp.where((at_line >= begin) & (at_line < begin + size), at_line + shift, new_line)
        new_column = jnp.where((at_column >= begin) & (at_column < begin + size), at_column + shift, new_column)
        longs, shorts, begin = longs + is_long, shorts + 1 - is_long, begin + size
    line[...] = new_line
    column[...] = new_column


def to_places(line, first, count):
    rows = lax.broadcasted_iota(jnp.int32, (count, line.shape[1]), 0) + first
    return (rows == line[0:1, :]).astype(F32).astype(BF16)


def from_places(column, first, count):
    lanes = lax.broadcasted_iota(jnp.int32, (count, column.shape[0]), 1)
    return (lanes == column[pl.ds(first, count), 0:1]).astype(F32).astype(BF16)


def fill_bias(bias):
    def crop(at):
        found = jnp.zeros(at.shape, jnp.int32)
        for end in [LONG] + [2 * LONG + SHORT * j for j in range(9)]:
            found = found + (at >= end).astype(jnp.int32)
        return found

    for i, (row, rows, col, cols, low, high) in enumerate(TILES):
        at_row = lax.broadcasted_iota(jnp.int32, (rows, 1), 0) + row
        at_col = lax.broadcasted_iota(jnp.int32, (1, cols), 1) + col
        same = crop(at_row) == jnp.where((at_col >= low) & (at_col < high), crop(at_col), -1)
        bias[i, :rows, :cols] = jnp.where(same, 0.0, -1e30).astype(F32)


def head_part(block, h):
    lane = lax.broadcasted_iota(jnp.int32, (1, 128), 1)
    keep = lane < 64 if h == 0 else lane >= 64
    return jnp.where(keep, block, jnp.zeros_like(block))


def first_half(a, b):
    lane = lax.broadcasted_iota(jnp.int32, (1, 128), 1)
    return jnp.where(lane < 64, a, b)


def rows_from(tile, new, old):
    row, rows, low = tile[0], tile[1], tile[4]
    if row == low:
        return new
    return jnp.where(lax.broadcasted_iota(jnp.int32, (rows, 1), 0) + row >= low, new, old)


def norm_rows(tok, vec, normed):
    def tile(i, _):
        at = pl.ds(pl.multiple_of(i * QT, QT), QT)
        normal, _inverse = normalize(tok[at, :])
        normed[at, :] = (normal * vec[0:1, :] + vec[1:2, :]).astype(BF16)
        return 0
    lax.fori_loop(0, tok.shape[0] // QT, tile, 0)


def project_in(vec, wa, normed, proj):
    def block(i, _):
        at = pl.ds(pl.multiple_of(i * QT, QT), QT)
        proj[0, at, :] = (nn(normed[at, :], wa[0]) + vec[2:3, :]).astype(BF16)
        proj[1, at, :] = nn(normed[at, :], wa[1]).astype(BF16)
        proj[2, at, :] = (nn(normed[at, :], wa[2]) + vec[3:4, :]).astype(BF16)
        return 0
    lax.fori_loop(0, normed.shape[0] // QT, block, 0)


def move_rows(one_hot, src, dst):
    def block(i, _):
        first = pl.multiple_of(i * QT, QT)
        dst[pl.ds(first, QT), :] = nn(one_hot(first, QT), src[...]).astype(BF16)
        return 0
    lax.fori_loop(0, src.shape[0] // QT, block, 0)


def attend(p, proj, bias, att, lse):
    cols = pl.ds(pl.multiple_of(p * 128, 128), 128)
    lane = lax.broadcasted_iota(jnp.int32, (1, 128), 1)
    for i, tile in enumerate(TILES):
        row, rows, col, wide = tile[:4]
        at, keys = pl.ds(row, rows), pl.ds(col, wide)
        q = proj[0, at, cols] * jnp.asarray(0.125, BF16)
        k, v = proj[1, keys, cols], proj[2, keys, cols]
        outs = []
        logs = lse[at, :]
        for h in (0, 1):
            scores = nt(head_part(q, h), k) + bias[i, :rows, :wide]
            largest = jnp.max(scores, axis=-1, keepdims=True)
            weights = jnp.exp(scores - largest)
            total = jnp.sum(weights, axis=-1, keepdims=True)
            low = (weights * (1.0 / total)).astype(BF16)
            outs.append(nn(low, v))
            logs = jnp.where(lane == 2 * p + h, largest + jnp.log(total), logs)
        lse[at, :] = rows_from(tile, logs, lse[at, :])
        att[at, cols] = rows_from(tile, first_half(*outs), att[at, cols].astype(F32)).astype(BF16)


def attend_back(p, proj, gatt, bias, lse_t, dq):
    cols = pl.ds(pl.multiple_of(p * 128, 128), 128)
    dq[...] = jnp.zeros_like(dq)
    dks, dvs = [], []
    for i, tile in enumerate(TILES):
        row, rows, col, wide = tile[:4]
        at, queries = pl.ds(row, rows), pl.ds(col, wide)
        k, v = proj[1, at, cols], proj[2, at, cols]
        g = gatt[queries, cols]
        scaled = proj[0, queries, cols] * jnp.asarray(0.125, BF16)
        dk, dv, dqs = [], [], []
        for h in (0, 1):
            scores = nt(head_part(k, h), scaled) + bias[i, :rows, :wide]
            probs = jnp.exp(scores - lse_t[pl.ds(2 * p + h, 1), queries])
            grad = nt(head_part(v, h), g)
            dot = jnp.sum(probs * grad, axis=0, keepdims=True)
            low = (probs * (grad - dot)).astype(BF16)
            dv.append(nn(probs.astype(BF16), g))
            dk.append(nn(low, scaled))
            dqs.append(tn(low, k))
        dq[queries, :] += first_half(*dqs) * 0.125
        dks.append(first_half(*dk))
        dvs.append(first_half(*dv))
    for i, tile in enumerate(TILES):
        at = pl.ds(tile[0], tile[1])
        proj[1, at, cols] = rows_from(tile, dks[i], proj[1, at, cols].astype(F32)).astype(BF16)
        proj[2, at, cols] = rows_from(tile, dvs[i], proj[2, at, cols].astype(F32)).astype(BF16)
    proj[0, :, cols] = dq[...].astype(BF16)


def weight_grads(normed, gproj, gout):
    def block(q, _):
        def part(m, _):
            col = pl.ds(pl.multiple_of(m * 384, 128), 384)
            gout[:, q, :, col] = tn(normed[...], gproj[q, :, col]).astype(BF16).reshape(8, ROWS, 384)
            return 0
        return lax.fori_loop(0, 2, part, 0)
    lax.fori_loop(0, 3, block, 0)


def row_grads(column, wide, total, vec, wa, gproj, vg):

    def tile(i, _):
        first = pl.multiple_of(i * QT, QT)
        at = pl.ds(first, QT)
        back = from_places(column, first, QT)
        parts = [nn(back, gproj[j]).astype(BF16) for j in range(3)]
        grad = nt(parts[0], wa[0]) + nt(parts[1], wa[1]) + nt(parts[2], wa[2])
        normal, inverse = normalize(wide[at, :D])
        vg[0:1, :] += col_sum(grad * normal)
        vg[1:2, :] += col_sum(grad)
        vg[2:3, :] += col_sum(parts[0].astype(F32))
        vg[3:4, :] += col_sum(parts[2].astype(F32))
        total[at, :] = total[at, :] + norm_pull(grad, normal, inverse, vec[0:1, :])
        return 0
    lax.fori_loop(0, total.shape[0] // QT, tile, 0)


def convert_piece(w, lin, piece):
    if w == 2:
        for q in range(4):
            for m in range(6):
                piece[q, :, 128 * m : 128 * m + 128] = lin[pl.ds(4608 + 576 * q + m, ROWS, stride=6), :].astype(BF16)
        return
    for q in range(4):
        for m in range(6):
            if w == 1:
                at = pl.ds(2304 + 6 * q + m, ROWS, stride=24)
            elif q == 3:
                at = pl.ds(1728 + m, ROWS, stride=6)
            else:
                at = pl.ds(6 * q + m, ROWS, stride=18)
            piece[q, :, 128 * m : 128 * m + 128] = lin[at, :].astype(BF16)


def to_rows(flat, lin, first, count):
    def body(i, _):
        at = first + i * 48
        value = flat[:, pl.ds(pl.multiple_of(at * 128, 6144), 6144)]
        lin[pl.ds(pl.multiple_of(at, 48), 48), :] = value.reshape(48, 128)
        return 0
    lax.fori_loop(0, count // 48, body, 0, unroll=8)


def weight_strip(w, ref, t):
    if w == 2:
        return ref.at[t]
    return ref.at[:, pl.ds(pl.multiple_of(t * ROWS, 16), ROWS), :]


def weight_block(w, ref, t, q, lead=0, count=ROWS):
    if w == 2:
        return ref.at[t, q, pl.ds(lead, count), :]
    return ref.at[q, pl.ds(pl.multiple_of(t * ROWS + lead, 16), count), :]


def front_kernel(
    lens, master, tok_in,
    wa, wb, wc, vec, fb1, normed, proj, att, lse_out,
    tok, early, flat, lin, pv, pieces, wv, wa_in, bias, line, column, att_in, lse,
    ls, zs, zr, xs, xr, ys, yr, ds, dr, cs, cr, vs, vr, es, er,
):
    first_in = pltpu.make_async_copy(master.at[pl.ds(0, 2304 * 128)], early.at[0], ls.at[6])
    first_in.start()
    weights_in = pltpu.make_async_copy(master, flat.at[0], ls.at[5])
    weights_in.start()
    tok_load = pltpu.make_async_copy(tok_in, tok, ls.at[7])
    tok_load.start()
    g, t, z, c, gx, gy = place()
    fulls = (wa, wb, wc)
    peers = [lax.rem(t + k, 8) for k in range(1, 8)]
    barrier = pltpu.get_barrier_semaphore()
    for target in [(g, p) for p in peers] + [(gx, t), (gy, t)]:
        pl.semaphore_signal(barrier, inc=1, device_id=target, device_id_type=MESH_ID)
    first_in.wait()
    to_rows(early, lin, 0, 2304)
    convert_piece(0, lin, pieces.at[0])
    pl.semaphore_wait(barrier, 9)
    other = t + 1 - 2 * c

    def z_copy(w, d, s):
        step = 1 if d == 0 else -1
        src_t = t - 2 * step * s
        src = pieces.at[w, g] if s == 0 else weight_block(w, fulls[w], src_t, g)
        ok = (z - s >= 0) & (z + 1 < NZ) if d == 0 else (z + s < NZ) & (z - 1 >= 0)
        return ok, remote(src, weight_block(w, fulls[w], src_t, g), zs.at[w, d, s], zr.at[w, d, s], (g, t + 2 * step))

    def extra_copy(w, d, s):
        step = 1 if d == 0 else -1
        src_t = t - 2 * step * s
        src = pieces.at[w, 3 - g, pl.ds(0, 32)] if s == 0 else weight_block(w, fulls[w], src_t, 3 - g, 0, 32)
        ok = (z - s >= 0) & (z + 1 < NZ) if d == 0 else (z + s < NZ) & (z - 1 >= 0)
        dst = weight_block(w, fulls[w], src_t, 3 - g, 0, 32)
        return ok, remote(src, dst, es.at[w, d, s], er.at[w, d, s], (g, t + 2 * step))

    def extra_wait(w, d, s):
        blk = weight_block(w, fulls[w], from_t(d, s), 3 - g, 0, 32)
        remote(blk, blk, es.at[w, d, s], er.at[w, d, s], (g, other)).wait_recv()

    def from_t(d, s):
        return t - 2 * (s + 1) if d == 0 else t + 2 * (s + 1)

    def here(d, s):
        return z - s - 1 >= 0 if d == 0 else z + s + 1 < NZ

    def z_wait(w, d, s):
        blk = weight_block(w, fulls[w], from_t(d, s), g)
        remote(blk, blk, zs.at[w, d, s], zr.at[w, d, s], (g, other)).wait_recv()

    def side_copy(w, d, s, axis):
        blk = weight_block(w, fulls[w], from_t(d, s), g)
        sems = (xs, xr) if axis == 0 else (ys, yr)
        return remote(blk, blk, sems[0].at[w, d, s], sems[1].at[w, d, s], (gx if axis == 0 else gy, t))

    def side_wait(w, d, s, axis):
        blk = weight_block(w, fulls[w], from_t(d, s), gx if axis == 0 else gy)
        sems = (xs, xr) if axis == 0 else (ys, yr)
        remote(blk, blk, sems[0].at[w, d, s], sems[1].at[w, d, s], (gx, t)).wait_recv()

    def diag_copy(w, d, s, axis):
        blk = weight_block(w, fulls[w], from_t(d, s), gx if axis == 0 else gy, 32 + 32 * axis, 32)
        return remote(blk, blk, ds.at[w, d, s, axis], dr.at[w, d, s, axis], (gy if axis == 0 else gx, t))

    def diag_wait(w, d, s, axis):
        blk = weight_block(w, fulls[w], from_t(d, s), 3 - g, 32 + 32 * axis, 32)
        remote(blk, blk, ds.at[w, d, s, axis], dr.at[w, d, s, axis], (gx, t)).wait_recv()

    def core_copy(w, d, s):
        blk = weight_strip(w, fulls[w], from_t(d, s))
        return remote(blk, blk, cs.at[w, d, s], cr.at[w, d, s], (g, other))

    def core_wait(w, d, s):
        blk = weight_strip(w, fulls[w], from_t(d, s) + 1 - 2 * c)
        remote(blk, blk, cs.at[w, d, s], cr.at[w, d, s], (g, other)).wait_recv()

    def own_copy(w):
        return remote(pieces.at[w], weight_strip(w, fulls[w], t), cs.at[w, 2, 0], cr.at[w, 2, 0], (g, other))

    def own_wait(w):
        blk = weight_strip(w, fulls[w], other)
        remote(blk, blk, cs.at[w, 2, 0], cr.at[w, 2, 0], (g, other)).wait_recv()

    def own_local(w):
        return pltpu.make_async_copy(pieces.at[w], weight_strip(w, fulls[w], t), ls.at[w])

    def both(s, fn):
        for d in (0, 1):
            @pl.when(here(d, s))
            def _():
                fn(d)

    def start_z(w, s, kind=None):
        for d in (0, 1):
            ok, copy = (kind or z_copy)(w, d, s)

            @pl.when(ok)
            def _():
                copy.start()

    def arrive(n):
        w, s = divmod(n, 3)
        both(s, lambda d: z_wait(w, d, s))
        if s < 2:
            start_z(w, s + 1)

        def sides(d):
            side_copy(w, d, s, 0).start()
            side_copy(w, d, s, 1).start()
        both(s, sides)
        if s == 0 and w < 2:
            start_z(w + 1, 0)
            own_copy(w + 1).start()
            start_z(w + 1, 0, extra_copy)

    def cross(n):
        w, s = divmod(n, 3)

        def fn(d):
            for axis in (0, 1):
                side_wait(w, d, s, axis)
                diag_copy(w, d, s, axis).start()
            extra_wait(w, d, s)
        both(s, fn)
        if s < 2:
            start_z(w, s + 1, extra_copy)

    def finish(n):
        w, s = divmod(n, 3)

        def fn(d):
            diag_wait(w, d, s, 0)
            diag_wait(w, d, s, 1)
            core_copy(w, d, s).start()
        both(s, fn)

    def drain(w):
        own_wait(w)
        own_local(w).wait()
        for s in range(3):
            both(s, lambda d: core_wait(w, d, s))

    start_z(0, 0)
    own_copy(0).start()
    start_z(0, 0, extra_copy)
    own_local(0).start()
    weights_in.wait()
    pv[...] = jnp.zeros_like(pv)
    for j in range(14):
        low = flat[:, pl.ds(6912 * 128 + ROWS * j, ROWS)].astype(BF16)
        pv[j : j + 1, :ROWS] = low.astype(F32)
    local_v = pltpu.make_async_copy(pv, wv.at[t], ls.at[3])
    local_v.start()
    v_copies = [remote(pv, wv.at[t], vs.at[k], vr.at[k], (g, peers[k])) for k in range(7)]
    for copy in v_copies:
        copy.start()
    to_rows(flat, lin, 2304, 4608)
    for w in (1, 2):
        convert_piece(w, lin, pieces.at[w])
        own_local(w).start()
    fill_bias(bias)
    find_places(lens, line, column)
    att_in[...] = jnp.zeros_like(att_in)
    lse[...] = jnp.zeros_like(lse)
    arrive(0)
    local_v.wait()
    for k in range(7):
        remote(pv, wv.at[lax.rem(t + 7 - k, 8)], vs.at[k], vr.at[k], (g, peers[k])).wait_recv()
    for k in range(8):
        vec[:, ROWS * k : ROWS * k + ROWS] = wv[k, :, :ROWS]
        for j in range(4):
            lead = 4 * ROWS * k + ROWS * j
            fb1[0:1, lead : lead + ROWS] = wv[k, 8 + j : 9 + j, :ROWS]
    arrive(1)
    cross(0)
    tok_load.wait()
    norm_rows(tok, vec, att)
    move_rows(lambda first, count: to_places(line, first, count), att, normed)
    arrive(2)
    cross(1)
    finish(0)
    arrive(3)
    cross(2)
    finish(1)
    finish(2)
    drain(0)
    load = pltpu.make_async_copy(wa.at[pl.ds(0, 3)], wa_in, ls.at[4])
    load.start()
    load.wait()
    project_in(vec, wa_in, normed, proj)
    arrive(4)
    cross(3)
    events = [
        [(arrive, 5), (arrive, 6), (cross, 4), (finish, 3)],
        [(arrive, 7), (cross, 5), (finish, 4)],
        [(arrive, 8), (cross, 6), (finish, 5)],
        [(cross, 7), (finish, 6)],
        [(cross, 8), (finish, 7)],
        [(finish, 8)],
    ]
    for p in range(6):
        attend(p, proj, bias, att_in, lse)
        for event, n in events[p]:
            event(n)
    move_rows(lambda first, count: from_places(column, first, count), att_in, att)
    lse_out[...] = lse[...].T[:16]
    drain(1)
    drain(2)
    for copy in v_copies:
        copy.wait_send()
    for w in range(3):
        own_copy(w).wait_send()
        for s in range(3):
            for d in (0, 1):
                for kind in (z_copy, extra_copy):
                    ok, copy = kind(w, d, s)

                    @pl.when(ok)
                    def _():
                        copy.wait_send()

            def sent(d):
                side_copy(w, d, s, 0).wait_send()
                side_copy(w, d, s, 1).wait_send()
                diag_copy(w, d, s, 0).wait_send()
                diag_copy(w, d, s, 1).wait_send()
                core_copy(w, d, s).wait_send()
            both(s, sent)


def front(lens, master, tok):
    vm = pl.BlockSpec(memory_space=pltpu.VMEM)
    rows = tok.shape[0]
    S = jax.ShapeDtypeStruct
    return pl.pallas_call(
        front_kernel,
        name="front",
        out_shape=[
            S((4, D, D), BF16), S((4, D, D), BF16), S((8, 4, ROWS, D), BF16),
            S((16, D), F32), S((8, MLP), F32),
            S((rows, D), BF16), S((3, rows, D), BF16), S((rows, D), BF16), S((16, rows), F32),
        ],
        in_specs=[pl.BlockSpec(memory_space=pltpu.SMEM)] + [ANY, ANY],
        out_specs=[ANY] * 3 + [vm] * 6,
        scratch_shapes=[
            pltpu.VMEM((rows, D), F32),
            pltpu.VMEM((1, 2304 * 128), F32),
            pltpu.VMEM((1, master.shape[0]), F32),
            pltpu.VMEM((6912, 128), F32),
            pltpu.VMEM((16, 128), F32),
            pltpu.VMEM((3, 4, ROWS, D), BF16),
            pltpu.VMEM((8, 16, 128), F32),
            pltpu.VMEM((3, D, D), BF16),
            pltpu.VMEM((4, 288, 384), F32),
            pltpu.VMEM((8, rows), jnp.int32),
            pltpu.VMEM((rows, 128), jnp.int32),
            pltpu.VMEM((rows, D), BF16),
            pltpu.VMEM((rows, 128), F32),
            DMA((8,)),
            DMA((3, 2, 3)), DMA((3, 2, 3)),
            DMA((3, 2, 3)), DMA((3, 2, 3)),
            DMA((3, 2, 3)), DMA((3, 2, 3)),
            DMA((3, 2, 3, 2)), DMA((3, 2, 3, 2)),
            DMA((3, 3, 3)), DMA((3, 3, 3)),
            DMA((7,)), DMA((7,)),
            DMA((3, 2, 3)), DMA((3, 2, 3)),
        ],
        compiler_params=pltpu.CompilerParams(collective_id=0, has_side_effects=True, vmem_limit_bytes=60 * 2**20),
    )(lens, master, tok)


def valid_rows(lens, first, count):
    total = jnp.int32(0)
    for j in range(lens.shape[1]):
        total = total + lens[0, j]
    at = lax.broadcasted_iota(jnp.int32, (count, 1), 0) + first
    return (at < total).astype(F32)


def forward_kernel(
    lens, tok_in, cot_in, att_in, wa, wb_in, wc_in, vec, fb1,
    bo_out, slope_out, n2_out, hid_out, vg,
    tok, cot, att, wp, wb, wc, bo, slope, n2, hid, ls, os,
):
    pairs = [(att_in, att), (wa.at[3], wp), (tok_in, tok), (wb_in, wb), (wc_in, wc), (cot_in, cot)]
    loads = [pltpu.make_async_copy(src, dst, ls.at[i]) for i, (src, dst) in enumerate(pairs)]
    for copy in loads:
        copy.start()
    vg[...] = jnp.zeros_like(vg)
    rows = tok.shape[0]

    def row(j):
        return vec[j : j + 1, :]

    def stores(i):
        at = pl.ds(i * TILE, TILE)
        trio = [(slope, slope_out), (n2, n2_out), (hid, hid_out), (bo, bo_out)]
        return [pltpu.make_async_copy(a.at[at, :], b.at[at, :], os.at[i, n]) for n, (a, b) in enumerate(trio)]

    for copy in loads[:3]:
        copy.wait()
    for i in range(rows // TILE):
        at = pl.ds(i * TILE, TILE)
        middle = tok[at, :] + row(5) * (nn(att[at, :], wp[...]) + row(4))
        normal, _inverse = normalize(middle)
        bo[at, :] = middle
        n2[at, :] = (normal * row(6) + row(7)).astype(BF16)
        if i == 0:
            loads[3].wait()

        def hidden(q, _):
            low = pl.ds(pl.multiple_of(q * D, D), D)
            pre = nn(n2[at, :], wb[q]) + fb1[0:1, low]
            h, s = gelu_and_slope(pre)
            hid[at, low] = h.astype(BF16)
            slope[at, low] = s.astype(BF16)
            return 0
        lax.fori_loop(0, 4, hidden, 0)
        if i == 0:
            loads[4].wait()
            loads[5].wait()
        for copy in stores(i)[:3]:
            copy.start()
        branch_two = nn(hid[at, :], wc[...]) + row(12)
        bo[at, :] += row(13) * branch_two
        back = cot[at, :] * valid_rows(lens, i * TILE, TILE)
        low_back = (row(13) * back).astype(BF16)
        vg[13:14, :] += col_sum(back * branch_two)
        vg[12:13, :] += col_sum(low_back.astype(F32))
        stores(i)[3].start()
    for i in range(rows // TILE):
        for copy in stores(i):
            copy.wait()


def forward(lens, tok, cot, att, wa, wb, wc, vec, fb1):
    vm = pl.BlockSpec(memory_space=pltpu.VMEM)
    rows = tok.shape[0]
    S = jax.ShapeDtypeStruct
    V = pltpu.VMEM
    return pl.pallas_call(
        forward_kernel,
        name="mlp_forward",
        out_shape=[S((rows, D), F32), S((rows, MLP), BF16), S((rows, D), BF16), S((rows, MLP), BF16), S((16, D), F32)],
        in_specs=[pl.BlockSpec(memory_space=pltpu.SMEM)] + [ANY] * 6 + [vm] * 2,
        out_specs=[ANY] * 4 + [vm],
        scratch_shapes=[
            V((rows, D), F32), V((rows, D), F32), V((rows, D), BF16), V((D, D), BF16),
            V((4, D, D), BF16), V((MLP, D), BF16), V((rows, D), F32), V((rows, MLP), BF16),
            V((rows, D), BF16), V((rows, MLP), BF16),
            DMA((6,)), DMA((4, 4)),
        ],
        compiler_params=pltpu.CompilerParams(vmem_limit_bytes=62 * 2**20),
    )(lens, tok, cot, att, wa, wb, wc, vec, fb1)


ORDER = (2, 1, 0)
FIRST = (3, 0, 2, 1)


def back_kernel(
    lens, vec, vg_in, tok, cot, wa, wb_in, wc_in, att_in, slope_in, hid_in, n2_in, normed_in, proj_in, lse_in,
    gin, lin_out, sv, sq,
    line, column, wide, tall, gatt, gout, gb, own, core, zbuf, vg, vg1, gv, vbuf, qbuf,
    ls, hs, cs, cr, zs, zr, vs, vr, qs, qr,
):
    g, t, z, c, gx, gy = place()
    peers = [lax.rem(t + k, 8) for k in range(1, 8)]
    rows = tok.shape[0]
    other = t + 1 - 2 * c

    def local(pairs, first):
        return [pltpu.make_async_copy(src, dst, ls.at[first + i]) for i, (src, dst) in enumerate(pairs)]

    loads = local([(tok, wide), (cot, tall)], 0)
    for copy in loads:
        copy.start()
    greet([(g, p) for p in peers], 7)

    def own_at(w, k):
        return own.at[k] if w == 2 else (gout, gb)[w].at[2 * k + c]

    def core_copy(w, k):
        return remote((gout, gb, gout)[w].at[2 * k + 1 - c], core.at[w, k], cs.at[w, k], cr.at[w, k], (g, other))

    def begin(w):
        for k in FIRST:
            core_copy(w, k).start()

    def slot(d, k, to):
        return k - to if d == 0 else 4 - (to - k)

    def total_of(w, k, q, at, extra):
        mine = own_at(w, k)
        total = mine[q, at, :].astype(F32) + core[w, k, q, at, :].astype(F32)
        for d in extra:
            total = total + zbuf[w, slot(d, k, z), q, at, :].astype(F32)
        return total

    def add_rows(w, k, h, extra):
        for q in (2 * h, 2 * h + 1):
            def body(i, _):
                at = pl.ds(pl.multiple_of(i * 32, 32), 32)
                own_at(w, k)[q, at, :] = total_of(w, k, q, at, extra).astype(BF16)
                return 0
            lax.fori_loop(0, ROWS // 32, body, 0)

    def lay_out(lin, w, k, h, extra):
        for q in (2 * h, 2 * h + 1):
            if w == 2:
                base, stride = 4608 + 576 * q, 6
            elif w == 1:
                base, stride = 2304 + 6 * q, 24
            else:
                base, stride = (1728, 6) if q == 3 else (6 * q, 18)

            def body(i, _):
                at = pl.ds(pl.multiple_of(i * 32, 32), 32)
                total = total_of(w, k, q, at, extra)
                for m in range(6):
                    lin[pl.ds(base + m + i * (32 * stride), 32, stride=stride), :] = total[:, 128 * m : 128 * m + 128]
                return 0
            lax.fori_loop(0, ROWS // 32, body, 0)

    def z_copy(w, d, k, h):
        step = 1 if d == 0 else -1
        at = pl.ds(2 * h, 2)
        return remote(
            own_at(w, k).at[at],
            zbuf.at[w, slot(d, k, z + step), at],
            zs.at[w, d, k, h],
            zr.at[w, d, k, h],
            (g, t + 2 * step),
        )

    def z_wait(w, d, k, h):
        here = zbuf.at[w, slot(d, k, z), pl.ds(2 * h, 2)]
        remote(here, here, zs.at[w, d, k, h], zr.at[w, d, k, h], (g, other)).wait_recv()

    def ready(w, k):
        core_copy(w, k).wait_recv()

    def pass_on(i, d, j, h):
        w = ORDER[i]
        reach = NZ - 1 - z if d == 0 else z
        k = z + j if d == 0 else z - j
        first = z == 0 if d == 0 else z == NZ - 1

        @pl.when(j <= reach)
        def _():
            if h == 0:
                ready(w, k)

            @pl.when(first)
            def _():
                add_rows(w, k, h, ())

            @pl.when(jnp.logical_not(first))
            def _():
                z_wait(w, d, k, h)
                add_rows(w, k, h, (d,))

            if i > 0:
                @pl.when(j == reach)
                def _():
                    z_copy(ORDER[i - 1], d, z + 1 if d == 0 else z - 1, h).wait_send()
            if j < NZ - 1:
                @pl.when(j < reach)
                def _():
                    z_copy(w, d, k + 1 if d == 0 else k - 1, h).wait_send()
            z_copy(w, d, k, h).start()

    def settle(lin, i):
        w = ORDER[i]
        ready(w, z)
        for h in (0, 1):
            for cond, dirs in ((z == 0, (1,)), (z == NZ - 1, (0,)), ((z > 0) & (z < NZ - 1), (0, 1))):
                @pl.when(cond)
                def _():
                    for d in dirs:
                        z_wait(w, d, z, h)
                    lay_out(lin, w, z, h, dirs)

    steps = [(i, j, h) for i in range(3) for j in (3, 2, 1) for h in (0, 1)]

    def run(lo, hi):
        for i, j, h in steps[lo:hi]:
            pass_on(i, 0, j, h)
            pass_on(i, 1, j, h)

    find_places(lens, line, column)
    vg[...] = vg_in[...]
    vg1[...] = jnp.zeros_like(vg1)

    def mlp_part(wp, wb, wc, grads, n2, att, gb1):
        inner = local([(att_in, att), (wa.at[3], wp), (wc_in, wc), (wb_in, wb), (n2_in, n2)], 2)

        def hidden_load(q):
            low = pl.ds(q * D, D)
            return pltpu.make_async_copy(hid_in.at[:, low], grads.at[:, low], hs.at[q])

        def slope_load(i):
            at = pl.ds(i * TILE, TILE)
            return pltpu.make_async_copy(slope_in.at[at, :], grads.at[at, :], hs.at[4 + i])

        for q in FIRST:
            hidden_load(q).start()
        for copy in inner:
            copy.start()

        def row(j):
            return vec[j : j + 1, :]

        for copy in loads:
            copy.wait()
        for i in range(rows // TILE):
            at = pl.ds(i * TILE, TILE)
            tall[at, :] = tall[at, :] * valid_rows(lens, i * TILE, TILE)
            gb1[at, :] = (row(13) * tall[at, :]).astype(BF16)
        for q in FIRST:
            hidden_load(q).wait()

            for t_at, dst in ((2 * q + 1 - c, gout.at[2 * q + 1 - c]), (2 * q + c, own.at[q])):
                low = pl.ds(pl.multiple_of(t_at * 384, 128), 384)
                dst[...] = tn(grads[:, low], gb1[...]).astype(BF16).reshape(4, ROWS, D)
            core_copy(2, q).start()
        for i in range(rows // TILE):
            slope_load(i).start()
        run(0, 2)
        for copy in inner:
            copy.wait()

        def tile(i):
            at = pl.ds(i * TILE, TILE)
            slope_load(i).wait()
            branch_one = nn(att[at, :], wp[...]) + row(4)
            normal, inverse = normalize(wide[at, :] + row(5) * branch_one)
            low_back = gb1[at, :]

            def backward(q, total):
                low = pl.ds(pl.multiple_of(q * D, D), D)
                grad = nt(low_back, wc[low, :]) * grads[at, low].astype(F32)
                grad = grad.astype(BF16)
                grads[at, low] = grad
                vg1[0:1, low] += col_sum(grad.astype(F32))
                return total + nt(grad, wb[q])
            grad_n2 = lax.fori_loop(0, 4, backward, jnp.zeros((TILE, D), F32))
            vg[6:7, :] += col_sum(grad_n2 * normal)
            vg[7:8, :] += col_sum(grad_n2)
            grad_mid = tall[at, :] + norm_pull(grad_n2, normal, inverse, row(6))
            tall[at, :] = grad_mid
            vg[5:6, :] += col_sum(grad_mid * branch_one)
            low_one = (row(5) * grad_mid).astype(BF16)
            gb1[at, :] = low_one
            vg[4:5, :] += col_sum(low_one.astype(F32))
            gatt[at, :] = nt(low_one, wp[...]).astype(BF16)

        for i in range(rows // TILE):
            tile(i)
            run(2 + 2 * i, 4 + 2 * i)

        def fc1(q, _):
            def part(m, _):
                low = pl.ds(pl.multiple_of(q * D + m * 384, 128), 384)
                col = pl.ds(pl.multiple_of(m * 384, 128), 384)
                gb[:, q, :, col] = tn(n2[...], grads[:, low]).astype(BF16).reshape(8, ROWS, 384)
                return 0
            return lax.fori_loop(0, 2, part, 0)
        lax.fori_loop(0, 4, fc1, 0)
        begin(1)

        for q in FIRST:
            core_copy(2, q).wait_send()

        def proj_part(m, _):
            col = pl.ds(pl.multiple_of(m * 384, 128), 384)
            gout[:, 3, :, col] = tn(att[...], gb1[:, col]).astype(BF16).reshape(8, ROWS, 384)
            return 0
        lax.fori_loop(0, 2, proj_part, 0)

    pl.run_scoped(
        mlp_part,
        pltpu.VMEM((D, D), BF16),
        pltpu.VMEM((4, D, D), BF16),
        pltpu.VMEM((MLP, D), BF16),
        pltpu.VMEM((rows, MLP), BF16),
        pltpu.VMEM((rows, D), BF16),
        pltpu.VMEM((rows, D), BF16),
        pltpu.VMEM((rows, D), BF16),
    )
    v_copies = [remote(gv.at[peers[k]], vbuf.at[k], vs.at[k], vr.at[k], (g, peers[k])) for k in range(7)]
    q_copies = [remote(qbuf.at[7], qbuf.at[k], qs.at[k], qr.at[k], (g, peers[k])) for k in range(7)]

    def attention_part(lin, bias, lse_t, gatt_at, dq, wa_v, normed, proj):
        inner = local([(proj_in, proj), (lse_in, lse_t), (wa.at[pl.ds(0, 3)], wa_v), (normed_in, normed)], 8)
        for copy in inner:
            copy.start()
        run(6, 7)
        fill_bias(bias)
        move_rows(lambda first, count: to_places(line, first, count), gatt, gatt_at)
        for copy in inner:
            copy.wait()
        for p in range(6):
            attend_back(p, proj, gatt_at, bias, lse_t, dq)
            if p == 0:
                settle(lin, 0)
            if p < 5:
                run(7 + p, 8 + p)
        weight_grads(normed, proj, gout)
        begin(0)
        run(12, 14)
        row_grads(column, wide, tall, vec, wa_v, proj, vg)
        store = pltpu.make_async_copy(tall, gin, ls.at[12])
        store.start()
        for k in range(8):
            gv[k, :, :ROWS] = vg[:, ROWS * k : ROWS * k + ROWS]
            for j in range(4):
                lead = 4 * ROWS * k + ROWS * j
                gv[k, 8 + j : 9 + j, :ROWS] = vg1[0:1, lead : lead + ROWS]
        for copy in v_copies:
            copy.start()
        run(14, 15)
        settle(lin, 1)
        run(15, 18)
        for k in range(7):
            v_copies[k].wait_recv()
        total = gv[t]
        for k in range(7):
            total = total + vbuf[k]
        lane = lax.broadcasted_iota(jnp.int32, (16, 128), 1)
        across = lax.broadcasted_iota(jnp.int32, (16, 128), 0)
        total = jnp.where((lane < ROWS) & (across < 14), total, 0.0)
        sv[...] = total

        def square(i, acc):
            v = lin[pl.ds(pl.multiple_of(i * 64, 64), 64), :]
            return acc + v * v
        acc = lax.fori_loop(36, 108, square, jnp.zeros((64, 128), F32))
        settle(lin, 2)
        lin_store = pltpu.make_async_copy(lin, lin_out, ls.at[13])
        lin_store.start()

        acc = lax.fori_loop(0, 36, square, acc)
        qbuf[7] = jnp.full((8, 128), jnp.sum(acc) + jnp.sum(total * total), F32)
        for copy in q_copies:
            copy.start()
        store.wait()
        lin_store.wait()

    pl.run_scoped(
        attention_part,
        pltpu.VMEM((6912, 128), F32),
        pltpu.VMEM((4, 288, 384), F32),
        pltpu.VMEM((16, rows), F32),
        pltpu.VMEM((rows, D), BF16),
        pltpu.VMEM((rows, 128), F32),
        pltpu.VMEM((3, D, D), BF16),
        pltpu.VMEM((rows, D), BF16),
        pltpu.VMEM((3, rows, D), BF16),
    )
    for w in range(2):
        for k in range(NZ):
            core_copy(w, k).wait_send()
    for h in (0, 1):
        @pl.when(z < NZ - 1)
        def _():
            z_copy(0, 0, z + 1, h).wait_send()

        @pl.when(z > 0)
        def _():
            z_copy(0, 1, z - 1, h).wait_send()
    for k in range(7):
        q_copies[k].wait_recv()
    acc = qbuf[7]
    for k in range(7):
        acc = acc + qbuf[k]
    sq[...] = acc
    for k in range(7):
        q_copies[k].wait_send()
        v_copies[k].wait_send()


def back(lens, vec, vg, tok, cot, wa, wb, wc, att, slope, hid, n2, normed, proj, lse_t):
    vm = pl.BlockSpec(memory_space=pltpu.VMEM)
    rows = tok.shape[0]
    S = jax.ShapeDtypeStruct
    V = pltpu.VMEM
    return pl.pallas_call(
        back_kernel,
        name="back",
        out_shape=[S((rows, D), F32), S((6912, 128), F32), S((16, 128), F32), S((8, 128), F32)],
        in_specs=[pl.BlockSpec(memory_space=pltpu.SMEM)] + [vm] * 2 + [ANY] * 12,
        out_specs=[ANY] * 2 + [vm] * 2,
        scratch_shapes=[
            V((8, rows), jnp.int32),
            V((rows, 128), jnp.int32),
            V((rows, D), F32),
            V((rows, D), F32),
            V((rows, D), BF16),
            V((8, 4, ROWS, D), BF16),
            V((8, 4, ROWS, D), BF16),
            V((NZ, 4, ROWS, D), BF16),
            V((3, NZ, 4, ROWS, D), BF16),
            V((3, 5, 4, ROWS, D), BF16),
            V((16, D), F32),
            V((8, MLP), F32),
            V((8, 16, 128), F32),
            V((7, 16, 128), F32),
            V((8, 8, 128), F32),
            DMA((14,)), DMA((8,)), DMA((3, NZ)), DMA((3, NZ)),
            DMA((3, 2, NZ, 2)), DMA((3, 2, NZ, 2)),
            DMA((7,)), DMA((7,)), DMA((7,)), DMA((7,)),
        ],
        compiler_params=pltpu.CompilerParams(
            collective_id=1, has_side_effects=True, vmem_limit_bytes=63 * 2**20
        ),
    )(lens, vec, vg, tok, cot, wa, wb, wc, att, slope, hid, n2, normed, proj, lse_t)


PARTS = 6912
SUM_H, SUM_Q, SUM_E = PARTS // 2, PARTS // 4, PARTS // 8
MATRIX_WIDTH = PARTS * 128
VECTOR_WIDTH = 14 * ROWS
BLOCKS = 4
BLOCK = MATRIX_WIDTH // BLOCKS
CHUNK = 6144


def adam_kernel(grad, sv, sq, master, first, second, first_new, second_new, diff, tail, vector_out, norm_out, tail_grad):
    i = pl.program_id(0)
    norm = jnp.sqrt(sq[0:1, 0:1])
    scale = clip_limit / (norm + 1e-06)
    step_rate = base_rate * rate_scale

    def adam(value, old_first, old_second, weight):
        clipped = value * scale
        new_first = beta_first * old_first + (1.0 - beta_first) * clipped
        new_second = beta_second * old_second + (1.0 - beta_second) * clipped * clipped
        root = jnp.sqrt(new_second * (1.0 / (1.0 - beta_second**adam_count))) + adam_epsilon
        ahead = new_first * (1.0 / (1.0 - beta_first**adam_count)) / root
        if weight is not None:
            ahead = ahead + weight_decay * weight
        return new_first, new_second, step_rate * ahead

    @pl.when(i < BLOCKS)
    def _():
        def body(n, _):
            flat = pl.ds(pl.multiple_of(n * CHUNK, CHUNK), CHUNK)
            at = pl.ds(pl.multiple_of(n * (CHUNK // 128), CHUNK // 128), CHUNK // 128)
            first_new[:, flat], second_new[:, flat], ahead = adam(
                grad[at, :].reshape(1, CHUNK), first[:, flat], second[:, flat], master[flat].reshape(1, CHUNK)
            )
            diff[at, :] = ahead.reshape(CHUNK // 128, 128).astype(BF16)
            return 0
        lax.fori_loop(0, BLOCK // CHUNK, body, 0, unroll=12)

    @pl.when(i == BLOCKS)
    def _():
        norm_out[...] = norm
        for j in range(14):
            tail_grad[0:1, ROWS * j : ROWS * j + ROWS] = sv[j : j + 1, :ROWS]
        vector_out[...] = tail_grad[...] / jnp.sqrt(F32(8 * 1024))
        at = pl.ds(0, VECTOR_WIDTH)
        first_new[:, at], second_new[:, at], ahead = adam(tail_grad[...], first[:, at], second[:, at], None)
        tail[...] = jnp.zeros_like(tail)
        tail[:, at] = ahead


def adam_step(grad, sv, sq, master, first, second):
    S = jax.ShapeDtypeStruct
    n = master.shape[0]

    def whole(shape):
        return pl.BlockSpec(shape, lambda i: (0, 0))

    line = pl.BlockSpec((1, BLOCK), lambda i: (0, i))
    rows = pl.BlockSpec((PARTS // BLOCKS, 128), lambda i: (jnp.minimum(i, BLOCKS - 1), 0))
    return pl.pallas_call(
        adam_kernel,
        name="adam",
        grid=(BLOCKS + 1,),
        out_shape=[
            S((1, n), F32), S((1, n), F32), S((PARTS, 128), BF16), S((1, 1408), F32), S((1, VECTOR_WIDTH), F32), S((1, 1), F32)
        ],
        in_specs=[rows, whole((16, 128)), whole((8, 128)), pl.BlockSpec((BLOCK,), lambda i: (i,)), line, line],
        out_specs=[line, line, rows, whole((1, 1408)), whole((1, VECTOR_WIDTH)), whole((1, 1))],
        scratch_shapes=[pltpu.VMEM((1, VECTOR_WIDTH), F32)],
    )(grad, sv, sq, master, first, second)


def outer_kernel(mean, tail, master, momentum, mean_out, momentum_out, weights_out):
    i = pl.program_id(0)

    def step(flat, average):
        new_momentum = outer_beta * momentum[flat] + average
        mean_out[flat] = average
        momentum_out[flat] = new_momentum
        weights_out[flat] = master[flat] - outer_rate * (average + outer_beta * new_momentum)

    @pl.when(i < BLOCKS)
    def _():
        def body(n, _):
            flat = pl.ds(pl.multiple_of(n * CHUNK, CHUNK), CHUNK)
            at = pl.ds(pl.multiple_of(n * (CHUNK // 128), CHUNK // 128), CHUNK // 128)
            step(flat, mean[at, :].astype(F32).reshape(CHUNK))
            return 0
        lax.fori_loop(0, BLOCK // CHUNK, body, 0, unroll=12)

    @pl.when(i == BLOCKS)
    def _():
        step(pl.ds(0, 1408), tail[0, :])


def outer_step(mean, tail, master, momentum):
    n = master.shape[0]
    line = pl.BlockSpec((BLOCK,), lambda i: (i,))
    return pl.pallas_call(
        outer_kernel,
        name="outer",
        grid=(BLOCKS + 1,),
        out_shape=[jax.ShapeDtypeStruct((n,), F32)] * 3,
        in_specs=[
            pl.BlockSpec((PARTS // BLOCKS, 128), lambda i: (jnp.minimum(i, BLOCKS - 1), 0)),
            pl.BlockSpec((1, 1408), lambda i: (0, 0)), line, line,
        ],
        out_specs=[line] * 3,
    )(mean, tail, master, momentum)


def mean_kernel(diff, tail, mean, tail_mean, part, mid, buf, tails, ss, rs, ts, tr):
    g, t, z, c, gx, gy = place()
    peers = [gx, gy, 3 - g]
    greet([(peer, t) for peer in peers], 3)
    xi, yi = lax.rem(g, 2), lax.div(g, 2)
    hop = [((gx, t), (gy, t)), ((gy, t), (gx, t))]
    mine = [(xi, yi), (yi, xi)]

    def at(h, i, j):
        return h * SUM_H + i * SUM_Q + j * SUM_E

    def to_sum(h, e):
        a, b = mine[h]
        j = 1 - b if e == 0 else b
        src = rows_at(diff, at(h, 1 - a, j), SUM_E)
        return remote(src, part.at[h, e], ss.at[h, e], rs.at[h, e], hop[h][0])

    def over(h):
        return remote(mid.at[h], buf.at[h], ss.at[h, 2], rs.at[h, 2], hop[h][1])

    def share(h, e):
        a, b = mine[h]
        block = rows_at(mean, at(h, a, 1 - b if e == 2 else b), SUM_E)
        return remote(block, block, ss.at[h, 3 + e], rs.at[h, 3 + e], hop[h][1 if e == 0 else 0])

    def landed(h, e):
        a, b = mine[h]
        block = rows_at(mean, at(h, a, 1 - b) if e == 0 else at(h, 1 - a, 1 - b if e == 2 else b), SUM_E)
        remote(block, block, ss.at[h, 3 + e], rs.at[h, 3 + e], hop[h][0]).wait_recv()

    def add(fn):
        def body(i, _):
            fn(pl.multiple_of(i * 96, 96))
            return 0
        lax.fori_loop(0, SUM_E // 96, body, 0)

    for e in (0, 1):
        for h in (0, 1):
            to_sum(h, e).start()
    t_copies = [remote(tail, tails.at[k], ts.at[k], tr.at[k], (peers[k], t)) for k in range(3)]
    for copy in t_copies:
        copy.start()
    for h in (0, 1):
        a, b = mine[h]
        to_sum(h, 0).wait_recv()

        def first(i):
            total = diff[pl.ds(pl.multiple_of(at(h, a, 1 - b) + i, 32), 96), :].astype(F32)
            mid[h, pl.ds(i, 96), :] = (total + part[h, 0, pl.ds(i, 96), :].astype(F32)).astype(BF16)
        add(first)
        over(h).start()
    for h in (0, 1):
        a, b = mine[h]
        to_sum(h, 1).wait_recv()
        over(h).wait_recv()

        def second(i):
            here = pl.ds(pl.multiple_of(at(h, a, b) + i, 32), 96)
            local = pl.ds(i, 96)
            total = diff[here, :].astype(F32) + part[h, 1, local, :].astype(F32) + buf[h, local, :].astype(F32)
            mean[here, :] = (total * 0.25).astype(BF16)
        add(second)
        share(h, 0).start()
        share(h, 1).start()
    for copy in t_copies:
        copy.wait_recv()
    tail_mean[...] = (tail[...] + tails[0] + tails[1] + tails[2]) * 0.25
    for h in (0, 1):
        landed(h, 0)
        share(h, 2).start()
    for h in (0, 1):
        landed(h, 1)
        landed(h, 2)
        for e in (0, 1):
            to_sum(h, e).wait_send()
        over(h).wait_send()
        for e in range(3):
            share(h, e).wait_send()
    for copy in t_copies:
        copy.wait_send()


def mean_groups(diff, tail):
    vm = pl.BlockSpec(memory_space=pltpu.VMEM)
    S = jax.ShapeDtypeStruct
    V = pltpu.VMEM
    return pl.pallas_call(
        mean_kernel,
        name="mean_groups",
        out_shape=[S((PARTS, 128), BF16), S((1, 1408), F32)],
        in_specs=[vm] * 2,
        out_specs=[vm] * 2,
        scratch_shapes=[
            V((2, 2, SUM_E, 128), BF16), V((2, SUM_E, 128), BF16), V((2, SUM_E, 128), BF16), V((3, 1, 1408), F32),
            DMA((2, 6)), DMA((2, 6)), DMA((3,)), DMA((3,)),
        ],
        compiler_params=pltpu.CompilerParams(collective_id=2, has_side_effects=True),
    )(diff, tail)


def on_small_slice(tokens, cotangent, crop_lengths, master, first_moment, second_moment, outer_momentum):
    wa, wb, wc, vec, fb1, normed, projected, attended, lse = front(crop_lengths, master, tokens)
    block_output, slope, normed_two, hidden, vg = forward(
        crop_lengths, tokens, cotangent, attended, wa, wb, wc.reshape(MLP, D), vec, fb1
    )
    input_grad, grad_lin, sv, sq = back(
        crop_lengths, vec, vg, tokens, cotangent, wa, wb, wc.reshape(MLP, D), attended, slope, hidden, normed_two,
        normed, projected, lse
    )
    moment_one, moment_two, difference, tail, vector_part, norm = adam_step(
        grad_lin, sv, sq, master, first_moment, second_moment
    )
    mean, tail_mean = mean_groups(difference, tail)
    mean_difference, outer_new, new_weights = outer_step(mean, tail_mean, master, outer_momentum)
    return (
        block_output,
        input_grad,
        norm.reshape(1),
        vector_part,
        moment_one,
        moment_two,
        mean_difference,
        outer_new,
        new_weights,
    )


def solution(mesh):
    small = mesh.shape["grp"] == 4 and mesh.shape["tok"] == 8
    return jax.shard_map(
        on_small_slice if small else on_device,
        mesh=mesh,
        in_specs=(
            P(("grp", "tok"), None),
            P(("grp", "tok"), None),
            P(("grp", "tok"), None),
            P("tok"),
            P("grp", "tok"),
            P("grp", "tok"),
            P("tok"),
        ),
        out_specs=(
            P(("grp", "tok"), None),
            P(("grp", "tok"), None),
            P("grp"),
            P("grp", "tok"),
            P("grp", "tok"),
            P("grp", "tok"),
            P("tok"),
            P("tok"),
            P("tok"),
        ),
        check_vma=False,
    )
```

```python
import jax
import jax.numpy as jnp
from jax import lax
from jax.experimental import pallas as pl
from jax.experimental.pallas import tpu as pltpu
from jax.sharding import PartitionSpec as P

D = 768
MLP = 3072
HEADS = 12
HEAD_DIM = 64
ROWS = D // 8
ANY = pl.BlockSpec(memory_space=pl.ANY)
DMA = pltpu.SemaphoreType.DMA
MESH_ID = pl.DeviceIdType.MESH
NZ = 4
F32, BF16 = jnp.float32, jnp.bfloat16


def place():
    g = lax.axis_index("grp")
    t = lax.axis_index("tok")
    z, c = lax.div(t, 2), lax.rem(t, 2)
    gx = g + 1 - 2 * lax.rem(g, 2)
    gy = g + 2 - 4 * lax.div(g, 2)
    return g, t, z, c, gx, gy


def greet(targets, count):
    barrier = pltpu.get_barrier_semaphore()
    for target in targets:
        pl.semaphore_signal(barrier, inc=1, device_id=target, device_id_type=MESH_ID)
    pl.semaphore_wait(barrier, count)


def remote(src, dst, send, recv, target):
    return pltpu.make_async_remote_copy(
        src_ref=src, dst_ref=dst, send_sem=send, recv_sem=recv,
        device_id=target, device_id_type=MESH_ID,
    )


clip_limit = 3.0
beta_first = 0.9
beta_second = 0.999
adam_epsilon = 1e-08
weight_decay = 0.04
adam_count = 10.0
base_rate = 0.075
rate_scale = 0.9**6
outer_rate = 0.7
outer_beta = 0.9
norm_epsilon = 1e-06


def member_extents():
    return [(D, 3 * D), (D, D), (D, MLP), (MLP, D)] + [(D,)] * 8 + [(MLP,), (D,), (D,)]


def member_sizes():
    sizes_list = []
    for extent in member_extents():
        length = 1
        for member in extent:
            length = length * member
        sizes_list.append(length)
    return sizes_list


def split_params(flat_params, owners):
    table = flat_params.reshape(owners, -1)
    members = []
    offset = 0
    for extent, length in zip(member_extents(), member_sizes()):
        width = length // owners
        members.append(table[:, offset : offset + width].reshape(extent))
        offset = offset + width
    return members


def join_table(members, owners):
    return jnp.concatenate([member.reshape(owners, -1) for member in members], axis=1)


def layer_norm(values, norm_gain, norm_shift):
    center = values - jnp.mean(values, axis=-1, keepdims=True)
    spread = jnp.mean(center * center, axis=-1, keepdims=True)
    return center * lax.rsqrt(spread + norm_epsilon) * norm_gain + norm_shift


def pack_layout(lengths_row, row_count):
    ends_at = jnp.cumsum(lengths_row)
    position = jnp.arange(row_count, dtype=jnp.int32)
    segment = jnp.sum((position[:, None] >= ends_at[None, :]).astype(jnp.int32), axis=1)
    validity = (position < ends_at[-1]).astype(jnp.float32)
    return (segment, validity)


def cross_rows(left_side, right_side):
    return lax.dot_general(
        left_side, right_side, (((0,), (0,)), ((), ())), preferred_element_type=jnp.float32
    )


def times_transposed(left_side, right_side):
    return lax.dot_general(
        left_side, right_side, (((1,), (1,)), ((), ())), preferred_element_type=jnp.float32
    )


def on_device(tokens, cotangent, crop_lengths, master, first_moment, second_moment, outer_momentum):
    row_count = tokens.shape[0]
    pair_count = HEADS // 2
    score_scale = HEAD_DIM ** (-0.5)
    owners = lax.axis_size("tok")
    segment, validity = pack_layout(crop_lengths[0], row_count)
    allowed = segment[:, None] == segment[None, :]
    master_low = master.astype(jnp.bfloat16)
    gathered = split_params(lax.all_gather(master_low, "tok", axis=0, tiled=True), owners)
    w_qkv, w_proj, w_fc1, w_fc2 = gathered[:4]
    (
        gain_one,
        shift_one,
        query_bias,
        value_bias,
        proj_bias,
        scale_one,
        gain_two,
        shift_two,
        fc1_bias,
        fc2_bias,
        scale_two,
    ) = [member.astype(jnp.float32) for member in gathered[4:]]

    def to_pairs(block_cols):
        return jnp.moveaxis(block_cols.reshape(row_count, pair_count, 2 * HEAD_DIM), 1, 0)

    def from_pairs(paired):
        return jnp.moveaxis(paired, 0, 1).reshape(row_count, D)

    normed = layer_norm(tokens, gain_one, shift_one).astype(jnp.bfloat16)
    qkv_bias = jnp.concatenate([query_bias, jnp.zeros_like(query_bias), value_bias])
    projected = (jnp.dot(normed, w_qkv, preferred_element_type=jnp.float32) + qkv_bias).astype(
        jnp.bfloat16
    )
    query_pairs = to_pairs(projected[:, :D])
    key_pairs = to_pairs(projected[:, D : 2 * D])
    value_pairs = to_pairs(projected[:, 2 * D :])

    def forward_pair(pair_item):
        queries, keys_pair, values_pair = [
            member.reshape(row_count, 2, HEAD_DIM) for member in pair_item
        ]
        raw_scores = jnp.einsum(
            "qhd,khd->hqk", queries, keys_pair, preferred_element_type=jnp.float32
        )
        scores = jnp.where(allowed[None], raw_scores * score_scale, -1e30)
        largest = jnp.max(scores, axis=-1, keepdims=True)
        weights_exp = jnp.exp(scores - largest)
        totals = jnp.sum(weights_exp, axis=-1, keepdims=True)
        weights_low = (weights_exp / totals).astype(jnp.bfloat16)
        attended_pair = jnp.einsum(
            "hqk,khd->qhd", weights_low, values_pair, preferred_element_type=jnp.float32
        )
        return (attended_pair.reshape(row_count, 2 * HEAD_DIM), (largest + jnp.log(totals))[..., 0])

    attended_pairs, log_totals = lax.map(forward_pair, (query_pairs, key_pairs, value_pairs))
    attended = from_pairs(attended_pairs).astype(jnp.bfloat16)
    branch_one = jnp.dot(attended, w_proj, preferred_element_type=jnp.float32) + proj_bias
    middle = tokens + scale_one * branch_one
    normed_two = layer_norm(middle, gain_two, shift_two).astype(jnp.bfloat16)
    hidden_pre = jnp.dot(normed_two, w_fc1, preferred_element_type=jnp.float32) + fc1_bias
    hidden = jax.nn.gelu(hidden_pre, approximate=False).astype(jnp.bfloat16)
    branch_two = jnp.dot(hidden, w_fc2, preferred_element_type=jnp.float32) + fc2_bias
    block_output = middle + scale_two * branch_two
    back_out = cotangent * validity[:, None]
    grad_branch_two = (scale_two * back_out).astype(jnp.bfloat16)
    grad_scale_two = jnp.sum(back_out * branch_two, axis=0)
    grad_fc2_bias = jnp.sum(grad_branch_two.astype(jnp.float32), axis=0)
    grad_w_fc2 = cross_rows(hidden, grad_branch_two)
    grad_hidden = times_transposed(grad_branch_two, w_fc2)
    gelu_pull = jax.vjp(lambda values: jax.nn.gelu(values, approximate=False), hidden_pre)[1]
    grad_pre = gelu_pull(grad_hidden)[0].astype(jnp.bfloat16)
    grad_fc1_bias = jnp.sum(grad_pre.astype(jnp.float32), axis=0)
    grad_w_fc1 = cross_rows(normed_two, grad_pre)
    grad_normed_two = times_transposed(grad_pre, w_fc1)
    norm_pull = jax.vjp(layer_norm, middle, gain_two, shift_two)[1]
    grad_middle_part, grad_gain_two, grad_shift_two = norm_pull(grad_normed_two)
    grad_middle = back_out + grad_middle_part
    grad_scale_one = jnp.sum(grad_middle * branch_one, axis=0)
    grad_branch_one = (scale_one * grad_middle).astype(jnp.bfloat16)
    grad_proj_bias = jnp.sum(grad_branch_one.astype(jnp.float32), axis=0)
    grad_w_proj = cross_rows(attended, grad_branch_one)
    grad_attended = times_transposed(grad_branch_one, w_proj).astype(jnp.bfloat16)

    def backward_pair(pair_item):
        queries, keys_pair, values_pair, grad_pair = [
            member.reshape(row_count, 2, HEAD_DIM) for member in pair_item[:4]
        ]
        log_total = pair_item[4]
        raw_scores = jnp.einsum(
            "qhd,khd->hqk", queries, keys_pair, preferred_element_type=jnp.float32
        )
        scores = jnp.where(allowed[None], raw_scores * score_scale, -1e30)
        weights_soft = jnp.exp(scores - log_total[..., None])
        grad_values = jnp.einsum(
            "hqk,qhd->khd",
            weights_soft.astype(jnp.bfloat16),
            grad_pair,
            preferred_element_type=jnp.float32,
        )
        grad_weights = jnp.einsum(
            "qhd,khd->hqk", grad_pair, values_pair, preferred_element_type=jnp.float32
        )
        row_dot = jnp.sum(weights_soft * grad_weights, axis=-1, keepdims=True)
        grad_scores = (weights_soft * (grad_weights - row_dot)).astype(jnp.bfloat16)
        grad_queries = (
            jnp.einsum("hqk,khd->qhd", grad_scores, keys_pair, preferred_element_type=jnp.float32)
            * score_scale
        )
        grad_keys = (
            jnp.einsum("hqk,qhd->khd", grad_scores, queries, preferred_element_type=jnp.float32)
            * score_scale
        )
        return (
            grad_queries.reshape(row_count, 2 * HEAD_DIM),
            grad_keys.reshape(row_count, 2 * HEAD_DIM),
            grad_values.reshape(row_count, 2 * HEAD_DIM),
        )

    grad_q_pairs, grad_k_pairs, grad_v_pairs = lax.map(
        backward_pair, (query_pairs, key_pairs, value_pairs, to_pairs(grad_attended), log_totals)
    )
    grad_projected = jnp.concatenate(
        [from_pairs(grad_q_pairs), from_pairs(grad_k_pairs), from_pairs(grad_v_pairs)], axis=1
    ).astype(jnp.bfloat16)
    grad_query_bias = jnp.sum(grad_projected[:, :D].astype(jnp.float32), axis=0)
    grad_value_bias = jnp.sum(grad_projected[:, 2 * D :].astype(jnp.float32), axis=0)
    grad_w_qkv = cross_rows(normed, grad_projected)
    grad_normed = times_transposed(grad_projected, w_qkv)
    first_pull = jax.vjp(layer_norm, tokens, gain_one, shift_one)[1]
    grad_tokens_part, grad_gain_one, grad_shift_one = first_pull(grad_normed)
    input_grad = grad_middle + grad_tokens_part
    all_members = [
        grad_w_qkv,
        grad_w_proj,
        grad_w_fc1,
        grad_w_fc2,
        grad_gain_one,
        grad_shift_one,
        grad_query_bias,
        grad_value_bias,
        grad_proj_bias,
        grad_scale_one,
        grad_gain_two,
        grad_shift_two,
        grad_fc1_bias,
        grad_fc2_bias,
        grad_scale_two,
    ]
    received = lax.all_to_all(
        join_table(all_members, owners).astype(jnp.bfloat16),
        "tok",
        split_axis=0,
        concat_axis=0,
        tiled=True,
    ).astype(jnp.float32)
    summed = jnp.sum(received, axis=0)
    matrix_width = (4 * D * D + 2 * D * MLP) // owners
    vector_part = summed[matrix_width:] / (owners * row_count) ** 0.5
    square_total = lax.psum(jnp.sum(summed * summed), "tok")
    norm_value = jnp.sqrt(square_total)
    clipped = summed * (clip_limit / (norm_value + 1e-06))
    moment_one = beta_first * first_moment[0] + (1.0 - beta_first) * clipped
    moment_two = beta_second * second_moment[0] + (1.0 - beta_second) * clipped * clipped
    corrected_one = moment_one / (1.0 - beta_first**adam_count)
    corrected_two = moment_two / (1.0 - beta_second**adam_count)
    shard_size = master.shape[0]
    local_index = jnp.arange(shard_size, dtype=jnp.int32)
    decay_mask = (local_index < matrix_width).astype(jnp.float32)
    step_rate = base_rate * rate_scale
    updated = master - step_rate * (
        corrected_one / (jnp.sqrt(corrected_two) + adam_epsilon)
        + weight_decay * decay_mask * master
    )
    mean_difference = lax.psum((master - updated).astype(jnp.bfloat16), "grp").astype(
        jnp.float32
    ) / lax.axis_size("grp")
    outer_new = outer_beta * outer_momentum + mean_difference
    new_weights = master - outer_rate * (mean_difference + outer_beta * outer_new)
    return (
        block_output,
        input_grad,
        norm_value.reshape(1),
        vector_part[None],
        moment_one[None],
        moment_two[None],
        mean_difference,
        outer_new,
        new_weights,
    )


def rows_at(ref, start, count):
    return ref.at[pl.ds(pl.multiple_of(start, 16), count), :]


TILE = 512


def nn(a, b):
    return lax.dot_general(a, b, (((1,), (0,)), ((), ())), preferred_element_type=F32)


def nt(a, b):
    return lax.dot_general(a, b, (((1,), (1,)), ((), ())), preferred_element_type=F32)


def tn(a, b):
    return lax.dot_general(a, b, (((0,), (0,)), ((), ())), preferred_element_type=F32)


def normalize(values):
    center = values - jnp.mean(values, axis=-1, keepdims=True)
    spread = jnp.mean(center * center, axis=-1, keepdims=True)
    inverse = lax.rsqrt(spread + norm_epsilon)
    return center * inverse, inverse


def norm_pull(grad, normal, inverse, gain):
    scaled = grad * gain
    return inverse * (
        scaled
        - jnp.mean(scaled, axis=-1, keepdims=True)
        - normal * jnp.mean(scaled * normal, axis=-1, keepdims=True)
    )


def gelu_and_slope(x):
    phi = 0.5 * (1.0 + lax.erf(x * 0.7071067811865476))
    return x * phi, phi + x * jnp.exp(-0.5 * x * x) * 0.3989422804014327


def col_sum(x):
    return jnp.sum(x, axis=0, keepdims=True)


QT = 256
LONG, SHORT = 261, 54
TILES = (
    (0, 272, 0, 384, 0, 261),
    (256, 272, 256, 384, 261, 522),
    (512, 288, 512, 384, 522, 792),
    (784, 240, 768, 256, 792, 1024),
)


def find_places(lens, line, column):
    crops = lens.shape[1]
    longs, shorts, begin = jnp.int32(0), jnp.int32(0), jnp.int32(0)
    at_line = lax.broadcasted_iota(jnp.int32, line.shape, 1)
    at_column = lax.broadcasted_iota(jnp.int32, column.shape, 0)
    new_line, new_column = at_line, at_column
    for j in range(crops):
        size = lens[0, j]
        is_long = (size == LONG).astype(jnp.int32)
        place_at = is_long * (longs * LONG) + (1 - is_long) * (2 * LONG + shorts * SHORT)
        shift = place_at - begin
        new_line = jnp.where((at_line >= begin) & (at_line < begin + size), at_line + shift, new_line)
        new_column = jnp.where((at_column >= begin) & (at_column < begin + size), at_column + shift, new_column)
        longs, shorts, begin = longs + is_long, shorts + 1 - is_long, begin + size
    line[...] = new_line
    column[...] = new_column


def to_places(line, first, count):
    rows = lax.broadcasted_iota(jnp.int32, (count, line.shape[1]), 0) + first
    return (rows == line[0:1, :]).astype(F32).astype(BF16)


def from_places(column, first, count):
    lanes = lax.broadcasted_iota(jnp.int32, (count, column.shape[0]), 1)
    return (lanes == column[pl.ds(first, count), 0:1]).astype(F32).astype(BF16)


def fill_bias(bias):
    def crop(at):
        found = jnp.zeros(at.shape, jnp.int32)
        for end in [LONG] + [2 * LONG + SHORT * j for j in range(9)]:
            found = found + (at >= end).astype(jnp.int32)
        return found

    for i, (row, rows, col, cols, low, high) in enumerate(TILES):
        at_row = lax.broadcasted_iota(jnp.int32, (rows, 1), 0) + row
        at_col = lax.broadcasted_iota(jnp.int32, (1, cols), 1) + col
        same = crop(at_row) == jnp.where((at_col >= low) & (at_col < high), crop(at_col), -1)
        bias[i, :rows, :cols] = jnp.where(same, 0.0, -1e30).astype(F32)


def head_part(block, h):
    lane = lax.broadcasted_iota(jnp.int32, (1, 128), 1)
    keep = lane < 64 if h == 0 else lane >= 64
    return jnp.where(keep, block, jnp.zeros_like(block))


def first_half(a, b):
    lane = lax.broadcasted_iota(jnp.int32, (1, 128), 1)
    return jnp.where(lane < 64, a, b)


def rows_from(tile, new, old):
    row, rows, low = tile[0], tile[1], tile[4]
    if row == low:
        return new
    return jnp.where(lax.broadcasted_iota(jnp.int32, (rows, 1), 0) + row >= low, new, old)


def norm_rows(tok, vec, normed):
    def tile(i, _):
        at = pl.ds(pl.multiple_of(i * QT, QT), QT)
        normal, _inverse = normalize(tok[at, :])
        normed[at, :] = (normal * vec[0:1, :] + vec[1:2, :]).astype(BF16)
        return 0
    lax.fori_loop(0, tok.shape[0] // QT, tile, 0)


def project_in(vec, wa, normed, proj):
    def block(i, _):
        at = pl.ds(pl.multiple_of(i * QT, QT), QT)
        proj[0, at, :] = (nn(normed[at, :], wa[0]) + vec[2:3, :]).astype(BF16)
        proj[1, at, :] = nn(normed[at, :], wa[1]).astype(BF16)
        proj[2, at, :] = (nn(normed[at, :], wa[2]) + vec[3:4, :]).astype(BF16)
        return 0
    lax.fori_loop(0, normed.shape[0] // QT, block, 0)


def move_rows(one_hot, src, dst):
    def block(i, _):
        first = pl.multiple_of(i * QT, QT)
        dst[pl.ds(first, QT), :] = nn(one_hot(first, QT), src[...]).astype(BF16)
        return 0
    lax.fori_loop(0, src.shape[0] // QT, block, 0)


def attend(p, proj, bias, att, lse):
    cols = pl.ds(pl.multiple_of(p * 128, 128), 128)
    lane = lax.broadcasted_iota(jnp.int32, (1, 128), 1)
    for i, tile in enumerate(TILES):
        row, rows, col, wide = tile[:4]
        at, keys = pl.ds(row, rows), pl.ds(col, wide)
        q = proj[0, at, cols] * jnp.asarray(0.125, BF16)
        k, v = proj[1, keys, cols], proj[2, keys, cols]
        outs = []
        logs = lse[at, :]
        for h in (0, 1):
            scores = nt(head_part(q, h), k) + bias[i, :rows, :wide]
            largest = jnp.max(scores, axis=-1, keepdims=True)
            weights = jnp.exp(scores - largest)
            total = jnp.sum(weights, axis=-1, keepdims=True)
            low = (weights * (1.0 / total)).astype(BF16)
            outs.append(nn(low, v))
            logs = jnp.where(lane == 2 * p + h, largest + jnp.log(total), logs)
        lse[at, :] = rows_from(tile, logs, lse[at, :])
        att[at, cols] = rows_from(tile, first_half(*outs), att[at, cols].astype(F32)).astype(BF16)


def attend_back(p, proj, gatt, bias, lse_t, dq):
    cols = pl.ds(pl.multiple_of(p * 128, 128), 128)
    dq[...] = jnp.zeros_like(dq)
    dks, dvs = [], []
    for i, tile in enumerate(TILES):
        row, rows, col, wide = tile[:4]
        at, queries = pl.ds(row, rows), pl.ds(col, wide)
        k, v = proj[1, at, cols], proj[2, at, cols]
        g = gatt[queries, cols]
        scaled = proj[0, queries, cols] * jnp.asarray(0.125, BF16)
        dk, dv, dqs = [], [], []
        for h in (0, 1):
            scores = nt(head_part(k, h), scaled) + bias[i, :rows, :wide]
            probs = jnp.exp(scores - lse_t[pl.ds(2 * p + h, 1), queries])
            grad = nt(head_part(v, h), g)
            dot = jnp.sum(probs * grad, axis=0, keepdims=True)
            low = (probs * (grad - dot)).astype(BF16)
            dv.append(nn(probs.astype(BF16), g))
            dk.append(nn(low, scaled))
            dqs.append(tn(low, k))
        dq[queries, :] += first_half(*dqs) * 0.125
        dks.append(first_half(*dk))
        dvs.append(first_half(*dv))
    for i, tile in enumerate(TILES):
        at = pl.ds(tile[0], tile[1])
        proj[1, at, cols] = rows_from(tile, dks[i], proj[1, at, cols].astype(F32)).astype(BF16)
        proj[2, at, cols] = rows_from(tile, dvs[i], proj[2, at, cols].astype(F32)).astype(BF16)
    proj[0, :, cols] = dq[...].astype(BF16)


def weight_grads(normed, gproj, gout):
    def block(q, _):
        def part(m, _):
            col = pl.ds(pl.multiple_of(m * 384, 128), 384)
            gout[:, q, :, col] = tn(normed[...], gproj[q, :, col]).astype(BF16).reshape(8, ROWS, 384)
            return 0
        return lax.fori_loop(0, 2, part, 0)
    lax.fori_loop(0, 3, block, 0)


def row_grads(column, wide, total, vec, wa, gproj, vg):

    def tile(i, _):
        first = pl.multiple_of(i * QT, QT)
        at = pl.ds(first, QT)
        back = from_places(column, first, QT)
        parts = [nn(back, gproj[j]).astype(BF16) for j in range(3)]
        grad = nt(parts[0], wa[0]) + nt(parts[1], wa[1]) + nt(parts[2], wa[2])
        normal, inverse = normalize(wide[at, :D])
        vg[0:1, :] += col_sum(grad * normal)
        vg[1:2, :] += col_sum(grad)
        vg[2:3, :] += col_sum(parts[0].astype(F32))
        vg[3:4, :] += col_sum(parts[2].astype(F32))
        total[at, :] = total[at, :] + norm_pull(grad, normal, inverse, vec[0:1, :])
        return 0
    lax.fori_loop(0, total.shape[0] // QT, tile, 0)


def convert_piece(w, lin, piece):
    if w == 2:
        for q in range(4):
            for m in range(6):
                piece[q, :, 128 * m : 128 * m + 128] = lin[pl.ds(4608 + 576 * q + m, ROWS, stride=6), :].astype(BF16)
        return
    for q in range(4):
        for m in range(6):
            if w == 1:
                at = pl.ds(2304 + 6 * q + m, ROWS, stride=24)
            elif q == 3:
                at = pl.ds(1728 + m, ROWS, stride=6)
            else:
                at = pl.ds(6 * q + m, ROWS, stride=18)
            piece[q, :, 128 * m : 128 * m + 128] = lin[at, :].astype(BF16)


def to_rows(flat, lin, first, count):
    def body(i, _):
        at = first + i * 48
        value = flat[:, pl.ds(pl.multiple_of(at * 128, 6144), 6144)]
        lin[pl.ds(pl.multiple_of(at, 48), 48), :] = value.reshape(48, 128)
        return 0
    lax.fori_loop(0, count // 48, body, 0, unroll=8)


def weight_strip(w, ref, t):
    if w == 2:
        return ref.at[t]
    return ref.at[:, pl.ds(pl.multiple_of(t * ROWS, 16), ROWS), :]


def weight_block(w, ref, t, q, lead=0, count=ROWS):
    if w == 2:
        return ref.at[t, q, pl.ds(lead, count), :]
    return ref.at[q, pl.ds(pl.multiple_of(t * ROWS + lead, 16), count), :]


def front_kernel(
    lens, master, tok_in,
    wa, wb, wc, vec, fb1, normed, proj, att, lse_out,
    tok, early, flat, lin, pv, pieces, wv, wa_in, bias, line, column, att_in, lse,
    ls, zs, zr, xs, xr, ys, yr, ds, dr, cs, cr, vs, vr, es, er,
):
    first_in = pltpu.make_async_copy(master.at[pl.ds(0, 2304 * 128)], early.at[0], ls.at[6])
    first_in.start()
    weights_in = pltpu.make_async_copy(master, flat.at[0], ls.at[5])
    weights_in.start()
    tok_load = pltpu.make_async_copy(tok_in, tok, ls.at[7])
    tok_load.start()
    g, t, z, c, gx, gy = place()
    fulls = (wa, wb, wc)
    peers = [lax.rem(t + k, 8) for k in range(1, 8)]
    barrier = pltpu.get_barrier_semaphore()
    for target in [(g, p) for p in peers] + [(gx, t), (gy, t)]:
        pl.semaphore_signal(barrier, inc=1, device_id=target, device_id_type=MESH_ID)
    first_in.wait()
    to_rows(early, lin, 0, 2304)
    convert_piece(0, lin, pieces.at[0])
    pl.semaphore_wait(barrier, 9)
    other = t + 1 - 2 * c

    def z_copy(w, d, s):
        step = 1 if d == 0 else -1
        src_t = t - 2 * step * s
        src = pieces.at[w, g] if s == 0 else weight_block(w, fulls[w], src_t, g)
        ok = (z - s >= 0) & (z + 1 < NZ) if d == 0 else (z + s < NZ) & (z - 1 >= 0)
        return ok, remote(src, weight_block(w, fulls[w], src_t, g), zs.at[w, d, s], zr.at[w, d, s], (g, t + 2 * step))

    def extra_copy(w, d, s):
        step = 1 if d == 0 else -1
        src_t = t - 2 * step * s
        src = pieces.at[w, 3 - g, pl.ds(0, 32)] if s == 0 else weight_block(w, fulls[w], src_t, 3 - g, 0, 32)
        ok = (z - s >= 0) & (z + 1 < NZ) if d == 0 else (z + s < NZ) & (z - 1 >= 0)
        dst = weight_block(w, fulls[w], src_t, 3 - g, 0, 32)
        return ok, remote(src, dst, es.at[w, d, s], er.at[w, d, s], (g, t + 2 * step))

    def extra_wait(w, d, s):
        blk = weight_block(w, fulls[w], from_t(d, s), 3 - g, 0, 32)
        remote(blk, blk, es.at[w, d, s], er.at[w, d, s], (g, other)).wait_recv()

    def from_t(d, s):
        return t - 2 * (s + 1) if d == 0 else t + 2 * (s + 1)

    def here(d, s):
        return z - s - 1 >= 0 if d == 0 else z + s + 1 < NZ

    def z_wait(w, d, s):
        blk = weight_block(w, fulls[w], from_t(d, s), g)
        remote(blk, blk, zs.at[w, d, s], zr.at[w, d, s], (g, other)).wait_recv()

    def side_copy(w, d, s, axis):
        blk = weight_block(w, fulls[w], from_t(d, s), g)
        sems = (xs, xr) if axis == 0 else (ys, yr)
        return remote(blk, blk, sems[0].at[w, d, s], sems[1].at[w, d, s], (gx if axis == 0 else gy, t))

    def side_wait(w, d, s, axis):
        blk = weight_block(w, fulls[w], from_t(d, s), gx if axis == 0 else gy)
        sems = (xs, xr) if axis == 0 else (ys, yr)
        remote(blk, blk, sems[0].at[w, d, s], sems[1].at[w, d, s], (gx, t)).wait_recv()

    def diag_copy(w, d, s, axis):
        blk = weight_block(w, fulls[w], from_t(d, s), gx if axis == 0 else gy, 32 + 32 * axis, 32)
        return remote(blk, blk, ds.at[w, d, s, axis], dr.at[w, d, s, axis], (gy if axis == 0 else gx, t))

    def diag_wait(w, d, s, axis):
        blk = weight_block(w, fulls[w], from_t(d, s), 3 - g, 32 + 32 * axis, 32)
        remote(blk, blk, ds.at[w, d, s, axis], dr.at[w, d, s, axis], (gx, t)).wait_recv()

    def core_copy(w, d, s):
        blk = weight_strip(w, fulls[w], from_t(d, s))
        return remote(blk, blk, cs.at[w, d, s], cr.at[w, d, s], (g, other))

    def core_wait(w, d, s):
        blk = weight_strip(w, fulls[w], from_t(d, s) + 1 - 2 * c)
        remote(blk, blk, cs.at[w, d, s], cr.at[w, d, s], (g, other)).wait_recv()

    def own_copy(w):
        return remote(pieces.at[w], weight_strip(w, fulls[w], t), cs.at[w, 2, 0], cr.at[w, 2, 0], (g, other))

    def own_wait(w):
        blk = weight_strip(w, fulls[w], other)
        remote(blk, blk, cs.at[w, 2, 0], cr.at[w, 2, 0], (g, other)).wait_recv()

    def own_local(w):
        return pltpu.make_async_copy(pieces.at[w], weight_strip(w, fulls[w], t), ls.at[w])

    def both(s, fn):
        for d in (0, 1):
            @pl.when(here(d, s))
            def _():
                fn(d)

    def start_z(w, s, kind=None):
        for d in (0, 1):
            ok, copy = (kind or z_copy)(w, d, s)

            @pl.when(ok)
            def _():
                copy.start()

    def arrive(n):
        w, s = divmod(n, 3)
        both(s, lambda d: z_wait(w, d, s))
        if s < 2:
            start_z(w, s + 1)

        def sides(d):
            side_copy(w, d, s, 0).start()
            side_copy(w, d, s, 1).start()
        both(s, sides)
        if s == 0 and w < 2:
            start_z(w + 1, 0)
            own_copy(w + 1).start()
            start_z(w + 1, 0, extra_copy)

    def cross(n):
        w, s = divmod(n, 3)

        def fn(d):
            for axis in (0, 1):
                side_wait(w, d, s, axis)
                diag_copy(w, d, s, axis).start()
            extra_wait(w, d, s)
        both(s, fn)
        if s < 2:
            start_z(w, s + 1, extra_copy)

    def finish(n):
        w, s = divmod(n, 3)

        def fn(d):
            diag_wait(w, d, s, 0)
            diag_wait(w, d, s, 1)
            core_copy(w, d, s).start()
        both(s, fn)

    def drain(w):
        own_wait(w)
        own_local(w).wait()
        for s in range(3):
            both(s, lambda d: core_wait(w, d, s))

    start_z(0, 0)
    own_copy(0).start()
    start_z(0, 0, extra_copy)
    own_local(0).start()
    weights_in.wait()
    pv[...] = jnp.zeros_like(pv)
    for j in range(14):
        low = flat[:, pl.ds(6912 * 128 + ROWS * j, ROWS)].astype(BF16)
        pv[j : j + 1, :ROWS] = low.astype(F32)
    local_v = pltpu.make_async_copy(pv, wv.at[t], ls.at[3])
    local_v.start()
    v_copies = [remote(pv, wv.at[t], vs.at[k], vr.at[k], (g, peers[k])) for k in range(7)]
    for copy in v_copies:
        copy.start()
    to_rows(flat, lin, 2304, 4608)
    for w in (1, 2):
        convert_piece(w, lin, pieces.at[w])
        own_local(w).start()
    fill_bias(bias)
    find_places(lens, line, column)
    att_in[...] = jnp.zeros_like(att_in)
    lse[...] = jnp.zeros_like(lse)
    arrive(0)
    local_v.wait()
    for k in range(7):
        remote(pv, wv.at[lax.rem(t + 7 - k, 8)], vs.at[k], vr.at[k], (g, peers[k])).wait_recv()
    for k in range(8):
        vec[:, ROWS * k : ROWS * k + ROWS] = wv[k, :, :ROWS]
        for j in range(4):
            lead = 4 * ROWS * k + ROWS * j
            fb1[0:1, lead : lead + ROWS] = wv[k, 8 + j : 9 + j, :ROWS]
    arrive(1)
    cross(0)
    tok_load.wait()
    norm_rows(tok, vec, att)
    move_rows(lambda first, count: to_places(line, first, count), att, normed)
    arrive(2)
    cross(1)
    finish(0)
    arrive(3)
    cross(2)
    finish(1)
    finish(2)
    drain(0)
    load = pltpu.make_async_copy(wa.at[pl.ds(0, 3)], wa_in, ls.at[4])
    load.start()
    load.wait()
    project_in(vec, wa_in, normed, proj)
    arrive(4)
    cross(3)
    events = [
        [(arrive, 5), (arrive, 6), (cross, 4), (finish, 3)],
        [(arrive, 7), (cross, 5), (finish, 4)],
        [(arrive, 8), (cross, 6), (finish, 5)],
        [(cross, 7), (finish, 6)],
        [(cross, 8), (finish, 7)],
        [(finish, 8)],
    ]
    for p in range(6):
        attend(p, proj, bias, att_in, lse)
        for event, n in events[p]:
            event(n)
    move_rows(lambda first, count: from_places(column, first, count), att_in, att)
    lse_out[...] = lse[...].T[:16]
    drain(1)
    drain(2)
    for copy in v_copies:
        copy.wait_send()
    for w in range(3):
        own_copy(w).wait_send()
        for s in range(3):
            for d in (0, 1):
                for kind in (z_copy, extra_copy):
                    ok, copy = kind(w, d, s)

                    @pl.when(ok)
                    def _():
                        copy.wait_send()

            def sent(d):
                side_copy(w, d, s, 0).wait_send()
                side_copy(w, d, s, 1).wait_send()
                diag_copy(w, d, s, 0).wait_send()
                diag_copy(w, d, s, 1).wait_send()
                core_copy(w, d, s).wait_send()
            both(s, sent)


def front(lens, master, tok):
    vm = pl.BlockSpec(memory_space=pltpu.VMEM)
    rows = tok.shape[0]
    S = jax.ShapeDtypeStruct
    return pl.pallas_call(
        front_kernel,
        name="front",
        out_shape=[
            S((4, D, D), BF16), S((4, D, D), BF16), S((8, 4, ROWS, D), BF16),
            S((16, D), F32), S((8, MLP), F32),
            S((rows, D), BF16), S((3, rows, D), BF16), S((rows, D), BF16), S((16, rows), F32),
        ],
        in_specs=[pl.BlockSpec(memory_space=pltpu.SMEM)] + [ANY, ANY],
        out_specs=[ANY] * 3 + [vm] * 6,
        scratch_shapes=[
            pltpu.VMEM((rows, D), F32),
            pltpu.VMEM((1, 2304 * 128), F32),
            pltpu.VMEM((1, master.shape[0]), F32),
            pltpu.VMEM((6912, 128), F32),
            pltpu.VMEM((16, 128), F32),
            pltpu.VMEM((3, 4, ROWS, D), BF16),
            pltpu.VMEM((8, 16, 128), F32),
            pltpu.VMEM((3, D, D), BF16),
            pltpu.VMEM((4, 288, 384), F32),
            pltpu.VMEM((8, rows), jnp.int32),
            pltpu.VMEM((rows, 128), jnp.int32),
            pltpu.VMEM((rows, D), BF16),
            pltpu.VMEM((rows, 128), F32),
            DMA((8,)),
            DMA((3, 2, 3)), DMA((3, 2, 3)),
            DMA((3, 2, 3)), DMA((3, 2, 3)),
            DMA((3, 2, 3)), DMA((3, 2, 3)),
            DMA((3, 2, 3, 2)), DMA((3, 2, 3, 2)),
            DMA((3, 3, 3)), DMA((3, 3, 3)),
            DMA((7,)), DMA((7,)),
            DMA((3, 2, 3)), DMA((3, 2, 3)),
        ],
        compiler_params=pltpu.CompilerParams(collective_id=0, has_side_effects=True, vmem_limit_bytes=60 * 2**20),
    )(lens, master, tok)


def valid_rows(lens, first, count):
    total = jnp.int32(0)
    for j in range(lens.shape[1]):
        total = total + lens[0, j]
    at = lax.broadcasted_iota(jnp.int32, (count, 1), 0) + first
    return (at < total).astype(F32)


def forward_kernel(
    lens, tok_in, cot_in, att_in, wa, wb_in, wc_in, vec, fb1,
    bo_out, slope_out, n2_out, hid_out, vg,
    tok, cot, att, wp, wb, wc, bo, slope, n2, hid, ls, os,
):
    pairs = [(att_in, att), (wa.at[3], wp), (tok_in, tok), (wb_in, wb), (wc_in, wc), (cot_in, cot)]
    loads = [pltpu.make_async_copy(src, dst, ls.at[i]) for i, (src, dst) in enumerate(pairs)]
    for copy in loads:
        copy.start()
    vg[...] = jnp.zeros_like(vg)
    rows = tok.shape[0]

    def row(j):
        return vec[j : j + 1, :]

    def stores(i):
        at = pl.ds(i * TILE, TILE)
        trio = [(slope, slope_out), (n2, n2_out), (hid, hid_out), (bo, bo_out)]
        return [pltpu.make_async_copy(a.at[at, :], b.at[at, :], os.at[i, n]) for n, (a, b) in enumerate(trio)]

    for copy in loads[:3]:
        copy.wait()
    for i in range(rows // TILE):
        at = pl.ds(i * TILE, TILE)
        middle = tok[at, :] + row(5) * (nn(att[at, :], wp[...]) + row(4))
        normal, _inverse = normalize(middle)
        bo[at, :] = middle
        n2[at, :] = (normal * row(6) + row(7)).astype(BF16)
        if i == 0:
            loads[3].wait()

        def hidden(q, _):
            low = pl.ds(pl.multiple_of(q * D, D), D)
            pre = nn(n2[at, :], wb[q]) + fb1[0:1, low]
            h, s = gelu_and_slope(pre)
            hid[at, low] = h.astype(BF16)
            slope[at, low] = s.astype(BF16)
            return 0
        lax.fori_loop(0, 4, hidden, 0)
        if i == 0:
            loads[4].wait()
            loads[5].wait()
        for copy in stores(i)[:3]:
            copy.start()
        branch_two = nn(hid[at, :], wc[...]) + row(12)
        bo[at, :] += row(13) * branch_two
        back = cot[at, :] * valid_rows(lens, i * TILE, TILE)
        low_back = (row(13) * back).astype(BF16)
        vg[13:14, :] += col_sum(back * branch_two)
        vg[12:13, :] += col_sum(low_back.astype(F32))
        stores(i)[3].start()
    for i in range(rows // TILE):
        for copy in stores(i):
            copy.wait()


def forward(lens, tok, cot, att, wa, wb, wc, vec, fb1):
    vm = pl.BlockSpec(memory_space=pltpu.VMEM)
    rows = tok.shape[0]
    S = jax.ShapeDtypeStruct
    V = pltpu.VMEM
    return pl.pallas_call(
        forward_kernel,
        name="mlp_forward",
        out_shape=[S((rows, D), F32), S((rows, MLP), BF16), S((rows, D), BF16), S((rows, MLP), BF16), S((16, D), F32)],
        in_specs=[pl.BlockSpec(memory_space=pltpu.SMEM)] + [ANY] * 6 + [vm] * 2,
        out_specs=[ANY] * 4 + [vm],
        scratch_shapes=[
            V((rows, D), F32), V((rows, D), F32), V((rows, D), BF16), V((D, D), BF16),
            V((4, D, D), BF16), V((MLP, D), BF16), V((rows, D), F32), V((rows, MLP), BF16),
            V((rows, D), BF16), V((rows, MLP), BF16),
            DMA((6,)), DMA((4, 4)),
        ],
        compiler_params=pltpu.CompilerParams(vmem_limit_bytes=62 * 2**20),
    )(lens, tok, cot, att, wa, wb, wc, vec, fb1)


ORDER = (2, 1, 0)
FIRST = (3, 0, 2, 1)


def back_kernel(
    lens, vec, vg_in, tok, cot, wa, wb_in, wc_in, att_in, slope_in, hid_in, n2_in, normed_in, proj_in, lse_in,
    gin, lin_out, sv, sq,
    line, column, wide, tall, gatt, gout, gb, own, core, zbuf, vg, vg1, gv, vbuf, qbuf,
    ls, hs, cs, cr, zs, zr, vs, vr, qs, qr,
):
    g, t, z, c, gx, gy = place()
    peers = [lax.rem(t + k, 8) for k in range(1, 8)]
    rows = tok.shape[0]
    other = t + 1 - 2 * c

    def local(pairs, first):
        return [pltpu.make_async_copy(src, dst, ls.at[first + i]) for i, (src, dst) in enumerate(pairs)]

    loads = local([(tok, wide), (cot, tall)], 0)
    for copy in loads:
        copy.start()
    greet([(g, p) for p in peers], 7)

    def own_at(w, k):
        return own.at[k] if w == 2 else (gout, gb)[w].at[2 * k + c]

    def core_copy(w, k):
        return remote((gout, gb, gout)[w].at[2 * k + 1 - c], core.at[w, k], cs.at[w, k], cr.at[w, k], (g, other))

    def begin(w):
        for k in FIRST:
            core_copy(w, k).start()

    def slot(d, k, to):
        return k - to if d == 0 else 4 - (to - k)

    def total_of(w, k, q, at, extra):
        mine = own_at(w, k)
        total = mine[q, at, :].astype(F32) + core[w, k, q, at, :].astype(F32)
        for d in extra:
            total = total + zbuf[w, slot(d, k, z), q, at, :].astype(F32)
        return total

    def add_rows(w, k, h, extra):
        for q in (2 * h, 2 * h + 1):
            def body(i, _):
                at = pl.ds(pl.multiple_of(i * 32, 32), 32)
                own_at(w, k)[q, at, :] = total_of(w, k, q, at, extra).astype(BF16)
                return 0
            lax.fori_loop(0, ROWS // 32, body, 0)

    def lay_out(lin, w, k, h, extra):
        for q in (2 * h, 2 * h + 1):
            if w == 2:
                base, stride = 4608 + 576 * q, 6
            elif w == 1:
                base, stride = 2304 + 6 * q, 24
            else:
                base, stride = (1728, 6) if q == 3 else (6 * q, 18)

            def body(i, _):
                at = pl.ds(pl.multiple_of(i * 32, 32), 32)
                total = total_of(w, k, q, at, extra)
                for m in range(6):
                    lin[pl.ds(base + m + i * (32 * stride), 32, stride=stride), :] = total[:, 128 * m : 128 * m + 128]
                return 0
            lax.fori_loop(0, ROWS // 32, body, 0)

    def z_copy(w, d, k, h):
        step = 1 if d == 0 else -1
        at = pl.ds(2 * h, 2)
        return remote(
            own_at(w, k).at[at],
            zbuf.at[w, slot(d, k, z + step), at],
            zs.at[w, d, k, h],
            zr.at[w, d, k, h],
            (g, t + 2 * step),
        )

    def z_wait(w, d, k, h):
        here = zbuf.at[w, slot(d, k, z), pl.ds(2 * h, 2)]
        remote(here, here, zs.at[w, d, k, h], zr.at[w, d, k, h], (g, other)).wait_recv()

    def ready(w, k):
        core_copy(w, k).wait_recv()

    def pass_on(i, d, j, h):
        w = ORDER[i]
        reach = NZ - 1 - z if d == 0 else z
        k = z + j if d == 0 else z - j
        first = z == 0 if d == 0 else z == NZ - 1

        @pl.when(j <= reach)
        def _():
            if h == 0:
                ready(w, k)

            @pl.when(first)
            def _():
                add_rows(w, k, h, ())

            @pl.when(jnp.logical_not(first))
            def _():
                z_wait(w, d, k, h)
                add_rows(w, k, h, (d,))

            if i > 0:
                @pl.when(j == reach)
                def _():
                    z_copy(ORDER[i - 1], d, z + 1 if d == 0 else z - 1, h).wait_send()
            if j < NZ - 1:
                @pl.when(j < reach)
                def _():
                    z_copy(w, d, k + 1 if d == 0 else k - 1, h).wait_send()
            z_copy(w, d, k, h).start()

    def settle(lin, i):
        w = ORDER[i]
        ready(w, z)
        for h in (0, 1):
            for cond, dirs in ((z == 0, (1,)), (z == NZ - 1, (0,)), ((z > 0) & (z < NZ - 1), (0, 1))):
                @pl.when(cond)
                def _():
                    for d in dirs:
                        z_wait(w, d, z, h)
                    lay_out(lin, w, z, h, dirs)

    steps = [(i, j, h) for i in range(3) for j in (3, 2, 1) for h in (0, 1)]

    def run(lo, hi):
        for i, j, h in steps[lo:hi]:
            pass_on(i, 0, j, h)
            pass_on(i, 1, j, h)

    find_places(lens, line, column)
    vg[...] = vg_in[...]
    vg1[...] = jnp.zeros_like(vg1)

    def mlp_part(wp, wb, wc, grads, n2, att, gb1):
        inner = local([(att_in, att), (wa.at[3], wp), (wc_in, wc), (wb_in, wb), (n2_in, n2)], 2)

        def hidden_load(q):
            low = pl.ds(q * D, D)
            return pltpu.make_async_copy(hid_in.at[:, low], grads.at[:, low], hs.at[q])

        def slope_load(i):
            at = pl.ds(i * TILE, TILE)
            return pltpu.make_async_copy(slope_in.at[at, :], grads.at[at, :], hs.at[4 + i])

        for q in FIRST:
            hidden_load(q).start()
        for copy in inner:
            copy.start()

        def row(j):
            return vec[j : j + 1, :]

        for copy in loads:
            copy.wait()
        for i in range(rows // TILE):
            at = pl.ds(i * TILE, TILE)
            tall[at, :] = tall[at, :] * valid_rows(lens, i * TILE, TILE)
            gb1[at, :] = (row(13) * tall[at, :]).astype(BF16)
        for q in FIRST:
            hidden_load(q).wait()

            for t_at, dst in ((2 * q + 1 - c, gout.at[2 * q + 1 - c]), (2 * q + c, own.at[q])):
                low = pl.ds(pl.multiple_of(t_at * 384, 128), 384)
                dst[...] = tn(grads[:, low], gb1[...]).astype(BF16).reshape(4, ROWS, D)
            core_copy(2, q).start()
        for i in range(rows // TILE):
            slope_load(i).start()
        run(0, 2)
        for copy in inner:
            copy.wait()

        def tile(i):
            at = pl.ds(i * TILE, TILE)
            slope_load(i).wait()
            branch_one = nn(att[at, :], wp[...]) + row(4)
            normal, inverse = normalize(wide[at, :] + row(5) * branch_one)
            low_back = gb1[at, :]

            def backward(q, total):
                low = pl.ds(pl.multiple_of(q * D, D), D)
                grad = nt(low_back, wc[low, :]) * grads[at, low].astype(F32)
                grad = grad.astype(BF16)
                grads[at, low] = grad
                vg1[0:1, low] += col_sum(grad.astype(F32))
                return total + nt(grad, wb[q])
            grad_n2 = lax.fori_loop(0, 4, backward, jnp.zeros((TILE, D), F32))
            vg[6:7, :] += col_sum(grad_n2 * normal)
            vg[7:8, :] += col_sum(grad_n2)
            grad_mid = tall[at, :] + norm_pull(grad_n2, normal, inverse, row(6))
            tall[at, :] = grad_mid
            vg[5:6, :] += col_sum(grad_mid * branch_one)
            low_one = (row(5) * grad_mid).astype(BF16)
            gb1[at, :] = low_one
            vg[4:5, :] += col_sum(low_one.astype(F32))
            gatt[at, :] = nt(low_one, wp[...]).astype(BF16)

        for i in range(rows // TILE):
            tile(i)
            run(2 + 2 * i, 4 + 2 * i)

        def fc1(q, _):
            def part(m, _):
                low = pl.ds(pl.multiple_of(q * D + m * 384, 128), 384)
                col = pl.ds(pl.multiple_of(m * 384, 128), 384)
                gb[:, q, :, col] = tn(n2[...], grads[:, low]).astype(BF16).reshape(8, ROWS, 384)
                return 0
            return lax.fori_loop(0, 2, part, 0)
        lax.fori_loop(0, 4, fc1, 0)
        begin(1)

        for q in FIRST:
            core_copy(2, q).wait_send()

        def proj_part(m, _):
            col = pl.ds(pl.multiple_of(m * 384, 128), 384)
            gout[:, 3, :, col] = tn(att[...], gb1[:, col]).astype(BF16).reshape(8, ROWS, 384)
            return 0
        lax.fori_loop(0, 2, proj_part, 0)

    pl.run_scoped(
        mlp_part,
        pltpu.VMEM((D, D), BF16),
        pltpu.VMEM((4, D, D), BF16),
        pltpu.VMEM((MLP, D), BF16),
        pltpu.VMEM((rows, MLP), BF16),
        pltpu.VMEM((rows, D), BF16),
        pltpu.VMEM((rows, D), BF16),
        pltpu.VMEM((rows, D), BF16),
    )
    v_copies = [remote(gv.at[peers[k]], vbuf.at[k], vs.at[k], vr.at[k], (g, peers[k])) for k in range(7)]
    q_copies = [remote(qbuf.at[7], qbuf.at[k], qs.at[k], qr.at[k], (g, peers[k])) for k in range(7)]

    def attention_part(lin, bias, lse_t, gatt_at, dq, wa_v, normed, proj):
        inner = local([(proj_in, proj), (lse_in, lse_t), (wa.at[pl.ds(0, 3)], wa_v), (normed_in, normed)], 8)
        for copy in inner:
            copy.start()
        run(6, 7)
        fill_bias(bias)
        move_rows(lambda first, count: to_places(line, first, count), gatt, gatt_at)
        for copy in inner:
            copy.wait()
        for p in range(6):
            attend_back(p, proj, gatt_at, bias, lse_t, dq)
            if p == 0:
                settle(lin, 0)
            if p < 5:
                run(7 + p, 8 + p)
        weight_grads(normed, proj, gout)
        begin(0)
        run(12, 14)
        row_grads(column, wide, tall, vec, wa_v, proj, vg)
        store = pltpu.make_async_copy(tall, gin, ls.at[12])
        store.start()
        for k in range(8):
            gv[k, :, :ROWS] = vg[:, ROWS * k : ROWS * k + ROWS]
            for j in range(4):
                lead = 4 * ROWS * k + ROWS * j
                gv[k, 8 + j : 9 + j, :ROWS] = vg1[0:1, lead : lead + ROWS]
        for copy in v_copies:
            copy.start()
        run(14, 15)
        settle(lin, 1)
        run(15, 18)
        for k in range(7):
            v_copies[k].wait_recv()
        total = gv[t]
        for k in range(7):
            total = total + vbuf[k]
        lane = lax.broadcasted_iota(jnp.int32, (16, 128), 1)
        across = lax.broadcasted_iota(jnp.int32, (16, 128), 0)
        total = jnp.where((lane < ROWS) & (across < 14), total, 0.0)
        sv[...] = total

        def square(i, acc):
            v = lin[pl.ds(pl.multiple_of(i * 64, 64), 64), :]
            return acc + v * v
        acc = lax.fori_loop(36, 108, square, jnp.zeros((64, 128), F32))
        settle(lin, 2)
        lin_store = pltpu.make_async_copy(lin, lin_out, ls.at[13])
        lin_store.start()

        acc = lax.fori_loop(0, 36, square, acc)
        qbuf[7] = jnp.full((8, 128), jnp.sum(acc) + jnp.sum(total * total), F32)
        for copy in q_copies:
            copy.start()
        store.wait()
        lin_store.wait()

    pl.run_scoped(
        attention_part,
        pltpu.VMEM((6912, 128), F32),
        pltpu.VMEM((4, 288, 384), F32),
        pltpu.VMEM((16, rows), F32),
        pltpu.VMEM((rows, D), BF16),
        pltpu.VMEM((rows, 128), F32),
        pltpu.VMEM((3, D, D), BF16),
        pltpu.VMEM((rows, D), BF16),
        pltpu.VMEM((3, rows, D), BF16),
    )
    for w in range(2):
        for k in range(NZ):
            core_copy(w, k).wait_send()
    for h in (0, 1):
        @pl.when(z < NZ - 1)
        def _():
            z_copy(0, 0, z + 1, h).wait_send()

        @pl.when(z > 0)
        def _():
            z_copy(0, 1, z - 1, h).wait_send()
    for k in range(7):
        q_copies[k].wait_recv()
    acc = qbuf[7]
    for k in range(7):
        acc = acc + qbuf[k]
    sq[...] = acc
    for k in range(7):
        q_copies[k].wait_send()
        v_copies[k].wait_send()


def back(lens, vec, vg, tok, cot, wa, wb, wc, att, slope, hid, n2, normed, proj, lse_t):
    vm = pl.BlockSpec(memory_space=pltpu.VMEM)
    rows = tok.shape[0]
    S = jax.ShapeDtypeStruct
    V = pltpu.VMEM
    return pl.pallas_call(
        back_kernel,
        name="back",
        out_shape=[S((rows, D), F32), S((6912, 128), F32), S((16, 128), F32), S((8, 128), F32)],
        in_specs=[pl.BlockSpec(memory_space=pltpu.SMEM)] + [vm] * 2 + [ANY] * 12,
        out_specs=[ANY] * 2 + [vm] * 2,
        scratch_shapes=[
            V((8, rows), jnp.int32),
            V((rows, 128), jnp.int32),
            V((rows, D), F32),
            V((rows, D), F32),
            V((rows, D), BF16),
            V((8, 4, ROWS, D), BF16),
            V((8, 4, ROWS, D), BF16),
            V((NZ, 4, ROWS, D), BF16),
            V((3, NZ, 4, ROWS, D), BF16),
            V((3, 5, 4, ROWS, D), BF16),
            V((16, D), F32),
            V((8, MLP), F32),
            V((8, 16, 128), F32),
            V((7, 16, 128), F32),
            V((8, 8, 128), F32),
            DMA((14,)), DMA((8,)), DMA((3, NZ)), DMA((3, NZ)),
            DMA((3, 2, NZ, 2)), DMA((3, 2, NZ, 2)),
            DMA((7,)), DMA((7,)), DMA((7,)), DMA((7,)),
        ],
        compiler_params=pltpu.CompilerParams(
            collective_id=1, has_side_effects=True, vmem_limit_bytes=63 * 2**20
        ),
    )(lens, vec, vg, tok, cot, wa, wb, wc, att, slope, hid, n2, normed, proj, lse_t)


PARTS = 6912
SUM_H, SUM_Q, SUM_E = PARTS // 2, PARTS // 4, PARTS // 8
MATRIX_WIDTH = PARTS * 128
VECTOR_WIDTH = 14 * ROWS
BLOCKS = 2
BLOCK = MATRIX_WIDTH // BLOCKS
CHUNK = 6144


def adam_kernel(grad, sv, sq, master, first, second, first_new, second_new, diff, tail, vector_out, norm_out, tail_grad):
    i = pl.program_id(0)
    norm = jnp.sqrt(sq[0:1, 0:1])
    scale = clip_limit / (norm + 1e-06)
    step_rate = base_rate * rate_scale

    def adam(value, old_first, old_second, weight):
        clipped = value * scale
        new_first = beta_first * old_first + (1.0 - beta_first) * clipped
        new_second = beta_second * old_second + (1.0 - beta_second) * clipped * clipped
        root = jnp.sqrt(new_second * (1.0 / (1.0 - beta_second**adam_count))) + adam_epsilon
        ahead = new_first * (1.0 / (1.0 - beta_first**adam_count)) / root
        if weight is not None:
            ahead = ahead + weight_decay * weight
        return new_first, new_second, step_rate * ahead

    @pl.when(i < BLOCKS)
    def _():
        def body(n, _):
            flat = pl.ds(pl.multiple_of(n * CHUNK, CHUNK), CHUNK)
            at = pl.ds(pl.multiple_of(n * (CHUNK // 128), CHUNK // 128), CHUNK // 128)
            first_new[:, flat], second_new[:, flat], ahead = adam(
                grad[at, :].reshape(1, CHUNK), first[:, flat], second[:, flat], master[flat].reshape(1, CHUNK)
            )
            diff[at, :] = ahead.reshape(CHUNK // 128, 128).astype(BF16)
            return 0
        lax.fori_loop(0, BLOCK // CHUNK, body, 0, unroll=24)

    @pl.when(i == BLOCKS)
    def _():
        norm_out[...] = norm
        for j in range(14):
            tail_grad[0:1, ROWS * j : ROWS * j + ROWS] = sv[j : j + 1, :ROWS]
        vector_out[...] = tail_grad[...] / jnp.sqrt(F32(8 * 1024))
        at = pl.ds(0, VECTOR_WIDTH)
        first_new[:, at], second_new[:, at], ahead = adam(tail_grad[...], first[:, at], second[:, at], None)
        tail[...] = jnp.zeros_like(tail)
        tail[:, at] = ahead


def adam_step(grad, sv, sq, master, first, second):
    S = jax.ShapeDtypeStruct
    n = master.shape[0]

    def whole(shape):
        return pl.BlockSpec(shape, lambda i: (0, 0))

    line = pl.BlockSpec((1, BLOCK), lambda i: (0, i))
    rows = pl.BlockSpec((PARTS // BLOCKS, 128), lambda i: (jnp.minimum(i, BLOCKS - 1), 0))
    return pl.pallas_call(
        adam_kernel,
        name="adam",
        grid=(BLOCKS + 1,),
        out_shape=[
            S((1, n), F32), S((1, n), F32), S((PARTS, 128), BF16), S((1, 1408), F32), S((1, VECTOR_WIDTH), F32), S((1, 1), F32)
        ],
        in_specs=[rows, whole((16, 128)), whole((8, 128)), pl.BlockSpec((BLOCK,), lambda i: (i,)), line, line],
        out_specs=[line, line, rows, whole((1, 1408)), whole((1, VECTOR_WIDTH)), whole((1, 1))],
        scratch_shapes=[pltpu.VMEM((1, VECTOR_WIDTH), F32)],
        compiler_params=pltpu.CompilerParams(vmem_limit_bytes=48 * 2**20),
    )(grad, sv, sq, master, first, second)


def outer_kernel(mean, tail, master, momentum, mean_out, momentum_out, weights_out):
    i = pl.program_id(0)

    def step(flat, average):
        new_momentum = outer_beta * momentum[flat] + average
        mean_out[flat] = average
        momentum_out[flat] = new_momentum
        weights_out[flat] = master[flat] - outer_rate * (average + outer_beta * new_momentum)

    @pl.when(i < BLOCKS)
    def _():
        def body(n, _):
            flat = pl.ds(pl.multiple_of(n * CHUNK, CHUNK), CHUNK)
            at = pl.ds(pl.multiple_of(n * (CHUNK // 128), CHUNK // 128), CHUNK // 128)
            step(flat, mean[at, :].astype(F32).reshape(CHUNK))
            return 0
        lax.fori_loop(0, BLOCK // CHUNK, body, 0, unroll=24)

    @pl.when(i == BLOCKS)
    def _():
        step(pl.ds(0, 1408), tail[0, :])


def outer_step(mean, tail, master, momentum):
    n = master.shape[0]
    line = pl.BlockSpec((BLOCK,), lambda i: (i,))
    return pl.pallas_call(
        outer_kernel,
        name="outer",
        grid=(BLOCKS + 1,),
        out_shape=[jax.ShapeDtypeStruct((n,), F32)] * 3,
        in_specs=[
            pl.BlockSpec((PARTS // BLOCKS, 128), lambda i: (jnp.minimum(i, BLOCKS - 1), 0)),
            pl.BlockSpec((1, 1408), lambda i: (0, 0)), line, line,
        ],
        out_specs=[line] * 3,
        compiler_params=pltpu.CompilerParams(vmem_limit_bytes=48 * 2**20),
    )(mean, tail, master, momentum)


def mean_kernel(diff, tail, mean, tail_mean, part, mid, buf, tails, ss, rs, ts, tr):
    g, t, z, c, gx, gy = place()
    peers = [gx, gy, 3 - g]
    greet([(peer, t) for peer in peers], 3)
    xi, yi = lax.rem(g, 2), lax.div(g, 2)
    hop = [((gx, t), (gy, t)), ((gy, t), (gx, t))]
    mine = [(xi, yi), (yi, xi)]

    def at(h, i, j):
        return h * SUM_H + i * SUM_Q + j * SUM_E

    def to_sum(h, e):
        a, b = mine[h]
        j = 1 - b if e == 0 else b
        src = rows_at(diff, at(h, 1 - a, j), SUM_E)
        return remote(src, part.at[h, e], ss.at[h, e], rs.at[h, e], hop[h][0])

    def over(h):
        return remote(mid.at[h], buf.at[h], ss.at[h, 2], rs.at[h, 2], hop[h][1])

    def share(h, e):
        a, b = mine[h]
        block = rows_at(mean, at(h, a, 1 - b if e == 2 else b), SUM_E)
        return remote(block, block, ss.at[h, 3 + e], rs.at[h, 3 + e], hop[h][1 if e == 0 else 0])

    def landed(h, e):
        a, b = mine[h]
        block = rows_at(mean, at(h, a, 1 - b) if e == 0 else at(h, 1 - a, 1 - b if e == 2 else b), SUM_E)
        remote(block, block, ss.at[h, 3 + e], rs.at[h, 3 + e], hop[h][0]).wait_recv()

    def add(fn):
        def body(i, _):
            fn(pl.multiple_of(i * 96, 96))
            return 0
        lax.fori_loop(0, SUM_E // 96, body, 0)

    for e in (0, 1):
        for h in (0, 1):
            to_sum(h, e).start()
    t_copies = [remote(tail, tails.at[k], ts.at[k], tr.at[k], (peers[k], t)) for k in range(3)]
    for copy in t_copies:
        copy.start()
    for h in (0, 1):
        a, b = mine[h]
        to_sum(h, 0).wait_recv()

        def first(i):
            total = diff[pl.ds(pl.multiple_of(at(h, a, 1 - b) + i, 32), 96), :].astype(F32)
            mid[h, pl.ds(i, 96), :] = (total + part[h, 0, pl.ds(i, 96), :].astype(F32)).astype(BF16)
        add(first)
        over(h).start()
    for h in (0, 1):
        a, b = mine[h]
        to_sum(h, 1).wait_recv()
        over(h).wait_recv()

        def second(i):
            here = pl.ds(pl.multiple_of(at(h, a, b) + i, 32), 96)
            local = pl.ds(i, 96)
            total = diff[here, :].astype(F32) + part[h, 1, local, :].astype(F32) + buf[h, local, :].astype(F32)
            mean[here, :] = (total * 0.25).astype(BF16)
        add(second)
        share(h, 0).start()
        share(h, 1).start()
    for copy in t_copies:
        copy.wait_recv()
    tail_mean[...] = (tail[...] + tails[0] + tails[1] + tails[2]) * 0.25
    for h in (0, 1):
        landed(h, 0)
        share(h, 2).start()
    for h in (0, 1):
        landed(h, 1)
        landed(h, 2)
        for e in (0, 1):
            to_sum(h, e).wait_send()
        over(h).wait_send()
        for e in range(3):
            share(h, e).wait_send()
    for copy in t_copies:
        copy.wait_send()


def mean_groups(diff, tail):
    vm = pl.BlockSpec(memory_space=pltpu.VMEM)
    S = jax.ShapeDtypeStruct
    V = pltpu.VMEM
    return pl.pallas_call(
        mean_kernel,
        name="mean_groups",
        out_shape=[S((PARTS, 128), BF16), S((1, 1408), F32)],
        in_specs=[vm] * 2,
        out_specs=[vm] * 2,
        scratch_shapes=[
            V((2, 2, SUM_E, 128), BF16), V((2, SUM_E, 128), BF16), V((2, SUM_E, 128), BF16), V((3, 1, 1408), F32),
            DMA((2, 6)), DMA((2, 6)), DMA((3,)), DMA((3,)),
        ],
        compiler_params=pltpu.CompilerParams(collective_id=2, has_side_effects=True),
    )(diff, tail)


def on_small_slice(tokens, cotangent, crop_lengths, master, first_moment, second_moment, outer_momentum):
    wa, wb, wc, vec, fb1, normed, projected, attended, lse = front(crop_lengths, master, tokens)
    block_output, slope, normed_two, hidden, vg = forward(
        crop_lengths, tokens, cotangent, attended, wa, wb, wc.reshape(MLP, D), vec, fb1
    )
    input_grad, grad_lin, sv, sq = back(
        crop_lengths, vec, vg, tokens, cotangent, wa, wb, wc.reshape(MLP, D), attended, slope, hidden, normed_two,
        normed, projected, lse
    )
    moment_one, moment_two, difference, tail, vector_part, norm = adam_step(
        grad_lin, sv, sq, master, first_moment, second_moment
    )
    mean, tail_mean = mean_groups(difference, tail)
    mean_difference, outer_new, new_weights = outer_step(mean, tail_mean, master, outer_momentum)
    return (
        block_output,
        input_grad,
        norm.reshape(1),
        vector_part,
        moment_one,
        moment_two,
        mean_difference,
        outer_new,
        new_weights,
    )


def solution(mesh):
    small = mesh.shape["grp"] == 4 and mesh.shape["tok"] == 8
    return jax.shard_map(
        on_small_slice if small else on_device,
        mesh=mesh,
        in_specs=(
            P(("grp", "tok"), None),
            P(("grp", "tok"), None),
            P(("grp", "tok"), None),
            P("tok"),
            P("grp", "tok"),
            P("grp", "tok"),
            P("tok"),
        ),
        out_specs=(
            P(("grp", "tok"), None),
            P(("grp", "tok"), None),
            P("grp"),
            P("grp", "tok"),
            P("grp", "tok"),
            P("grp", "tok"),
            P("tok"),
            P("tok"),
            P("tok"),
        ),
        check_vma=False,
    )
```
